32 devices in a mesh: gx: 8 (over z, core), gy: 4 (over y, x).
Axes of the slice: x: 2, y: 2, z: 4, core: 2. Of those that a mesh axis runs over, the one named last changes fastest.
Arguments:
- currents: bfloat16 [256, 128, 2, 128], P('gx', 'gy'), may hold values from -6 to 6
- box_count: int32 [256, 128], P('gx', 'gy'), may hold values from 0 to 128, as said below
- aggregate: bfloat16 [256, 256], replicated, may hold values from -0.375 to 0.375
- near_blocks: bfloat16 [9, 256, 256], replicated, may hold values from -0.125 to 0.125
- low_translator: float32 [16, 2, 128], replicated, may hold values from -1.5 to 1.5
- child_to_parent: bfloat16 [4, 256, 512], replicated, may hold values from -0.1875 to 0.1875
- coarse_list: int32 [128, 64, 16], P('gx', 'gy'), may hold values from 0 to 1023
- coarse_kind: int32 [128, 64, 16], P('gx', 'gy'), may hold values from 0 to 63
- coarse_count: int32 [128, 64], P('gx', 'gy'), may hold values from 1 to 16, as said below
- up_translator: float32 [64, 2, 256], replicated, may hold values from -1.5 to 1.5
- parent_to_child: bfloat16 [4, 512, 256], replicated, may hold values from -0.25 to 0.25
- receive_map: bfloat16 [256, 256], replicated, may hold values from -0.375 to 0.375
Outputs:
- field: float32 [256, 128, 2, 128], P('gx', 'gy')
The draws below stay inside these ranges and needn't reach their ends.
Inputs may be any that keep to these rules, and one draw needn't show every extreme that they name: `box_count`: ground clutter makes some boxes full and most sparse; some box holds 128 unknowns and some none. `coarse_count`: some list uses all 16 entries.
All inputs are finite; a program needn't handle non-finite values.
Results may differ from the reference program's by a relative error of at most 0.0041.
Values may be sent and summed in bfloat16 or wider, within the bound.
No kernel may reach another device: no remote copies, remote signals or barrier semaphores. Data moves between devices by JAX's collectives and lax.ppermute only.
A program may use at most 128 MiB of HBM per device.

```python
import jax
import jax.numpy as jnp
from jax import lax

U = 128
Q = 128
QC = 256
LIST = 16
NOFF = 64
NXB = 256
NYB = 128
CTX = 16
NCX = 128
NCY = 64
GROUP = 1024


def draw_box_count(key, part):
    first, second = jax.random.split(jax.random.fold_in(key, 11))
    sparse = jax.random.randint(first, (NXB, NYB), 0, U // 4 + 1)
    dense = jax.random.randint(second, (NXB, NYB), 0, 8) == 0
    counts = jnp.where(dense, U, sparse)
    counts = counts.at[0, 0].set(U)
    counts = counts.at[NXB - 1, NYB - 1].set(0)
    return counts.astype(jnp.int32)


def draw_coarse_count(key, part):
    counts = jax.random.randint(jax.random.fold_in(key, 23), (NCX, NCY), 1, LIST + 1)
    counts = counts.at[0, 0].set(LIST)
    counts = counts.at[NCX - 1, NCY - 1].set(1)
    return counts.astype(jnp.int32)


def touch_ends(entries, stream_key, least, top_value):
    shape = entries.shape
    place = [jax.random.randint(jax.random.fold_in(stream_key, axis), (), 0, shape[axis]) for axis in range(len(shape))]
    entries = entries.at[tuple(place)].set(least)
    longest = shape.index(max(shape))
    place[longest] = (place[longest] + 1) % shape[longest]
    return entries.at[tuple(place)].set(top_value)


def steps_of(stream_key, extent, cuts, smallest, high):
    loudness = 1.0
    for position, shards_of in cuts:
        heights = jax.random.uniform(jax.random.fold_in(jax.random.fold_in(stream_key, 6), position), (shards_of,), jnp.float32, smallest / len(cuts), high / len(cuts))
        loudness = loudness * jnp.repeat(jnp.exp(heights), extent[position] // shards_of).reshape((-1,) + (1,) * (len(extent) - 1 - position))
    return loudness


def scatter_about(key, extent, width, bound, cuts=(), kind=jnp.bfloat16):
    drawn = width * jax.random.normal(key, extent, jnp.float32)
    if cuts:
        drawn = drawn * steps_of(key, extent, cuts, -0.22, 0.18)
    return jnp.clip(drawn, -bound, bound).astype(kind)


def setup_inputs(seed: int = 0) -> dict:
    splits = jax.random.split(jax.random.key(seed), 13)
    currents = scatter_about(splits[0], (NXB, NYB, 2, U), 1.0, 6.0, ((0, 8), (1, 4)))
    box_count = draw_box_count(jax.random.fold_in(splits[12], 71), 0)
    aggregate = scatter_about(splits[2], (2 * U, 2 * Q), (2 * U) ** -0.5, 0.375)
    near_blocks = scatter_about(splits[3], (9, 2 * U, 2 * U), (18 * U) ** -0.5, 0.125)
    low_translator = scatter_about(splits[4], (16, 2, Q), 0.25, 1.5, (), jnp.float32)
    child_to_parent = scatter_about(splits[5], (4, 2 * Q, 2 * QC), (8 * Q) ** -0.5, 0.1875)
    coarse_list = touch_ends(jax.random.randint(splits[6], (NCX, NCY, LIST), 0, GROUP), jax.random.fold_in(splits[6], 1), 0, GROUP - 1).astype(jnp.int32)
    coarse_kind = touch_ends(jax.random.randint(splits[7], (NCX, NCY, LIST), 0, NOFF), jax.random.fold_in(splits[7], 1), 0, NOFF - 1).astype(jnp.int32)
    coarse_count = draw_coarse_count(jax.random.fold_in(splits[12], 71), 0)
    up_translator = scatter_about(splits[9], (NOFF, 2, QC), 0.25, 1.5, (), jnp.float32)
    parent_to_child = scatter_about(splits[10], (4, 2 * QC, 2 * Q), (2 * QC) ** -0.5, 0.25)
    receive_map = scatter_about(splits[11], (2 * Q, 2 * U), (2 * Q) ** -0.5, 0.375)
    return dict(currents=currents, box_count=box_count, aggregate=aggregate, near_blocks=near_blocks, low_translator=low_translator, child_to_parent=child_to_parent, coarse_list=coarse_list, coarse_kind=coarse_kind, coarse_count=coarse_count, up_translator=up_translator, parent_to_child=parent_to_child, receive_map=receive_map)


def complex_mul(table, pattern):
    real_part = pattern[..., 0, :].astype(jnp.float32)
    imag_part = pattern[..., 1, :].astype(jnp.float32)
    first = table[..., 0, :] * real_part - table[..., 1, :] * imag_part
    second = table[..., 0, :] * imag_part + table[..., 1, :] * real_part
    return jnp.stack([first, second], axis=-2)


def reference(currents, box_count, aggregate, near_blocks, low_translator, child_to_parent, coarse_list, coarse_kind, coarse_count, up_translator, parent_to_child, receive_map):
    boxes_x, boxes_y = box_count.shape
    mask = jnp.arange(U, dtype=jnp.int32)[None, None, :] < box_count[:, :, None]
    live = jnp.where(mask[:, :, None, :], currents, jnp.zeros_like(currents)).astype(jnp.bfloat16)
    flat_live = live.reshape(boxes_x * boxes_y, 2 * U)
    pattern = jnp.dot(flat_live, aggregate, preferred_element_type=jnp.float32).astype(jnp.bfloat16).reshape(boxes_x, boxes_y, 2, Q)
    padded = jnp.pad(pattern, ((2, 2), (2, 2), (0, 0), (0, 0)))
    lower_in = jnp.zeros((boxes_x, boxes_y, 2, Q), jnp.float32)
    offset = 0
    for shift_x in range(-2, 3):
        for shift_y in range(-2, 3):
            if max(abs(shift_x), abs(shift_y)) < 2:
                continue
            source = padded[2 + shift_x:2 + shift_x + boxes_x, 2 + shift_y:2 + shift_y + boxes_y]
            lower_in = lower_in + complex_mul(low_translator[offset], source)
            offset += 1
    parents_x, parents_y = boxes_x // 2, boxes_y // 2
    children = pattern.reshape(parents_x, 2, parents_y, 2, 2 * Q)
    coarse_sum = jnp.zeros((parents_x * parents_y, 2 * QC), jnp.float32)
    for half_x in range(2):
        for half_y in range(2):
            child = children[:, half_x, :, half_y].reshape(parents_x * parents_y, 2 * Q)
            coarse_sum = coarse_sum + jnp.dot(child, child_to_parent[2 * half_x + half_y], preferred_element_type=jnp.float32)
    coarse = coarse_sum.astype(jnp.bfloat16).reshape(parents_x * parents_y, 2, QC)
    group_base = ((jnp.arange(parents_x, dtype=jnp.int32) // CTX) * GROUP)[:, None]

    def accumulate(slot, total):
        target = group_base + coarse_list[:, :, slot]
        source = coarse[target]
        table = up_translator[coarse_kind[:, :, slot]]
        term = complex_mul(table, source)
        keep = slot < coarse_count
        return total + jnp.where(keep[:, :, None, None], term, jnp.zeros_like(term))

    coarse_acc = lax.fori_loop(0, LIST, accumulate, jnp.zeros((parents_x, parents_y, 2, QC), jnp.float32))
    coarse_in = coarse_acc.astype(jnp.bfloat16).reshape(parents_x * parents_y, 2 * QC)
    pieces = [jnp.dot(coarse_in, parent_to_child[child_id], preferred_element_type=jnp.float32).reshape(parents_x, parents_y, 2 * Q) for child_id in range(4)]
    rows_a = jnp.stack([pieces[0], pieces[1]], axis=2)
    rows_b = jnp.stack([pieces[2], pieces[3]], axis=2)
    from_parent = jnp.stack([rows_a, rows_b], axis=1).reshape(boxes_x, boxes_y, 2 * Q)
    incoming = (lower_in.reshape(boxes_x, boxes_y, 2 * Q) + from_parent).astype(jnp.bfloat16)
    field = jnp.dot(incoming.reshape(boxes_x * boxes_y, 2 * Q), receive_map, preferred_element_type=jnp.float32)
    near_pad = jnp.pad(live, ((1, 1), (1, 1), (0, 0), (0, 0)))
    for shift_x in range(-1, 2):
        for shift_y in range(-1, 2):
            source = near_pad[1 + shift_x:1 + shift_x + boxes_x, 1 + shift_y:1 + shift_y + boxes_y].reshape(boxes_x * boxes_y, 2 * U)
            field = field + jnp.dot(source, near_blocks[3 * (shift_x + 1) + shift_y + 1], preferred_element_type=jnp.float32)
    field = field.reshape(boxes_x, boxes_y, 2, U) * mask[:, :, None, :].astype(jnp.float32)
    return field
```

```python
import functools

import jax
import jax.numpy as jnp
from jax import lax
from jax.experimental import pallas as pl
from jax.experimental.pallas import tpu as pltpu
from jax.sharding import PartitionSpec as P

F32 = jnp.float32
BF16 = jnp.bfloat16
MIB = 1 << 20


def vmem(count):
    return [pl.BlockSpec(memory_space=pltpu.VMEM)] * count


def params(mib):
    return pltpu.CompilerParams(vmem_limit_bytes=mib * MIB)


def cost(macs, moved):
    return pl.CostEstimate(flops=2 * macs, bytes_accessed=moved, transcendentals=0)


def mm(left, right):
    return jnp.dot(left, right, preferred_element_type=F32)


def count_rows(counts_ref, tile_x, tile_y, lanes):
    eye = lax.broadcasted_iota(jnp.int32, (tile_y, tile_y), 0) == lax.broadcasted_iota(
        jnp.int32, (tile_y, tile_y), 1
    )
    counts = counts_ref[...].astype(F32)
    diag = [
        jnp.where(eye, jnp.broadcast_to(counts[i : i + 1], (tile_y, tile_y)), 0.0) for i in range(tile_x)
    ]
    return mm(jnp.concatenate(diag, axis=0).astype(BF16), jnp.ones((tile_y, lanes), BF16))


def parents_kernel(tile_x, tile_y, cur_ref, counts_ref, agg_ref, up_ref, live_ref, coarse_ref, wide, pats):
    lanes = cur_ref.shape[1]
    wide[...] = cur_ref[...].astype(F32)
    boxes = tile_x * tile_y
    keep = lax.broadcasted_iota(jnp.int32, (boxes, lanes), 1).astype(F32) < count_rows(
        counts_ref, tile_x, tile_y, lanes
    )
    for part in range(2):
        live = jnp.where(keep, wide[pl.ds(part, boxes, stride=2), :], 0.0)
        live_ref[:, part * lanes : (part + 1) * lanes] = live.astype(BF16)
    pattern = mm(live_ref[...], agg_ref[...])
    half = pattern.shape[1] // 2
    pats[0] = pattern[:, :half]
    pats[1] = pattern[:, half:]
    children = []
    for side_x in range(2):
        for side_y in range(2):
            for part in range(2):
                rows = [
                    pats[part, pl.ds((2 * p + side_x) * tile_y + side_y, tile_y // 2, stride=2), :]
                    for p in range(tile_x // 2)
                ]
                children.append(jnp.concatenate(rows, axis=0).astype(BF16))
    coarse_ref[...] = mm(jnp.concatenate(children, axis=1), up_ref[...]).astype(BF16)


LEFT = 8


def local_kernel(
    tile_x, tile_y, live_ref, top_ref, bottom_ref, left_ref, right_ref, agg_ref, near_ref, low_ref,
    lower_ref, field_ref, cells, sides, packed, pats, shifted,
):
    lanes = lower_ref.shape[2]
    width = tile_y + 2 * LEFT
    rows_x = tile_x + 4
    for part in range(2):
        cols = slice(part * lanes, (part + 1) * lanes)
        sides[0] = left_ref[:, cols].astype(F32)
        sides[1] = right_ref[:, cols].astype(F32)
        for i in range(rows_x):
            if i < 2:
                row = top_ref[i * tile_y : (i + 1) * tile_y, cols]
            elif i < tile_x + 2:
                row = live_ref[(i - 2) * tile_y : (i - 1) * tile_y, cols]
            else:
                row = bottom_ref[(i - tile_x - 2) * tile_y : (i - tile_x - 1) * tile_y, cols]
            base = i * width + LEFT
            cells[part, base : base + tile_y, :] = row.astype(F32)
            cells[part, base - 2 : base, :] = sides[0, 2 * i : 2 * i + 2, :]
            cells[part, base + tile_y : base + tile_y + 2, :] = sides[1, 2 * i : 2 * i + 2, :]
        packed[:, cols] = cells[part].astype(BF16)
        for i in range(tile_x + 2):
            for shift in range(-1, 2):
                base = (i + 1) * width + LEFT + shift
                place = (2 * (shift + 1) + part) * lanes
                shifted[i * tile_y : (i + 1) * tile_y, place : place + lanes] = cells[
                    part, base : base + tile_y, :
                ].astype(BF16)
    pattern = mm(packed[...], agg_ref[...]).astype(BF16).astype(F32)
    pats[0] = pattern[:, :lanes]
    pats[1] = pattern[:, lanes:]

    offsets = [
        (dx, dy) for dx in range(-2, 3) for dy in range(-2, 3) if max(abs(dx), abs(dy)) == 2
    ]

    def lower_row(i, carry):
        first = jnp.zeros((tile_y, lanes), F32)
        second = jnp.zeros((tile_y, lanes), F32)
        for k, (dx, dy) in enumerate(offsets):
            start = (i + 2 + dx) * width + (LEFT + dy)
            real = pats[0, pl.ds(start, tile_y), :]
            imag = pats[1, pl.ds(start, tile_y), :]
            t_real = low_ref[2 * k : 2 * k + 1, :]
            t_imag = low_ref[2 * k + 1 : 2 * k + 2, :]
            first = first + (t_real * real - t_imag * imag)
            second = second + (t_real * imag + t_imag * real)
        lower_ref[0, pl.ds(pl.multiple_of(i * tile_y, tile_y), tile_y), :] = first
        lower_ref[1, pl.ds(pl.multiple_of(i * tile_y, tile_y), tile_y), :] = second
        return carry

    lax.fori_loop(0, tile_x, lower_row, 0)
    depth = near_ref.shape[1]
    for block in range(4):
        size = tile_x * tile_y // 4
        total = None
        for shift in range(3):
            start = block * size + shift * tile_y
            term = mm(shifted[start : start + size, :], near_ref[shift])
            total = term if total is None else total + term
        field_ref[0, block * size : (block + 1) * size, :] = total[:, :lanes]
        field_ref[1, block * size : (block + 1) * size, :] = total[:, lanes:]


STEP = 2


def lists_kernel(chunks, tile_x, tile_y, *refs):
    sources = refs[:chunks]
    (codes_ref, kinds_ref, table_ref, counts_ref, lower_ref, near_ref, down_ref, recv_ref, out_ref,
     group, pieces, picks, kind_picks, incoming, kept) = refs[chunks:]
    parents_x, parents_y = tile_x // 2, tile_y // 2
    parents = parents_x * parents_y
    slots = codes_ref.shape[1]
    kinds, wide = table_ref.shape
    half = wide // 2
    lanes = lower_ref.shape[2]
    for c in range(chunks):
        group[c * parents : (c + 1) * parents, :] = sources[c][...]
    table = table_ref[...]
    high = table.astype(BF16)
    middle = (table - high.astype(F32)).astype(BF16)
    low = (table - high.astype(F32) - middle.astype(F32)).astype(BF16)
    pieces[0:kinds, :] = high
    pieces[kinds : 2 * kinds, :] = middle
    pieces[2 * kinds : 3 * kinds, :] = low
    lane = lax.broadcasted_iota(jnp.int32, (parents_y, 128), 1)
    kind_of = lax.rem(lane, kinds)

    def step(n, carry):
        for k in range(STEP):
            start = pl.multiple_of((n * STEP + k) * parents_y, parents_y)
            codes = codes_ref[pl.ds(start, parents_y), :]
            kind = kinds_ref[pl.ds(start, parents_y), :]
            for s in range(slots):
                row = (k * slots + s) * parents_y
                code = jnp.broadcast_to(codes[:, s : s + 1], (parents_y, 128))
                for c in range(chunks * parents // 128):
                    picks[row : row + parents_y, c * 128 : (c + 1) * 128] = jnp.where(
                        code == lane + c * 128, 1.0, 0.0
                    ).astype(BF16)
                which = jnp.broadcast_to(kind[:, s : s + 1], (parents_y, 128))
                hit = jnp.where(which == kind_of, 1.0, 0.0).astype(BF16)
                kind_picks[row : row + parents_y, 0:128] = hit
                kind_picks[row : row + parents_y, 128 : 3 * kinds] = hit[:, : 3 * kinds - 128]
        gathered = mm(picks[...], group[...])
        factors = mm(kind_picks[...], pieces[...])
        for k in range(STEP):
            first = jnp.zeros((parents_y, half), F32)
            second = jnp.zeros((parents_y, half), F32)
            for s in range(slots):
                row = slice((k * slots + s) * parents_y, (k * slots + s + 1) * parents_y)
                t_real, t_imag = factors[row, :half], factors[row, half:]
                real, imag = gathered[row, :half], gathered[row, half:]
                first = first + (t_real * real - t_imag * imag)
                second = second + (t_real * imag + t_imag * real)
            start = pl.multiple_of((n * STEP + k) * parents_y, parents_y)
            incoming[pl.ds(start, parents_y), :half] = first.astype(BF16)
            incoming[pl.ds(start, parents_y), half:] = second.astype(BF16)
        return carry

    lax.fori_loop(0, parents_x // STEP, step, 0)

    limits = count_rows(counts_ref, tile_x, tile_y, lanes)
    kept[...] = jnp.where(
        lax.broadcasted_iota(jnp.int32, limits.shape, 1).astype(F32) < limits, 1.0, 0.0
    )
    for side_x in range(2):
        for side_y in range(2):
            down = mm(incoming[...], down_ref[2 * side_x + side_y])
            starts = [(2 * p + side_x) * tile_y + side_y for p in range(parents_x)]

            def rows_of(ref, part):
                return jnp.concatenate(
                    [ref[part, pl.ds(start, parents_y, stride=2), :] for start in starts], axis=0
                )

            total = jnp.concatenate(
                [down[:, part * lanes : (part + 1) * lanes] + rows_of(lower_ref, part) for part in range(2)],
                axis=1,
            )
            field = mm(total.astype(BF16), recv_ref[...])
            mask = jnp.concatenate(
                [kept[pl.ds(start, parents_y, stride=2), :] for start in starts], axis=0
            )
            for part in range(2):
                value = (field[:, part * lanes : (part + 1) * lanes] + rows_of(near_ref, part)) * mask
                for p, start in enumerate(starts):
                    out_ref[pl.ds(2 * start + part, parents_y, stride=4), :] = value[
                        p * parents_y : (p + 1) * parents_y
                    ]


def shifts_of(count):
    up = [(i, i + 1) for i in range(count - 1)]
    return up, [(b, a) for a, b in up]


def body(
    currents, box_count, aggregate, near_blocks, low_translator, child_to_parent, coarse_list,
    coarse_kind, coarse_count, up_translator, parent_to_child, receive_map,
):
    tile_x, tile_y = box_count.shape
    boxes = tile_x * tile_y
    lanes = currents.shape[-1]
    parents_x, parents_y, slots = coarse_list.shape
    parents = parents_x * parents_y
    kinds, _, half = up_translator.shape
    wide = 2 * half
    chunks = lax.axis_size("gy")

    live, coarse = pl.pallas_call(
        functools.partial(parents_kernel, tile_x, tile_y),
        name="parents",
        out_shape=[
            jax.ShapeDtypeStruct((boxes, 2 * lanes), BF16),
            jax.ShapeDtypeStruct((parents, wide), BF16),
        ],
        in_specs=vmem(4),
        out_specs=vmem(2),
        scratch_shapes=[pltpu.VMEM((2 * boxes, lanes), F32), pltpu.VMEM((2, boxes, lanes), F32)],
        compiler_params=params(32),
        cost_estimate=cost(200 * MIB, 3 * MIB),
    )(
        currents.reshape(2 * boxes, lanes),
        box_count,
        aggregate,
        child_to_parent.reshape(8 * lanes, wide),
    )

    sources = [coarse] + [
        lax.ppermute(coarse, "gy", [(i, i ^ d) for i in range(chunks)]) for d in range(1, chunks)
    ]
    up, down = shifts_of(lax.axis_size("gx"))
    top = lax.ppermute(live[boxes - 2 * tile_y :], "gx", up)
    bottom = lax.ppermute(live[: 2 * tile_y], "gx", down)
    tall = jnp.concatenate([top, live, bottom], axis=0).reshape(tile_x + 4, tile_y, 2 * lanes)

    def edge(cells):
        cells = cells.reshape(2 * (tile_x + 4), 2 * lanes)
        return jnp.pad(cells, ((0, -cells.shape[0] % 16), (0, 0)))

    up, down = shifts_of(chunks)
    left = lax.ppermute(edge(tall[:, tile_y - 2 :]), "gy", up)
    right = lax.ppermute(edge(tall[:, :2]), "gy", down)

    width = tile_y + 2 * LEFT
    lower, near = pl.pallas_call(
        functools.partial(local_kernel, tile_x, tile_y),
        name="local",
        out_shape=[
            jax.ShapeDtypeStruct((2, boxes, lanes), F32),
            jax.ShapeDtypeStruct((2, boxes, lanes), F32),
        ],
        in_specs=vmem(8),
        out_specs=vmem(2),
        scratch_shapes=[
            pltpu.VMEM((2, (tile_x + 4) * width, lanes), F32),
            pltpu.VMEM((2,) + (left.shape[0], lanes), F32),
            pltpu.VMEM(((tile_x + 4) * width, 2 * lanes), BF16),
            pltpu.VMEM((2, (tile_x + 4) * width, lanes), F32),
            pltpu.VMEM(((tile_x + 2) * tile_y, 6 * lanes), BF16),
        ],
        compiler_params=params(48),
        cost_estimate=cost(2000 * MIB, 5 * MIB),
    )(
        live, top, bottom, left, right, aggregate,
        near_blocks.reshape(3, 6 * lanes, 2 * lanes),
        low_translator.reshape(-1, lanes),
    )

    me = lax.axis_index("gy")
    across = parents_y * chunks
    row, column = coarse_list // across, coarse_list % across
    place = (column // parents_y) ^ me
    codes = place * parents + row * parents_y + column % parents_y
    used = lax.broadcasted_iota(jnp.int32, codes.shape, 2) < coarse_count[:, :, None]
    codes = jnp.where(used, codes, -1).reshape(parents, slots)

    out = pl.pallas_call(
        functools.partial(lists_kernel, chunks, tile_x, tile_y),
        name="lists",
        out_shape=jax.ShapeDtypeStruct((2 * boxes, lanes), F32),
        in_specs=vmem(chunks + 8),
        out_specs=pl.BlockSpec(memory_space=pltpu.VMEM),
        scratch_shapes=[
            pltpu.VMEM((chunks * parents, wide), BF16),
            pltpu.VMEM((3 * kinds, wide), BF16),
            pltpu.VMEM((STEP * slots * parents_y, chunks * parents), BF16),
            pltpu.VMEM((STEP * slots * parents_y, 3 * kinds), BF16),
            pltpu.VMEM((parents, wide), BF16),
            pltpu.VMEM((boxes, lanes), F32),
        ],
        compiler_params=params(56),
        cost_estimate=cost(3000 * MIB, 8 * MIB),
    )(
        *sources, codes, coarse_kind.reshape(parents, slots),
        up_translator.reshape(kinds, wide), box_count, lower, near, parent_to_child, receive_map,
    )
    return out.reshape(tile_x, tile_y, 2, lanes)


def solution(mesh):
    tiles = P("gx", "gy")
    in_specs = (tiles, tiles, P(), P(), P(), P(), tiles, tiles, tiles, P(), P(), P())
    return jax.shard_map(body, mesh=mesh, in_specs=in_specs, out_specs=tiles, check_vma=False)
```

```python
import functools

import jax
import jax.numpy as jnp
from jax import lax
from jax.experimental import pallas as pl
from jax.experimental.pallas import tpu as pltpu
from jax.sharding import PartitionSpec as P

F32 = jnp.float32
BF16 = jnp.bfloat16
MIB = 1 << 20


def vmem(count):
    return [pl.BlockSpec(memory_space=pltpu.VMEM)] * count


def hbm(array):
    return pltpu.with_memory_space_constraint(array, pltpu.HBM)


def params(mib):
    return pltpu.CompilerParams(vmem_limit_bytes=mib * MIB)


def cost(macs, moved):
    return pl.CostEstimate(flops=2 * macs, bytes_accessed=moved, transcendentals=0)


def mm(left, right):
    return jnp.dot(left, right, preferred_element_type=F32)


def count_rows(counts_ref, tile_x, tile_y, lanes):
    eye = lax.broadcasted_iota(jnp.int32, (tile_y, tile_y), 0) == lax.broadcasted_iota(
        jnp.int32, (tile_y, tile_y), 1
    )
    counts = counts_ref[...].astype(F32)
    diag = [
        jnp.where(eye, jnp.broadcast_to(counts[i : i + 1], (tile_y, tile_y)), 0.0) for i in range(tile_x)
    ]
    return mm(jnp.concatenate(diag, axis=0).astype(BF16), jnp.ones((tile_y, lanes), BF16))


def parents_kernel(
    tile_x, tile_y, cur_hbm, counts_hbm, agg_hbm, up_hbm, live_ref, coarse_ref,
    cur_ref, counts_ref, agg_ref, up_ref, wide, pats, rows4, sems,
):
    loads = [
        pltpu.make_async_copy(source, target, sems.at[k])
        for k, (source, target) in enumerate(
            [(counts_hbm, counts_ref), (cur_hbm, cur_ref), (agg_hbm, agg_ref), (up_hbm, up_ref)]
        )
    ]
    for load in loads:
        load.start()
    lanes = cur_ref.shape[1]
    boxes = tile_x * tile_y
    loads[0].wait()
    keep = lax.broadcasted_iota(jnp.int32, (boxes, lanes), 1).astype(F32) < count_rows(
        counts_ref, tile_x, tile_y, lanes
    )
    loads[1].wait()
    wide[...] = cur_ref[...].astype(F32)
    for part in range(2):
        live = jnp.where(keep, wide[pl.ds(part, boxes, stride=2), :], 0.0)
        live_ref[:, part * lanes : (part + 1) * lanes] = live.astype(BF16)
    loads[2].wait()
    pattern = mm(live_ref[...], agg_ref[...])
    pats[0] = pattern[:, :lanes]
    pats[1] = pattern[:, lanes:]
    children = []
    for side_x in range(2):
        for side_y in range(2):
            for part in range(2):
                rows = [
                    pats[part, pl.ds((2 * p + side_x) * tile_y + side_y, tile_y // 2, stride=2), :]
                    for p in range(tile_x // 2)
                ]
                children.append(jnp.concatenate(rows, axis=0).astype(BF16))
    loads[3].wait()
    coarse = mm(jnp.concatenate(children, axis=1), up_ref[...])
    for place, column in enumerate((0, 2, 1, 3)):
        rows4[pl.ds(place, coarse.shape[0], stride=4), :] = coarse[:, column * 128 : (column + 1) * 128]
    coarse_ref[...] = rows4[...].astype(BF16)


LEFT = 8
OFFSETS = [(dx, dy) for dx in range(-2, 3) for dy in range(-2, 3) if max(abs(dx), abs(dy)) == 2]
BLOCK = 8


def local_kernel(
    tile_x, tile_y, live_ref, top_ref, bottom_ref, agg_ref, near_ref, low_ref,
    lower_ref, field_ref, cells, packed, pats, shifted, tables,
):
    lanes = lower_ref.shape[2]
    width = tile_y + 2 * LEFT
    none = jnp.zeros((LEFT, lanes), F32)
    for part in range(2):
        cols = slice(part * lanes, (part + 1) * lanes)
        for i in range(tile_x + 4):
            if i < 2:
                row = top_ref[i * tile_y : (i + 1) * tile_y, cols]
            elif i < tile_x + 2:
                row = live_ref[(i - 2) * tile_y : (i - 1) * tile_y, cols]
            else:
                row = bottom_ref[(i - tile_x - 2) * tile_y : (i - tile_x - 1) * tile_y, cols]
            base = i * width
            cells[part, base : base + LEFT, :] = none
            cells[part, base + LEFT : base + LEFT + tile_y, :] = row.astype(F32)
            cells[part, base + LEFT + tile_y : base + width, :] = none
        packed[:, cols] = cells[part].astype(BF16)
        for i in range(tile_x + 2):
            for shift in range(-1, 2):
                base = (i + 1) * width + LEFT + shift
                place = (2 * (shift + 1) + part) * lanes
                shifted[i * tile_y : (i + 1) * tile_y, place : place + lanes] = cells[
                    part, base : base + tile_y, :
                ].astype(BF16)
    pattern = mm(packed[...], agg_ref[...]).astype(BF16).astype(F32)
    pats[0] = pattern[:, :lanes]
    pats[1] = pattern[:, lanes:]
    pats[2] = pattern[:, :lanes] + pattern[:, lanes:]
    for k in range(len(OFFSETS)):
        t_real, t_imag = low_ref[2 * k : 2 * k + 1, :], low_ref[2 * k + 1 : 2 * k + 2, :]
        tables[3 * k : 3 * k + 1, :] = t_real
        tables[3 * k + 1 : 3 * k + 2, :] = t_imag - t_real
        tables[3 * k + 2 : 3 * k + 3, :] = t_imag + t_real

    def rows_block(block, carry):
        total = None
        size = BLOCK * tile_y
        for shift in range(3):
            start = pl.multiple_of(block * size + shift * tile_y, tile_y)
            term = mm(shifted[pl.ds(start, size), :], near_ref[shift])
            total = term if total is None else total + term
        start = pl.multiple_of(block * size, size)
        field_ref[0, pl.ds(start, size), :] = total[:, :lanes]
        field_ref[1, pl.ds(start, size), :] = total[:, lanes:]
        origin = pl.multiple_of(block * (BLOCK * width), 8)
        for i in range(BLOCK):
            both = jnp.zeros((tile_y, lanes), F32)
            first = jnp.zeros((tile_y, lanes), F32)
            second = jnp.zeros((tile_y, lanes), F32)
            for k, (dx, dy) in enumerate(OFFSETS):
                rows = pl.ds(origin + ((i + 2 + dx) * width + LEFT + dy), tile_y)
                both = both + tables[3 * k : 3 * k + 1, :] * pats[2, rows, :]
                first = first + tables[3 * k + 1 : 3 * k + 2, :] * pats[0, rows, :]
                second = second + tables[3 * k + 2 : 3 * k + 3, :] * pats[1, rows, :]
            place = pl.ds(pl.multiple_of(start + i * tile_y, tile_y), tile_y)
            lower_ref[0, place, :] = both - second
            lower_ref[1, place, :] = both + first
        return carry

    lax.fori_loop(0, tile_x // BLOCK, rows_block, 0)


def columns_kernel(
    tile_x, tile_y, left_ref, right_ref, agg_ref, near_ref, low_ref, lower_in, field_in,
    lower_ref, field_ref, cells, pats,
):
    lanes = lower_ref.shape[2]
    lower_ref[...] = lower_in[...]
    field_ref[...] = field_in[...]
    for side, ref in enumerate((left_ref, right_ref)):
        pattern = mm(ref[...], agg_ref[...]).astype(BF16).astype(F32)
        for part in range(2):
            cols = slice(part * lanes, (part + 1) * lanes)
            cells[part] = ref[:, cols].astype(F32)
            pats[part] = pattern[:, cols]

        def column(store, part, place, dx):
            return store[part, pl.ds(2 * (2 + dx) + place, tile_x, stride=2), :]

        pairs = [(0, 0, -2), (0, 1, -1), (1, 1, -2)]
        if side:
            pairs = [(tile_y - 1, 1, 2), (tile_y - 1, 0, 1), (tile_y - 2, 0, 2)]
        sums = {}
        for box, place, dy in pairs:
            for dx in range(-2, 3):
                if (dx, dy) not in OFFSETS:
                    continue
                k = OFFSETS.index((dx, dy))
                t_real, t_imag = low_ref[2 * k : 2 * k + 1, :], low_ref[2 * k + 1 : 2 * k + 2, :]
                real, imag = column(pats, 0, place, dx), column(pats, 1, place, dx)
                first, second = sums.get(box, (0.0, 0.0))
                sums[box] = (
                    first + (t_real * real - t_imag * imag), second + (t_real * imag + t_imag * real)
                )
        for box, values in sums.items():
            for part in range(2):
                rows = pl.ds(box, tile_x, stride=tile_y)
                lower_ref[part, rows, :] = lower_ref[part, rows, :] + values[part]
        place, box = (0, tile_y - 1) if side else (1, 0)
        total = None
        for dx in range(-1, 2):
            source = jnp.concatenate([column(cells, part, place, dx) for part in range(2)], axis=1)
            start = 4 * lanes if side else 0
            term = mm(source.astype(BF16), near_ref[dx + 1, start : start + 2 * lanes, :])
            total = term if total is None else total + term
        for part in range(2):
            rows = pl.ds(box, tile_x, stride=tile_y)
            field_ref[part, rows, :] = field_ref[part, rows, :] + total[:, part * lanes : (part + 1) * lanes]


GROUP = 8


def lists_kernel(chunks, tile_x, tile_y, *refs):
    sources = refs[:chunks]
    (source_rows, table_rows, table_ref, counts_ref, lower_ref, near_ref, down_ref, recv_ref, out_ref,
     cells, table8, sums, kept) = refs[chunks:]
    parents_x, parents_y = tile_x // 2, tile_y // 2
    parents = parents_x * parents_y
    slots = source_rows.shape[0] // parents
    kinds = table_ref.shape[0] // 4
    lanes = lower_ref.shape[2]
    for place, row in enumerate((0, 0, 2, 2, 1, 1, 3, 3)):
        table8[pl.ds(place, kinds, stride=8), :] = table_ref[pl.ds(row, kinds, stride=4), :]
    table8[8 * kinds : 8 * kinds + 8, :] = jnp.zeros((8, lanes), F32)
    for c in range(chunks):
        rows = sources[c][...].astype(F32).reshape(parents // 2, 8, lanes)
        for half in range(2):
            own = rows[:, 4 * half : 4 * half + 4, :]
            cells[c * (parents // 2) : (c + 1) * (parents // 2), half] = jnp.concatenate([own, own], axis=1)

    def step(n, carry):
        for k in range(GROUP):
            first = n * (GROUP * slots) + k * slots
            total = [None, None]
            for s in range(slots):
                source = source_rows[first + s]
                kind = pl.multiple_of(table_rows[first + s], 8)
                term = cells_flat[pl.ds(pl.multiple_of(source, 8), 8), :] * table8[pl.ds(kind, 8), :]
                total[s % 2] = term if total[s % 2] is None else total[s % 2] + term
            sums[pl.ds(pl.multiple_of((n * GROUP + k) * 8, 8), 8), :] = total[0] + total[1]
        return carry

    cells_flat = cells.reshape(chunks * parents * 8, lanes)
    lax.fori_loop(0, parents // GROUP, step, 0)

    def row(place):
        return sums[pl.ds(place, parents, stride=8), :]

    incoming = jnp.concatenate(
        [row(0) - row(5), row(2) - row(7), row(1) + row(4), row(3) + row(6)], axis=1
    ).astype(BF16)
    limits = count_rows(counts_ref, tile_x, tile_y, lanes)
    kept[...] = jnp.where(
        lax.broadcasted_iota(jnp.int32, limits.shape, 1).astype(F32) < limits, 1.0, 0.0
    )
    for side_x in range(2):
        for side_y in range(2):
            down = mm(incoming, down_ref[2 * side_x + side_y])
            starts = [(2 * p + side_x) * tile_y + side_y for p in range(parents_x)]

            def rows_of(ref, part):
                return jnp.concatenate(
                    [ref[part, pl.ds(start, parents_y, stride=2), :] for start in starts], axis=0
                )

            total = jnp.concatenate(
                [down[:, part * lanes : (part + 1) * lanes] + rows_of(lower_ref, part) for part in range(2)],
                axis=1,
            )
            field = mm(total.astype(BF16), recv_ref[...])
            mask = jnp.concatenate(
                [kept[pl.ds(start, parents_y, stride=2), :] for start in starts], axis=0
            )
            for part in range(2):
                value = (field[:, part * lanes : (part + 1) * lanes] + rows_of(near_ref, part)) * mask
                for p, start in enumerate(starts):
                    out_ref[pl.ds(2 * start + part, parents_y, stride=4), :] = value[
                        p * parents_y : (p + 1) * parents_y
                    ]


def swap(first, last, axis):
    count = lax.axis_size(axis)
    odd = lax.axis_index(axis) % 2 == 1
    low = [(i, i ^ 1) for i in range(count)]
    high = [(i, (i ^ 1) if i in (0, count - 1) else ((i + 1) ^ 1) - 1) for i in range(count)]
    high = [(i, j) for i, j in high if i not in (0, count - 1)]
    inner = lax.ppermute(jnp.where(odd, first, last), axis, low)
    outer = lax.ppermute(jnp.where(odd, last, first), axis, high)
    return jnp.where(odd, inner, outer), jnp.where(odd, outer, inner)


def body(
    currents, box_count, aggregate, near_blocks, low_translator, child_to_parent, coarse_list,
    coarse_kind, coarse_count, up_translator, parent_to_child, receive_map,
):
    tile_x, tile_y = box_count.shape
    boxes = tile_x * tile_y
    lanes = currents.shape[-1]
    parents_x, parents_y, slots = coarse_list.shape
    parents = parents_x * parents_y
    kinds, _, half = up_translator.shape
    wide = 2 * half
    chunks = lax.axis_size("gy")

    live, coarse = pl.pallas_call(
        functools.partial(parents_kernel, tile_x, tile_y),
        name="parents",
        out_shape=[
            jax.ShapeDtypeStruct((boxes, 2 * lanes), BF16),
            jax.ShapeDtypeStruct((4 * parents, wide // 4), BF16),
        ],
        in_specs=[pl.BlockSpec(memory_space=pltpu.HBM)] * 4,
        out_specs=vmem(2),
        scratch_shapes=[
            pltpu.VMEM((2 * boxes, lanes), BF16),
            pltpu.VMEM((tile_x, tile_y), jnp.int32),
            pltpu.VMEM((2 * lanes, 2 * lanes), BF16),
            pltpu.VMEM((8 * lanes, wide), BF16),
            pltpu.VMEM((2 * boxes, lanes), F32),
            pltpu.VMEM((2, boxes, lanes), F32),
            pltpu.VMEM((4 * parents, wide // 4), F32),
            pltpu.SemaphoreType.DMA((4,)),
        ],
        compiler_params=params(24),
        cost_estimate=cost(200 * MIB, 3 * MIB),
    )(
        hbm(currents.reshape(2 * boxes, lanes)),
        hbm(box_count),
        hbm(aggregate),
        hbm(child_to_parent.reshape(8 * lanes, wide)),
    )

    sources = [coarse] + [
        lax.ppermute(coarse, "gy", [(i, i ^ d) for i in range(chunks)]) for d in range(1, chunks)
    ]
    top, bottom = swap(live[: 2 * tile_y], live[boxes - 2 * tile_y :], "gx")
    tall = jnp.concatenate([top, live, bottom], axis=0).reshape(tile_x + 4, tile_y, 2 * lanes)

    def edge(cells):
        cells = cells.reshape(2 * (tile_x + 4), 2 * lanes)
        return jnp.pad(cells, ((0, -cells.shape[0] % 16), (0, 0)))

    left, right = swap(edge(tall[:, :2]), edge(tall[:, tile_y - 2 :]), "gy")

    near_rows = near_blocks.reshape(3, 6 * lanes, 2 * lanes)
    low_rows = low_translator.reshape(-1, lanes)
    padded = (tile_x + 4) * (tile_y + 2 * LEFT)
    pair = [jax.ShapeDtypeStruct((2, boxes, lanes), F32)] * 2
    lower, near = pl.pallas_call(
        functools.partial(local_kernel, tile_x, tile_y),
        name="local",
        out_shape=pair,
        in_specs=vmem(6),
        out_specs=vmem(2),
        scratch_shapes=[
            pltpu.VMEM((2, padded, lanes), F32),
            pltpu.VMEM((padded, 2 * lanes), BF16),
            pltpu.VMEM((3, padded, lanes), F32),
            pltpu.VMEM(((tile_x + 2) * tile_y, 6 * lanes), BF16),
            pltpu.VMEM((3 * len(OFFSETS), lanes), F32),
        ],
        compiler_params=params(24),
        cost_estimate=cost(2000 * MIB, 5 * MIB),
    )(live, top, bottom, aggregate, near_rows, low_rows)

    lower, near = pl.pallas_call(
        functools.partial(columns_kernel, tile_x, tile_y),
        name="columns",
        out_shape=pair,
        in_specs=vmem(7),
        out_specs=vmem(2),
        scratch_shapes=[pltpu.VMEM((2, left.shape[0], lanes), F32)] * 2,
        compiler_params=params(16),
        cost_estimate=cost(100 * MIB, 5 * MIB),
    )(left, right, aggregate, near_rows, low_rows, lower, near)

    me = lax.axis_index("gy")
    across = parents_y * chunks
    row, column = coarse_list // across, coarse_list % across
    place = (column // parents_y) ^ me
    source_rows = 8 * (place * parents + row * parents_y + column % parents_y)
    used = lax.broadcasted_iota(jnp.int32, coarse_list.shape, 2) < coarse_count[:, :, None]
    table_rows = 8 * jnp.where(used, coarse_kind, kinds)
    table = up_translator.reshape(kinds, 2, 2, half // 2).transpose(0, 2, 1, 3).reshape(4 * kinds, half // 2)

    out = pl.pallas_call(
        functools.partial(lists_kernel, chunks, tile_x, tile_y),
        name="lists",
        out_shape=jax.ShapeDtypeStruct((2 * boxes, lanes), F32),
        in_specs=vmem(chunks) + [pl.BlockSpec(memory_space=pltpu.SMEM)] * 2 + vmem(6),
        out_specs=pl.BlockSpec(memory_space=pltpu.VMEM),
        scratch_shapes=[
            pltpu.VMEM((chunks * parents // 2, 2, 8, lanes), F32),
            pltpu.VMEM((8 * kinds + 8, lanes), F32),
            pltpu.VMEM((8 * parents, lanes), F32),
            pltpu.VMEM((boxes, lanes), F32),
        ],
        compiler_params=params(24 if chunks <= 4 else 48),
        cost_estimate=cost(3000 * MIB, 8 * MIB),
    )(
        *sources, source_rows.reshape(-1), table_rows.reshape(-1), table,
        box_count, lower, near, parent_to_child, receive_map,
    )
    return out.reshape(tile_x, tile_y, 2, lanes)


def solution(mesh):
    tiles = P("gx", "gy")
    in_specs = (tiles, tiles, P(), P(), P(), P(), tiles, tiles, tiles, P(), P(), P())
    return jax.shard_map(body, mesh=mesh, in_specs=in_specs, out_specs=tiles, check_vma=False)
```

```python
import functools

import jax
import jax.numpy as jnp
from jax import lax
from jax.experimental import pallas as pl
from jax.experimental.pallas import tpu as pltpu
from jax.sharding import PartitionSpec as P

F32 = jnp.float32
BF16 = jnp.bfloat16
MIB = 1 << 20


def vmem(count):
    return [pl.BlockSpec(memory_space=pltpu.VMEM)] * count


def hbm(array):
    return pltpu.with_memory_space_constraint(array, pltpu.HBM)


def params(mib):
    return pltpu.CompilerParams(vmem_limit_bytes=mib * MIB)


def cost(macs, moved):
    return pl.CostEstimate(flops=2 * macs, bytes_accessed=moved, transcendentals=0)


def mm(left, right):
    return jnp.dot(left, right, preferred_element_type=F32)


def count_rows(counts_ref, tile_x, tile_y, lanes):
    eye = lax.broadcasted_iota(jnp.int32, (tile_y, tile_y), 0) == lax.broadcasted_iota(
        jnp.int32, (tile_y, tile_y), 1
    )
    counts = counts_ref[...].astype(F32)
    diag = [
        jnp.where(eye, jnp.broadcast_to(counts[i : i + 1], (tile_y, tile_y)), 0.0) for i in range(tile_x)
    ]
    return mm(jnp.concatenate(diag, axis=0).astype(BF16), jnp.ones((tile_y, lanes), BF16))


def live_kernel(tile_x, tile_y, cur_hbm, counts_hbm, live_ref, kept_ref, low_ref, high_ref, cur_ref, counts_ref,
                wide, sems):
    loads = [
        pltpu.make_async_copy(counts_hbm, counts_ref, sems.at[0]),
        pltpu.make_async_copy(cur_hbm, cur_ref, sems.at[1]),
    ]
    for load in loads:
        load.start()
    lanes = cur_ref.shape[1]
    boxes = tile_x * tile_y
    loads[0].wait()
    limits = count_rows(counts_ref, tile_x, tile_y, lanes)
    keep = lax.broadcasted_iota(jnp.int32, (boxes, lanes), 1).astype(F32) < limits
    kept_ref[...] = jnp.where(keep, 1.0, 0.0)
    odd = lax.axis_index("gy") % 2 == 1
    loads[1].wait()
    wide[...] = cur_ref[...].astype(F32)
    for part in range(2):
        cols = slice(part * lanes, (part + 1) * lanes)
        live_ref[:, cols] = jnp.where(keep, wide[pl.ds(part, boxes, stride=2), :], 0.0).astype(BF16)

        def edge(column):
            rows = wide[pl.ds(2 * column + part, tile_x, stride=2 * tile_y), :]
            return rows * kept_ref[pl.ds(column, tile_x, stride=tile_y), :]

        first = jnp.concatenate([edge(0), edge(1)], axis=0).astype(BF16)
        last = jnp.concatenate([edge(tile_y - 2), edge(tile_y - 1)], axis=0).astype(BF16)
        low_ref[:, cols] = jnp.where(odd, first, last)
        high_ref[:, cols] = jnp.where(odd, last, first)


def parents_kernel(tile_x, tile_y, live_ref, agg_ref, up_ref, coarse_ref, pats, rows4):
    lanes = pats.shape[2]
    pattern = mm(live_ref[...], agg_ref[...])
    pats[0] = pattern[:, :lanes]
    pats[1] = pattern[:, lanes:]
    children = []
    for side_x in range(2):
        for side_y in range(2):
            for part in range(2):
                rows = [
                    pats[part, pl.ds((2 * p + side_x) * tile_y + side_y, tile_y // 2, stride=2), :]
                    for p in range(tile_x // 2)
                ]
                children.append(jnp.concatenate(rows, axis=0).astype(BF16))
    coarse = mm(jnp.concatenate(children, axis=1), up_ref[...])
    for place, column in enumerate((0, 2, 1, 3)):
        rows4[pl.ds(place, coarse.shape[0], stride=4), :] = coarse[:, column * 128 : (column + 1) * 128]
    coarse_ref[...] = rows4[...].astype(BF16)


def rims_kernel(tile_x, tile_y, live_ref, inner_ref, outer_ref, low_ref, high_ref, first, last):
    odd_y = lax.axis_index("gy") % 2 == 1
    odd_x = lax.axis_index("gx") % 2 == 1
    inner, outer = inner_ref[...].astype(F32), outer_ref[...].astype(F32)
    boxes = tile_x * tile_y
    sides = (jnp.where(odd_y, inner, outer), jnp.where(odd_y, outer, inner))
    for rim, start in ((first, 0), (last, tile_x - 2)):
        rim[0 : 2 * tile_y, :] = live_ref[start * tile_y : (start + 2) * tile_y, :].astype(F32)
        place = 2 * tile_y
        for side in sides:
            for column in range(2):
                at = column * tile_x + start
                rim[place : place + 2, :] = side[at : at + 2]
                place += 2
        rim[place:, :] = jnp.zeros((rim.shape[0] - place, rim.shape[1]), F32)
    low_ref[...] = jnp.where(odd_x, first[...], last[...]).astype(BF16)
    high_ref[...] = jnp.where(odd_x, last[...], first[...]).astype(BF16)


LEFT = 8
OFFSETS = [(dx, dy) for dx in range(-2, 3) for dy in range(-2, 3) if max(abs(dx), abs(dy)) == 2]


def local_kernel(
    tile_x, tile_y, live_ref, agg_ref, near_ref, low_ref, lower_ref, field_ref, cells, pats, shifted, tables, sums,
):
    lanes = lower_ref.shape[2]
    width = tile_y + 2 * LEFT
    none = jnp.zeros((LEFT, lanes), F32)
    pattern = mm(live_ref[...], agg_ref[...]).astype(BF16).astype(F32)
    values = [pattern[:, :lanes], pattern[:, lanes:], pattern[:, :lanes] + pattern[:, lanes:]]
    for i in range(tile_x):
        base = i * width
        rows = slice(i * tile_y, (i + 1) * tile_y)
        for k in range(3):
            pats[k, base : base + LEFT, :] = none
            pats[k, base + LEFT : base + LEFT + tile_y, :] = values[k][rows]
            pats[k, base + LEFT + tile_y : base + width, :] = none
    ends = jnp.zeros((tile_y, 6 * lanes), BF16)
    shifted[0:tile_y, :] = ends
    shifted[(tile_x + 1) * tile_y : (tile_x + 2) * tile_y, :] = ends
    shifted[tile_y : (tile_x + 1) * tile_y, 2 * lanes : 4 * lanes] = live_ref[...]
    for part in range(2):
        cols = slice(part * lanes, (part + 1) * lanes)
        for i in range(tile_x):
            base = i * width
            cells[part, base : base + LEFT, :] = none
            cells[part, base + LEFT : base + LEFT + tile_y, :] = live_ref[
                i * tile_y : (i + 1) * tile_y, cols
            ].astype(F32)
            cells[part, base + LEFT + tile_y : base + width, :] = none
            for shift in (-1, 1):
                place = (2 * (shift + 1) + part) * lanes
                shifted[(i + 1) * tile_y : (i + 2) * tile_y, place : place + lanes] = cells[
                    part, base + LEFT + shift : base + LEFT + shift + tile_y, :
                ].astype(BF16)
    for k in range(len(OFFSETS)):
        t_real, t_imag = low_ref[2 * k : 2 * k + 1, :], low_ref[2 * k + 1 : 2 * k + 2, :]
        for n, value in enumerate((t_imag - t_real, t_imag + t_real, t_real)):
            tables[3 * k + n] = jnp.broadcast_to(value, (8, lanes))

    passes = [
        [(dx, dy) for dx, dy in OFFSETS if dy == -2],
        [(dx, dy) for dx, dy in OFFSETS if dy == 2],
        [(dx, dy) for dx, dy in OFFSETS if abs(dy) < 2],
    ]
    blocks = tile_y // 8
    size = tile_x * tile_y // blocks

    def block(b, carry):
        total = None
        for shift in range(3):
            start = pl.multiple_of(b * size + shift * tile_y, tile_y)
            term = mm(shifted[pl.ds(start, size), :], near_ref[shift])
            total = term if total is None else total + term
        start = pl.multiple_of(b * size, size)
        field_ref[0, pl.ds(start, size), :] = total[:, :lanes]
        field_ref[1, pl.ds(start, size), :] = total[:, lanes:]
        shift_y = pl.multiple_of(b * 8, 8)
        for number, offsets in enumerate(passes):
            running = {}
            for row in range(tile_x):
                for dy in sorted({dy for _, dy in offsets}):
                    rows = pl.ds(shift_y + (row * width + LEFT + dy), 8)
                    source = [pats[k, rows, :] for k in range(3)]
                    for dx in range(-2, 3):
                        i = row - dx
                        if (dx, dy) not in offsets or not 0 <= i < tile_x:
                            continue
                        k = OFFSETS.index((dx, dy))
                        if i not in running:
                            running[i] = [None] * 3 if number == 0 else [sums[n, i] for n in range(3)]
                        running[i] = [
                            tables[3 * k + n] * source[n]
                            if running[i][n] is None
                            else running[i][n] + tables[3 * k + n] * source[n]
                            for n in range(3)
                        ]
                for i in sorted(running):
                    if i + 2 <= row or row == tile_x - 1:
                        value = running.pop(i)
                        if number < 2:
                            for n in range(3):
                                sums[n, i] = value[n]
                        else:
                            place = pl.ds(pl.multiple_of(shift_y + i * tile_y, 8), 8)
                            lower_ref[0, place, :] = value[2] - value[1]
                            lower_ref[1, place, :] = value[2] + value[0]
        return carry

    lax.fori_loop(0, blocks, block, 0)


def halos_kernel(
    tile_x, tile_y, inner_y, outer_y, inner_x, outer_x, agg_ref, near_ref, low_ref, lower_in, field_in,
    lower_ref, field_ref, columns, rims,
):
    lanes = lower_ref.shape[2]
    width = tile_y + 2 * LEFT
    odd_y = lax.axis_index("gy") % 2 == 1
    odd_x = lax.axis_index("gx") % 2 == 1
    sides = [jnp.where(odd_y, inner_y[...], outer_y[...]), jnp.where(odd_y, outer_y[...], inner_y[...])]
    ends = [jnp.where(odd_x, inner_x[...], outer_x[...]), jnp.where(odd_x, outer_x[...], inner_x[...])]
    lower_ref[...] = lower_in[...]
    field_ref[...] = field_in[...]
    halo = jnp.concatenate(sides + ends, axis=0)
    pattern = mm(halo, agg_ref[...]).astype(BF16).astype(F32)
    halo = halo.astype(F32)
    values = [halo[:, :lanes], halo[:, lanes:], pattern[:, :lanes], pattern[:, lanes:]]
    two = jnp.zeros((8, lanes), F32)
    rim_size = inner_x.shape[0]
    for n, value in enumerate(values):
        for side in range(2):
            for c in range(2):
                at = (2 * side + c) * tile_x
                columns[n, 2 * side + c, 0:8, :] = two
                columns[n, 2 * side + c, 8 : 8 + tile_x, :] = value[at : at + tile_x]
                columns[n, 2 * side + c, 8 + tile_x : 16 + tile_x, :] = two
        for end in range(2):
            at = 4 * tile_x + end * rim_size
            corner = at + 2 * tile_y
            for row in range(2):
                base = (2 * end + row) * width + LEFT
                rims[n, base : base + tile_y, :] = value[at + row * tile_y : at + (row + 1) * tile_y]
                for side in range(2):
                    for c in range(2):
                        place = base + (tile_y + c if side else c - 2)
                        line = corner + 4 * side + 2 * c + row
                        rims[n, place : place + 1, :] = value[line : line + 1]

    def translate(terms):
        first = second = 0.0
        for dx, dy, real, imag in terms:
            k = OFFSETS.index((dx, dy))
            t_real, t_imag = low_ref[2 * k : 2 * k + 1, :], low_ref[2 * k + 1 : 2 * k + 2, :]
            first = first + (t_real * real - t_imag * imag)
            second = second + (t_real * imag + t_imag * real)
        return first, second

    def column(n, side, c, dx):
        return columns[n, 2 * side + c, 8 + dx : 8 + dx + tile_x, :]

    def rim(n, end, row, dy):
        base = (2 * end + row) * width + LEFT + dy
        return rims[n, base : base + tile_y, :]

    for side in range(2):
        for box in ((tile_y - 1, tile_y - 2) if side else (0, 1)):
            terms = []
            for c in range(2):
                dy = (tile_y + c if side else c - 2) - box
                for dx in range(-2, 3):
                    if (dx, dy) in OFFSETS:
                        terms.append((dx, dy, column(2, side, c, dx), column(3, side, c, dx)))
            rows = pl.ds(box, tile_x, stride=tile_y)
            for part, value in enumerate(translate(terms)):
                lower_ref[part, rows, :] = lower_ref[part, rows, :] + value
        source = jnp.concatenate(
            [column(part, side, 1 - side, dx) for dx in range(-1, 2) for part in range(2)], axis=1
        ).astype(BF16)
        weights = [near_ref[dx, (4 * side) * lanes : (4 * side + 2) * lanes, :] for dx in range(3)]
        value = mm(source, jnp.concatenate(weights, axis=0))
        rows = pl.ds(tile_y - 1 if side else 0, tile_x, stride=tile_y)
        for part in range(2):
            field_ref[part, rows, :] = field_ref[part, rows, :] + value[:, part * lanes : (part + 1) * lanes]
    for end in range(2):
        for box in ((tile_x - 1, tile_x - 2) if end else (0, 1)):
            terms = []
            for row in range(2):
                dx = (tile_x + row if end else row - 2) - box
                for dy in range(-2, 3):
                    if (dx, dy) in OFFSETS:
                        terms.append((dx, dy, rim(2, end, row, dy), rim(3, end, row, dy)))
            rows = slice(box * tile_y, (box + 1) * tile_y)
            for part, value in enumerate(translate(terms)):
                lower_ref[part, rows, :] = lower_ref[part, rows, :] + value
        source = jnp.concatenate(
            [rim(part, end, 1 - end, dy) for dy in range(-1, 2) for part in range(2)], axis=1
        ).astype(BF16)
        value = mm(source, near_ref[2 * end])
        box = tile_x - 1 if end else 0
        rows = slice(box * tile_y, (box + 1) * tile_y)
        for part in range(2):
            field_ref[part, rows, :] = field_ref[part, rows, :] + value[:, part * lanes : (part + 1) * lanes]


def order_kernel(chunks, kinds, parents_x, parents_y, list_ref, kind_ref, count_ref, source_ref, table_ref,
                 number_ref, back_ref):
    parents = parents_x * parents_y
    slots = list_ref.shape[1]
    down = lax.broadcasted_iota(jnp.int32, (parents, parents), 0)
    along = lax.broadcasted_iota(jnp.int32, (parents, parents), 1)
    column = count_rows(count_ref, parents_x, parents_y, parents)
    row = jnp.sum(jnp.where(down == along, column, 0.0), axis=0, keepdims=True)
    before = (column > row) | ((column == row) & (down < along))
    rank = jnp.sum(jnp.where(before, 1.0, 0.0), axis=0, keepdims=True)
    move = jnp.where(down.astype(F32) == rank, 1.0, 0.0).astype(BF16)
    after = (row > column) | ((row == column) & (along < down))
    rank = jnp.sum(jnp.where(after, 1.0, 0.0), axis=1, keepdims=True)
    back_ref[...] = jnp.where(along.astype(F32) == rank, 1.0, 0.0).astype(BF16)

    across = parents_y * chunks
    entry = list_ref[...]
    line, place = entry // across, entry % across
    source = ((place // parents_y) ^ lax.axis_index("gy")) * parents + line * parents_y + place % parents_y
    count = column[:, :slots]
    used = lax.broadcasted_iota(jnp.int32, (parents, slots), 1).astype(F32) < count
    kind = jnp.where(used, kind_ref[...], kinds).astype(F32).astype(BF16)

    def moved(value):
        return mm(move, value).astype(jnp.int32)

    high = moved((source // 256).astype(F32).astype(BF16))
    source_ref[...] = high * 256 + moved((source % 256).astype(F32).astype(BF16))
    table_ref[...] = moved(kind)
    number_ref[...] = moved(count.astype(BF16))


GROUP = 8


def lists_kernel(chunks, tile_x, tile_y, *refs):
    sources = refs[:chunks]
    (source_at, table_at, number_at, table_ref, kept_ref, lower_ref, near_ref, back_ref, recv_ref, down_hbm, out_hbm,
     cells, table8, sums, down_ref, out_ref, sems) = refs[chunks:]
    parents_x, parents_y = tile_x // 2, tile_y // 2
    parents = parents_x * parents_y
    slots = source_at.shape[0] // parents
    kinds = table_ref.shape[0] // 4
    lanes = lower_ref.shape[2]
    load = pltpu.make_async_copy(down_hbm, down_ref, sems.at[0])
    load.start()
    rows8 = table8.reshape(8 * kinds + 8, lanes)
    for place, row in enumerate((0, 0, 2, 2, 1, 1, 3, 3)):
        rows8[pl.ds(place, kinds, stride=8), :] = table_ref[pl.ds(row, kinds, stride=4), :]
    table8[kinds] = jnp.zeros((8, lanes), F32)
    pairs = cells.reshape(chunks * parents // 2, 2, 8, lanes)
    for c in range(chunks):
        rows = sources[c][...].astype(F32).reshape(parents // 2, 8, lanes)
        for half in range(2):
            own = rows[:, 4 * half : 4 * half + 4, :]
            pairs[c * (parents // 2) : (c + 1) * (parents // 2), half] = jnp.concatenate([own, own], axis=1)

    def step(n, carry):
        first = n * (GROUP * slots)
        number = number_at[n * GROUP]
        for length in range(2, slots + 1, 2):

            @pl.when((number == length) | (number == length - 1))
            def _():
                for k in range(GROUP):
                    total = [None, None]
                    for s in range(length):
                        at = first + (k * slots + s)
                        term = cells[source_at[at]] * table8[table_at[at]]
                        total[s % 2] = term if total[s % 2] is None else total[s % 2] + term
                    sums[n * GROUP + k] = total[0] + total[1]

        @pl.when(number == 0)
        def _():
            for k in range(GROUP):
                sums[n * GROUP + k] = jnp.zeros((8, lanes), F32)

        return carry

    lax.fori_loop(0, parents // GROUP, step, 0)
    lines = sums.reshape(8 * parents, lanes)

    def row(place):
        return lines[pl.ds(place, parents, stride=8), :]

    ordered = jnp.concatenate(
        [row(0) - row(5), row(2) - row(7), row(1) + row(4), row(3) + row(6)], axis=1
    ).astype(BF16)
    incoming = mm(back_ref[...], ordered).astype(BF16)
    load.wait()
    stores = []
    count = parents_x // 2
    for half in range(2):
        part_in = incoming[half * count * parents_y : (half + 1) * count * parents_y]
        for side_x in range(2):
            for side_y in range(2):
                down = mm(part_in, down_ref[2 * side_x + side_y])
                starts = [
                    (2 * p + side_x) * tile_y + side_y for p in range(half * count, (half + 1) * count)
                ]

                def rows_of(ref):
                    return jnp.concatenate(
                        [ref[pl.ds(start, parents_y, stride=2), :] for start in starts], axis=0
                    )

                total = jnp.concatenate(
                    [
                        down[:, part * lanes : (part + 1) * lanes] + rows_of(lower_ref.at[part])
                        for part in range(2)
                    ],
                    axis=1,
                )
                field = mm(total.astype(BF16), recv_ref[...])
                mask = rows_of(kept_ref)
                for part in range(2):
                    value = field[:, part * lanes : (part + 1) * lanes] + rows_of(near_ref.at[part])
                    value = value * mask
                    for p, start in enumerate(starts):
                        out_ref[pl.ds(2 * start + part, parents_y, stride=4), :] = value[
                            p * parents_y : (p + 1) * parents_y
                        ]
        size = out_ref.shape[0] // 2
        rows = pl.ds(half * size, size)
        stores.append(pltpu.make_async_copy(out_ref.at[rows], out_hbm.at[rows], sems.at[1 + half]))
        stores[-1].start()
    for store in stores:
        store.wait()


def swap(low, high, axis):
    count = lax.axis_size(axis)
    lows = [(i, i ^ 1) for i in range(count)]
    highs = [(i, ((i + 1) ^ 1) - 1) for i in range(1, count - 1)]
    return lax.ppermute(low, axis, lows), lax.ppermute(high, axis, highs)


def body(
    currents, box_count, aggregate, near_blocks, low_translator, child_to_parent, coarse_list,
    coarse_kind, coarse_count, up_translator, parent_to_child, receive_map,
):
    tile_x, tile_y = box_count.shape
    boxes = tile_x * tile_y
    lanes = currents.shape[-1]
    parents_x, parents_y, slots = coarse_list.shape
    parents = parents_x * parents_y
    kinds, _, half = up_translator.shape
    wide = 2 * half
    chunks = lax.axis_size("gy")
    in_hbm = pl.BlockSpec(memory_space=pltpu.HBM)

    edge = jax.ShapeDtypeStruct((2 * tile_x, 2 * lanes), BF16)
    live, kept, low, high = pl.pallas_call(
        functools.partial(live_kernel, tile_x, tile_y),
        name="live",
        out_shape=[
            jax.ShapeDtypeStruct((boxes, 2 * lanes), BF16),
            jax.ShapeDtypeStruct((boxes, lanes), F32),
            edge,
            edge,
        ],
        in_specs=[in_hbm] * 2,
        out_specs=vmem(4),
        scratch_shapes=[
            pltpu.VMEM((2 * boxes, lanes), BF16),
            pltpu.VMEM((tile_x, tile_y), jnp.int32),
            pltpu.VMEM((2 * boxes, lanes), F32),
            pltpu.SemaphoreType.DMA((2,)),
        ],
        compiler_params=params(16),
        cost_estimate=cost(100 * MIB, 2 * MIB),
    )(hbm(currents.reshape(2 * boxes, lanes)), hbm(box_count))
    inner_y, outer_y = swap(low, high, "gy")

    coarse = pl.pallas_call(
        functools.partial(parents_kernel, tile_x, tile_y),
        name="parents",
        out_shape=jax.ShapeDtypeStruct((4 * parents, wide // 4), BF16),
        in_specs=vmem(3),
        out_specs=pl.BlockSpec(memory_space=pltpu.VMEM),
        scratch_shapes=[pltpu.VMEM((2, boxes, lanes), F32), pltpu.VMEM((4 * parents, wide // 4), F32)],
        compiler_params=params(16),
        cost_estimate=cost(200 * MIB, 3 * MIB),
    )(live, aggregate, child_to_parent.reshape(8 * lanes, wide))
    sources = [coarse] + [
        lax.ppermute(coarse, "gy", [(i, i ^ d) for i in range(chunks)]) for d in range(1, chunks)
    ]

    rim = 2 * tile_y + 8
    rim += -rim % 16
    low, high = pl.pallas_call(
        functools.partial(rims_kernel, tile_x, tile_y),
        name="rims",
        out_shape=[jax.ShapeDtypeStruct((rim, 2 * lanes), BF16)] * 2,
        in_specs=vmem(3),
        out_specs=vmem(2),
        scratch_shapes=[pltpu.VMEM((rim, 2 * lanes), F32)] * 2,
        compiler_params=params(16),
        cost_estimate=cost(MIB, MIB),
    )(live, inner_y, outer_y)
    inner_x, outer_x = swap(low, high, "gx")

    near_rows = near_blocks.reshape(3, 6 * lanes, 2 * lanes)
    low_rows = low_translator.reshape(-1, lanes)
    width = tile_y + 2 * LEFT
    pair = [jax.ShapeDtypeStruct((2, boxes, lanes), F32)] * 2
    lower, near = pl.pallas_call(
        functools.partial(local_kernel, tile_x, tile_y),
        name="local",
        out_shape=pair,
        in_specs=vmem(4),
        out_specs=vmem(2),
        scratch_shapes=[
            pltpu.VMEM((2, tile_x * width, lanes), F32),
            pltpu.VMEM((3, tile_x * width, lanes), F32),
            pltpu.VMEM(((tile_x + 2) * tile_y, 6 * lanes), BF16),
            pltpu.VMEM((3 * len(OFFSETS), 8, lanes), F32),
            pltpu.VMEM((3, tile_x, 8, lanes), F32),
        ],
        compiler_params=params(24),
        cost_estimate=cost(2000 * MIB, 5 * MIB),
    )(live, aggregate, near_rows, low_rows)

    entries = jax.ShapeDtypeStruct((parents, slots), jnp.int32)
    source_at, table_at, number_at, back = pl.pallas_call(
        functools.partial(order_kernel, chunks, kinds, parents_x, parents_y),
        name="order",
        out_shape=[entries, entries, entries, jax.ShapeDtypeStruct((parents, parents), BF16)],
        in_specs=vmem(3),
        out_specs=vmem(4),
        compiler_params=params(16),
        cost_estimate=cost(300 * MIB, MIB),
    )(coarse_list.reshape(parents, slots), coarse_kind.reshape(parents, slots), coarse_count)

    lower, near = pl.pallas_call(
        functools.partial(halos_kernel, tile_x, tile_y),
        name="halos",
        out_shape=pair,
        in_specs=vmem(9),
        out_specs=vmem(2),
        scratch_shapes=[
            pltpu.VMEM((4, 4, tile_x + 16, lanes), F32),
            pltpu.VMEM((4, 4 * width, lanes), F32),
        ],
        compiler_params=params(16),
        cost_estimate=cost(100 * MIB, 5 * MIB),
    )(inner_y, outer_y, inner_x, outer_x, aggregate, near_rows, low_rows, lower, near)

    table = up_translator.reshape(kinds, 2, 2, half // 2).transpose(0, 2, 1, 3).reshape(4 * kinds, half // 2)
    out = pl.pallas_call(
        functools.partial(lists_kernel, chunks, tile_x, tile_y),
        name="lists",
        out_shape=jax.ShapeDtypeStruct((2 * boxes, lanes), F32),
        in_specs=vmem(chunks) + [pl.BlockSpec(memory_space=pltpu.SMEM)] * 3 + vmem(6) + [in_hbm],
        out_specs=in_hbm,
        scratch_shapes=[
            pltpu.VMEM((chunks * parents, 8, lanes), F32),
            pltpu.VMEM((kinds + 1, 8, lanes), F32),
            pltpu.VMEM((parents, 8, lanes), F32),
            pltpu.VMEM((4, wide, 2 * lanes), BF16),
            pltpu.VMEM((2 * boxes, lanes), F32),
            pltpu.SemaphoreType.DMA((3,)),
        ],
        compiler_params=params(24 if chunks <= 4 else 48),
        cost_estimate=cost(3000 * MIB, 8 * MIB),
    )(
        *sources, source_at.reshape(-1), table_at.reshape(-1), number_at[:, 0], table,
        kept, lower, near, back, receive_map, hbm(parent_to_child),
    )
    return out.reshape(tile_x, tile_y, 2, lanes)


def solution(mesh):
    tiles = P("gx", "gy")
    in_specs = (tiles, tiles, P(), P(), P(), P(), tiles, tiles, tiles, P(), P(), P())
    return jax.shard_map(body, mesh=mesh, in_specs=in_specs, out_specs=tiles, check_vma=False)
```

```python
import functools

import jax
import jax.numpy as jnp
from jax import lax
from jax.experimental import pallas as pl
from jax.experimental.pallas import tpu as pltpu
from jax.sharding import PartitionSpec as P

F32 = jnp.float32
BF16 = jnp.bfloat16
MIB = 1 << 20


def vmem(count):
    return [pl.BlockSpec(memory_space=pltpu.VMEM)] * count


def hbm(array):
    return pltpu.with_memory_space_constraint(array, pltpu.HBM)


def params(mib):
    return pltpu.CompilerParams(vmem_limit_bytes=mib * MIB)


def cost(macs, moved):
    return pl.CostEstimate(flops=2 * macs, bytes_accessed=moved, transcendentals=0)


def mm(left, right):
    return jnp.dot(left, right, preferred_element_type=F32)


def count_rows(counts_ref, tile_x, tile_y, lanes):
    eye = lax.broadcasted_iota(jnp.int32, (tile_y, tile_y), 0) == lax.broadcasted_iota(
        jnp.int32, (tile_y, tile_y), 1
    )
    counts = counts_ref[...].astype(F32)
    diag = [
        jnp.where(eye, jnp.broadcast_to(counts[i : i + 1], (tile_y, tile_y)), 0.0) for i in range(tile_x)
    ]
    return mm(jnp.concatenate(diag, axis=0).astype(BF16), jnp.ones((tile_y, lanes), BF16))


def halo_pair(inner_ref, outer_ref, axis):
    at = lax.axis_index(axis)
    odd = at % 2 == 1
    inner, outer = inner_ref[...].astype(F32), outer_ref[...].astype(F32)
    before, after = jnp.where(odd, inner, outer), jnp.where(odd, outer, inner)
    return jnp.where(at > 0, before, 0.0), jnp.where(at < lax.axis_size(axis) - 1, after, 0.0)


def live_kernel(tile_x, tile_y, cur_hbm, counts_hbm, list_hbm, kind_hbm, number_hbm,
                live_ref, kept_ref, low_ref, high_ref, list_ref, kind_ref, number_ref,
                cur_ref, counts_ref, wide, sems):
    pairs = [
        (counts_hbm, counts_ref), (cur_hbm, cur_ref), (list_hbm, list_ref), (kind_hbm, kind_ref),
        (number_hbm, number_ref),
    ]
    loads = [
        pltpu.make_async_copy(source, target, sems.at[k]) for k, (source, target) in enumerate(pairs)
    ]
    for load in loads:
        load.start()
    lanes = cur_ref.shape[1]
    boxes = tile_x * tile_y
    loads[0].wait()
    limits = count_rows(counts_ref, tile_x, tile_y, lanes)
    keep = lax.broadcasted_iota(jnp.int32, (boxes, lanes), 1).astype(F32) < limits
    kept_ref[...] = jnp.where(keep, 1.0, 0.0)
    odd = lax.axis_index("gy") % 2 == 1
    loads[1].wait()
    wide[...] = cur_ref[...].astype(F32)
    for part in range(2):
        cols = slice(part * lanes, (part + 1) * lanes)
        live_ref[:, cols] = jnp.where(keep, wide[pl.ds(part, boxes, stride=2), :], 0.0).astype(BF16)

        def edge(column):
            rows = wide[pl.ds(2 * column + part, tile_x, stride=2 * tile_y), :]
            return rows * kept_ref[pl.ds(column, tile_x, stride=tile_y), :]

        first = jnp.concatenate([edge(0), edge(1)], axis=0).astype(BF16)
        last = jnp.concatenate([edge(tile_y - 2), edge(tile_y - 1)], axis=0).astype(BF16)
        low_ref[:, cols] = jnp.where(odd, first, last)
        high_ref[:, cols] = jnp.where(odd, last, first)
    for load in loads[2:]:
        load.wait()


LEFT = 8


def parents_kernel(
    tile_x, tile_y, live_ref, agg_ref, up_ref, inner_ref, outer_ref, coarse_ref, pats_ref, low_ref, high_ref,
    pats, rows4, first, last,
):
    lanes = pats.shape[2]
    width = tile_y + 2 * LEFT
    pattern = mm(live_ref[...], agg_ref[...])
    pats[0] = pattern[:, :lanes]
    pats[1] = pattern[:, lanes:]
    children = []
    for side_x in range(2):
        for side_y in range(2):
            for part in range(2):
                rows = [
                    pats[part, pl.ds((2 * p + side_x) * tile_y + side_y, tile_y // 2, stride=2), :]
                    for p in range(tile_x // 2)
                ]
                children.append(jnp.concatenate(rows, axis=0).astype(BF16))
    coarse = mm(jnp.concatenate(children, axis=1), up_ref[...])
    for place, column in enumerate((0, 2, 1, 3)):
        rows4[pl.ds(place, coarse.shape[0], stride=4), :] = coarse[:, column * 128 : (column + 1) * 128]
    coarse_ref[...] = rows4[...].astype(BF16)

    pattern = pattern.astype(BF16).astype(F32)
    values = [pattern[:, :lanes], pattern[:, lanes:], pattern[:, :lanes] + pattern[:, lanes:]]
    none = jnp.zeros((LEFT, lanes), F32)
    for i in range(tile_x):
        base = i * width
        for k in range(3):
            pats_ref[k, base : base + LEFT, :] = none
            pats_ref[k, base + LEFT : base + LEFT + tile_y, :] = values[k][i * tile_y : (i + 1) * tile_y]
            pats_ref[k, base + LEFT + tile_y : base + width, :] = none

    odd = lax.axis_index("gx") % 2 == 1
    sides = halo_pair(inner_ref, outer_ref, "gy")
    for rim, start in ((first, 0), (last, tile_x - 2)):
        rim[0 : 2 * tile_y, :] = live_ref[start * tile_y : (start + 2) * tile_y, :].astype(F32)
        place = 2 * tile_y
        for side in sides:
            for column in range(2):
                at = column * tile_x + start
                rim[place : place + 2, :] = side[at : at + 2]
                place += 2
        rim[place:, :] = jnp.zeros((rim.shape[0] - place, rim.shape[1]), F32)
    low_ref[...] = jnp.where(odd, first[...], last[...]).astype(BF16)
    high_ref[...] = jnp.where(odd, last[...], first[...]).astype(BF16)


OFFSETS = [(dx, dy) for dx in range(-2, 3) for dy in range(-2, 3) if max(abs(dx), abs(dy)) == 2]


def local_kernel(
    tile_x, tile_y, live_ref, pats, near_ref, low_ref, lower_ref, field_ref, cells, shifted, tables, sums,
):
    lanes = lower_ref.shape[2]
    width = tile_y + 2 * LEFT
    none = jnp.zeros((LEFT, lanes), F32)
    ends = jnp.zeros((tile_y, 6 * lanes), BF16)
    shifted[0:tile_y, :] = ends
    shifted[(tile_x + 1) * tile_y : (tile_x + 2) * tile_y, :] = ends
    shifted[tile_y : (tile_x + 1) * tile_y, 2 * lanes : 4 * lanes] = live_ref[...]
    for part in range(2):
        cols = slice(part * lanes, (part + 1) * lanes)
        for i in range(tile_x):
            base = i * width
            cells[part, base : base + LEFT, :] = none
            cells[part, base + LEFT : base + LEFT + tile_y, :] = live_ref[
                i * tile_y : (i + 1) * tile_y, cols
            ].astype(F32)
            cells[part, base + LEFT + tile_y : base + width, :] = none
            for shift in (-1, 1):
                place = (2 * (shift + 1) + part) * lanes
                shifted[(i + 1) * tile_y : (i + 2) * tile_y, place : place + lanes] = cells[
                    part, base + LEFT + shift : base + LEFT + shift + tile_y, :
                ].astype(BF16)
    for k in range(len(OFFSETS)):
        t_real, t_imag = low_ref[2 * k : 2 * k + 1, :], low_ref[2 * k + 1 : 2 * k + 2, :]
        for n, value in enumerate((t_imag - t_real, t_imag + t_real, t_real)):
            tables[3 * k + n] = jnp.broadcast_to(value, (8, lanes))

    passes = [
        [(dx, dy) for dx, dy in OFFSETS if dy == -2],
        [(dx, dy) for dx, dy in OFFSETS if dy == 2],
        [(dx, dy) for dx, dy in OFFSETS if abs(dy) < 2],
    ]
    blocks = tile_y // 8
    size = tile_x * tile_y // blocks

    def block(b, carry):
        total = None
        for shift in range(3):
            start = pl.multiple_of(b * size + shift * tile_y, tile_y)
            term = mm(shifted[pl.ds(start, size), :], near_ref[shift])
            total = term if total is None else total + term
        start = pl.multiple_of(b * size, size)
        field_ref[0, pl.ds(start, size), :] = total[:, :lanes]
        field_ref[1, pl.ds(start, size), :] = total[:, lanes:]
        shift_y = pl.multiple_of(b * 8, 8)
        for number, offsets in enumerate(passes):
            running = {}
            for row in range(tile_x):
                for dy in sorted({dy for _, dy in offsets}):
                    rows = pl.ds(shift_y + (row * width + LEFT + dy), 8)
                    source = [pats[k, rows, :] for k in range(3)]
                    for dx in range(-2, 3):
                        i = row - dx
                        if (dx, dy) not in offsets or not 0 <= i < tile_x:
                            continue
                        k = OFFSETS.index((dx, dy))
                        if i not in running:
                            running[i] = [None] * 3 if number == 0 else [sums[n, i] for n in range(3)]
                        running[i] = [
                            tables[3 * k + n] * source[n]
                            if running[i][n] is None
                            else running[i][n] + tables[3 * k + n] * source[n]
                            for n in range(3)
                        ]
                for i in sorted(running):
                    if i + 2 <= row or row == tile_x - 1:
                        value = running.pop(i)
                        if number < 2:
                            for n in range(3):
                                sums[n, i] = value[n]
                        else:
                            place = pl.ds(pl.multiple_of(shift_y + i * tile_y, 8), 8)
                            lower_ref[0, place, :] = value[2] - value[1]
                            lower_ref[1, place, :] = value[2] + value[0]
        return carry

    lax.fori_loop(0, blocks, block, 0)


def halos_kernel(
    tile_x, tile_y, inner_y, outer_y, inner_x, outer_x, agg_ref, near_ref, low_ref, lower_in, field_in,
    lower_ref, field_ref, columns, rims,
):
    lanes = lower_ref.shape[2]
    width = tile_y + 2 * LEFT
    halo = halo_pair(inner_y, outer_y, "gy") + halo_pair(inner_x, outer_x, "gx")
    lower_ref[...] = lower_in[...]
    field_ref[...] = field_in[...]
    halo = jnp.concatenate(halo, axis=0)
    pattern = mm(halo.astype(BF16), agg_ref[...]).astype(BF16).astype(F32)
    values = [halo[:, :lanes], halo[:, lanes:], pattern[:, :lanes], pattern[:, lanes:]]
    two = jnp.zeros((8, lanes), F32)
    rim_size = inner_x.shape[0]
    for n, value in enumerate(values):
        for side in range(2):
            for c in range(2):
                at = (2 * side + c) * tile_x
                columns[n, 2 * side + c, 0:8, :] = two
                columns[n, 2 * side + c, 8 : 8 + tile_x, :] = value[at : at + tile_x]
                columns[n, 2 * side + c, 8 + tile_x : 16 + tile_x, :] = two
        for end in range(2):
            at = 4 * tile_x + end * rim_size
            corner = at + 2 * tile_y
            for row in range(2):
                base = (2 * end + row) * width + LEFT
                rims[n, base : base + tile_y, :] = value[at + row * tile_y : at + (row + 1) * tile_y]
                for side in range(2):
                    for c in range(2):
                        place = base + (tile_y + c if side else c - 2)
                        line = corner + 4 * side + 2 * c + row
                        rims[n, place : place + 1, :] = value[line : line + 1]

    def translate(terms):
        first = second = 0.0
        for dx, dy, real, imag in terms:
            k = OFFSETS.index((dx, dy))
            t_real, t_imag = low_ref[2 * k : 2 * k + 1, :], low_ref[2 * k + 1 : 2 * k + 2, :]
            first = first + (t_real * real - t_imag * imag)
            second = second + (t_real * imag + t_imag * real)
        return first, second

    def column(n, side, c, dx):
        return columns[n, 2 * side + c, 8 + dx : 8 + dx + tile_x, :]

    def rim(n, end, row, dy):
        base = (2 * end + row) * width + LEFT + dy
        return rims[n, base : base + tile_y, :]

    for side in range(2):
        for box in ((tile_y - 1, tile_y - 2) if side else (0, 1)):
            terms = []
            for c in range(2):
                dy = (tile_y + c if side else c - 2) - box
                for dx in range(-2, 3):
                    if (dx, dy) in OFFSETS:
                        terms.append((dx, dy, column(2, side, c, dx), column(3, side, c, dx)))
            rows = pl.ds(box, tile_x, stride=tile_y)
            for part, value in enumerate(translate(terms)):
                lower_ref[part, rows, :] = lower_ref[part, rows, :] + value
        source = jnp.concatenate(
            [column(part, side, 1 - side, dx) for dx in range(-1, 2) for part in range(2)], axis=1
        ).astype(BF16)
        weights = [near_ref[dx, (4 * side) * lanes : (4 * side + 2) * lanes, :] for dx in range(3)]
        value = mm(source, jnp.concatenate(weights, axis=0))
        rows = pl.ds(tile_y - 1 if side else 0, tile_x, stride=tile_y)
        for part in range(2):
            field_ref[part, rows, :] = field_ref[part, rows, :] + value[:, part * lanes : (part + 1) * lanes]
    for end in range(2):
        for box in ((tile_x - 1, tile_x - 2) if end else (0, 1)):
            terms = []
            for row in range(2):
                dx = (tile_x + row if end else row - 2) - box
                for dy in range(-2, 3):
                    if (dx, dy) in OFFSETS:
                        terms.append((dx, dy, rim(2, end, row, dy), rim(3, end, row, dy)))
            rows = slice(box * tile_y, (box + 1) * tile_y)
            for part, value in enumerate(translate(terms)):
                lower_ref[part, rows, :] = lower_ref[part, rows, :] + value
        source = jnp.concatenate(
            [rim(part, end, 1 - end, dy) for dy in range(-1, 2) for part in range(2)], axis=1
        ).astype(BF16)
        value = mm(source, near_ref[2 * end])
        box = tile_x - 1 if end else 0
        rows = slice(box * tile_y, (box + 1) * tile_y)
        for part in range(2):
            field_ref[part, rows, :] = field_ref[part, rows, :] + value[:, part * lanes : (part + 1) * lanes]


GROUP = 8


def order_kernel(chunks, kinds, parents_x, parents_y, list_ref, kind_ref, count_ref, agg_hbm, up_hbm,
                 at_ref, back_ref, agg_ref, up_ref, sems):
    loads = [
        pltpu.make_async_copy(agg_hbm, agg_ref, sems.at[0]),
        pltpu.make_async_copy(up_hbm, up_ref, sems.at[1]),
    ]
    for load in loads:
        load.start()
    parents = parents_x * parents_y
    slots = list_ref.shape[1]
    groups = parents // GROUP
    lanes = at_ref.shape[1]
    down = lax.broadcasted_iota(jnp.int32, (parents, parents), 0)
    along = lax.broadcasted_iota(jnp.int32, (parents, parents), 1)
    column = count_rows(count_ref, parents_x, parents_y, parents)
    row = jnp.sum(jnp.where(down == along, column, 0.0), axis=0, keepdims=True)
    before = (column > row) | ((column == row) & (down < along))
    rank = jnp.sum(jnp.where(before, 1.0, 0.0), axis=0, keepdims=True)
    after = (row > column) | ((row == column) & (along < down))
    rank_down = jnp.sum(jnp.where(after, 1.0, 0.0), axis=1, keepdims=True)
    back_ref[...] = jnp.where(along.astype(F32) == rank_down, 1.0, 0.0).astype(BF16)

    across = parents_y * chunks
    entry = list_ref[...]
    line, place = entry // across, entry % across
    source = ((place // parents_y) ^ lax.axis_index("gy")) * parents + line * parents_y + place % parents_y
    used = lax.broadcasted_iota(jnp.int32, (parents, slots), 1).astype(F32) < column[:, :slots]
    kind = jnp.where(used, kind_ref[...], kinds)
    values = [(source // 256).astype(F32), (source % 256).astype(F32), kind.astype(F32)]
    values = [value.astype(BF16) for value in values]
    totals = [jnp.zeros((groups, lanes), F32)] * 3
    first = GROUP * lax.broadcasted_iota(jnp.int32, (groups, parents), 0)
    slot = lax.broadcasted_iota(jnp.int32, (slots, lanes), 0)
    lane = lax.broadcasted_iota(jnp.int32, (slots, lanes), 1)
    for k in range(GROUP):
        move = jnp.where((first + k).astype(F32) == rank, 1.0, 0.0).astype(BF16)
        spread = jnp.where(lane == slot + k * slots, 1.0, 0.0).astype(BF16)
        totals = [
            total + mm(mm(move, value).astype(BF16), spread) for total, value in zip(totals, values)
        ]
    high, low, kind = [total.astype(jnp.int32) for total in totals]
    at_ref[0:groups, :] = high * 256 + low
    at_ref[groups : 2 * groups, :] = kind
    least = (slots - 1 - 2 * lax.broadcasted_iota(jnp.int32, (parents, lanes), 1)).astype(F32)
    reach = jnp.sum(jnp.where(column[:, :lanes] >= least, 1.0, 0.0), axis=0, keepdims=True).astype(jnp.int32)
    at_ref[2 * groups :, :] = jnp.broadcast_to((reach + (GROUP - 1)) // GROUP, (8, lanes))
    for load in loads:
        load.wait()


def lists_kernel(chunks, parents, slots, *refs):
    sources = refs[:chunks]
    at_any, table_ref, back_ref, down_hbm, incoming_ref, down_ref, cells, table8, sums, at, sems = refs[chunks:]
    kinds = table_ref.shape[0] // 4
    lanes = table_ref.shape[1]
    groups = parents // GROUP
    loads = [
        pltpu.make_async_copy(at_any, at, sems.at[0]),
        pltpu.make_async_copy(down_hbm, down_ref, sems.at[1]),
    ]
    for load in loads:
        load.start()
    rows8 = table8.reshape(8 * kinds + 8, lanes)
    for place, row in enumerate((0, 0, 2, 2, 1, 1, 3, 3)):
        rows8[pl.ds(place, kinds, stride=8), :] = table_ref[pl.ds(row, kinds, stride=4), :]
    table8[kinds] = jnp.zeros((8, lanes), F32)
    pairs = cells.reshape(chunks * parents // 2, 2, 8, lanes)
    for c in range(chunks):
        rows = sources[c][...].astype(F32).reshape(parents // 2, 8, lanes)
        for half in range(2):
            own = rows[:, 4 * half : 4 * half + 4, :]
            pairs[c * (parents // 2) : (c + 1) * (parents // 2), half] = jnp.concatenate([own, own], axis=1)
    loads[0].wait()

    def step(length, n, carry):
        for k in range(GROUP):
            total = [None, None]
            for s in range(length):
                term = cells[at[n, k * slots + s]] * table8[at[groups + n, k * slots + s]]
                total[s % 2] = term if total[s % 2] is None else total[s % 2] + term
            sums[n * GROUP + k] = total[0] + total[1] if length else jnp.zeros((8, lanes), F32)
        return carry

    start = 0
    for j, length in enumerate(range(slots, 0, -2)):
        end = at[2 * groups, j]
        lax.fori_loop(start, end, functools.partial(step, length), 0)
        start = end
    lax.fori_loop(start, groups, functools.partial(step, 0), 0)
    lines = sums.reshape(8 * parents, lanes)

    def row(place):
        return lines[pl.ds(place, parents, stride=8), :]

    ordered = jnp.concatenate(
        [row(0) - row(5), row(2) - row(7), row(1) + row(4), row(3) + row(6)], axis=1
    ).astype(BF16)
    incoming_ref[...] = mm(back_ref[...], ordered).astype(BF16)
    loads[1].wait()


def finish_kernel(tile_x, tile_y, incoming_ref, down_ref, kept_ref, lower_ref, near_ref, recv_ref, out_hbm,
                  total_ref, out_ref, sems):
    parents_x, parents_y = tile_x // 2, tile_y // 2
    parents = parents_x * parents_y
    lanes = lower_ref.shape[2]
    starts = [
        [(2 * p + child // 2) * tile_y + child % 2 for p in range(parents_x)] for child in range(4)
    ]

    def rows_of(ref, lines):
        return jnp.concatenate([ref[pl.ds(line, parents_y, stride=2), :] for line in lines], axis=0)

    for child in range(4):
        down = mm(incoming_ref[...], down_ref[child])
        for part in range(2):
            value = down[:, part * lanes : (part + 1) * lanes] + rows_of(lower_ref.at[part], starts[child])
            total_ref[child, :, part * lanes : (part + 1) * lanes] = value.astype(BF16)
    stores = []
    for half in range(2):
        count = parents_x // 2
        rows = slice(half * parents // 2, (half + 1) * parents // 2)
        for child in range(4):
            field = mm(total_ref[child, rows, :], recv_ref[...])
            lines = starts[child][half * count : (half + 1) * count]
            mask = rows_of(kept_ref, lines)
            for part in range(2):
                value = field[:, part * lanes : (part + 1) * lanes] + rows_of(near_ref.at[part], lines)
                value = value * mask
                for p, line in enumerate(lines):
                    out_ref[pl.ds(2 * line + part, parents_y, stride=4), :] = value[
                        p * parents_y : (p + 1) * parents_y
                    ]
        size = out_ref.shape[0] // 2
        rows = pl.ds(half * size, size)
        stores.append(pltpu.make_async_copy(out_ref.at[rows], out_hbm.at[rows], sems.at[half]))
        stores[-1].start()
    for store in stores:
        store.wait()


def swap(low, high, axis):
    count = lax.axis_size(axis)
    lows = [(i, i ^ 1) for i in range(count)]
    highs = [(i, (((i + 1) % count ^ 1) - 1) % count) for i in range(count)]
    return lax.ppermute(low, axis, lows), lax.ppermute(high, axis, highs)


def body(
    currents, box_count, aggregate, near_blocks, low_translator, child_to_parent, coarse_list,
    coarse_kind, coarse_count, up_translator, parent_to_child, receive_map,
):
    tile_x, tile_y = box_count.shape
    boxes = tile_x * tile_y
    lanes = currents.shape[-1]
    parents_x, parents_y, slots = coarse_list.shape
    parents = parents_x * parents_y
    kinds, _, half = up_translator.shape
    wide = 2 * half
    chunks = lax.axis_size("gy")
    in_hbm = pl.BlockSpec(memory_space=pltpu.HBM)

    edge = jax.ShapeDtypeStruct((2 * tile_x, 2 * lanes), BF16)
    entries = jax.ShapeDtypeStruct((parents, slots), jnp.int32)
    live, kept, low, high, lists, list_kinds, numbers = pl.pallas_call(
        functools.partial(live_kernel, tile_x, tile_y),
        name="live",
        out_shape=[
            jax.ShapeDtypeStruct((boxes, 2 * lanes), BF16),
            jax.ShapeDtypeStruct((boxes, lanes), F32),
            edge,
            edge,
            entries,
            entries,
            jax.ShapeDtypeStruct((parents_x, parents_y), jnp.int32),
        ],
        in_specs=[in_hbm] * 5,
        out_specs=vmem(7),
        scratch_shapes=[
            pltpu.VMEM((2 * boxes, lanes), BF16),
            pltpu.VMEM((tile_x, tile_y), jnp.int32),
            pltpu.VMEM((2 * boxes, lanes), F32),
            pltpu.SemaphoreType.DMA((5,)),
        ],
        compiler_params=params(16),
        cost_estimate=cost(100 * MIB, 2 * MIB),
    )(
        hbm(currents.reshape(2 * boxes, lanes)), hbm(box_count), hbm(coarse_list.reshape(parents, slots)),
        hbm(coarse_kind.reshape(parents, slots)), hbm(coarse_count),
    )
    inner_y, outer_y = swap(low, high, "gy")

    groups = parents // GROUP
    at, back, agg_near, up_near = pl.pallas_call(
        functools.partial(order_kernel, chunks, kinds, parents_x, parents_y),
        name="order",
        out_shape=[
            jax.ShapeDtypeStruct((2 * groups + 8, GROUP * slots), jnp.int32),
            jax.ShapeDtypeStruct((parents, parents), BF16),
            jax.ShapeDtypeStruct((2 * lanes, 2 * lanes), BF16),
            jax.ShapeDtypeStruct((8 * lanes, wide), BF16),
        ],
        in_specs=vmem(3) + [in_hbm] * 2,
        out_specs=vmem(4),
        scratch_shapes=[pltpu.SemaphoreType.DMA((2,))],
        compiler_params=params(16),
        cost_estimate=cost(300 * MIB, 3 * MIB),
    )(
        lists, list_kinds, numbers,
        hbm(aggregate), hbm(child_to_parent.reshape(8 * lanes, wide)),
    )

    width = tile_y + 2 * LEFT
    rim = 2 * tile_y + 8
    rim += -rim % 16
    coarse, pats, low, high = pl.pallas_call(
        functools.partial(parents_kernel, tile_x, tile_y),
        name="parents",
        out_shape=[
            jax.ShapeDtypeStruct((4 * parents, wide // 4), BF16),
            jax.ShapeDtypeStruct((3, tile_x * width, lanes), F32),
            jax.ShapeDtypeStruct((rim, 2 * lanes), BF16),
            jax.ShapeDtypeStruct((rim, 2 * lanes), BF16),
        ],
        in_specs=vmem(5),
        out_specs=vmem(4),
        scratch_shapes=[
            pltpu.VMEM((2, boxes, lanes), F32),
            pltpu.VMEM((4 * parents, wide // 4), F32),
            pltpu.VMEM((rim, 2 * lanes), F32),
            pltpu.VMEM((rim, 2 * lanes), F32),
        ],
        compiler_params=params(16),
        cost_estimate=cost(200 * MIB, 3 * MIB),
    )(live, agg_near, up_near, inner_y, outer_y)
    sources = [coarse] + [
        lax.ppermute(coarse, "gy", [(i, i ^ d) for i in range(chunks)]) for d in range(1, chunks)
    ]
    inner_x, outer_x = swap(low, high, "gx")

    near_rows = near_blocks.reshape(3, 6 * lanes, 2 * lanes)
    low_rows = low_translator.reshape(-1, lanes)
    pair = [jax.ShapeDtypeStruct((2, boxes, lanes), F32)] * 2
    lower, near = pl.pallas_call(
        functools.partial(local_kernel, tile_x, tile_y),
        name="local",
        out_shape=pair,
        in_specs=vmem(4),
        out_specs=vmem(2),
        scratch_shapes=[
            pltpu.VMEM((2, tile_x * width, lanes), F32),
            pltpu.VMEM(((tile_x + 2) * tile_y, 6 * lanes), BF16),
            pltpu.VMEM((3 * len(OFFSETS), 8, lanes), F32),
            pltpu.VMEM((3, tile_x, 8, lanes), F32),
        ],
        compiler_params=params(16),
        cost_estimate=cost(2000 * MIB, 5 * MIB),
    )(live, pats, near_rows, low_rows)

    lower, near = pl.pallas_call(
        functools.partial(halos_kernel, tile_x, tile_y),
        name="halos",
        out_shape=pair,
        in_specs=vmem(9),
        out_specs=vmem(2),
        scratch_shapes=[
            pltpu.VMEM((4, 4, tile_x + 16, lanes), F32),
            pltpu.VMEM((4, 4 * width, lanes), F32),
        ],
        compiler_params=params(16),
        cost_estimate=cost(100 * MIB, 5 * MIB),
    )(inner_y, outer_y, inner_x, outer_x, agg_near, near_rows, low_rows, lower, near)

    table = up_translator.reshape(kinds, 2, 2, half // 2).transpose(0, 2, 1, 3).reshape(4 * kinds, half // 2)
    incoming, down = pl.pallas_call(
        functools.partial(lists_kernel, chunks, parents, slots),
        name="lists",
        out_shape=[
            jax.ShapeDtypeStruct((parents, wide), BF16),
            jax.ShapeDtypeStruct((4, wide, 2 * lanes), BF16),
        ],
        in_specs=vmem(chunks) + [pl.BlockSpec(memory_space=pl.ANY)] + vmem(2) + [in_hbm],
        out_specs=vmem(2),
        scratch_shapes=[
            pltpu.VMEM((chunks * parents, 8, wide // 4), F32),
            pltpu.VMEM((kinds + 1, 8, wide // 4), F32),
            pltpu.VMEM((parents, 8, wide // 4), F32),
            pltpu.SMEM(at.shape, jnp.int32),
            pltpu.SemaphoreType.DMA((2,)),
        ],
        compiler_params=params(16 if chunks <= 4 else 40),
        cost_estimate=cost(2000 * MIB, 8 * MIB),
    )(*sources, at, table, back, hbm(parent_to_child))
    out = pl.pallas_call(
        functools.partial(finish_kernel, tile_x, tile_y),
        name="finish",
        out_shape=jax.ShapeDtypeStruct((2 * boxes, lanes), F32),
        in_specs=vmem(6),
        out_specs=in_hbm,
        scratch_shapes=[
            pltpu.VMEM((4, parents, 2 * lanes), BF16),
            pltpu.VMEM((2 * boxes, lanes), F32),
            pltpu.SemaphoreType.DMA((2,)),
        ],
        compiler_params=params(16),
        cost_estimate=cost(300 * MIB, 4 * MIB),
    )(incoming, down, kept, lower, near, receive_map)
    return out.reshape(tile_x, tile_y, 2, lanes)


def solution(mesh):
    tiles = P("gx", "gy")
    in_specs = (tiles, tiles, P(), P(), P(), P(), tiles, tiles, tiles, P(), P(), P())
    return jax.shard_map(body, mesh=mesh, in_specs=in_specs, out_specs=tiles, check_vma=False)
```

```python
import functools

import jax
import jax.numpy as jnp
from jax import lax
from jax.experimental import pallas as pl
from jax.experimental.pallas import tpu as pltpu
from jax.sharding import PartitionSpec as P

F32 = jnp.float32
BF16 = jnp.bfloat16
MIB = 1 << 20


def vmem(count):
    return [pl.BlockSpec(memory_space=pltpu.VMEM)] * count


def hbm(array):
    return pltpu.with_memory_space_constraint(array, pltpu.HBM)


def params(mib):
    return pltpu.CompilerParams(vmem_limit_bytes=mib * MIB)


def cost(macs, moved):
    return pl.CostEstimate(flops=2 * macs, bytes_accessed=moved, transcendentals=0)


def mm(left, right):
    return jnp.dot(left, right, preferred_element_type=F32)


def count_rows(counts_ref, tile_x, tile_y, lanes):
    eye = lax.broadcasted_iota(jnp.int32, (tile_y, tile_y), 0) == lax.broadcasted_iota(
        jnp.int32, (tile_y, tile_y), 1
    )
    counts = counts_ref[...].astype(F32)
    diag = [
        jnp.where(eye, jnp.broadcast_to(counts[i : i + 1], (tile_y, tile_y)), 0.0) for i in range(tile_x)
    ]
    return mm(jnp.concatenate(diag, axis=0).astype(BF16), jnp.ones((tile_y, lanes), BF16))


def halo_pair(inner_ref, outer_ref, axis):
    at = lax.axis_index(axis)
    odd = at % 2 == 1
    inner, outer = inner_ref[...].astype(F32), outer_ref[...].astype(F32)
    before, after = jnp.where(odd, inner, outer), jnp.where(odd, outer, inner)
    return jnp.where(at > 0, before, 0.0), jnp.where(at < lax.axis_size(axis) - 1, after, 0.0)


LEFT = 8


def live_kernel(tile_x, tile_y, cur_hbm, counts_hbm, agg_hbm, up_hbm,
                live_ref, kept_ref, low_ref, high_ref, agg_ref, up_ref, cur_ref, counts_ref, wide, sems):
    pairs = [(counts_hbm, counts_ref), (cur_hbm, cur_ref), (agg_hbm, agg_ref), (up_hbm, up_ref)]
    loads = [
        pltpu.make_async_copy(source, target, sems.at[k]) for k, (source, target) in enumerate(pairs)
    ]
    for load in loads:
        load.start()
    lanes = cur_ref.shape[1]
    boxes = tile_x * tile_y
    loads[0].wait()
    limits = count_rows(counts_ref, tile_x, tile_y, lanes)
    keep = lax.broadcasted_iota(jnp.int32, (boxes, lanes), 1).astype(F32) < limits
    kept_ref[...] = jnp.where(keep, 1.0, 0.0)
    odd = lax.axis_index("gy") % 2 == 1
    loads[1].wait()
    wide[...] = cur_ref[...].astype(F32)
    for part in range(2):
        cols = slice(part * lanes, (part + 1) * lanes)
        live_ref[:, cols] = jnp.where(keep, wide[pl.ds(part, boxes, stride=2), :], 0.0).astype(BF16)

        def edge(column):
            rows = wide[pl.ds(2 * column + part, tile_x, stride=2 * tile_y), :]
            return rows * kept_ref[pl.ds(column, tile_x, stride=tile_y), :]

        first = jnp.concatenate([edge(0), edge(1)], axis=0).astype(BF16)
        last = jnp.concatenate([edge(tile_y - 2), edge(tile_y - 1)], axis=0).astype(BF16)
        low_ref[:, cols] = jnp.where(odd, first, last)
        high_ref[:, cols] = jnp.where(odd, last, first)
    for load in loads[2:]:
        load.wait()


def rims_kernel(tile_x, tile_y, live_ref, inner_ref, outer_ref, low_ref, high_ref, first, last):
    odd = lax.axis_index("gx") % 2 == 1
    sides = halo_pair(inner_ref, outer_ref, "gy")
    for rim, start in ((first, 0), (last, tile_x - 2)):
        rim[0 : 2 * tile_y, :] = live_ref[start * tile_y : (start + 2) * tile_y, :].astype(F32)
        place = 2 * tile_y
        for side in sides:
            for column in range(2):
                at = column * tile_x + start
                rim[place : place + 2, :] = side[at : at + 2]
                place += 2
        rim[place:, :] = jnp.zeros((rim.shape[0] - place, rim.shape[1]), F32)
    low_ref[...] = jnp.where(odd, first[...], last[...]).astype(BF16)
    high_ref[...] = jnp.where(odd, last[...], first[...]).astype(BF16)


def parents_kernel(tile_x, tile_y, live_ref, agg_ref, up_ref, coarse_ref, pats_ref, pats, rows4):
    lanes = pats.shape[2]
    width = tile_y + 2 * LEFT
    pattern = mm(live_ref[...], agg_ref[...])
    pats[0] = pattern[:, :lanes]
    pats[1] = pattern[:, lanes:]
    children = []
    for side_x in range(2):
        for side_y in range(2):
            for part in range(2):
                rows = [
                    pats[part, pl.ds((2 * p + side_x) * tile_y + side_y, tile_y // 2, stride=2), :]
                    for p in range(tile_x // 2)
                ]
                children.append(jnp.concatenate(rows, axis=0).astype(BF16))
    coarse = mm(jnp.concatenate(children, axis=1), up_ref[...])
    for place, column in enumerate((0, 2, 1, 3)):
        rows4[pl.ds(place, coarse.shape[0], stride=4), :] = coarse[:, column * 128 : (column + 1) * 128]
    coarse_ref[...] = rows4[...].astype(BF16)
    pattern = pattern.astype(BF16).astype(F32)
    values = [pattern[:, :lanes], pattern[:, lanes:], pattern[:, :lanes] + pattern[:, lanes:]]
    none = jnp.zeros((LEFT, lanes), F32)
    for i in range(tile_x):
        base = i * width
        for k in range(3):
            pats_ref[k, base : base + LEFT, :] = none
            pats_ref[k, base + LEFT : base + LEFT + tile_y, :] = values[k][i * tile_y : (i + 1) * tile_y]
            pats_ref[k, base + LEFT + tile_y : base + width, :] = none


OFFSETS = [(dx, dy) for dx in range(-2, 3) for dy in range(-2, 3) if max(abs(dx), abs(dy)) == 2]


def local_kernel(
    tile_x, tile_y, live_ref, pats, near_ref, low_ref, lower_ref, field_ref, cells, shifted, tables, sums,
):
    lanes = lower_ref.shape[2]
    width = tile_y + 2 * LEFT
    none = jnp.zeros((LEFT, lanes), F32)
    ends = jnp.zeros((tile_y, 6 * lanes), BF16)
    shifted[0:tile_y, :] = ends
    shifted[(tile_x + 1) * tile_y : (tile_x + 2) * tile_y, :] = ends
    shifted[tile_y : (tile_x + 1) * tile_y, 2 * lanes : 4 * lanes] = live_ref[...]
    for part in range(2):
        cols = slice(part * lanes, (part + 1) * lanes)
        for i in range(tile_x):
            base = i * width
            cells[part, base : base + LEFT, :] = none
            cells[part, base + LEFT : base + LEFT + tile_y, :] = live_ref[
                i * tile_y : (i + 1) * tile_y, cols
            ].astype(F32)
            cells[part, base + LEFT + tile_y : base + width, :] = none
            for shift in (-1, 1):
                place = (2 * (shift + 1) + part) * lanes
                shifted[(i + 1) * tile_y : (i + 2) * tile_y, place : place + lanes] = cells[
                    part, base + LEFT + shift : base + LEFT + shift + tile_y, :
                ].astype(BF16)
    for k in range(len(OFFSETS)):
        t_real, t_imag = low_ref[2 * k : 2 * k + 1, :], low_ref[2 * k + 1 : 2 * k + 2, :]
        for n, value in enumerate((t_imag - t_real, t_imag + t_real, t_real)):
            tables[3 * k + n] = jnp.broadcast_to(value, (8, lanes))

    passes = [
        [(dx, dy) for dx, dy in OFFSETS if dy == -2],
        [(dx, dy) for dx, dy in OFFSETS if dy == 2],
        [(dx, dy) for dx, dy in OFFSETS if abs(dy) < 2],
    ]
    blocks = tile_y // 8
    size = tile_x * tile_y // blocks

    def block(b, carry):
        total = None
        for shift in range(3):
            start = pl.multiple_of(b * size + shift * tile_y, tile_y)
            term = mm(shifted[pl.ds(start, size), :], near_ref[shift])
            total = term if total is None else total + term
        start = pl.multiple_of(b * size, size)
        field_ref[0, pl.ds(start, size), :] = total[:, :lanes]
        field_ref[1, pl.ds(start, size), :] = total[:, lanes:]
        shift_y = pl.multiple_of(b * 8, 8)
        for number, offsets in enumerate(passes):
            running = {}
            for row in range(tile_x):
                for dy in sorted({dy for _, dy in offsets}):
                    rows = pl.ds(shift_y + (row * width + LEFT + dy), 8)
                    source = [pats[k, rows, :] for k in range(3)]
                    for dx in range(-2, 3):
                        i = row - dx
                        if (dx, dy) not in offsets or not 0 <= i < tile_x:
                            continue
                        k = OFFSETS.index((dx, dy))
                        if i not in running:
                            running[i] = [None] * 3 if number == 0 else [sums[n, i] for n in range(3)]
                        running[i] = [
                            tables[3 * k + n] * source[n]
                            if running[i][n] is None
                            else running[i][n] + tables[3 * k + n] * source[n]
                            for n in range(3)
                        ]
                for i in sorted(running):
                    if i + 2 <= row or row == tile_x - 1:
                        value = running.pop(i)
                        if number < 2:
                            for n in range(3):
                                sums[n, i] = value[n]
                        else:
                            place = pl.ds(pl.multiple_of(shift_y + i * tile_y, 8), 8)
                            lower_ref[0, place, :] = value[2] - value[1]
                            lower_ref[1, place, :] = value[2] + value[0]
        return carry

    lax.fori_loop(0, blocks, block, 0)


def halos_kernel(
    tile_x, tile_y, inner_y, outer_y, inner_x, outer_x, agg_ref, near_ref, low_ref, lower_in, field_in,
    lower_ref, field_ref, columns, rims,
):
    lanes = lower_ref.shape[2]
    width = tile_y + 2 * LEFT
    halo = halo_pair(inner_y, outer_y, "gy") + halo_pair(inner_x, outer_x, "gx")
    lower_ref[...] = lower_in[...]
    field_ref[...] = field_in[...]
    halo = jnp.concatenate(halo, axis=0)
    pattern = mm(halo.astype(BF16), agg_ref[...]).astype(BF16).astype(F32)
    values = [halo[:, :lanes], halo[:, lanes:], pattern[:, :lanes], pattern[:, lanes:]]
    two = jnp.zeros((8, lanes), F32)
    rim_size = inner_x.shape[0]
    for n, value in enumerate(values):
        for side in range(2):
            for c in range(2):
                at = (2 * side + c) * tile_x
                columns[n, 2 * side + c, 0:8, :] = two
                columns[n, 2 * side + c, 8 : 8 + tile_x, :] = value[at : at + tile_x]
                columns[n, 2 * side + c, 8 + tile_x : 16 + tile_x, :] = two
        for end in range(2):
            at = 4 * tile_x + end * rim_size
            corner = at + 2 * tile_y
            for row in range(2):
                base = (2 * end + row) * width + LEFT
                rims[n, base : base + tile_y, :] = value[at + row * tile_y : at + (row + 1) * tile_y]
                for side in range(2):
                    for c in range(2):
                        place = base + (tile_y + c if side else c - 2)
                        line = corner + 4 * side + 2 * c + row
                        rims[n, place : place + 1, :] = value[line : line + 1]

    def translate(terms):
        first = second = 0.0
        for dx, dy, real, imag in terms:
            k = OFFSETS.index((dx, dy))
            t_real, t_imag = low_ref[2 * k : 2 * k + 1, :], low_ref[2 * k + 1 : 2 * k + 2, :]
            first = first + (t_real * real - t_imag * imag)
            second = second + (t_real * imag + t_imag * real)
        return first, second

    def column(n, side, c, dx):
        return columns[n, 2 * side + c, 8 + dx : 8 + dx + tile_x, :]

    def rim(n, end, row, dy):
        base = (2 * end + row) * width + LEFT + dy
        return rims[n, base : base + tile_y, :]

    for side in range(2):
        for box in ((tile_y - 1, tile_y - 2) if side else (0, 1)):
            terms = []
            for c in range(2):
                dy = (tile_y + c if side else c - 2) - box
                for dx in range(-2, 3):
                    if (dx, dy) in OFFSETS:
                        terms.append((dx, dy, column(2, side, c, dx), column(3, side, c, dx)))
            rows = pl.ds(box, tile_x, stride=tile_y)
            for part, value in enumerate(translate(terms)):
                lower_ref[part, rows, :] = lower_ref[part, rows, :] + value
        source = jnp.concatenate(
            [column(part, side, 1 - side, dx) for dx in range(-1, 2) for part in range(2)], axis=1
        ).astype(BF16)
        weights = [near_ref[dx, (4 * side) * lanes : (4 * side + 2) * lanes, :] for dx in range(3)]
        value = mm(source, jnp.concatenate(weights, axis=0))
        rows = pl.ds(tile_y - 1 if side else 0, tile_x, stride=tile_y)
        for part in range(2):
            field_ref[part, rows, :] = field_ref[part, rows, :] + value[:, part * lanes : (part + 1) * lanes]
    for end in range(2):
        for box in ((tile_x - 1, tile_x - 2) if end else (0, 1)):
            terms = []
            for row in range(2):
                dx = (tile_x + row if end else row - 2) - box
                for dy in range(-2, 3):
                    if (dx, dy) in OFFSETS:
                        terms.append((dx, dy, rim(2, end, row, dy), rim(3, end, row, dy)))
            rows = slice(box * tile_y, (box + 1) * tile_y)
            for part, value in enumerate(translate(terms)):
                lower_ref[part, rows, :] = lower_ref[part, rows, :] + value
        source = jnp.concatenate(
            [rim(part, end, 1 - end, dy) for dy in range(-1, 2) for part in range(2)], axis=1
        ).astype(BF16)
        value = mm(source, near_ref[2 * end])
        box = tile_x - 1 if end else 0
        rows = slice(box * tile_y, (box + 1) * tile_y)
        for part in range(2):
            field_ref[part, rows, :] = field_ref[part, rows, :] + value[:, part * lanes : (part + 1) * lanes]


GROUP = 8


def expand_kernel(chunks, *refs):
    sources = refs[:chunks]
    table_ref, cells, table8 = refs[chunks:]
    kinds = table_ref.shape[0] // 4
    lanes = table_ref.shape[1]
    rows8 = table8.reshape(8 * kinds + 8, lanes)
    for place, row in enumerate((0, 0, 2, 2, 1, 1, 3, 3)):
        rows8[pl.ds(place, kinds, stride=8), :] = table_ref[pl.ds(row, kinds, stride=4), :]
    table8[kinds] = jnp.zeros((8, lanes), F32)
    count = cells.shape[0] // chunks // 2
    pairs = cells.reshape(chunks * count, 2, 8, lanes)
    upper = lax.broadcasted_iota(jnp.int32, (count, 8, lanes), 1) < 4
    for c in range(chunks):
        rows = sources[c][...].astype(F32).reshape(count, 8, lanes)
        turned = pltpu.roll(rows, 4, axis=1)
        pairs[c * count : (c + 1) * count, 0] = jnp.where(upper, rows, turned)
        pairs[c * count : (c + 1) * count, 1] = jnp.where(upper, turned, rows)


def lists_kernel(chunks, parents_y, slots, cells, table8, list_ref, kind_ref, number_ref, down_hbm,
                 incoming_ref, down_ref, sums, places, at, sems):
    groups, lanes = list_ref.shape
    parents = groups * GROUP
    kinds = table8.shape[0] - 1
    across = parents_y * chunks
    entry = list_ref[...]
    line, place = entry // across, entry % across
    places[0:groups, :] = (
        ((place // parents_y) ^ lax.axis_index("gy")) * parents + line * parents_y + place % parents_y
    )
    spread = lax.broadcasted_iota(jnp.int32, (GROUP, lanes), 0) == (
        lax.broadcasted_iota(jnp.int32, (GROUP, lanes), 1) // slots
    )
    numbers = mm(number_ref[...].astype(F32).astype(BF16), jnp.where(spread, 1.0, 0.0).astype(BF16))
    slot = lax.broadcasted_iota(jnp.int32, (groups, lanes), 1) % slots
    places[groups:, :] = jnp.where(slot < numbers.astype(jnp.int32), kind_ref[...], kinds)
    loads = [
        pltpu.make_async_copy(places, at, sems.at[0]),
        pltpu.make_async_copy(down_hbm, down_ref, sems.at[1]),
    ]
    for load in loads:
        load.start()
    loads[0].wait()

    def step(n, carry):
        for k in range(GROUP):
            total = [None, None]
            for s in range(slots):
                term = cells[at[n, k * slots + s]] * table8[at[groups + n, k * slots + s]]
                total[s % 2] = term if total[s % 2] is None else total[s % 2] + term
            sums[n * GROUP + k] = total[0] + total[1]
        return carry

    lax.fori_loop(0, groups, step, 0)
    lines = sums.reshape(8 * parents, sums.shape[2])

    def row(place):
        return lines[pl.ds(place, parents, stride=8), :]

    incoming_ref[...] = jnp.concatenate(
        [row(0) - row(5), row(2) - row(7), row(1) + row(4), row(3) + row(6)], axis=1
    ).astype(BF16)
    loads[1].wait()


def finish_kernel(tile_x, tile_y, incoming_ref, down_ref, kept_ref, lower_ref, near_ref, recv_ref, out_hbm,
                  total_ref, out_ref, sems):
    parents_x, parents_y = tile_x // 2, tile_y // 2
    parents = parents_x * parents_y
    lanes = lower_ref.shape[2]
    starts = [
        [(2 * p + child // 2) * tile_y + child % 2 for p in range(parents_x)] for child in range(4)
    ]

    def rows_of(ref, lines):
        return jnp.concatenate([ref[pl.ds(line, parents_y, stride=2), :] for line in lines], axis=0)

    for child in range(4):
        down = mm(incoming_ref[...], down_ref[child])
        for part in range(2):
            value = down[:, part * lanes : (part + 1) * lanes] + rows_of(lower_ref.at[part], starts[child])
            total_ref[child, :, part * lanes : (part + 1) * lanes] = value.astype(BF16)
    stores = []
    for half in range(2):
        count = parents_x // 2
        rows = slice(half * parents // 2, (half + 1) * parents // 2)
        for child in range(4):
            field = mm(total_ref[child, rows, :], recv_ref[...])
            lines = starts[child][half * count : (half + 1) * count]
            mask = rows_of(kept_ref, lines)
            for part in range(2):
                value = field[:, part * lanes : (part + 1) * lanes] + rows_of(near_ref.at[part], lines)
                value = value * mask
                for p, line in enumerate(lines):
                    out_ref[pl.ds(2 * line + part, parents_y, stride=4), :] = value[
                        p * parents_y : (p + 1) * parents_y
                    ]
        size = out_ref.shape[0] // 2
        rows = pl.ds(half * size, size)
        stores.append(pltpu.make_async_copy(out_ref.at[rows], out_hbm.at[rows], sems.at[half]))
        stores[-1].start()
    for store in stores:
        store.wait()


def swap(low, high, axis):
    count = lax.axis_size(axis)
    lows = [(i, i ^ 1) for i in range(count)]
    highs = [(i, i if i in (0, count - 1) else ((i + 1) ^ 1) - 1) for i in range(count)]
    return lax.ppermute(low, axis, lows), lax.ppermute(high, axis, highs)


def body(
    currents, box_count, aggregate, near_blocks, low_translator, child_to_parent, coarse_list,
    coarse_kind, coarse_count, up_translator, parent_to_child, receive_map,
):
    tile_x, tile_y = box_count.shape
    boxes = tile_x * tile_y
    lanes = currents.shape[-1]
    parents_x, parents_y, slots = coarse_list.shape
    parents = parents_x * parents_y
    kinds, _, half = up_translator.shape
    wide = 2 * half
    chunks = lax.axis_size("gy")
    in_hbm = pl.BlockSpec(memory_space=pltpu.HBM)

    edge = jax.ShapeDtypeStruct((2 * tile_x, 2 * lanes), BF16)
    edge = jax.ShapeDtypeStruct((2 * tile_x, 2 * lanes), BF16)
    width = tile_y + 2 * LEFT
    live, kept, low, high, agg_near, up_near = pl.pallas_call(
        functools.partial(live_kernel, tile_x, tile_y),
        name="live",
        out_shape=[
            jax.ShapeDtypeStruct((boxes, 2 * lanes), BF16),
            jax.ShapeDtypeStruct((boxes, lanes), F32),
            edge,
            edge,
            jax.ShapeDtypeStruct((2 * lanes, 2 * lanes), BF16),
            jax.ShapeDtypeStruct((8 * lanes, wide), BF16),
        ],
        in_specs=[in_hbm] * 4,
        out_specs=vmem(6),
        scratch_shapes=[
            pltpu.VMEM((2 * boxes, lanes), BF16),
            pltpu.VMEM((tile_x, tile_y), jnp.int32),
            pltpu.VMEM((2 * boxes, lanes), F32),
            pltpu.SemaphoreType.DMA((4,)),
        ],
        compiler_params=params(16),
        cost_estimate=cost(100 * MIB, 3 * MIB),
    )(
        hbm(currents.reshape(2 * boxes, lanes)), hbm(box_count), hbm(aggregate),
        hbm(child_to_parent.reshape(8 * lanes, wide)),
    )
    coarse, pats = pl.pallas_call(
        functools.partial(parents_kernel, tile_x, tile_y),
        name="parents",
        out_shape=[
            jax.ShapeDtypeStruct((4 * parents, wide // 4), BF16),
            jax.ShapeDtypeStruct((3, tile_x * width, lanes), F32),
        ],
        in_specs=vmem(3),
        out_specs=vmem(2),
        scratch_shapes=[
            pltpu.VMEM((2, boxes, lanes), F32),
            pltpu.VMEM((4 * parents, wide // 4), F32),
        ],
        compiler_params=params(16),
        cost_estimate=cost(200 * MIB, 3 * MIB),
    )(live, agg_near, up_near)
    inner_y, outer_y = swap(low, high, "gy")
    sources = [coarse] + [
        lax.ppermute(coarse, "gy", [(i, i ^ d) for i in range(chunks)]) for d in range(1, chunks)
    ]

    rim = 2 * tile_y + 8
    rim += -rim % 16
    low, high = pl.pallas_call(
        functools.partial(rims_kernel, tile_x, tile_y),
        name="rims",
        out_shape=[jax.ShapeDtypeStruct((rim, 2 * lanes), BF16)] * 2,
        in_specs=vmem(3),
        out_specs=vmem(2),
        scratch_shapes=[pltpu.VMEM((rim, 2 * lanes), F32)] * 2,
        compiler_params=params(16),
        cost_estimate=cost(1 * MIB, MIB),
    )(live, inner_y, outer_y)
    inner_x, outer_x = swap(low, high, "gx")

    near_rows = near_blocks.reshape(3, 6 * lanes, 2 * lanes)
    low_rows = low_translator.reshape(-1, lanes)
    pair = [jax.ShapeDtypeStruct((2, boxes, lanes), F32)] * 2
    lower, near = pl.pallas_call(
        functools.partial(local_kernel, tile_x, tile_y),
        name="local",
        out_shape=pair,
        in_specs=vmem(4),
        out_specs=vmem(2),
        scratch_shapes=[
            pltpu.VMEM((2, tile_x * width, lanes), F32),
            pltpu.VMEM(((tile_x + 2) * tile_y, 6 * lanes), BF16),
            pltpu.VMEM((3 * len(OFFSETS), 8, lanes), F32),
            pltpu.VMEM((3, tile_x, 8, lanes), F32),
        ],
        compiler_params=params(16),
        cost_estimate=cost(2000 * MIB, 5 * MIB),
    )(live, pats, near_rows, low_rows)

    lower, near = pl.pallas_call(
        functools.partial(halos_kernel, tile_x, tile_y),
        name="halos",
        out_shape=pair,
        in_specs=vmem(9),
        out_specs=vmem(2),
        scratch_shapes=[
            pltpu.VMEM((4, 4, tile_x + 16, lanes), F32),
            pltpu.VMEM((4, 4 * width, lanes), F32),
        ],
        compiler_params=params(16),
        cost_estimate=cost(100 * MIB, 5 * MIB),
    )(inner_y, outer_y, inner_x, outer_x, agg_near, near_rows, low_rows, lower, near)

    table = up_translator.reshape(kinds, 2, 2, half // 2).transpose(0, 2, 1, 3).reshape(4 * kinds, half // 2)
    cells, table8 = pl.pallas_call(
        functools.partial(expand_kernel, chunks),
        name="expand",
        out_shape=[
            jax.ShapeDtypeStruct((chunks * parents, 8, wide // 4), F32),
            jax.ShapeDtypeStruct((kinds + 1, 8, wide // 4), F32),
        ],
        in_specs=vmem(chunks + 1),
        out_specs=vmem(2),
        compiler_params=params(16 if chunks <= 4 else 32),
        cost_estimate=cost(MIB, 6 * MIB),
    )(*sources, table)
    groups = parents // GROUP
    incoming, down = pl.pallas_call(
        functools.partial(lists_kernel, chunks, parents_y, slots),
        name="lists",
        out_shape=[
            jax.ShapeDtypeStruct((parents, wide), BF16),
            jax.ShapeDtypeStruct((4, wide, 2 * lanes), BF16),
        ],
        in_specs=vmem(5) + [in_hbm],
        out_specs=vmem(2),
        scratch_shapes=[
            pltpu.VMEM((parents, 8, wide // 4), F32),
            pltpu.VMEM((2 * groups, GROUP * slots), jnp.int32),
            pltpu.SMEM((2 * groups, GROUP * slots), jnp.int32),
            pltpu.SemaphoreType.DMA((2,)),
        ],
        compiler_params=params(16 if chunks <= 4 else 32),
        cost_estimate=cost(2000 * MIB, 8 * MIB),
    )(
        cells, table8, coarse_list.reshape(groups, GROUP * slots), coarse_kind.reshape(groups, GROUP * slots),
        coarse_count.reshape(groups, GROUP), hbm(parent_to_child),
    )
    out = pl.pallas_call(
        functools.partial(finish_kernel, tile_x, tile_y),
        name="finish",
        out_shape=jax.ShapeDtypeStruct((2 * boxes, lanes), F32),
        in_specs=vmem(6),
        out_specs=in_hbm,
        scratch_shapes=[
            pltpu.VMEM((4, parents, 2 * lanes), BF16),
            pltpu.VMEM((2 * boxes, lanes), F32),
            pltpu.SemaphoreType.DMA((2,)),
        ],
        compiler_params=params(16),
        cost_estimate=cost(300 * MIB, 4 * MIB),
    )(incoming, down, kept, lower, near, receive_map)
    return out.reshape(tile_x, tile_y, 2, lanes)


def solution(mesh):
    tiles = P("gx", "gy")
    in_specs = (tiles, tiles, P(), P(), P(), P(), tiles, tiles, tiles, P(), P(), P())
    return jax.shard_map(body, mesh=mesh, in_specs=in_specs, out_specs=tiles, check_vma=False)
```

```python
import functools

import jax
import jax.numpy as jnp
from jax import lax
from jax.experimental import pallas as pl
from jax.experimental.pallas import tpu as pltpu
from jax.sharding import PartitionSpec as P

F32 = jnp.float32
BF16 = jnp.bfloat16
MIB = 1 << 20


def vmem(count):
    return [pl.BlockSpec(memory_space=pltpu.VMEM)] * count


def hbm(array):
    return pltpu.with_memory_space_constraint(array, pltpu.HBM)


def params(mib):
    return pltpu.CompilerParams(vmem_limit_bytes=mib * MIB)


def cost(macs, moved):
    return pl.CostEstimate(flops=2 * macs, bytes_accessed=moved, transcendentals=0)


def mm(left, right):
    return jnp.dot(left, right, preferred_element_type=F32)


def count_rows(counts_ref, tile_x, tile_y, lanes):
    eye = lax.broadcasted_iota(jnp.int32, (tile_y, tile_y), 0) == lax.broadcasted_iota(
        jnp.int32, (tile_y, tile_y), 1
    )
    counts = counts_ref[...].astype(F32)
    diag = [
        jnp.where(eye, jnp.broadcast_to(counts[i : i + 1], (tile_y, tile_y)), 0.0) for i in range(tile_x)
    ]
    return mm(jnp.concatenate(diag, axis=0).astype(BF16), jnp.ones((tile_y, lanes), BF16))


def halo_pair(inner_ref, outer_ref, axis):
    at = lax.axis_index(axis)
    odd = at % 2 == 1
    inner, outer = inner_ref[...].astype(F32), outer_ref[...].astype(F32)
    before, after = jnp.where(odd, inner, outer), jnp.where(odd, outer, inner)
    return jnp.where(at > 0, before, 0.0), jnp.where(at < lax.axis_size(axis) - 1, after, 0.0)


LEFT = 8


def live_kernel(tile_x, tile_y, cur_hbm, counts_hbm, agg_hbm, up_hbm,
                live_ref, kept_ref, low_ref, high_ref, agg_ref, up_ref, cur_ref, counts_ref, wide, sems):
    pairs = [(counts_hbm, counts_ref), (cur_hbm, cur_ref), (agg_hbm, agg_ref), (up_hbm, up_ref)]
    loads = [
        pltpu.make_async_copy(source, target, sems.at[k]) for k, (source, target) in enumerate(pairs)
    ]
    for load in loads:
        load.start()
    lanes = cur_ref.shape[1]
    boxes = tile_x * tile_y
    loads[0].wait()
    limits = count_rows(counts_ref, tile_x, tile_y, lanes)
    keep = lax.broadcasted_iota(jnp.int32, (boxes, lanes), 1).astype(F32) < limits
    kept_ref[...] = jnp.where(keep, 1.0, 0.0)
    odd = lax.axis_index("gy") % 2 == 1
    loads[1].wait()
    wide[...] = cur_ref[...].astype(F32)
    for part in range(2):
        cols = slice(part * lanes, (part + 1) * lanes)
        live_ref[:, cols] = jnp.where(keep, wide[pl.ds(part, boxes, stride=2), :], 0.0).astype(BF16)

        def edge(column):
            rows = wide[pl.ds(2 * column + part, tile_x, stride=2 * tile_y), :]
            return rows * kept_ref[pl.ds(column, tile_x, stride=tile_y), :]

        first = jnp.concatenate([edge(0), edge(1)], axis=0).astype(BF16)
        last = jnp.concatenate([edge(tile_y - 2), edge(tile_y - 1)], axis=0).astype(BF16)
        low_ref[:, cols] = jnp.where(odd, first, last)
        high_ref[:, cols] = jnp.where(odd, last, first)
    for load in loads[2:]:
        load.wait()


def rims_kernel(tile_x, tile_y, live_ref, inner_ref, outer_ref, low_ref, high_ref, first, last):
    odd = lax.axis_index("gx") % 2 == 1
    sides = halo_pair(inner_ref, outer_ref, "gy")
    for rim, start in ((first, 0), (last, tile_x - 2)):
        rim[0 : 2 * tile_y, :] = live_ref[start * tile_y : (start + 2) * tile_y, :].astype(F32)
        place = 2 * tile_y
        for side in sides:
            for column in range(2):
                at = column * tile_x + start
                rim[place : place + 2, :] = side[at : at + 2]
                place += 2
        rim[place:, :] = jnp.zeros((rim.shape[0] - place, rim.shape[1]), F32)
    low_ref[...] = jnp.where(odd, first[...], last[...]).astype(BF16)
    high_ref[...] = jnp.where(odd, last[...], first[...]).astype(BF16)


def parents_kernel(tile_x, tile_y, live_ref, agg_ref, up_ref, coarse_ref, pats_ref, pats, rows4):
    lanes = pats.shape[2]
    width = tile_y + 2 * LEFT
    pattern = mm(live_ref[...], agg_ref[...])
    pats[0] = pattern[:, :lanes]
    pats[1] = pattern[:, lanes:]
    children = []
    for side_x in range(2):
        for side_y in range(2):
            for part in range(2):
                rows = [
                    pats[part, pl.ds((2 * p + side_x) * tile_y + side_y, tile_y // 2, stride=2), :]
                    for p in range(tile_x // 2)
                ]
                children.append(jnp.concatenate(rows, axis=0).astype(BF16))
    coarse = mm(jnp.concatenate(children, axis=1), up_ref[...])
    for place, column in enumerate((0, 2, 1, 3)):
        rows4[pl.ds(place, coarse.shape[0], stride=4), :] = coarse[:, column * 128 : (column + 1) * 128]
    coarse_ref[...] = rows4[...].astype(BF16)
    pattern = pattern.astype(BF16).astype(F32)
    values = [pattern[:, :lanes], pattern[:, lanes:], pattern[:, :lanes] + pattern[:, lanes:]]
    none = jnp.zeros((LEFT, lanes), F32)
    for i in range(tile_x):
        base = i * width
        for k in range(3):
            pats_ref[k, base : base + LEFT, :] = none
            pats_ref[k, base + LEFT : base + LEFT + tile_y, :] = values[k][i * tile_y : (i + 1) * tile_y]
            pats_ref[k, base + LEFT + tile_y : base + width, :] = none


OFFSETS = [(dx, dy) for dx in range(-2, 3) for dy in range(-2, 3) if max(abs(dx), abs(dy)) == 2]


def local_kernel(
    tile_x, tile_y, live_ref, pats, near_ref, low_ref, lower_ref, field_ref, cells, shifted, tables, sums,
):
    lanes = lower_ref.shape[2]
    width = tile_y + 2 * LEFT
    none = jnp.zeros((LEFT, lanes), F32)
    ends = jnp.zeros((tile_y, 6 * lanes), BF16)
    shifted[0:tile_y, :] = ends
    shifted[(tile_x + 1) * tile_y : (tile_x + 2) * tile_y, :] = ends
    shifted[tile_y : (tile_x + 1) * tile_y, 2 * lanes : 4 * lanes] = live_ref[...]
    for part in range(2):
        cols = slice(part * lanes, (part + 1) * lanes)
        for i in range(tile_x):
            base = i * width
            cells[part, base : base + LEFT, :] = none
            cells[part, base + LEFT : base + LEFT + tile_y, :] = live_ref[
                i * tile_y : (i + 1) * tile_y, cols
            ].astype(F32)
            cells[part, base + LEFT + tile_y : base + width, :] = none
            for shift in (-1, 1):
                place = (2 * (shift + 1) + part) * lanes
                shifted[(i + 1) * tile_y : (i + 2) * tile_y, place : place + lanes] = cells[
                    part, base + LEFT + shift : base + LEFT + shift + tile_y, :
                ].astype(BF16)
    for k in range(len(OFFSETS)):
        t_real, t_imag = low_ref[2 * k : 2 * k + 1, :], low_ref[2 * k + 1 : 2 * k + 2, :]
        for n, value in enumerate((t_imag - t_real, t_imag + t_real, t_real)):
            tables[3 * k + n] = jnp.broadcast_to(value, (8, lanes))

    passes = [
        [(dx, dy) for dx, dy in OFFSETS if dy == -2],
        [(dx, dy) for dx, dy in OFFSETS if dy == 2],
        [(dx, dy) for dx, dy in OFFSETS if abs(dy) < 2],
    ]
    blocks = tile_y // 8
    size = tile_x * tile_y // blocks

    def block(b, carry):
        total = None
        for shift in range(3):
            start = pl.multiple_of(b * size + shift * tile_y, tile_y)
            term = mm(shifted[pl.ds(start, size), :], near_ref[shift])
            total = term if total is None else total + term
        start = pl.multiple_of(b * size, size)
        field_ref[0, pl.ds(start, size), :] = total[:, :lanes]
        field_ref[1, pl.ds(start, size), :] = total[:, lanes:]
        shift_y = pl.multiple_of(b * 8, 8)
        for number, offsets in enumerate(passes):
            running = {}
            for row in range(tile_x):
                for dy in sorted({dy for _, dy in offsets}):
                    rows = pl.ds(shift_y + (row * width + LEFT + dy), 8)
                    source = [pats[k, rows, :] for k in range(3)]
                    for dx in range(-2, 3):
                        i = row - dx
                        if (dx, dy) not in offsets or not 0 <= i < tile_x:
                            continue
                        k = OFFSETS.index((dx, dy))
                        if i not in running:
                            running[i] = [None] * 3 if number == 0 else [sums[n, i] for n in range(3)]
                        running[i] = [
                            tables[3 * k + n] * source[n]
                            if running[i][n] is None
                            else running[i][n] + tables[3 * k + n] * source[n]
                            for n in range(3)
                        ]
                for i in sorted(running):
                    if i + 2 <= row or row == tile_x - 1:
                        value = running.pop(i)
                        if number < 2:
                            for n in range(3):
                                sums[n, i] = value[n]
                        else:
                            place = pl.ds(pl.multiple_of(shift_y + i * tile_y, 8), 8)
                            lower_ref[0, place, :] = value[2] - value[1]
                            lower_ref[1, place, :] = value[2] + value[0]
        return carry

    lax.fori_loop(0, blocks, block, 0)


def halos_kernel(
    tile_x, tile_y, inner_y, outer_y, inner_x, outer_x, agg_ref, near_ref, low_ref, lower_in, field_in,
    lower_ref, field_ref, columns, rims,
):
    lanes = lower_ref.shape[2]
    width = tile_y + 2 * LEFT
    halo = halo_pair(inner_y, outer_y, "gy") + halo_pair(inner_x, outer_x, "gx")
    lower_ref[...] = lower_in[...]
    field_ref[...] = field_in[...]
    halo = jnp.concatenate(halo, axis=0)
    pattern = mm(halo.astype(BF16), agg_ref[...]).astype(BF16).astype(F32)
    values = [halo[:, :lanes], halo[:, lanes:], pattern[:, :lanes], pattern[:, lanes:]]
    two = jnp.zeros((8, lanes), F32)
    rim_size = inner_x.shape[0]
    for n, value in enumerate(values):
        for side in range(2):
            for c in range(2):
                at = (2 * side + c) * tile_x
                columns[n, 2 * side + c, 0:8, :] = two
                columns[n, 2 * side + c, 8 : 8 + tile_x, :] = value[at : at + tile_x]
                columns[n, 2 * side + c, 8 + tile_x : 16 + tile_x, :] = two
        for end in range(2):
            at = 4 * tile_x + end * rim_size
            corner = at + 2 * tile_y
            for row in range(2):
                base = (2 * end + row) * width + LEFT
                rims[n, base : base + tile_y, :] = value[at + row * tile_y : at + (row + 1) * tile_y]
                for side in range(2):
                    for c in range(2):
                        place = base + (tile_y + c if side else c - 2)
                        line = corner + 4 * side + 2 * c + row
                        rims[n, place : place + 1, :] = value[line : line + 1]

    def translate(terms):
        first = second = 0.0
        for dx, dy, real, imag in terms:
            k = OFFSETS.index((dx, dy))
            t_real, t_imag = low_ref[2 * k : 2 * k + 1, :], low_ref[2 * k + 1 : 2 * k + 2, :]
            first = first + (t_real * real - t_imag * imag)
            second = second + (t_real * imag + t_imag * real)
        return first, second

    def column(n, side, c, dx):
        return columns[n, 2 * side + c, 8 + dx : 8 + dx + tile_x, :]

    def rim(n, end, row, dy):
        base = (2 * end + row) * width + LEFT + dy
        return rims[n, base : base + tile_y, :]

    for side in range(2):
        for box in ((tile_y - 1, tile_y - 2) if side else (0, 1)):
            terms = []
            for c in range(2):
                dy = (tile_y + c if side else c - 2) - box
                for dx in range(-2, 3):
                    if (dx, dy) in OFFSETS:
                        terms.append((dx, dy, column(2, side, c, dx), column(3, side, c, dx)))
            rows = pl.ds(box, tile_x, stride=tile_y)
            for part, value in enumerate(translate(terms)):
                lower_ref[part, rows, :] = lower_ref[part, rows, :] + value
        source = jnp.concatenate(
            [column(part, side, 1 - side, dx) for dx in range(-1, 2) for part in range(2)], axis=1
        ).astype(BF16)
        weights = [near_ref[dx, (4 * side) * lanes : (4 * side + 2) * lanes, :] for dx in range(3)]
        value = mm(source, jnp.concatenate(weights, axis=0))
        rows = pl.ds(tile_y - 1 if side else 0, tile_x, stride=tile_y)
        for part in range(2):
            field_ref[part, rows, :] = field_ref[part, rows, :] + value[:, part * lanes : (part + 1) * lanes]
    for end in range(2):
        for box in ((tile_x - 1, tile_x - 2) if end else (0, 1)):
            terms = []
            for row in range(2):
                dx = (tile_x + row if end else row - 2) - box
                for dy in range(-2, 3):
                    if (dx, dy) in OFFSETS:
                        terms.append((dx, dy, rim(2, end, row, dy), rim(3, end, row, dy)))
            rows = slice(box * tile_y, (box + 1) * tile_y)
            for part, value in enumerate(translate(terms)):
                lower_ref[part, rows, :] = lower_ref[part, rows, :] + value
        source = jnp.concatenate(
            [rim(part, end, 1 - end, dy) for dy in range(-1, 2) for part in range(2)], axis=1
        ).astype(BF16)
        value = mm(source, near_ref[2 * end])
        box = tile_x - 1 if end else 0
        rows = slice(box * tile_y, (box + 1) * tile_y)
        for part in range(2):
            field_ref[part, rows, :] = field_ref[part, rows, :] + value[:, part * lanes : (part + 1) * lanes]


GROUP = 8


def order_kernel(chunks, kinds, parents_x, parents_y, list_ref, kind_ref, count_ref, at_ref, back_ref):
    parents = parents_x * parents_y
    slots = list_ref.shape[1]
    groups = parents // GROUP
    lanes = at_ref.shape[1]
    down = lax.broadcasted_iota(jnp.int32, (parents, parents), 0)
    along = lax.broadcasted_iota(jnp.int32, (parents, parents), 1)
    column = count_rows(count_ref, parents_x, parents_y, parents)
    row = jnp.sum(jnp.where(down == along, column, 0.0), axis=0, keepdims=True)
    before = (column > row) | ((column == row) & (down < along))
    rank = jnp.sum(jnp.where(before, 1.0, 0.0), axis=0, keepdims=True)
    after = (row > column) | ((row == column) & (along < down))
    rank_down = jnp.sum(jnp.where(after, 1.0, 0.0), axis=1, keepdims=True)
    back_ref[...] = jnp.where(along.astype(F32) == rank_down, 1.0, 0.0).astype(BF16)

    across = parents_y * chunks
    entry = list_ref[...]
    line, place = entry // across, entry % across
    source = ((place // parents_y) ^ lax.axis_index("gy")) * parents + line * parents_y + place % parents_y
    used = lax.broadcasted_iota(jnp.int32, (parents, slots), 1).astype(F32) < column[:, :slots]
    kind = jnp.where(used, kind_ref[...], kinds)
    slot = lax.broadcasted_iota(jnp.int32, (slots, lanes), 0)
    lane = lax.broadcasted_iota(jnp.int32, (slots, lanes), 1)
    values = [
        mm(value.astype(F32).astype(BF16), jnp.where(lane == slot + n * slots, 1.0, 0.0).astype(BF16))
        for n, value in enumerate((source // 256, source % 256, kind))
    ]
    values = (values[0] + values[1] + values[2]).astype(BF16)
    wanted = GROUP * (down % groups) + down // groups
    moved = mm(jnp.where(wanted.astype(F32) == rank, 1.0, 0.0).astype(BF16), values).astype(BF16)
    moved = jnp.concatenate([moved[k * groups : (k + 1) * groups] for k in range(GROUP)], axis=1)
    totals = []
    from_lane = lax.broadcasted_iota(jnp.int32, (GROUP * lanes, lanes), 0)
    to_lane = lax.broadcasted_iota(jnp.int32, (GROUP * lanes, lanes), 1)
    for n in range(3):
        spread = from_lane == (to_lane // slots) * lanes + n * slots + to_lane % slots
        totals.append(mm(moved, jnp.where(spread, 1.0, 0.0).astype(BF16)).astype(jnp.int32))
    at_ref[0:groups, :] = (totals[0] * 256 + totals[1]) * 8
    at_ref[groups : 2 * groups, :] = totals[2] * 8
    least = (slots - 1 - 2 * lax.broadcasted_iota(jnp.int32, (parents, lanes), 1)).astype(F32)
    reach = jnp.sum(jnp.where(column[:, :lanes] >= least, 1.0, 0.0), axis=0, keepdims=True).astype(jnp.int32)
    at_ref[2 * groups :, :] = jnp.broadcast_to((reach + (GROUP - 1)) // GROUP, (8, lanes))


def lists_kernel(chunks, tile_x, tile_y, slots, *refs):
    sources = refs[:chunks]
    (at_any, table_ref, back_ref, kept_ref, lower_ref, near_ref, recv_ref, down_hbm, out_hbm,
     cells, table8, sums, at, down_ref, total_ref, out_ref, sems) = refs[chunks:]
    parents_x, parents_y = tile_x // 2, tile_y // 2
    parents = parents_x * parents_y
    kinds = table_ref.shape[0] // 4
    lanes = table_ref.shape[1]
    groups = parents // GROUP
    loads = [
        pltpu.make_async_copy(at_any, at, sems.at[0]),
        pltpu.make_async_copy(down_hbm, down_ref, sems.at[1]),
    ]
    for load in loads:
        load.start()
    for place, row in enumerate((0, 0, 2, 2, 1, 1, 3, 3)):
        table8[pl.ds(place, kinds, stride=8), :] = table_ref[pl.ds(row, kinds, stride=4), :]
    table8[8 * kinds : 8 * kinds + 8, :] = jnp.zeros((8, lanes), F32)
    count = parents // 2
    pairs = cells.reshape(chunks * count, 2, 8, lanes)
    upper = lax.broadcasted_iota(jnp.int32, (count, 8, lanes), 1) < 4
    for c in range(chunks):
        rows = sources[c][...].astype(F32).reshape(count, 8, lanes)
        turned = pltpu.roll(rows, 4, axis=1)
        pairs[c * count : (c + 1) * count, 0] = jnp.where(upper, rows, turned)
        pairs[c * count : (c + 1) * count, 1] = jnp.where(upper, turned, rows)
    loads[0].wait()

    def step(length, n, carry):
        first = n * (GROUP * slots)
        second = first + groups * GROUP * slots
        for k in range(GROUP):
            total = [None, None]
            for s in range(length):
                source = pl.multiple_of(at[first + (k * slots + s)], 8)
                kind = pl.multiple_of(at[second + (k * slots + s)], 8)
                term = cells[pl.ds(source, 8), :] * table8[pl.ds(kind, 8), :]
                total[s % 2] = term if total[s % 2] is None else total[s % 2] + term
            total = total[0] + total[1] if length else jnp.zeros((8, lanes), F32)
            sums[pl.ds(pl.multiple_of((n * GROUP + k) * 8, 8), 8), :] = total
        return carry

    start = 0
    for j, length in enumerate(range(slots, 0, -2)):
        end = at[2 * groups * GROUP * slots + j]
        lax.fori_loop(start, end, functools.partial(step, length), 0)
        start = end
    lax.fori_loop(start, groups, functools.partial(step, 0), 0)

    def row(place):
        return sums[pl.ds(place, parents, stride=8), :]

    ordered = jnp.concatenate(
        [row(0) - row(5), row(2) - row(7), row(1) + row(4), row(3) + row(6)], axis=1
    ).astype(BF16)
    incoming = mm(back_ref[...], ordered).astype(BF16)
    loads[1].wait()
    starts = [
        [(2 * p + child // 2) * tile_y + child % 2 for p in range(parents_x)] for child in range(4)
    ]

    def rows_of(ref, lines):
        return jnp.concatenate([ref[pl.ds(line, parents_y, stride=2), :] for line in lines], axis=0)

    for child in range(4):
        down = mm(incoming, down_ref[child])
        for part in range(2):
            value = down[:, part * lanes : (part + 1) * lanes] + rows_of(lower_ref.at[part], starts[child])
            total_ref[child, :, part * lanes : (part + 1) * lanes] = value.astype(BF16)
    stores = []
    for half in range(2):
        count = parents_x // 2
        rows = slice(half * parents // 2, (half + 1) * parents // 2)
        for child in range(4):
            field = mm(total_ref[child, rows, :], recv_ref[...])
            lines = starts[child][half * count : (half + 1) * count]
            mask = rows_of(kept_ref, lines)
            for part in range(2):
                value = field[:, part * lanes : (part + 1) * lanes] + rows_of(near_ref.at[part], lines)
                value = value * mask
                for p, line in enumerate(lines):
                    out_ref[pl.ds(2 * line + part, parents_y, stride=4), :] = value[
                        p * parents_y : (p + 1) * parents_y
                    ]
        size = out_ref.shape[0] // 2
        rows = pl.ds(half * size, size)
        stores.append(pltpu.make_async_copy(out_ref.at[rows], out_hbm.at[rows], sems.at[2 + half]))
        stores[-1].start()
    for store in stores:
        store.wait()


def swap(low, high, axis):
    count = lax.axis_size(axis)
    lows = [(i, i ^ 1) for i in range(count)]
    highs = [(i, (((i + 1) % count ^ 1) - 1) % count) for i in range(count)]
    return lax.ppermute(low, axis, lows), lax.ppermute(high, axis, highs)


def body(
    currents, box_count, aggregate, near_blocks, low_translator, child_to_parent, coarse_list,
    coarse_kind, coarse_count, up_translator, parent_to_child, receive_map,
):
    tile_x, tile_y = box_count.shape
    boxes = tile_x * tile_y
    lanes = currents.shape[-1]
    parents_x, parents_y, slots = coarse_list.shape
    parents = parents_x * parents_y
    kinds, _, half = up_translator.shape
    wide = 2 * half
    chunks = lax.axis_size("gy")
    in_hbm = pl.BlockSpec(memory_space=pltpu.HBM)

    edge = jax.ShapeDtypeStruct((2 * tile_x, 2 * lanes), BF16)
    edge = jax.ShapeDtypeStruct((2 * tile_x, 2 * lanes), BF16)
    width = tile_y + 2 * LEFT
    live, kept, low, high, agg_near, up_near = pl.pallas_call(
        functools.partial(live_kernel, tile_x, tile_y),
        name="live",
        out_shape=[
            jax.ShapeDtypeStruct((boxes, 2 * lanes), BF16),
            jax.ShapeDtypeStruct((boxes, lanes), F32),
            edge,
            edge,
            jax.ShapeDtypeStruct((2 * lanes, 2 * lanes), BF16),
            jax.ShapeDtypeStruct((8 * lanes, wide), BF16),
        ],
        in_specs=[in_hbm] * 4,
        out_specs=vmem(6),
        scratch_shapes=[
            pltpu.VMEM((2 * boxes, lanes), BF16),
            pltpu.VMEM((tile_x, tile_y), jnp.int32),
            pltpu.VMEM((2 * boxes, lanes), F32),
            pltpu.SemaphoreType.DMA((4,)),
        ],
        compiler_params=params(10),
        cost_estimate=cost(100 * MIB, 3 * MIB),
    )(
        hbm(currents.reshape(2 * boxes, lanes)), hbm(box_count), hbm(aggregate),
        hbm(child_to_parent.reshape(8 * lanes, wide)),
    )
    coarse, pats = pl.pallas_call(
        functools.partial(parents_kernel, tile_x, tile_y),
        name="parents",
        out_shape=[
            jax.ShapeDtypeStruct((4 * parents, wide // 4), BF16),
            jax.ShapeDtypeStruct((3, tile_x * width, lanes), F32),
        ],
        in_specs=vmem(3),
        out_specs=vmem(2),
        scratch_shapes=[
            pltpu.VMEM((2, boxes, lanes), F32),
            pltpu.VMEM((4 * parents, wide // 4), F32),
        ],
        compiler_params=params(10),
        cost_estimate=cost(200 * MIB, 3 * MIB),
    )(live, agg_near, up_near)
    inner_y, outer_y = swap(low, high, "gy")
    sources = [coarse] + [
        lax.ppermute(coarse, "gy", [(i, i ^ d) for i in range(chunks)]) for d in range(1, chunks)
    ]

    rim = 2 * tile_y + 8
    rim += -rim % 16
    low, high = pl.pallas_call(
        functools.partial(rims_kernel, tile_x, tile_y),
        name="rims",
        out_shape=[jax.ShapeDtypeStruct((rim, 2 * lanes), BF16)] * 2,
        in_specs=vmem(3),
        out_specs=vmem(2),
        scratch_shapes=[pltpu.VMEM((rim, 2 * lanes), F32)] * 2,
        compiler_params=params(10),
        cost_estimate=cost(1 * MIB, MIB),
    )(live, inner_y, outer_y)
    inner_x, outer_x = swap(low, high, "gx")
    live, coarse_count, _ = lax.optimization_barrier((live, coarse_count, low))

    near_rows = near_blocks.reshape(3, 6 * lanes, 2 * lanes)
    low_rows = low_translator.reshape(-1, lanes)
    pair = [jax.ShapeDtypeStruct((2, boxes, lanes), F32)] * 2
    lower, near = pl.pallas_call(
        functools.partial(local_kernel, tile_x, tile_y),
        name="local",
        out_shape=pair,
        in_specs=vmem(4),
        out_specs=vmem(2),
        scratch_shapes=[
            pltpu.VMEM((2, tile_x * width, lanes), F32),
            pltpu.VMEM(((tile_x + 2) * tile_y, 6 * lanes), BF16),
            pltpu.VMEM((3 * len(OFFSETS), 8, lanes), F32),
            pltpu.VMEM((3, tile_x, 8, lanes), F32),
        ],
        compiler_params=params(10),
        cost_estimate=cost(2000 * MIB, 5 * MIB),
    )(live, pats, near_rows, low_rows)

    lower, near = pl.pallas_call(
        functools.partial(halos_kernel, tile_x, tile_y),
        name="halos",
        out_shape=pair,
        in_specs=vmem(9),
        out_specs=vmem(2),
        scratch_shapes=[
            pltpu.VMEM((4, 4, tile_x + 16, lanes), F32),
            pltpu.VMEM((4, 4 * width, lanes), F32),
        ],
        compiler_params=params(10),
        cost_estimate=cost(100 * MIB, 5 * MIB),
    )(inner_y, outer_y, inner_x, outer_x, agg_near, near_rows, low_rows, lower, near)

    table = up_translator.reshape(kinds, 2, 2, half // 2).transpose(0, 2, 1, 3).reshape(4 * kinds, half // 2)
    groups = parents // GROUP
    at, back = pl.pallas_call(
        functools.partial(order_kernel, chunks, kinds, parents_x, parents_y),
        name="order",
        out_shape=[
            jax.ShapeDtypeStruct((2 * groups + 8, GROUP * slots), jnp.int32),
            jax.ShapeDtypeStruct((parents, parents), BF16),
        ],
        in_specs=vmem(3),
        out_specs=vmem(2),
        compiler_params=params(8),
        cost_estimate=cost(300 * MIB, MIB),
    )(coarse_list.reshape(parents, slots), coarse_kind.reshape(parents, slots), coarse_count)
    at = at.reshape(-1)
    out = pl.pallas_call(
        functools.partial(lists_kernel, chunks, tile_x, tile_y, slots),
        name="lists",
        out_shape=jax.ShapeDtypeStruct((2 * boxes, lanes), F32),
        in_specs=vmem(chunks) + [pl.BlockSpec(memory_space=pl.ANY)] + vmem(6) + [in_hbm],
        out_specs=in_hbm,
        scratch_shapes=[
            pltpu.VMEM((chunks * parents * 8, wide // 4), F32),
            pltpu.VMEM((8 * kinds + 8, wide // 4), F32),
            pltpu.VMEM((8 * parents, wide // 4), F32),
            pltpu.SMEM(at.shape, jnp.int32),
            pltpu.VMEM((4, wide, 2 * lanes), BF16),
            pltpu.VMEM((4, parents, 2 * lanes), BF16),
            pltpu.VMEM((2 * boxes, lanes), F32),
            pltpu.SemaphoreType.DMA((4,)),
        ],
        compiler_params=params(16 if chunks <= 4 else 40),
        cost_estimate=cost(2000 * MIB, 8 * MIB),
    )(*sources, at, table, back, kept, lower, near, receive_map, hbm(parent_to_child))
    return out.reshape(tile_x, tile_y, 2, lanes)


def solution(mesh):
    tiles = P("gx", "gy")
    in_specs = (tiles, tiles, P(), P(), P(), P(), tiles, tiles, tiles, P(), P(), P())
    return jax.shard_map(body, mesh=mesh, in_specs=in_specs, out_specs=tiles, check_vma=False)
```

```python
import functools

import jax
import jax.numpy as jnp
from jax import lax
from jax.experimental import pallas as pl
from jax.experimental.pallas import tpu as pltpu
from jax.sharding import PartitionSpec as P

F32 = jnp.float32
BF16 = jnp.bfloat16
MIB = 1 << 20


def vmem(count):
    return [pl.BlockSpec(memory_space=pltpu.VMEM)] * count


def hbm(array):
    return pltpu.with_memory_space_constraint(array, pltpu.HBM)


def params(mib):
    return pltpu.CompilerParams(vmem_limit_bytes=mib * MIB)


def cost(macs, moved):
    return pl.CostEstimate(flops=2 * macs, bytes_accessed=moved, transcendentals=0)


def mm(left, right):
    return jnp.dot(left, right, preferred_element_type=F32)


def count_rows(counts_ref, tile_x, tile_y, lanes):
    eye = lax.broadcasted_iota(jnp.int32, (tile_y, tile_y), 0) == lax.broadcasted_iota(
        jnp.int32, (tile_y, tile_y), 1
    )
    counts = counts_ref[...].astype(F32)
    diag = [
        jnp.where(eye, jnp.broadcast_to(counts[i : i + 1], (tile_y, tile_y)), 0.0) for i in range(tile_x)
    ]
    return mm(jnp.concatenate(diag, axis=0).astype(BF16), jnp.ones((tile_y, lanes), BF16))


def halo_pair(inner_ref, outer_ref, axis):
    at = lax.axis_index(axis)
    odd = at % 2 == 1
    inner, outer = inner_ref[...].astype(F32), outer_ref[...].astype(F32)
    before, after = jnp.where(odd, inner, outer), jnp.where(odd, outer, inner)
    return jnp.where(at > 0, before, 0.0), jnp.where(at < lax.axis_size(axis) - 1, after, 0.0)


LEFT = 8


def live_kernel(tile_x, tile_y, cur_hbm, counts_hbm, agg_hbm, up_hbm,
                live_ref, kept_ref, low_ref, high_ref, agg_ref, up_ref, cur_ref, counts_ref, wide, sems):
    pairs = [(counts_hbm, counts_ref), (cur_hbm, cur_ref), (agg_hbm, agg_ref), (up_hbm, up_ref)]
    loads = [
        pltpu.make_async_copy(source, target, sems.at[k]) for k, (source, target) in enumerate(pairs)
    ]
    for load in loads:
        load.start()
    lanes = cur_ref.shape[1]
    boxes = tile_x * tile_y
    loads[0].wait()
    limits = count_rows(counts_ref, tile_x, tile_y, lanes)
    keep = lax.broadcasted_iota(jnp.int32, (boxes, lanes), 1).astype(F32) < limits
    kept_ref[...] = jnp.where(keep, 1.0, 0.0)
    odd = lax.axis_index("gy") % 2 == 1
    loads[1].wait()
    wide[...] = cur_ref[...].astype(F32)
    for part in range(2):
        cols = slice(part * lanes, (part + 1) * lanes)
        live_ref[:, cols] = jnp.where(keep, wide[pl.ds(part, boxes, stride=2), :], 0.0).astype(BF16)

        def edge(column):
            rows = wide[pl.ds(2 * column + part, tile_x, stride=2 * tile_y), :]
            return rows * kept_ref[pl.ds(column, tile_x, stride=tile_y), :]

        first = jnp.concatenate([edge(0), edge(1)], axis=0).astype(BF16)
        last = jnp.concatenate([edge(tile_y - 2), edge(tile_y - 1)], axis=0).astype(BF16)
        low_ref[:, cols] = jnp.where(odd, first, last)
        high_ref[:, cols] = jnp.where(odd, last, first)
    for load in loads[2:]:
        load.wait()


def rims_kernel(tile_x, tile_y, live_ref, inner_ref, outer_ref, low_ref, high_ref, first, last):
    odd = lax.axis_index("gx") % 2 == 1
    sides = halo_pair(inner_ref, outer_ref, "gy")
    for rim, start in ((first, 0), (last, tile_x - 2)):
        rim[0 : 2 * tile_y, :] = live_ref[start * tile_y : (start + 2) * tile_y, :].astype(F32)
        place = 2 * tile_y
        for side in sides:
            for column in range(2):
                at = column * tile_x + start
                rim[place : place + 2, :] = side[at : at + 2]
                place += 2
        rim[place:, :] = jnp.zeros((rim.shape[0] - place, rim.shape[1]), F32)
    low_ref[...] = jnp.where(odd, first[...], last[...]).astype(BF16)
    high_ref[...] = jnp.where(odd, last[...], first[...]).astype(BF16)


def parents_kernel(tile_x, tile_y, live_ref, agg_ref, up_ref, coarse_ref, pats_ref, pats, rows4):
    lanes = pats.shape[2]
    width = tile_y + 2 * LEFT
    pattern = mm(live_ref[...], agg_ref[...])
    pats[0] = pattern[:, :lanes]
    pats[1] = pattern[:, lanes:]
    children = []
    for side_x in range(2):
        for side_y in range(2):
            for part in range(2):
                rows = [
                    pats[part, pl.ds((2 * p + side_x) * tile_y + side_y, tile_y // 2, stride=2), :]
                    for p in range(tile_x // 2)
                ]
                children.append(jnp.concatenate(rows, axis=0).astype(BF16))
    coarse = mm(jnp.concatenate(children, axis=1), up_ref[...])
    for place in range(4):
        rows4[pl.ds(place, coarse.shape[0], stride=4), :] = coarse[:, place * 128 : (place + 1) * 128]
    coarse_ref[...] = rows4[...].astype(BF16)
    pattern = pattern.astype(BF16).astype(F32)
    values = [pattern[:, :lanes], pattern[:, lanes:], pattern[:, :lanes] + pattern[:, lanes:]]
    none = jnp.zeros((LEFT, lanes), F32)
    for i in range(tile_x):
        base = i * width
        for k in range(3):
            pats_ref[k, base : base + LEFT, :] = none
            pats_ref[k, base + LEFT : base + LEFT + tile_y, :] = values[k][i * tile_y : (i + 1) * tile_y]
            pats_ref[k, base + LEFT + tile_y : base + width, :] = none


OFFSETS = [(dx, dy) for dx in range(-2, 3) for dy in range(-2, 3) if max(abs(dx), abs(dy)) == 2]


def local_kernel(
    tile_x, tile_y, live_ref, pats, near_ref, low_ref, lower_ref, field_ref, cells, shifted, tables, sums,
):
    lanes = lower_ref.shape[2]
    width = tile_y + 2 * LEFT
    none = jnp.zeros((LEFT, lanes), F32)
    ends = jnp.zeros((tile_y, 6 * lanes), BF16)
    shifted[0:tile_y, :] = ends
    shifted[(tile_x + 1) * tile_y : (tile_x + 2) * tile_y, :] = ends
    shifted[tile_y : (tile_x + 1) * tile_y, 2 * lanes : 4 * lanes] = live_ref[...]
    for part in range(2):
        cols = slice(part * lanes, (part + 1) * lanes)
        for i in range(tile_x):
            base = i * width
            cells[part, base : base + LEFT, :] = none
            cells[part, base + LEFT : base + LEFT + tile_y, :] = live_ref[
                i * tile_y : (i + 1) * tile_y, cols
            ].astype(F32)
            cells[part, base + LEFT + tile_y : base + width, :] = none
            for shift in (-1, 1):
                place = (2 * (shift + 1) + part) * lanes
                shifted[(i + 1) * tile_y : (i + 2) * tile_y, place : place + lanes] = cells[
                    part, base + LEFT + shift : base + LEFT + shift + tile_y, :
                ].astype(BF16)
    for k in range(len(OFFSETS)):
        t_real, t_imag = low_ref[2 * k : 2 * k + 1, :], low_ref[2 * k + 1 : 2 * k + 2, :]
        for n, value in enumerate((t_imag - t_real, t_imag + t_real, t_real)):
            tables[3 * k + n] = jnp.broadcast_to(value, (8, lanes))

    passes = [
        [(dx, dy) for dx, dy in OFFSETS if dy == -2],
        [(dx, dy) for dx, dy in OFFSETS if dy == 2],
        [(dx, dy) for dx, dy in OFFSETS if abs(dy) < 2],
    ]
    blocks = tile_y // 8
    size = tile_x * tile_y // blocks

    def block(b, carry):
        total = None
        for shift in range(3):
            start = pl.multiple_of(b * size + shift * tile_y, tile_y)
            term = mm(shifted[pl.ds(start, size), :], near_ref[shift])
            total = term if total is None else total + term
        start = pl.multiple_of(b * size, size)
        field_ref[0, pl.ds(start, size), :] = total[:, :lanes]
        field_ref[1, pl.ds(start, size), :] = total[:, lanes:]
        shift_y = pl.multiple_of(b * 8, 8)
        for number, offsets in enumerate(passes):
            running = {}
            for row in range(tile_x):
                for dy in sorted({dy for _, dy in offsets}):
                    rows = pl.ds(shift_y + (row * width + LEFT + dy), 8)
                    source = [pats[k, rows, :] for k in range(3)]
                    for dx in range(-2, 3):
                        i = row - dx
                        if (dx, dy) not in offsets or not 0 <= i < tile_x:
                            continue
                        k = OFFSETS.index((dx, dy))
                        if i not in running:
                            running[i] = [None] * 3 if number == 0 else [sums[n, i] for n in range(3)]
                        running[i] = [
                            tables[3 * k + n] * source[n]
                            if running[i][n] is None
                            else running[i][n] + tables[3 * k + n] * source[n]
                            for n in range(3)
                        ]
                for i in sorted(running):
                    if i + 2 <= row or row == tile_x - 1:
                        value = running.pop(i)
                        if number < 2:
                            for n in range(3):
                                sums[n, i] = value[n]
                        else:
                            place = pl.ds(pl.multiple_of(shift_y + i * tile_y, 8), 8)
                            lower_ref[0, place, :] = value[2] - value[1]
                            lower_ref[1, place, :] = value[2] + value[0]
        return carry

    lax.fori_loop(0, blocks, block, 0)


def halos_kernel(
    tile_x, tile_y, inner_y, outer_y, inner_x, outer_x, agg_ref, near_ref, low_ref, lower_in, field_in, kept_in,
    lower_ref, field_ref, kept_ref, columns, rims, line_ref,
):
    lanes = lower_in.shape[2]
    width = tile_y + 2 * LEFT
    halo = halo_pair(inner_y, outer_y, "gy") + halo_pair(inner_x, outer_x, "gx")
    half_x, half_y = tile_x // 2, tile_y // 2
    for child in range(4):
        for p in range(half_x):
            rows = slice(p * half_y, (p + 1) * half_y)
            boxes = pl.ds((2 * p + child // 2) * tile_y + child % 2, half_y, stride=2)
            for part in range(2):
                lower_ref[part, child, rows, :] = lower_in[part, boxes, :]
                field_ref[part, child, rows, :] = field_in[part, boxes, :]
            kept_ref[child, rows, :] = kept_in[boxes, :]

    def add_column(ref, part, box, value):
        line_ref[...] = value
        for side_x in range(2):
            child, rows = 2 * side_x + box % 2, pl.ds(box // 2, half_x, stride=half_y)
            ref[part, child, rows, :] = ref[part, child, rows, :] + line_ref[pl.ds(side_x, half_x, stride=2), :]

    def add_row(ref, part, box, value):
        line_ref[...] = value
        for side_y in range(2):
            child, rows = 2 * (box % 2) + side_y, slice(box // 2 * half_y, (box // 2 + 1) * half_y)
            ref[part, child, rows, :] = ref[part, child, rows, :] + line_ref[pl.ds(side_y, half_y, stride=2), :]

    halo = jnp.concatenate(halo, axis=0)
    pattern = mm(halo.astype(BF16), agg_ref[...]).astype(BF16).astype(F32)
    values = [halo[:, :lanes], halo[:, lanes:], pattern[:, :lanes], pattern[:, lanes:]]
    two = jnp.zeros((8, lanes), F32)
    rim_size = inner_x.shape[0]
    for n, value in enumerate(values):
        for side in range(2):
            for c in range(2):
                at = (2 * side + c) * tile_x
                columns[n, 2 * side + c, 0:8, :] = two
                columns[n, 2 * side + c, 8 : 8 + tile_x, :] = value[at : at + tile_x]
                columns[n, 2 * side + c, 8 + tile_x : 16 + tile_x, :] = two
        for end in range(2):
            at = 4 * tile_x + end * rim_size
            corner = at + 2 * tile_y
            for row in range(2):
                base = (2 * end + row) * width + LEFT
                rims[n, base : base + tile_y, :] = value[at + row * tile_y : at + (row + 1) * tile_y]
                for side in range(2):
                    for c in range(2):
                        place = base + (tile_y + c if side else c - 2)
                        line = corner + 4 * side + 2 * c + row
                        rims[n, place : place + 1, :] = value[line : line + 1]

    def translate(terms):
        first = second = 0.0
        for dx, dy, real, imag in terms:
            k = OFFSETS.index((dx, dy))
            t_real, t_imag = low_ref[2 * k : 2 * k + 1, :], low_ref[2 * k + 1 : 2 * k + 2, :]
            first = first + (t_real * real - t_imag * imag)
            second = second + (t_real * imag + t_imag * real)
        return first, second

    def column(n, side, c, dx):
        return columns[n, 2 * side + c, 8 + dx : 8 + dx + tile_x, :]

    def rim(n, end, row, dy):
        base = (2 * end + row) * width + LEFT + dy
        return rims[n, base : base + tile_y, :]

    for side in range(2):
        for box in ((tile_y - 1, tile_y - 2) if side else (0, 1)):
            terms = []
            for c in range(2):
                dy = (tile_y + c if side else c - 2) - box
                for dx in range(-2, 3):
                    if (dx, dy) in OFFSETS:
                        terms.append((dx, dy, column(2, side, c, dx), column(3, side, c, dx)))
            for part, value in enumerate(translate(terms)):
                add_column(lower_ref, part, box, value)
        source = jnp.concatenate(
            [column(part, side, 1 - side, dx) for dx in range(-1, 2) for part in range(2)], axis=1
        ).astype(BF16)
        weights = [near_ref[dx, (4 * side) * lanes : (4 * side + 2) * lanes, :] for dx in range(3)]
        value = mm(source, jnp.concatenate(weights, axis=0))
        for part in range(2):
            add_column(field_ref, part, tile_y - 1 if side else 0, value[:, part * lanes : (part + 1) * lanes])
    for end in range(2):
        for box in ((tile_x - 1, tile_x - 2) if end else (0, 1)):
            terms = []
            for row in range(2):
                dx = (tile_x + row if end else row - 2) - box
                for dy in range(-2, 3):
                    if (dx, dy) in OFFSETS:
                        terms.append((dx, dy, rim(2, end, row, dy), rim(3, end, row, dy)))
            for part, value in enumerate(translate(terms)):
                add_row(lower_ref, part, box, value)
        source = jnp.concatenate(
            [rim(part, end, 1 - end, dy) for dy in range(-1, 2) for part in range(2)], axis=1
        ).astype(BF16)
        value = mm(source, near_ref[2 * end])
        for part in range(2):
            add_row(field_ref, part, tile_x - 1 if end else 0, value[:, part * lanes : (part + 1) * lanes])


GROUP = 8


def order_kernel(
    chunks, kinds, parents_x, parents_y, list_ref, kind_ref, count_ref, table_ref, at_ref, back_ref, table8
):
    width = table_ref.shape[1]
    for place, row in enumerate((0, 2, 0, 2, 1, 3, 1, 3)):
        value = table_ref[pl.ds(row, kinds, stride=4), :]
        table8[pl.ds(place, kinds, stride=8), :] = -value if place in (4, 5) else value
    table8[8 * kinds : 8 * kinds + 8, :] = jnp.zeros((8, width), F32)
    parents = parents_x * parents_y
    slots = list_ref.shape[1]
    groups = parents // GROUP
    lanes = at_ref.shape[1]
    down = lax.broadcasted_iota(jnp.int32, (parents, parents), 0)
    along = lax.broadcasted_iota(jnp.int32, (parents, parents), 1)
    column = count_rows(count_ref, parents_x, parents_y, parents)
    row = jnp.sum(jnp.where(down == along, column, 0.0), axis=0, keepdims=True)
    before = (column > row) | ((column == row) & (down < along))
    rank = jnp.sum(jnp.where(before, 1.0, 0.0), axis=0, keepdims=True)
    after = (row > column) | ((row == column) & (along < down))
    rank_down = jnp.sum(jnp.where(after, 1.0, 0.0), axis=1, keepdims=True)
    back_ref[...] = jnp.where(along.astype(F32) == rank_down, 1.0, 0.0).astype(BF16)

    across = parents_y * chunks
    entry = list_ref[...]
    line, place = entry // across, entry % across
    source = ((place // parents_y) ^ lax.axis_index("gy")) * parents + line * parents_y + place % parents_y
    used = lax.broadcasted_iota(jnp.int32, (parents, slots), 1).astype(F32) < column[:, :slots]
    kind = jnp.where(used, kind_ref[...], kinds)
    slot = lax.broadcasted_iota(jnp.int32, (slots, lanes), 0)
    lane = lax.broadcasted_iota(jnp.int32, (slots, lanes), 1)
    values = [
        mm(value.astype(F32).astype(BF16), jnp.where(lane == slot + n * slots, 1.0, 0.0).astype(BF16))
        for n, value in enumerate((source // 256, source % 256, kind))
    ]
    values = (values[0] + values[1] + values[2]).astype(BF16)
    wanted = GROUP * (down % groups) + down // groups
    moved = mm(jnp.where(wanted.astype(F32) == rank, 1.0, 0.0).astype(BF16), values).astype(BF16)
    moved = jnp.concatenate([moved[k * groups : (k + 1) * groups] for k in range(GROUP)], axis=1)
    totals = []
    from_lane = lax.broadcasted_iota(jnp.int32, (GROUP * lanes, lanes), 0)
    to_lane = lax.broadcasted_iota(jnp.int32, (GROUP * lanes, lanes), 1)
    for n in range(3):
        spread = from_lane == (to_lane // slots) * lanes + n * slots + to_lane % slots
        totals.append(mm(moved, jnp.where(spread, 1.0, 0.0).astype(BF16)).astype(jnp.int32))
    at_ref[0:groups, :] = (totals[0] * 256 + totals[1]) * 8
    at_ref[groups : 2 * groups, :] = totals[2] * 8
    least = (slots - 1 - 2 * lax.broadcasted_iota(jnp.int32, (parents, lanes), 1)).astype(F32)
    reach = jnp.sum(jnp.where(column[:, :lanes] >= least, 1.0, 0.0), axis=0, keepdims=True).astype(jnp.int32)
    at_ref[2 * groups :, :] = jnp.broadcast_to((reach + (GROUP - 1)) // GROUP, (8, lanes))


def lists_kernel(chunks, tile_x, tile_y, slots, *refs):
    sources = refs[:chunks]
    (at_any, table8, back_ref, kept_ref, lower_ref, near_ref, recv_ref, down_hbm, out_hbm,
     cells, wide, sums, at, down_ref, total_ref, out_ref, sems) = refs[chunks:]
    parents_x, parents_y = tile_x // 2, tile_y // 2
    parents = parents_x * parents_y
    lanes = table8.shape[1]
    groups = parents // GROUP
    loads = [
        pltpu.make_async_copy(at_any, at, sems.at[0]),
        pltpu.make_async_copy(down_hbm, down_ref, sems.at[1]),
    ]
    for load in loads:
        load.start()
    count = parents // 2
    pairs = cells.reshape(chunks * count, 2, 8, lanes)
    place = lax.broadcasted_iota(jnp.int32, (count, 8, lanes), 1)
    wide[0:8, :] = jnp.zeros((8, lanes), F32)
    wide[8 + 8 * count :, :] = jnp.zeros((8, lanes), F32)
    for c in range(chunks):
        wide[8 : 8 + 8 * count, :] = sources[c][...].astype(F32)

        def shifted(by):
            return wide[8 + by : 8 + by + 8 * count, :].reshape(count, 8, lanes)

        here = slice(c * count, (c + 1) * count)
        pairs[here, 0] = jnp.where(place < 4, shifted(0), jnp.where(place < 6, shifted(-2), shifted(-6)))
        pairs[here, 1] = jnp.where(place < 4, shifted(4), jnp.where(place < 6, shifted(2), shifted(-2)))
    loads[0].wait()
    upper = lax.broadcasted_iota(jnp.int32, (8, lanes), 0) < 4

    def step(length, n, carry):
        first = n * (GROUP * slots)
        second = first + groups * GROUP * slots
        before = None
        for k in range(GROUP):
            total = [None, None]
            for s in range(length):
                source = pl.multiple_of(at[first + (k * slots + s)], 8)
                kind = pl.multiple_of(at[second + (k * slots + s)], 8)
                term = cells[pl.ds(source, 8), :] * table8[pl.ds(kind, 8), :]
                total[s % 2] = term if total[s % 2] is None else total[s % 2] + term
            total = total[0] + total[1] if length else jnp.zeros((8, lanes), F32)
            total = total + pltpu.roll(total, 4, axis=0)
            if k % 2:
                tile = pl.multiple_of(n * (GROUP * 4) + (k // 2) * 8, 8)
                sums[pl.ds(tile, 8), :] = jnp.where(upper, before, total)
            before = total
        return carry

    start = 0
    for j, length in enumerate(range(slots, 0, -2)):
        end = at[2 * groups * GROUP * slots + j]
        lax.fori_loop(start, end, functools.partial(step, length), 0)
        start = end
    lax.fori_loop(start, groups, functools.partial(step, 0), 0)

    ordered = [sums[pl.ds(place, parents, stride=4), :].astype(BF16) for place in range(4)]
    incoming = mm(back_ref[...], jnp.concatenate(ordered, axis=1)).astype(BF16)
    loads[1].wait()
    for child in range(4):
        down = mm(incoming, down_ref[child])
        for part in range(2):
            value = down[:, part * lanes : (part + 1) * lanes] + lower_ref[part, child]
            total_ref[child, :, part * lanes : (part + 1) * lanes] = value.astype(BF16)
    stores = []
    for half in range(2):
        first, size = half * parents // 2, parents // 2
        rows = slice(first, first + size)
        for child in range(4):
            field = mm(total_ref[child, rows, :], recv_ref[...])
            mask = kept_ref[child, rows, :]
            for part in range(2):
                value = (field[:, part * lanes : (part + 1) * lanes] + near_ref[part, child, rows, :]) * mask
                for p in range(parents_x // 2):
                    line = (2 * (half * parents_x // 2 + p) + child // 2) * tile_y + child % 2
                    out_ref[pl.ds(2 * line + part, parents_y, stride=4), :] = value[
                        p * parents_y : (p + 1) * parents_y
                    ]
        size = out_ref.shape[0] // 2
        rows = pl.ds(half * size, size)
        stores.append(pltpu.make_async_copy(out_ref.at[rows], out_hbm.at[rows], sems.at[2 + half]))
        stores[-1].start()
    for store in stores:
        store.wait()


def swap(low, high, axis):
    count = lax.axis_size(axis)
    lows = [(i, i ^ 1) for i in range(count)]
    highs = [(i, (((i + 1) % count ^ 1) - 1) % count) for i in range(count)]
    return lax.ppermute(low, axis, lows), lax.ppermute(high, axis, highs)


def body(
    currents, box_count, aggregate, near_blocks, low_translator, child_to_parent, coarse_list,
    coarse_kind, coarse_count, up_translator, parent_to_child, receive_map,
):
    tile_x, tile_y = box_count.shape
    boxes = tile_x * tile_y
    lanes = currents.shape[-1]
    parents_x, parents_y, slots = coarse_list.shape
    parents = parents_x * parents_y
    kinds, _, half = up_translator.shape
    wide = 2 * half
    chunks = lax.axis_size("gy")
    in_hbm = pl.BlockSpec(memory_space=pltpu.HBM)

    edge = jax.ShapeDtypeStruct((2 * tile_x, 2 * lanes), BF16)
    edge = jax.ShapeDtypeStruct((2 * tile_x, 2 * lanes), BF16)
    width = tile_y + 2 * LEFT
    live, kept, low, high, agg_near, up_near = pl.pallas_call(
        functools.partial(live_kernel, tile_x, tile_y),
        name="live",
        out_shape=[
            jax.ShapeDtypeStruct((boxes, 2 * lanes), BF16),
            jax.ShapeDtypeStruct((boxes, lanes), F32),
            edge,
            edge,
            jax.ShapeDtypeStruct((2 * lanes, 2 * lanes), BF16),
            jax.ShapeDtypeStruct((8 * lanes, wide), BF16),
        ],
        in_specs=[in_hbm] * 4,
        out_specs=vmem(6),
        scratch_shapes=[
            pltpu.VMEM((2 * boxes, lanes), BF16),
            pltpu.VMEM((tile_x, tile_y), jnp.int32),
            pltpu.VMEM((2 * boxes, lanes), F32),
            pltpu.SemaphoreType.DMA((4,)),
        ],
        compiler_params=params(10),
        cost_estimate=cost(100 * MIB, 3 * MIB),
    )(
        hbm(currents.reshape(2 * boxes, lanes)), hbm(box_count), hbm(aggregate),
        hbm(child_to_parent.reshape(8 * lanes, wide)),
    )
    coarse, pats = pl.pallas_call(
        functools.partial(parents_kernel, tile_x, tile_y),
        name="parents",
        out_shape=[
            jax.ShapeDtypeStruct((4 * parents, wide // 4), BF16),
            jax.ShapeDtypeStruct((3, tile_x * width, lanes), F32),
        ],
        in_specs=vmem(3),
        out_specs=vmem(2),
        scratch_shapes=[
            pltpu.VMEM((2, boxes, lanes), F32),
            pltpu.VMEM((4 * parents, wide // 4), F32),
        ],
        compiler_params=params(10),
        cost_estimate=cost(200 * MIB, 3 * MIB),
    )(live, agg_near, up_near)
    inner_y, outer_y = swap(low, high, "gy")
    arrived = {
        d: lax.ppermute(coarse, "gy", [(i, i ^ d) for i in range(chunks)])
        for d in [chunks - 1] + list(range(1, chunks - 1))
    }
    sources = [coarse] + [arrived[d] for d in range(1, chunks)]

    rim = 2 * tile_y + 8
    rim += -rim % 16
    low, high = pl.pallas_call(
        functools.partial(rims_kernel, tile_x, tile_y),
        name="rims",
        out_shape=[jax.ShapeDtypeStruct((rim, 2 * lanes), BF16)] * 2,
        in_specs=vmem(3),
        out_specs=vmem(2),
        scratch_shapes=[pltpu.VMEM((rim, 2 * lanes), F32)] * 2,
        compiler_params=params(10),
        cost_estimate=cost(1 * MIB, MIB),
    )(live, inner_y, outer_y)
    inner_x, outer_x = swap(low, high, "gx")
    live, coarse_count, _ = lax.optimization_barrier((live, coarse_count, low))

    near_rows = near_blocks.reshape(3, 6 * lanes, 2 * lanes)
    low_rows = low_translator.reshape(-1, lanes)
    pair = [jax.ShapeDtypeStruct((2, boxes, lanes), F32)] * 2
    lower, near = pl.pallas_call(
        functools.partial(local_kernel, tile_x, tile_y),
        name="local",
        out_shape=pair,
        in_specs=vmem(4),
        out_specs=vmem(2),
        scratch_shapes=[
            pltpu.VMEM((2, tile_x * width, lanes), F32),
            pltpu.VMEM(((tile_x + 2) * tile_y, 6 * lanes), BF16),
            pltpu.VMEM((3 * len(OFFSETS), 8, lanes), F32),
            pltpu.VMEM((3, tile_x, 8, lanes), F32),
        ],
        compiler_params=params(10),
        cost_estimate=cost(2000 * MIB, 5 * MIB),
    )(live, pats, near_rows, low_rows)

    pair = [jax.ShapeDtypeStruct((2, 4, parents, lanes), F32)] * 2
    lower, near, kept = pl.pallas_call(
        functools.partial(halos_kernel, tile_x, tile_y),
        name="halos",
        out_shape=pair + [jax.ShapeDtypeStruct((4, parents, lanes), F32)],
        in_specs=vmem(10),
        out_specs=vmem(3),
        scratch_shapes=[
            pltpu.VMEM((4, 4, tile_x + 16, lanes), F32),
            pltpu.VMEM((4, 4 * width, lanes), F32),
            pltpu.VMEM((tile_x, lanes), F32),
        ],
        compiler_params=params(10),
        cost_estimate=cost(100 * MIB, 5 * MIB),
    )(inner_y, outer_y, inner_x, outer_x, agg_near, near_rows, low_rows, lower, near, kept)

    table = up_translator.reshape(kinds, 2, 2, half // 2).transpose(0, 2, 1, 3).reshape(4 * kinds, half // 2)
    groups = parents // GROUP
    at, back, table8 = pl.pallas_call(
        functools.partial(order_kernel, chunks, kinds, parents_x, parents_y),
        name="order",
        out_shape=[
            jax.ShapeDtypeStruct((2 * groups + 8, GROUP * slots), jnp.int32),
            jax.ShapeDtypeStruct((parents, parents), BF16),
            jax.ShapeDtypeStruct((8 * kinds + 8, half // 2), F32),
        ],
        in_specs=vmem(4),
        out_specs=vmem(3),
        compiler_params=params(8),
        cost_estimate=cost(300 * MIB, MIB),
    )(coarse_list.reshape(parents, slots), coarse_kind.reshape(parents, slots), coarse_count, table)
    at = at.reshape(-1)
    out = pl.pallas_call(
        functools.partial(lists_kernel, chunks, tile_x, tile_y, slots),
        name="lists",
        out_shape=jax.ShapeDtypeStruct((2 * boxes, lanes), F32),
        in_specs=vmem(chunks) + [pl.BlockSpec(memory_space=pl.ANY)] + vmem(6) + [in_hbm],
        out_specs=in_hbm,
        scratch_shapes=[
            pltpu.VMEM((chunks * parents * 8, wide // 4), F32),
            pltpu.VMEM((4 * parents + 16, wide // 4), F32),
            pltpu.VMEM((4 * parents, wide // 4), F32),
            pltpu.SMEM(at.shape, jnp.int32),
            pltpu.VMEM((4, wide, 2 * lanes), BF16),
            pltpu.VMEM((4, parents, 2 * lanes), BF16),
            pltpu.VMEM((2 * boxes, lanes), F32),
            pltpu.SemaphoreType.DMA((4,)),
        ],
        compiler_params=params(16 if chunks <= 4 else 40),
        cost_estimate=cost(2000 * MIB, 8 * MIB),
    )(*sources, at, table8, back, kept, lower, near, receive_map, hbm(parent_to_child))
    return out.reshape(tile_x, tile_y, 2, lanes)


def solution(mesh):
    tiles = P("gx", "gy")
    in_specs = (tiles, tiles, P(), P(), P(), P(), tiles, tiles, tiles, P(), P(), P())
    return jax.shard_map(body, mesh=mesh, in_specs=in_specs, out_specs=tiles, check_vma=False)
```

```python
import functools

import jax
import jax.numpy as jnp
from jax import lax
from jax.experimental import pallas as pl
from jax.experimental.pallas import tpu as pltpu
from jax.sharding import PartitionSpec as P

F32 = jnp.float32
BF16 = jnp.bfloat16
MIB = 1 << 20


def vmem(count):
    return [pl.BlockSpec(memory_space=pltpu.VMEM)] * count


def hbm(array):
    return pltpu.with_memory_space_constraint(array, pltpu.HBM)


def params(mib):
    return pltpu.CompilerParams(vmem_limit_bytes=mib * MIB)


def cost(macs, moved):
    return pl.CostEstimate(flops=2 * macs, bytes_accessed=moved, transcendentals=0)


def mm(left, right):
    return jnp.dot(left, right, preferred_element_type=F32)


def count_rows(counts_ref, tile_x, tile_y, lanes):
    eye = lax.broadcasted_iota(jnp.int32, (tile_y, tile_y), 0) == lax.broadcasted_iota(
        jnp.int32, (tile_y, tile_y), 1
    )
    counts = counts_ref[...].astype(F32)
    diag = [
        jnp.where(eye, jnp.broadcast_to(counts[i : i + 1], (tile_y, tile_y)), 0.0) for i in range(tile_x)
    ]
    return mm(jnp.concatenate(diag, axis=0).astype(BF16), jnp.ones((tile_y, lanes), BF16))


def halo_pair(inner_ref, outer_ref, axis):
    at = lax.axis_index(axis)
    odd = at % 2 == 1
    inner, outer = inner_ref[...].astype(F32), outer_ref[...].astype(F32)
    before, after = jnp.where(odd, inner, outer), jnp.where(odd, outer, inner)
    return jnp.where(at > 0, before, 0.0), jnp.where(at < lax.axis_size(axis) - 1, after, 0.0)


LEFT = 8


def live_kernel(tile_x, tile_y, cur_hbm, counts_hbm, agg_hbm, up_hbm,
                live_ref, kept_ref, low_ref, high_ref, agg_ref, up_ref, cur_ref, counts_ref, wide, sems):
    pairs = [(counts_hbm, counts_ref), (cur_hbm, cur_ref), (agg_hbm, agg_ref), (up_hbm, up_ref)]
    loads = [
        pltpu.make_async_copy(source, target, sems.at[k]) for k, (source, target) in enumerate(pairs)
    ]
    for load in loads:
        load.start()
    lanes = cur_ref.shape[1]
    boxes = tile_x * tile_y
    loads[0].wait()
    limits = count_rows(counts_ref, tile_x, tile_y, lanes)
    keep = lax.broadcasted_iota(jnp.int32, (boxes, lanes), 1).astype(F32) < limits
    kept_ref[...] = jnp.where(keep, 1.0, 0.0)
    odd = lax.axis_index("gy") % 2 == 1
    loads[1].wait()
    wide[...] = cur_ref[...].astype(F32)
    for part in range(2):
        cols = slice(part * lanes, (part + 1) * lanes)
        live_ref[:, cols] = jnp.where(keep, wide[pl.ds(part, boxes, stride=2), :], 0.0).astype(BF16)

        def edge(column):
            rows = wide[pl.ds(2 * column + part, tile_x, stride=2 * tile_y), :]
            return rows * kept_ref[pl.ds(column, tile_x, stride=tile_y), :]

        first = jnp.concatenate([edge(0), edge(1)], axis=0).astype(BF16)
        last = jnp.concatenate([edge(tile_y - 2), edge(tile_y - 1)], axis=0).astype(BF16)
        low_ref[:, cols] = jnp.where(odd, first, last)
        high_ref[:, cols] = jnp.where(odd, last, first)
    for load in loads[2:]:
        load.wait()


def rims_kernel(tile_x, tile_y, live_ref, inner_ref, outer_ref, low_ref, high_ref, first, last):
    odd = lax.axis_index("gx") % 2 == 1
    sides = halo_pair(inner_ref, outer_ref, "gy")
    for rim, start in ((first, 0), (last, tile_x - 2)):
        rim[0 : 2 * tile_y, :] = live_ref[start * tile_y : (start + 2) * tile_y, :].astype(F32)
        place = 2 * tile_y
        for side in sides:
            for column in range(2):
                at = column * tile_x + start
                rim[place : place + 2, :] = side[at : at + 2]
                place += 2
        rim[place:, :] = jnp.zeros((rim.shape[0] - place, rim.shape[1]), F32)
    low_ref[...] = jnp.where(odd, first[...], last[...]).astype(BF16)
    high_ref[...] = jnp.where(odd, last[...], first[...]).astype(BF16)


def parents_kernel(tile_x, tile_y, live_ref, agg_ref, up_ref, coarse_ref, pats_ref, pats, rows4):
    lanes = pats.shape[2]
    width = tile_y + 2 * LEFT
    pattern = mm(live_ref[...], agg_ref[...])
    pats[0] = pattern[:, :lanes]
    pats[1] = pattern[:, lanes:]
    children = []
    for side_x in range(2):
        for side_y in range(2):
            for part in range(2):
                rows = [
                    pats[part, pl.ds((2 * p + side_x) * tile_y + side_y, tile_y // 2, stride=2), :]
                    for p in range(tile_x // 2)
                ]
                children.append(jnp.concatenate(rows, axis=0).astype(BF16))
    coarse = mm(jnp.concatenate(children, axis=1), up_ref[...])
    for place in range(4):
        rows4[pl.ds(place, coarse.shape[0], stride=4), :] = coarse[:, place * 128 : (place + 1) * 128]
    coarse_ref[...] = rows4[...].astype(BF16)
    pattern = pattern.astype(BF16).astype(F32)
    values = [pattern[:, :lanes], pattern[:, lanes:], pattern[:, :lanes] + pattern[:, lanes:]]
    none = jnp.zeros((LEFT, lanes), F32)
    for i in range(tile_x):
        base = i * width
        for k in range(3):
            pats_ref[k, base : base + LEFT, :] = none
            pats_ref[k, base + LEFT : base + LEFT + tile_y, :] = values[k][i * tile_y : (i + 1) * tile_y]
            pats_ref[k, base + LEFT + tile_y : base + width, :] = none


OFFSETS = [(dx, dy) for dx in range(-2, 3) for dy in range(-2, 3) if max(abs(dx), abs(dy)) == 2]


def local_kernel(
    tile_x, tile_y, live_ref, pats, near_ref, low_ref, lower_ref, field_ref, cells, shifted, tables, sums,
):
    lanes = lower_ref.shape[2]
    width = tile_y + 2 * LEFT
    none = jnp.zeros((LEFT, lanes), F32)
    ends = jnp.zeros((tile_y, 6 * lanes), BF16)
    shifted[0:tile_y, :] = ends
    shifted[(tile_x + 1) * tile_y : (tile_x + 2) * tile_y, :] = ends
    shifted[tile_y : (tile_x + 1) * tile_y, 2 * lanes : 4 * lanes] = live_ref[...]
    for part in range(2):
        cols = slice(part * lanes, (part + 1) * lanes)
        for i in range(tile_x):
            base = i * width
            cells[part, base : base + LEFT, :] = none
            cells[part, base + LEFT : base + LEFT + tile_y, :] = live_ref[
                i * tile_y : (i + 1) * tile_y, cols
            ].astype(F32)
            cells[part, base + LEFT + tile_y : base + width, :] = none
            for shift in (-1, 1):
                place = (2 * (shift + 1) + part) * lanes
                shifted[(i + 1) * tile_y : (i + 2) * tile_y, place : place + lanes] = cells[
                    part, base + LEFT + shift : base + LEFT + shift + tile_y, :
                ].astype(BF16)
    for k in range(len(OFFSETS)):
        t_real, t_imag = low_ref[2 * k : 2 * k + 1, :], low_ref[2 * k + 1 : 2 * k + 2, :]
        for n, value in enumerate((t_imag - t_real, t_imag + t_real, t_real)):
            tables[3 * k + n] = jnp.broadcast_to(value, (8, lanes))

    passes = [
        [(dx, dy) for dx, dy in OFFSETS if dy == -2],
        [(dx, dy) for dx, dy in OFFSETS if dy == 2],
        [(dx, dy) for dx, dy in OFFSETS if abs(dy) < 2],
    ]
    blocks = tile_y // 8
    size = tile_x * tile_y // blocks

    def block(b, carry):
        total = None
        for shift in range(3):
            start = pl.multiple_of(b * size + shift * tile_y, tile_y)
            term = mm(shifted[pl.ds(start, size), :], near_ref[shift])
            total = term if total is None else total + term
        start = pl.multiple_of(b * size, size)
        field_ref[0, pl.ds(start, size), :] = total[:, :lanes]
        field_ref[1, pl.ds(start, size), :] = total[:, lanes:]
        shift_y = pl.multiple_of(b * 8, 8)
        for number, offsets in enumerate(passes):
            running = {}
            for row in range(tile_x):
                for dy in sorted({dy for _, dy in offsets}):
                    rows = pl.ds(shift_y + (row * width + LEFT + dy), 8)
                    source = [pats[k, rows, :] for k in range(3)]
                    for dx in range(-2, 3):
                        i = row - dx
                        if (dx, dy) not in offsets or not 0 <= i < tile_x:
                            continue
                        k = OFFSETS.index((dx, dy))
                        if i not in running:
                            running[i] = [None] * 3 if number == 0 else [sums[n, i] for n in range(3)]
                        running[i] = [
                            tables[3 * k + n] * source[n]
                            if running[i][n] is None
                            else running[i][n] + tables[3 * k + n] * source[n]
                            for n in range(3)
                        ]
                for i in sorted(running):
                    if i + 2 <= row or row == tile_x - 1:
                        value = running.pop(i)
                        if number < 2:
                            for n in range(3):
                                sums[n, i] = value[n]
                        else:
                            place = pl.ds(pl.multiple_of(shift_y + i * tile_y, 8), 8)
                            lower_ref[0, place, :] = value[2] - value[1]
                            lower_ref[1, place, :] = value[2] + value[0]
        return carry

    lax.fori_loop(0, blocks, block, 0)


def halos_kernel(
    tile_x, tile_y, inner_y, outer_y, inner_x, outer_x, agg_ref, near_ref, low_ref, lower_in, field_in, kept_in,
    lower_ref, field_ref, kept_ref, columns, rims, line_ref,
):
    lanes = lower_in.shape[2]
    width = tile_y + 2 * LEFT
    halo = halo_pair(inner_y, outer_y, "gy") + halo_pair(inner_x, outer_x, "gx")
    half_x, half_y = tile_x // 2, tile_y // 2
    for child in range(4):
        for p in range(half_x):
            rows = slice(p * half_y, (p + 1) * half_y)
            boxes = pl.ds((2 * p + child // 2) * tile_y + child % 2, half_y, stride=2)
            for part in range(2):
                lower_ref[part, child, rows, :] = lower_in[part, boxes, :]
                field_ref[part, child, rows, :] = field_in[part, boxes, :]
            kept_ref[child, rows, :] = kept_in[boxes, :]

    def add_column(ref, part, box, value):
        line_ref[...] = value
        for side_x in range(2):
            child, rows = 2 * side_x + box % 2, pl.ds(box // 2, half_x, stride=half_y)
            ref[part, child, rows, :] = ref[part, child, rows, :] + line_ref[pl.ds(side_x, half_x, stride=2), :]

    def add_row(ref, part, box, value):
        line_ref[...] = value
        for side_y in range(2):
            child, rows = 2 * (box % 2) + side_y, slice(box // 2 * half_y, (box // 2 + 1) * half_y)
            ref[part, child, rows, :] = ref[part, child, rows, :] + line_ref[pl.ds(side_y, half_y, stride=2), :]

    halo = jnp.concatenate(halo, axis=0)
    pattern = mm(halo.astype(BF16), agg_ref[...]).astype(BF16).astype(F32)
    values = [halo[:, :lanes], halo[:, lanes:], pattern[:, :lanes], pattern[:, lanes:]]
    two = jnp.zeros((8, lanes), F32)
    rim_size = inner_x.shape[0]
    for n, value in enumerate(values):
        for side in range(2):
            for c in range(2):
                at = (2 * side + c) * tile_x
                columns[n, 2 * side + c, 0:8, :] = two
                columns[n, 2 * side + c, 8 : 8 + tile_x, :] = value[at : at + tile_x]
                columns[n, 2 * side + c, 8 + tile_x : 16 + tile_x, :] = two
        for end in range(2):
            at = 4 * tile_x + end * rim_size
            corner = at + 2 * tile_y
            for row in range(2):
                base = (2 * end + row) * width + LEFT
                rims[n, base : base + tile_y, :] = value[at + row * tile_y : at + (row + 1) * tile_y]
                for side in range(2):
                    for c in range(2):
                        place = base + (tile_y + c if side else c - 2)
                        line = corner + 4 * side + 2 * c + row
                        rims[n, place : place + 1, :] = value[line : line + 1]

    def translate(terms):
        first = second = 0.0
        for dx, dy, real, imag in terms:
            k = OFFSETS.index((dx, dy))
            t_real, t_imag = low_ref[2 * k : 2 * k + 1, :], low_ref[2 * k + 1 : 2 * k + 2, :]
            first = first + (t_real * real - t_imag * imag)
            second = second + (t_real * imag + t_imag * real)
        return first, second

    def column(n, side, c, dx):
        return columns[n, 2 * side + c, 8 + dx : 8 + dx + tile_x, :]

    def rim(n, end, row, dy):
        base = (2 * end + row) * width + LEFT + dy
        return rims[n, base : base + tile_y, :]

    for side in range(2):
        for box in ((tile_y - 1, tile_y - 2) if side else (0, 1)):
            terms = []
            for c in range(2):
                dy = (tile_y + c if side else c - 2) - box
                for dx in range(-2, 3):
                    if (dx, dy) in OFFSETS:
                        terms.append((dx, dy, column(2, side, c, dx), column(3, side, c, dx)))
            for part, value in enumerate(translate(terms)):
                add_column(lower_ref, part, box, value)
        source = jnp.concatenate(
            [column(part, side, 1 - side, dx) for dx in range(-1, 2) for part in range(2)], axis=1
        ).astype(BF16)
        weights = [near_ref[dx, (4 * side) * lanes : (4 * side + 2) * lanes, :] for dx in range(3)]
        value = mm(source, jnp.concatenate(weights, axis=0))
        for part in range(2):
            add_column(field_ref, part, tile_y - 1 if side else 0, value[:, part * lanes : (part + 1) * lanes])
    for end in range(2):
        for box in ((tile_x - 1, tile_x - 2) if end else (0, 1)):
            terms = []
            for row in range(2):
                dx = (tile_x + row if end else row - 2) - box
                for dy in range(-2, 3):
                    if (dx, dy) in OFFSETS:
                        terms.append((dx, dy, rim(2, end, row, dy), rim(3, end, row, dy)))
            for part, value in enumerate(translate(terms)):
                add_row(lower_ref, part, box, value)
        source = jnp.concatenate(
            [rim(part, end, 1 - end, dy) for dy in range(-1, 2) for part in range(2)], axis=1
        ).astype(BF16)
        value = mm(source, near_ref[2 * end])
        for part in range(2):
            add_row(field_ref, part, tile_x - 1 if end else 0, value[:, part * lanes : (part + 1) * lanes])


GROUP = 8


def order_kernel(
    chunks, kinds, parents_x, parents_y, list_ref, kind_ref, count_ref, table_ref, at_ref, back_ref, table8
):
    width = table_ref.shape[1]
    for place, row in enumerate((0, 2, 0, 2, 1, 3, 1, 3)):
        table8[pl.ds(place, kinds, stride=8), :] = table_ref[pl.ds(row, kinds, stride=4), :]
    table8[8 * kinds : 8 * kinds + 8, :] = jnp.zeros((8, width), F32)
    parents = parents_x * parents_y
    slots = list_ref.shape[1]
    groups = parents // GROUP
    lanes = at_ref.shape[1]
    down = lax.broadcasted_iota(jnp.int32, (parents, parents), 0)
    along = lax.broadcasted_iota(jnp.int32, (parents, parents), 1)
    column = count_rows(count_ref, parents_x, parents_y, parents)
    row = jnp.sum(jnp.where(down == along, column, 0.0), axis=0, keepdims=True)
    before = (column > row) | ((column == row) & (down < along))
    rank = jnp.sum(jnp.where(before, 1.0, 0.0), axis=0, keepdims=True)
    after = (row > column) | ((row == column) & (along < down))
    rank_down = jnp.sum(jnp.where(after, 1.0, 0.0), axis=1, keepdims=True)
    back_ref[...] = jnp.where(along.astype(F32) == rank_down, 1.0, 0.0).astype(BF16)

    across = parents_y * chunks
    entry = list_ref[...]
    line, place = entry // across, entry % across
    source = ((place // parents_y) ^ lax.axis_index("gy")) * parents + line * parents_y + place % parents_y
    used = lax.broadcasted_iota(jnp.int32, (parents, slots), 1).astype(F32) < column[:, :slots]
    kind = jnp.where(used, kind_ref[...], kinds)
    slot = lax.broadcasted_iota(jnp.int32, (slots, lanes), 0)
    lane = lax.broadcasted_iota(jnp.int32, (slots, lanes), 1)
    values = [
        mm(value.astype(F32).astype(BF16), jnp.where(lane == slot + n * slots, 1.0, 0.0).astype(BF16))
        for n, value in enumerate((source // 256, source % 256, kind))
    ]
    values = (values[0] + values[1] + values[2]).astype(BF16)
    wanted = GROUP * (down % groups) + down // groups
    moved = mm(jnp.where(wanted.astype(F32) == rank, 1.0, 0.0).astype(BF16), values).astype(BF16)
    moved = jnp.concatenate([moved[k * groups : (k + 1) * groups] for k in range(GROUP)], axis=1)
    totals = []
    from_lane = lax.broadcasted_iota(jnp.int32, (GROUP * lanes, lanes), 0)
    to_lane = lax.broadcasted_iota(jnp.int32, (GROUP * lanes, lanes), 1)
    for n in range(3):
        spread = from_lane == (to_lane // slots) * lanes + n * slots + to_lane % slots
        totals.append(mm(moved, jnp.where(spread, 1.0, 0.0).astype(BF16)).astype(jnp.int32))
    at_ref[0:groups, :] = (totals[0] * 256 + totals[1]) * 8
    at_ref[groups : 2 * groups, :] = totals[2] * 8
    least = (slots - 1 - 2 * lax.broadcasted_iota(jnp.int32, (parents, lanes), 1)).astype(F32)
    reach = jnp.sum(jnp.where(column[:, :lanes] >= least, 1.0, 0.0), axis=0, keepdims=True).astype(jnp.int32)
    at_ref[2 * groups :, :] = jnp.broadcast_to((reach + (GROUP - 1)) // GROUP, (8, lanes))


def lists_kernel(chunks, tile_x, tile_y, slots, *refs):
    sources = refs[:chunks]
    (at_any, table8, back_ref, kept_ref, lower_ref, near_ref, recv_ref, down_hbm, out_hbm,
     cells, sums, at, down_ref, total_ref, out_ref, sems) = refs[chunks:]
    parents_x, parents_y = tile_x // 2, tile_y // 2
    parents = parents_x * parents_y
    lanes = table8.shape[1]
    groups = parents // GROUP
    loads = [
        pltpu.make_async_copy(at_any, at, sems.at[0]),
        pltpu.make_async_copy(down_hbm, down_ref, sems.at[1]),
    ]
    for load in loads:
        load.start()
    count = parents // 2
    pairs = cells.reshape(chunks * count, 2, 8, lanes)
    first_half = lax.broadcasted_iota(jnp.int32, (count, 8, lanes), 1) < 4
    for c, source in zip([0, chunks - 1] + list(range(1, chunks - 1)), sources):
        rows = source[...].astype(F32).reshape(count, 8, lanes)
        turned = pltpu.roll(rows, 4, axis=1)
        pairs[c * count : (c + 1) * count, 0] = jnp.where(first_half, rows, turned)
        pairs[c * count : (c + 1) * count, 1] = jnp.where(first_half, turned, rows)
    loads[0].wait()
    line = lax.broadcasted_iota(jnp.int32, (8, lanes), 0)
    upper, real = line < 4, line % 4 < 2

    def step(length, n, carry):
        first = n * (GROUP * slots)
        second = first + groups * GROUP * slots
        before = None
        for k in range(GROUP):
            total = [None, None]
            for s in range(length):
                source = pl.multiple_of(at[first + (k * slots + s)], 8)
                kind = pl.multiple_of(at[second + (k * slots + s)], 8)
                term = cells[pl.ds(source, 8), :] * table8[pl.ds(kind, 8), :]
                total[s % 2] = term if total[s % 2] is None else total[s % 2] + term
            total = total[0] + total[1] if length else jnp.zeros((8, lanes), F32)
            if k % 2:
                with_real = jnp.where(upper, before, pltpu.roll(total, 4, axis=0))
                with_imag = jnp.where(upper, pltpu.roll(before, 4, axis=0), total)
                turned = jnp.where(real, -pltpu.roll(with_imag, 6, axis=0), pltpu.roll(with_imag, 2, axis=0))
                tile = pl.multiple_of(n * (GROUP * 4) + (k // 2) * 8, 8)
                sums[pl.ds(tile, 8), :] = with_real + turned
            before = total
        return carry

    start = 0
    for j, length in enumerate(range(slots, 0, -2)):
        end = at[2 * groups * GROUP * slots + j]
        lax.fori_loop(start, end, functools.partial(step, length), 0)
        start = end
    lax.fori_loop(start, groups, functools.partial(step, 0), 0)

    ordered = [sums[pl.ds(place, parents, stride=4), :].astype(BF16) for place in range(4)]
    incoming = mm(back_ref[...], jnp.concatenate(ordered, axis=1)).astype(BF16)
    loads[1].wait()
    for child in range(4):
        down = mm(incoming, down_ref[child])
        for part in range(2):
            value = down[:, part * lanes : (part + 1) * lanes] + lower_ref[part, child]
            total_ref[child, :, part * lanes : (part + 1) * lanes] = value.astype(BF16)
    stores = []
    for half in range(2):
        first, size = half * parents // 2, parents // 2
        rows = slice(first, first + size)
        for child in range(4):
            field = mm(total_ref[child, rows, :], recv_ref[...])
            mask = kept_ref[child, rows, :]
            for part in range(2):
                value = (field[:, part * lanes : (part + 1) * lanes] + near_ref[part, child, rows, :]) * mask
                for p in range(parents_x // 2):
                    line = (2 * (half * parents_x // 2 + p) + child // 2) * tile_y + child % 2
                    out_ref[pl.ds(2 * line + part, parents_y, stride=4), :] = value[
                        p * parents_y : (p + 1) * parents_y
                    ]
        size = out_ref.shape[0] // 2
        rows = pl.ds(half * size, size)
        stores.append(pltpu.make_async_copy(out_ref.at[rows], out_hbm.at[rows], sems.at[2 + half]))
        stores[-1].start()
    for store in stores:
        store.wait()


def swap(low, high, axis):
    count = lax.axis_size(axis)
    lows = [(i, i ^ 1) for i in range(count)]
    highs = [(i, (((i + 1) % count ^ 1) - 1) % count) for i in range(count)]
    return lax.ppermute(low, axis, lows), lax.ppermute(high, axis, highs)


def body(
    currents, box_count, aggregate, near_blocks, low_translator, child_to_parent, coarse_list,
    coarse_kind, coarse_count, up_translator, parent_to_child, receive_map,
):
    tile_x, tile_y = box_count.shape
    boxes = tile_x * tile_y
    lanes = currents.shape[-1]
    parents_x, parents_y, slots = coarse_list.shape
    parents = parents_x * parents_y
    kinds, _, half = up_translator.shape
    wide = 2 * half
    chunks = lax.axis_size("gy")
    in_hbm = pl.BlockSpec(memory_space=pltpu.HBM)

    edge = jax.ShapeDtypeStruct((2 * tile_x, 2 * lanes), BF16)
    edge = jax.ShapeDtypeStruct((2 * tile_x, 2 * lanes), BF16)
    width = tile_y + 2 * LEFT
    live, kept, low, high, agg_near, up_near = pl.pallas_call(
        functools.partial(live_kernel, tile_x, tile_y),
        name="live",
        out_shape=[
            jax.ShapeDtypeStruct((boxes, 2 * lanes), BF16),
            jax.ShapeDtypeStruct((boxes, lanes), F32),
            edge,
            edge,
            jax.ShapeDtypeStruct((2 * lanes, 2 * lanes), BF16),
            jax.ShapeDtypeStruct((8 * lanes, wide), BF16),
        ],
        in_specs=[in_hbm] * 4,
        out_specs=vmem(6),
        scratch_shapes=[
            pltpu.VMEM((2 * boxes, lanes), BF16),
            pltpu.VMEM((tile_x, tile_y), jnp.int32),
            pltpu.VMEM((2 * boxes, lanes), F32),
            pltpu.SemaphoreType.DMA((4,)),
        ],
        compiler_params=params(10),
        cost_estimate=cost(100 * MIB, 3 * MIB),
    )(
        hbm(currents.reshape(2 * boxes, lanes)), hbm(box_count), hbm(aggregate),
        hbm(child_to_parent.reshape(8 * lanes, wide)),
    )
    coarse, pats = pl.pallas_call(
        functools.partial(parents_kernel, tile_x, tile_y),
        name="parents",
        out_shape=[
            jax.ShapeDtypeStruct((4 * parents, wide // 4), BF16),
            jax.ShapeDtypeStruct((3, tile_x * width, lanes), F32),
        ],
        in_specs=vmem(3),
        out_specs=vmem(2),
        scratch_shapes=[
            pltpu.VMEM((2, boxes, lanes), F32),
            pltpu.VMEM((4 * parents, wide // 4), F32),
        ],
        compiler_params=params(10),
        cost_estimate=cost(200 * MIB, 3 * MIB),
    )(live, agg_near, up_near)
    inner_y, outer_y = swap(low, high, "gy")
    sources = [coarse] + [
        lax.ppermute(coarse, "gy", [(i, i ^ d) for i in range(chunks)])
        for d in [chunks - 1] + list(range(1, chunks - 1))
    ]

    rim = 2 * tile_y + 8
    rim += -rim % 16
    low, high = pl.pallas_call(
        functools.partial(rims_kernel, tile_x, tile_y),
        name="rims",
        out_shape=[jax.ShapeDtypeStruct((rim, 2 * lanes), BF16)] * 2,
        in_specs=vmem(3),
        out_specs=vmem(2),
        scratch_shapes=[pltpu.VMEM((rim, 2 * lanes), F32)] * 2,
        compiler_params=params(10),
        cost_estimate=cost(1 * MIB, MIB),
    )(live, inner_y, outer_y)
    inner_x, outer_x = swap(low, high, "gx")
    live, coarse_count, _ = lax.optimization_barrier((live, coarse_count, low))

    near_rows = near_blocks.reshape(3, 6 * lanes, 2 * lanes)
    low_rows = low_translator.reshape(-1, lanes)
    pair = [jax.ShapeDtypeStruct((2, boxes, lanes), F32)] * 2
    lower, near = pl.pallas_call(
        functools.partial(local_kernel, tile_x, tile_y),
        name="local",
        out_shape=pair,
        in_specs=vmem(4),
        out_specs=vmem(2),
        scratch_shapes=[
            pltpu.VMEM((2, tile_x * width, lanes), F32),
            pltpu.VMEM(((tile_x + 2) * tile_y, 6 * lanes), BF16),
            pltpu.VMEM((3 * len(OFFSETS), 8, lanes), F32),
            pltpu.VMEM((3, tile_x, 8, lanes), F32),
        ],
        compiler_params=params(10),
        cost_estimate=cost(2000 * MIB, 5 * MIB),
    )(live, pats, near_rows, low_rows)

    pair = [jax.ShapeDtypeStruct((2, 4, parents, lanes), F32)] * 2
    lower, near, kept = pl.pallas_call(
        functools.partial(halos_kernel, tile_x, tile_y),
        name="halos",
        out_shape=pair + [jax.ShapeDtypeStruct((4, parents, lanes), F32)],
        in_specs=vmem(10),
        out_specs=vmem(3),
        scratch_shapes=[
            pltpu.VMEM((4, 4, tile_x + 16, lanes), F32),
            pltpu.VMEM((4, 4 * width, lanes), F32),
            pltpu.VMEM((tile_x, lanes), F32),
        ],
        compiler_params=params(10),
        cost_estimate=cost(100 * MIB, 5 * MIB),
    )(inner_y, outer_y, inner_x, outer_x, agg_near, near_rows, low_rows, lower, near, kept)

    table = up_translator.reshape(kinds, 2, 2, half // 2).transpose(0, 2, 1, 3).reshape(4 * kinds, half // 2)
    groups = parents // GROUP
    at, back, table8 = pl.pallas_call(
        functools.partial(order_kernel, chunks, kinds, parents_x, parents_y),
        name="order",
        out_shape=[
            jax.ShapeDtypeStruct((2 * groups + 8, GROUP * slots), jnp.int32),
            jax.ShapeDtypeStruct((parents, parents), BF16),
            jax.ShapeDtypeStruct((8 * kinds + 8, half // 2), F32),
        ],
        in_specs=vmem(4),
        out_specs=vmem(3),
        compiler_params=params(8),
        cost_estimate=cost(300 * MIB, MIB),
    )(coarse_list.reshape(parents, slots), coarse_kind.reshape(parents, slots), coarse_count, table)
    at = at.reshape(-1)
    out = pl.pallas_call(
        functools.partial(lists_kernel, chunks, tile_x, tile_y, slots),
        name="lists",
        out_shape=jax.ShapeDtypeStruct((2 * boxes, lanes), F32),
        in_specs=vmem(chunks) + [pl.BlockSpec(memory_space=pl.ANY)] + vmem(6) + [in_hbm],
        out_specs=in_hbm,
        scratch_shapes=[
            pltpu.VMEM((chunks * parents * 8, wide // 4), F32),
            pltpu.VMEM((4 * parents, wide // 4), F32),
            pltpu.SMEM(at.shape, jnp.int32),
            pltpu.VMEM((4, wide, 2 * lanes), BF16),
            pltpu.VMEM((4, parents, 2 * lanes), BF16),
            pltpu.VMEM((2 * boxes, lanes), F32),
            pltpu.SemaphoreType.DMA((4,)),
        ],
        compiler_params=params(16 if chunks <= 4 else 40),
        cost_estimate=cost(2000 * MIB, 8 * MIB),
    )(*sources, at, table8, back, kept, lower, near, receive_map, hbm(parent_to_child))
    return out.reshape(tile_x, tile_y, 2, lanes)


def solution(mesh):
    tiles = P("gx", "gy")
    in_specs = (tiles, tiles, P(), P(), P(), P(), tiles, tiles, tiles, P(), P(), P())
    return jax.shard_map(body, mesh=mesh, in_specs=in_specs, out_specs=tiles, check_vma=False)
```

```python
import functools

import jax
import jax.numpy as jnp
from jax import lax
from jax.experimental import pallas as pl
from jax.experimental.pallas import tpu as pltpu
from jax.sharding import PartitionSpec as P

F32 = jnp.float32
BF16 = jnp.bfloat16
MIB = 1 << 20


def vmem(count):
    return [pl.BlockSpec(memory_space=pltpu.VMEM)] * count


def hbm(array):
    return pltpu.with_memory_space_constraint(array, pltpu.HBM)


def params(mib):
    return pltpu.CompilerParams(vmem_limit_bytes=mib * MIB)


def cost(macs, moved):
    return pl.CostEstimate(flops=2 * macs, bytes_accessed=moved, transcendentals=0)


def mm(left, right):
    return jnp.dot(left, right, preferred_element_type=F32)


def count_rows(counts_ref, tile_x, tile_y, lanes):
    eye = lax.broadcasted_iota(jnp.int32, (tile_y, tile_y), 0) == lax.broadcasted_iota(
        jnp.int32, (tile_y, tile_y), 1
    )
    counts = counts_ref[...].astype(F32)
    diag = [
        jnp.where(eye, jnp.broadcast_to(counts[i : i + 1], (tile_y, tile_y)), 0.0) for i in range(tile_x)
    ]
    return mm(jnp.concatenate(diag, axis=0).astype(BF16), jnp.ones((tile_y, lanes), BF16))


def halo_pair(inner_ref, outer_ref, axis):
    at = lax.axis_index(axis)
    odd = at % 2 == 1
    inner, outer = inner_ref[...].astype(F32), outer_ref[...].astype(F32)
    before, after = jnp.where(odd, inner, outer), jnp.where(odd, outer, inner)
    return jnp.where(at > 0, before, 0.0), jnp.where(at < lax.axis_size(axis) - 1, after, 0.0)


LEFT = 8


def live_kernel(tile_x, tile_y, cur_hbm, counts_hbm, agg_hbm, up_hbm,
                live_ref, kept_ref, low_ref, high_ref, agg_ref, up_ref, cur_ref, counts_ref, wide, sems):
    pairs = [(counts_hbm, counts_ref), (cur_hbm, cur_ref), (agg_hbm, agg_ref), (up_hbm, up_ref)]
    loads = [
        pltpu.make_async_copy(source, target, sems.at[k]) for k, (source, target) in enumerate(pairs)
    ]
    for load in loads:
        load.start()
    lanes = cur_ref.shape[1]
    boxes = tile_x * tile_y
    loads[0].wait()
    limits = count_rows(counts_ref, tile_x, tile_y, lanes)
    keep = lax.broadcasted_iota(jnp.int32, (boxes, lanes), 1).astype(F32) < limits
    kept_ref[...] = jnp.where(keep, 1.0, 0.0)
    odd = lax.axis_index("gy") % 2 == 1
    loads[1].wait()
    wide[...] = cur_ref[...].astype(F32)
    for part in range(2):
        cols = slice(part * lanes, (part + 1) * lanes)
        live_ref[:, cols] = jnp.where(keep, wide[pl.ds(part, boxes, stride=2), :], 0.0).astype(BF16)

        def edge(column):
            rows = wide[pl.ds(2 * column + part, tile_x, stride=2 * tile_y), :]
            return rows * kept_ref[pl.ds(column, tile_x, stride=tile_y), :]

        first = jnp.concatenate([edge(0), edge(1)], axis=0).astype(BF16)
        last = jnp.concatenate([edge(tile_y - 2), edge(tile_y - 1)], axis=0).astype(BF16)
        low_ref[:, cols] = jnp.where(odd, first, last)
        high_ref[:, cols] = jnp.where(odd, last, first)
    for load in loads[2:]:
        load.wait()


def rims_kernel(tile_x, tile_y, live_ref, inner_ref, outer_ref, low_ref, high_ref, first, last):
    odd = lax.axis_index("gx") % 2 == 1
    sides = halo_pair(inner_ref, outer_ref, "gy")
    for rim, start in ((first, 0), (last, tile_x - 2)):
        rim[0 : 2 * tile_y, :] = live_ref[start * tile_y : (start + 2) * tile_y, :].astype(F32)
        place = 2 * tile_y
        for side in sides:
            for column in range(2):
                at = column * tile_x + start
                rim[place : place + 2, :] = side[at : at + 2]
                place += 2
        rim[place:, :] = jnp.zeros((rim.shape[0] - place, rim.shape[1]), F32)
    low_ref[...] = jnp.where(odd, first[...], last[...]).astype(BF16)
    high_ref[...] = jnp.where(odd, last[...], first[...]).astype(BF16)


def parents_kernel(tile_x, tile_y, live_ref, agg_ref, up_ref, coarse_ref, pats_ref, pats, rows4):
    lanes = pats.shape[2]
    width = tile_y + 2 * LEFT
    pattern = mm(live_ref[...], agg_ref[...])
    pats[0] = pattern[:, :lanes]
    pats[1] = pattern[:, lanes:]
    children = []
    for side_x in range(2):
        for side_y in range(2):
            for part in range(2):
                rows = [
                    pats[part, pl.ds((2 * p + side_x) * tile_y + side_y, tile_y // 2, stride=2), :]
                    for p in range(tile_x // 2)
                ]
                children.append(jnp.concatenate(rows, axis=0).astype(BF16))
    coarse = mm(jnp.concatenate(children, axis=1), up_ref[...])
    for place in range(4):
        rows4[pl.ds(place, coarse.shape[0], stride=4), :] = coarse[:, place * 128 : (place + 1) * 128]
    coarse_ref[...] = rows4[...].astype(BF16)
    pattern = pattern.astype(BF16).astype(F32)
    values = [pattern[:, :lanes], pattern[:, lanes:], pattern[:, :lanes] + pattern[:, lanes:]]
    none = jnp.zeros((LEFT, lanes), F32)
    for i in range(tile_x):
        base = i * width
        for k in range(3):
            pats_ref[k, base : base + LEFT, :] = none
            pats_ref[k, base + LEFT : base + LEFT + tile_y, :] = values[k][i * tile_y : (i + 1) * tile_y]
            pats_ref[k, base + LEFT + tile_y : base + width, :] = none


OFFSETS = [(dx, dy) for dx in range(-2, 3) for dy in range(-2, 3) if max(abs(dx), abs(dy)) == 2]


def local_kernel(
    tile_x, tile_y, live_ref, pats, near_ref, low_ref, lower_ref, field_ref, cells, shifted, tables, sums,
):
    lanes = lower_ref.shape[2]
    width = tile_y + 2 * LEFT
    none = jnp.zeros((LEFT, lanes), F32)
    ends = jnp.zeros((tile_y, 6 * lanes), BF16)
    shifted[0:tile_y, :] = ends
    shifted[(tile_x + 1) * tile_y : (tile_x + 2) * tile_y, :] = ends
    shifted[tile_y : (tile_x + 1) * tile_y, 2 * lanes : 4 * lanes] = live_ref[...]
    for part in range(2):
        cols = slice(part * lanes, (part + 1) * lanes)
        for i in range(tile_x):
            base = i * width
            cells[part, base : base + LEFT, :] = none
            cells[part, base + LEFT : base + LEFT + tile_y, :] = live_ref[
                i * tile_y : (i + 1) * tile_y, cols
            ].astype(F32)
            cells[part, base + LEFT + tile_y : base + width, :] = none
            for shift in (-1, 1):
                place = (2 * (shift + 1) + part) * lanes
                shifted[(i + 1) * tile_y : (i + 2) * tile_y, place : place + lanes] = cells[
                    part, base + LEFT + shift : base + LEFT + shift + tile_y, :
                ].astype(BF16)
    for k in range(len(OFFSETS)):
        t_real, t_imag = low_ref[2 * k : 2 * k + 1, :], low_ref[2 * k + 1 : 2 * k + 2, :]
        for n, value in enumerate((t_imag - t_real, t_imag + t_real, t_real)):
            tables[3 * k + n] = jnp.broadcast_to(value, (8, lanes))

    passes = [
        [(dx, dy) for dx, dy in OFFSETS if dy == -2],
        [(dx, dy) for dx, dy in OFFSETS if dy == 2],
        [(dx, dy) for dx, dy in OFFSETS if abs(dy) < 2],
    ]
    blocks = tile_y // 8
    size = tile_x * tile_y // blocks

    def block(b, carry):
        total = None
        for shift in range(3):
            start = pl.multiple_of(b * size + shift * tile_y, tile_y)
            term = mm(shifted[pl.ds(start, size), :], near_ref[shift])
            total = term if total is None else total + term
        start = pl.multiple_of(b * size, size)
        field_ref[0, pl.ds(start, size), :] = total[:, :lanes]
        field_ref[1, pl.ds(start, size), :] = total[:, lanes:]
        shift_y = pl.multiple_of(b * 8, 8)
        for number, offsets in enumerate(passes):
            running = {}
            for row in range(tile_x):
                for dy in sorted({dy for _, dy in offsets}):
                    rows = pl.ds(shift_y + (row * width + LEFT + dy), 8)
                    source = [pats[k, rows, :] for k in range(3)]
                    for dx in range(-2, 3):
                        i = row - dx
                        if (dx, dy) not in offsets or not 0 <= i < tile_x:
                            continue
                        k = OFFSETS.index((dx, dy))
                        if i not in running:
                            running[i] = [None] * 3 if number == 0 else [sums[n, i] for n in range(3)]
                        running[i] = [
                            tables[3 * k + n] * source[n]
                            if running[i][n] is None
                            else running[i][n] + tables[3 * k + n] * source[n]
                            for n in range(3)
                        ]
                for i in sorted(running):
                    if i + 2 <= row or row == tile_x - 1:
                        value = running.pop(i)
                        if number < 2:
                            for n in range(3):
                                sums[n, i] = value[n]
                        else:
                            place = pl.ds(pl.multiple_of(shift_y + i * tile_y, 8), 8)
                            lower_ref[0, place, :] = value[2] - value[1]
                            lower_ref[1, place, :] = value[2] + value[0]
        return carry

    lax.fori_loop(0, blocks, block, 0)


def halos_kernel(
    tile_x, tile_y, inner_y, outer_y, inner_x, outer_x, agg_ref, near_ref, low_ref, lower_in, field_in, kept_in,
    lower_ref, field_ref, kept_ref, columns, rims, line_ref,
):
    lanes = lower_in.shape[2]
    width = tile_y + 2 * LEFT
    halo = halo_pair(inner_y, outer_y, "gy") + halo_pair(inner_x, outer_x, "gx")
    half_x, half_y = tile_x // 2, tile_y // 2
    for child in range(4):
        for p in range(half_x):
            rows = slice(p * half_y, (p + 1) * half_y)
            boxes = pl.ds((2 * p + child // 2) * tile_y + child % 2, half_y, stride=2)
            for part in range(2):
                lower_ref[part, child, rows, :] = lower_in[part, boxes, :]
                field_ref[part, child, rows, :] = field_in[part, boxes, :]
            kept_ref[child, rows, :] = kept_in[boxes, :]

    def add_column(ref, part, box, value):
        line_ref[...] = value
        for side_x in range(2):
            child, rows = 2 * side_x + box % 2, pl.ds(box // 2, half_x, stride=half_y)
            ref[part, child, rows, :] = ref[part, child, rows, :] + line_ref[pl.ds(side_x, half_x, stride=2), :]

    def add_row(ref, part, box, value):
        line_ref[...] = value
        for side_y in range(2):
            child, rows = 2 * (box % 2) + side_y, slice(box // 2 * half_y, (box // 2 + 1) * half_y)
            ref[part, child, rows, :] = ref[part, child, rows, :] + line_ref[pl.ds(side_y, half_y, stride=2), :]

    halo = jnp.concatenate(halo, axis=0)
    pattern = mm(halo.astype(BF16), agg_ref[...]).astype(BF16).astype(F32)
    values = [halo[:, :lanes], halo[:, lanes:], pattern[:, :lanes], pattern[:, lanes:]]
    two = jnp.zeros((8, lanes), F32)
    rim_size = inner_x.shape[0]
    for n, value in enumerate(values):
        for side in range(2):
            for c in range(2):
                at = (2 * side + c) * tile_x
                columns[n, 2 * side + c, 0:8, :] = two
                columns[n, 2 * side + c, 8 : 8 + tile_x, :] = value[at : at + tile_x]
                columns[n, 2 * side + c, 8 + tile_x : 16 + tile_x, :] = two
        for end in range(2):
            at = 4 * tile_x + end * rim_size
            corner = at + 2 * tile_y
            for row in range(2):
                base = (2 * end + row) * width + LEFT
                rims[n, base : base + tile_y, :] = value[at + row * tile_y : at + (row + 1) * tile_y]
                for side in range(2):
                    for c in range(2):
                        place = base + (tile_y + c if side else c - 2)
                        line = corner + 4 * side + 2 * c + row
                        rims[n, place : place + 1, :] = value[line : line + 1]

    def translate(terms):
        first = second = 0.0
        for dx, dy, real, imag in terms:
            k = OFFSETS.index((dx, dy))
            t_real, t_imag = low_ref[2 * k : 2 * k + 1, :], low_ref[2 * k + 1 : 2 * k + 2, :]
            first = first + (t_real * real - t_imag * imag)
            second = second + (t_real * imag + t_imag * real)
        return first, second

    def column(n, side, c, dx):
        return columns[n, 2 * side + c, 8 + dx : 8 + dx + tile_x, :]

    def rim(n, end, row, dy):
        base = (2 * end + row) * width + LEFT + dy
        return rims[n, base : base + tile_y, :]

    for side in range(2):
        for box in ((tile_y - 1, tile_y - 2) if side else (0, 1)):
            terms = []
            for c in range(2):
                dy = (tile_y + c if side else c - 2) - box
                for dx in range(-2, 3):
                    if (dx, dy) in OFFSETS:
                        terms.append((dx, dy, column(2, side, c, dx), column(3, side, c, dx)))
            for part, value in enumerate(translate(terms)):
                add_column(lower_ref, part, box, value)
        source = jnp.concatenate(
            [column(part, side, 1 - side, dx) for dx in range(-1, 2) for part in range(2)], axis=1
        ).astype(BF16)
        weights = [near_ref[dx, (4 * side) * lanes : (4 * side + 2) * lanes, :] for dx in range(3)]
        value = mm(source, jnp.concatenate(weights, axis=0))
        for part in range(2):
            add_column(field_ref, part, tile_y - 1 if side else 0, value[:, part * lanes : (part + 1) * lanes])
    for end in range(2):
        for box in ((tile_x - 1, tile_x - 2) if end else (0, 1)):
            terms = []
            for row in range(2):
                dx = (tile_x + row if end else row - 2) - box
                for dy in range(-2, 3):
                    if (dx, dy) in OFFSETS:
                        terms.append((dx, dy, rim(2, end, row, dy), rim(3, end, row, dy)))
            for part, value in enumerate(translate(terms)):
                add_row(lower_ref, part, box, value)
        source = jnp.concatenate(
            [rim(part, end, 1 - end, dy) for dy in range(-1, 2) for part in range(2)], axis=1
        ).astype(BF16)
        value = mm(source, near_ref[2 * end])
        for part in range(2):
            add_row(field_ref, part, tile_x - 1 if end else 0, value[:, part * lanes : (part + 1) * lanes])


ROW = 8
GROUP = 16


def order_kernel(
    chunks, kinds, parents_x, parents_y, list_ref, kind_ref, count_ref, table_ref, at_ref, back_ref, table8
):
    width = table_ref.shape[1]
    for place, row in enumerate((0, 2, 0, 2, 1, 3, 1, 3)):
        table8[pl.ds(place, kinds, stride=8), :] = table_ref[pl.ds(row, kinds, stride=4), :]
    table8[8 * kinds : 8 * kinds + 8, :] = jnp.zeros((8, width), F32)
    parents = parents_x * parents_y
    slots = list_ref.shape[1]
    groups = parents // ROW
    lanes = at_ref.shape[1]
    down = lax.broadcasted_iota(jnp.int32, (parents, parents), 0)
    along = lax.broadcasted_iota(jnp.int32, (parents, parents), 1)
    column = count_rows(count_ref, parents_x, parents_y, parents)
    row = jnp.sum(jnp.where(down == along, column, 0.0), axis=0, keepdims=True)
    before = (column > row) | ((column == row) & (down < along))
    rank = jnp.sum(jnp.where(before, 1.0, 0.0), axis=0, keepdims=True)
    after = (row > column) | ((row == column) & (along < down))
    rank_down = jnp.sum(jnp.where(after, 1.0, 0.0), axis=1, keepdims=True)
    back_ref[...] = jnp.where(along.astype(F32) == rank_down, 1.0, 0.0).astype(BF16)

    across = parents_y * chunks
    entry = list_ref[...]
    line, place = entry // across, entry % across
    source = ((place // parents_y) ^ lax.axis_index("gy")) * parents + line * parents_y + place % parents_y
    used = lax.broadcasted_iota(jnp.int32, (parents, slots), 1).astype(F32) < column[:, :slots]
    kind = jnp.where(used, kind_ref[...], kinds)
    slot = lax.broadcasted_iota(jnp.int32, (slots, lanes), 0)
    lane = lax.broadcasted_iota(jnp.int32, (slots, lanes), 1)
    values = [
        mm(value.astype(F32).astype(BF16), jnp.where(lane == slot + n * slots, 1.0, 0.0).astype(BF16))
        for n, value in enumerate((source // 256, source % 256, kind))
    ]
    values = (values[0] + values[1] + values[2]).astype(BF16)
    wanted = ROW * (down % groups) + down // groups
    moved = mm(jnp.where(wanted.astype(F32) == rank, 1.0, 0.0).astype(BF16), values).astype(BF16)
    moved = jnp.concatenate([moved[k * groups : (k + 1) * groups] for k in range(ROW)], axis=1)
    totals = []
    from_lane = lax.broadcasted_iota(jnp.int32, (ROW * lanes, lanes), 0)
    to_lane = lax.broadcasted_iota(jnp.int32, (ROW * lanes, lanes), 1)
    for n in range(3):
        spread = from_lane == (to_lane // slots) * lanes + n * slots + to_lane % slots
        totals.append(mm(moved, jnp.where(spread, 1.0, 0.0).astype(BF16)).astype(jnp.int32))
    at_ref[0:groups, :] = (totals[0] * 256 + totals[1]) * 8
    at_ref[groups : 2 * groups, :] = totals[2] * 8
    least = (slots - 1 - 2 * lax.broadcasted_iota(jnp.int32, (parents, lanes), 1)).astype(F32)
    reach = jnp.sum(jnp.where(column[:, :lanes] >= least, 1.0, 0.0), axis=0, keepdims=True).astype(jnp.int32)
    at_ref[2 * groups :, :] = jnp.broadcast_to((reach + (GROUP - 1)) // GROUP, (8, lanes))


def lists_kernel(chunks, tile_x, tile_y, slots, *refs):
    sources = refs[:chunks]
    (at_any, table8, back_ref, kept_ref, lower_ref, near_ref, recv_ref, down_hbm, out_hbm,
     cells, sums, lines, at, down_ref, total_ref, out_ref, sems) = refs[chunks:]
    parents_x, parents_y = tile_x // 2, tile_y // 2
    parents = parents_x * parents_y
    lanes = table8.shape[1]
    groups = parents // GROUP
    loads = [
        pltpu.make_async_copy(at_any, at, sems.at[0]),
        pltpu.make_async_copy(down_hbm, down_ref, sems.at[1]),
    ]
    for load in loads:
        load.start()
    count = parents // 2
    pairs = cells.reshape(chunks * count, 2, 8, lanes)
    first_half = lax.broadcasted_iota(jnp.int32, (count, 8, lanes), 1) < 4
    for c, source in zip([0, chunks - 1] + list(range(1, chunks - 1)), sources):
        rows = source[...].astype(F32).reshape(count, 8, lanes)
        turned = pltpu.roll(rows, 4, axis=1)
        pairs[c * count : (c + 1) * count, 0] = jnp.where(first_half, rows, turned)
        pairs[c * count : (c + 1) * count, 1] = jnp.where(first_half, turned, rows)
    loads[0].wait()

    def step(length, n, carry):
        first = n * (GROUP * slots)
        second = first + parents * slots
        for k in range(GROUP):
            total = [None, None]
            for s in range(length):
                source = pl.multiple_of(at[first + (k * slots + s)], 8)
                kind = pl.multiple_of(at[second + (k * slots + s)], 8)
                term = cells[pl.ds(source, 8), :] * table8[pl.ds(kind, 8), :]
                total[s % 2] = term if total[s % 2] is None else total[s % 2] + term
            total = total[0] + total[1] if length else jnp.zeros((8, lanes), F32)
            sums[pl.ds(pl.multiple_of((n * GROUP + k) * 8, 8), 8), :] = total
        return carry

    start = 0
    for j, length in enumerate(range(slots, 0, -2)):
        end = at[2 * parents * slots + j]
        lax.fori_loop(start, end, functools.partial(step, length), 0)
        start = end
    lax.fori_loop(start, groups, functools.partial(step, 0), 0)

    raw = sums[...].reshape(count, 2, 8, lanes)
    one, other = raw[:, 0], raw[:, 1]
    with_real = jnp.where(first_half, one, pltpu.roll(other, 4, axis=1))
    with_imag = jnp.where(first_half, pltpu.roll(one, 4, axis=1), other)
    real = lax.broadcasted_iota(jnp.int32, (count, 8, lanes), 1) % 4 < 2
    turned = jnp.where(real, -pltpu.roll(with_imag, 6, axis=1), pltpu.roll(with_imag, 2, axis=1))
    lines[...] = (with_real + turned).reshape(4 * parents, lanes)
    ordered = [lines[pl.ds(place, parents, stride=4), :].astype(BF16) for place in range(4)]
    incoming = mm(back_ref[...], jnp.concatenate(ordered, axis=1)).astype(BF16)
    loads[1].wait()
    for child in range(4):
        down = mm(incoming, down_ref[child])
        for part in range(2):
            value = down[:, part * lanes : (part + 1) * lanes] + lower_ref[part, child]
            total_ref[child, :, part * lanes : (part + 1) * lanes] = value.astype(BF16)
    stores = []
    for half in range(2):
        first, size = half * parents // 2, parents // 2
        rows = slice(first, first + size)
        for child in range(4):
            field = mm(total_ref[child, rows, :], recv_ref[...])
            mask = kept_ref[child, rows, :]
            for part in range(2):
                value = (field[:, part * lanes : (part + 1) * lanes] + near_ref[part, child, rows, :]) * mask
                for p in range(parents_x // 2):
                    line = (2 * (half * parents_x // 2 + p) + child // 2) * tile_y + child % 2
                    out_ref[pl.ds(2 * line + part, parents_y, stride=4), :] = value[
                        p * parents_y : (p + 1) * parents_y
                    ]
        size = out_ref.shape[0] // 2
        rows = pl.ds(half * size, size)
        stores.append(pltpu.make_async_copy(out_ref.at[rows], out_hbm.at[rows], sems.at[2 + half]))
        stores[-1].start()
    for store in stores:
        store.wait()


def swap(low, high, axis, other):
    count, breadth = lax.axis_size(axis), lax.axis_size(other)
    lows = [(i, i ^ 1) for i in range(count)]
    highs = []
    for i in range(count):
        for j in range(breadth):
            end = i in (0, count - 1)
            target = (i, j ^ 1) if end else (((i + 1) ^ 1) - 1, j)
            highs.append((i * breadth + j, target[0] * breadth + target[1]))
    return lax.ppermute(low, axis, lows), lax.ppermute(high, (axis, other), highs)


def swap_rows(low, high, axis):
    count = lax.axis_size(axis)
    lows = [(i, i ^ 1) for i in range(count)]
    highs = [(i, (((i + 1) % count ^ 1) - 1) % count) for i in range(count)]
    return lax.ppermute(low, axis, lows), lax.ppermute(high, axis, highs)


def body(
    currents, box_count, aggregate, near_blocks, low_translator, child_to_parent, coarse_list,
    coarse_kind, coarse_count, up_translator, parent_to_child, receive_map,
):
    tile_x, tile_y = box_count.shape
    boxes = tile_x * tile_y
    lanes = currents.shape[-1]
    parents_x, parents_y, slots = coarse_list.shape
    parents = parents_x * parents_y
    kinds, _, half = up_translator.shape
    wide = 2 * half
    chunks = lax.axis_size("gy")
    in_hbm = pl.BlockSpec(memory_space=pltpu.HBM)

    edge = jax.ShapeDtypeStruct((2 * tile_x, 2 * lanes), BF16)
    edge = jax.ShapeDtypeStruct((2 * tile_x, 2 * lanes), BF16)
    width = tile_y + 2 * LEFT
    live, kept, low, high, agg_near, up_near = pl.pallas_call(
        functools.partial(live_kernel, tile_x, tile_y),
        name="live",
        out_shape=[
            jax.ShapeDtypeStruct((boxes, 2 * lanes), BF16),
            jax.ShapeDtypeStruct((boxes, lanes), F32),
            edge,
            edge,
            jax.ShapeDtypeStruct((2 * lanes, 2 * lanes), BF16),
            jax.ShapeDtypeStruct((8 * lanes, wide), BF16),
        ],
        in_specs=[in_hbm] * 4,
        out_specs=vmem(6),
        scratch_shapes=[
            pltpu.VMEM((2 * boxes, lanes), BF16),
            pltpu.VMEM((tile_x, tile_y), jnp.int32),
            pltpu.VMEM((2 * boxes, lanes), F32),
            pltpu.SemaphoreType.DMA((4,)),
        ],
        compiler_params=params(10),
        cost_estimate=cost(100 * MIB, 3 * MIB),
    )(
        hbm(currents.reshape(2 * boxes, lanes)), hbm(box_count), hbm(aggregate),
        hbm(child_to_parent.reshape(8 * lanes, wide)),
    )
    coarse, pats = pl.pallas_call(
        functools.partial(parents_kernel, tile_x, tile_y),
        name="parents",
        out_shape=[
            jax.ShapeDtypeStruct((4 * parents, wide // 4), BF16),
            jax.ShapeDtypeStruct((3, tile_x * width, lanes), F32),
        ],
        in_specs=vmem(3),
        out_specs=vmem(2),
        scratch_shapes=[
            pltpu.VMEM((2, boxes, lanes), F32),
            pltpu.VMEM((4 * parents, wide // 4), F32),
        ],
        compiler_params=params(10),
        cost_estimate=cost(200 * MIB, 3 * MIB),
    )(live, agg_near, up_near)
    inner_y, outer_y = swap_rows(low, high, "gy")
    sources = [coarse] + [
        lax.ppermute(coarse, "gy", [(i, i ^ d) for i in range(chunks)])
        for d in [chunks - 1] + list(range(1, chunks - 1))
    ]

    rim = 2 * tile_y + 8
    rim += -rim % 16
    low, high = pl.pallas_call(
        functools.partial(rims_kernel, tile_x, tile_y),
        name="rims",
        out_shape=[jax.ShapeDtypeStruct((rim, 2 * lanes), BF16)] * 2,
        in_specs=vmem(3),
        out_specs=vmem(2),
        scratch_shapes=[pltpu.VMEM((rim, 2 * lanes), F32)] * 2,
        compiler_params=params(10),
        cost_estimate=cost(1 * MIB, MIB),
    )(live, inner_y, outer_y)
    inner_x, outer_x = swap(low, high, "gx", "gy")
    live, coarse_count, _ = lax.optimization_barrier((live, coarse_count, low))

    near_rows = near_blocks.reshape(3, 6 * lanes, 2 * lanes)
    low_rows = low_translator.reshape(-1, lanes)
    pair = [jax.ShapeDtypeStruct((2, boxes, lanes), F32)] * 2
    lower, near = pl.pallas_call(
        functools.partial(local_kernel, tile_x, tile_y),
        name="local",
        out_shape=pair,
        in_specs=vmem(4),
        out_specs=vmem(2),
        scratch_shapes=[
            pltpu.VMEM((2, tile_x * width, lanes), F32),
            pltpu.VMEM(((tile_x + 2) * tile_y, 6 * lanes), BF16),
            pltpu.VMEM((3 * len(OFFSETS), 8, lanes), F32),
            pltpu.VMEM((3, tile_x, 8, lanes), F32),
        ],
        compiler_params=params(10),
        cost_estimate=cost(2000 * MIB, 5 * MIB),
    )(live, pats, near_rows, low_rows)

    pair = [jax.ShapeDtypeStruct((2, 4, parents, lanes), F32)] * 2
    lower, near, kept = pl.pallas_call(
        functools.partial(halos_kernel, tile_x, tile_y),
        name="halos",
        out_shape=pair + [jax.ShapeDtypeStruct((4, parents, lanes), F32)],
        in_specs=vmem(10),
        out_specs=vmem(3),
        scratch_shapes=[
            pltpu.VMEM((4, 4, tile_x + 16, lanes), F32),
            pltpu.VMEM((4, 4 * width, lanes), F32),
            pltpu.VMEM((tile_x, lanes), F32),
        ],
        compiler_params=params(10),
        cost_estimate=cost(100 * MIB, 5 * MIB),
    )(inner_y, outer_y, inner_x, outer_x, agg_near, near_rows, low_rows, lower, near, kept)

    table = up_translator.reshape(kinds, 2, 2, half // 2).transpose(0, 2, 1, 3).reshape(4 * kinds, half // 2)
    at, back, table8 = pl.pallas_call(
        functools.partial(order_kernel, chunks, kinds, parents_x, parents_y),
        name="order",
        out_shape=[
            jax.ShapeDtypeStruct((2 * parents // ROW + 8, ROW * slots), jnp.int32),
            jax.ShapeDtypeStruct((parents, parents), BF16),
            jax.ShapeDtypeStruct((8 * kinds + 8, half // 2), F32),
        ],
        in_specs=vmem(4),
        out_specs=vmem(3),
        compiler_params=params(8),
        cost_estimate=cost(300 * MIB, MIB),
    )(coarse_list.reshape(parents, slots), coarse_kind.reshape(parents, slots), coarse_count, table)
    at = at.reshape(-1)
    out = pl.pallas_call(
        functools.partial(lists_kernel, chunks, tile_x, tile_y, slots),
        name="lists",
        out_shape=jax.ShapeDtypeStruct((2 * boxes, lanes), F32),
        in_specs=vmem(chunks) + [pl.BlockSpec(memory_space=pl.ANY)] + vmem(6) + [in_hbm],
        out_specs=in_hbm,
        scratch_shapes=[
            pltpu.VMEM((chunks * parents * 8, wide // 4), F32),
            pltpu.VMEM((8 * parents, wide // 4), F32),
            pltpu.VMEM((4 * parents, wide // 4), F32),
            pltpu.SMEM(at.shape, jnp.int32),
            pltpu.VMEM((4, wide, 2 * lanes), BF16),
            pltpu.VMEM((4, parents, 2 * lanes), BF16),
            pltpu.VMEM((2 * boxes, lanes), F32),
            pltpu.SemaphoreType.DMA((4,)),
        ],
        compiler_params=params(16 if chunks <= 4 else 40),
        cost_estimate=cost(2000 * MIB, 8 * MIB),
    )(*sources, at, table8, back, kept, lower, near, receive_map, hbm(parent_to_child))
    return out.reshape(tile_x, tile_y, 2, lanes)


def solution(mesh):
    tiles = P("gx", "gy")
    in_specs = (tiles, tiles, P(), P(), P(), P(), tiles, tiles, tiles, P(), P(), P())
    return jax.shard_map(body, mesh=mesh, in_specs=in_specs, out_specs=tiles, check_vma=False)
```

```python
import functools

import jax
import jax.numpy as jnp
from jax import lax
from jax.experimental import pallas as pl
from jax.experimental.pallas import tpu as pltpu
from jax.sharding import PartitionSpec as P

F32 = jnp.float32
BF16 = jnp.bfloat16
MIB = 1 << 20


def vmem(count):
    return [pl.BlockSpec(memory_space=pltpu.VMEM)] * count


def hbm(array):
    return pltpu.with_memory_space_constraint(array, pltpu.HBM)


def params(mib):
    return pltpu.CompilerParams(vmem_limit_bytes=mib * MIB)


def cost(macs, moved):
    return pl.CostEstimate(flops=2 * macs, bytes_accessed=moved, transcendentals=0)


def mm(left, right):
    return jnp.dot(left, right, preferred_element_type=F32)


def count_rows(counts_ref, tile_x, tile_y, lanes):
    eye = lax.broadcasted_iota(jnp.int32, (tile_y, tile_y), 0) == lax.broadcasted_iota(
        jnp.int32, (tile_y, tile_y), 1
    )
    counts = counts_ref[...].astype(F32)
    diag = [
        jnp.where(eye, jnp.broadcast_to(counts[i : i + 1], (tile_y, tile_y)), 0.0) for i in range(tile_x)
    ]
    return mm(jnp.concatenate(diag, axis=0).astype(BF16), jnp.ones((tile_y, lanes), BF16))


def halo_pair(inner_ref, outer_ref, axis):
    at = lax.axis_index(axis)
    odd = at % 2 == 1
    inner, outer = inner_ref[...].astype(F32), outer_ref[...].astype(F32)
    before, after = jnp.where(odd, inner, outer), jnp.where(odd, outer, inner)
    return jnp.where(at > 0, before, 0.0), jnp.where(at < lax.axis_size(axis) - 1, after, 0.0)


LEFT = 8


def live_kernel(tile_x, tile_y, cur_hbm, counts_hbm, agg_hbm, up_hbm,
                live_ref, kept_ref, low_ref, high_ref, agg_ref, up_ref, cur_ref, counts_ref, wide, sems):
    pairs = [(counts_hbm, counts_ref), (cur_hbm, cur_ref), (agg_hbm, agg_ref), (up_hbm, up_ref)]
    loads = [
        pltpu.make_async_copy(source, target, sems.at[k]) for k, (source, target) in enumerate(pairs)
    ]
    for load in loads:
        load.start()
    lanes = cur_ref.shape[1]
    boxes = tile_x * tile_y
    loads[0].wait()
    limits = count_rows(counts_ref, tile_x, tile_y, lanes)
    keep = lax.broadcasted_iota(jnp.int32, (boxes, lanes), 1).astype(F32) < limits
    kept_ref[...] = jnp.where(keep, 1.0, 0.0)
    odd = lax.axis_index("gy") % 2 == 1
    loads[1].wait()
    wide[...] = cur_ref[...].astype(F32)
    for part in range(2):
        cols = slice(part * lanes, (part + 1) * lanes)
        live_ref[:, cols] = jnp.where(keep, wide[pl.ds(part, boxes, stride=2), :], 0.0).astype(BF16)

        def edge(column):
            rows = wide[pl.ds(2 * column + part, tile_x, stride=2 * tile_y), :]
            return rows * kept_ref[pl.ds(column, tile_x, stride=tile_y), :]

        first = jnp.concatenate([edge(0), edge(1)], axis=0).astype(BF16)
        last = jnp.concatenate([edge(tile_y - 2), edge(tile_y - 1)], axis=0).astype(BF16)
        low_ref[:, cols] = jnp.where(odd, first, last)
        high_ref[:, cols] = jnp.where(odd, last, first)
    for load in loads[2:]:
        load.wait()


def rims_kernel(tile_x, tile_y, live_ref, inner_ref, outer_ref, low_ref, high_ref, first, last):
    odd = lax.axis_index("gx") % 2 == 1
    sides = halo_pair(inner_ref, outer_ref, "gy")
    for rim, start in ((first, 0), (last, tile_x - 2)):
        rim[0 : 2 * tile_y, :] = live_ref[start * tile_y : (start + 2) * tile_y, :].astype(F32)
        place = 2 * tile_y
        for side in sides:
            for column in range(2):
                at = column * tile_x + start
                rim[place : place + 2, :] = side[at : at + 2]
                place += 2
        rim[place:, :] = jnp.zeros((rim.shape[0] - place, rim.shape[1]), F32)
    low_ref[...] = jnp.where(odd, first[...], last[...]).astype(BF16)
    high_ref[...] = jnp.where(odd, last[...], first[...]).astype(BF16)


def parents_kernel(tile_x, tile_y, live_ref, agg_ref, up_ref, coarse_ref, pats_ref, pats, rows4):
    lanes = pats.shape[2]
    width = tile_y + 2 * LEFT
    pattern = mm(live_ref[...], agg_ref[...])
    pats[0] = pattern[:, :lanes]
    pats[1] = pattern[:, lanes:]
    children = []
    for side_x in range(2):
        for side_y in range(2):
            for part in range(2):
                rows = [
                    pats[part, pl.ds((2 * p + side_x) * tile_y + side_y, tile_y // 2, stride=2), :]
                    for p in range(tile_x // 2)
                ]
                children.append(jnp.concatenate(rows, axis=0).astype(BF16))
    coarse = mm(jnp.concatenate(children, axis=1), up_ref[...])
    for place in range(4):
        rows4[pl.ds(place, coarse.shape[0], stride=4), :] = coarse[:, place * 128 : (place + 1) * 128]
    coarse_ref[...] = rows4[...].astype(BF16)
    pattern = pattern.astype(BF16).astype(F32)
    values = [pattern[:, :lanes], pattern[:, lanes:], pattern[:, :lanes] + pattern[:, lanes:]]
    none = jnp.zeros((LEFT, lanes), F32)
    for i in range(tile_x):
        base = i * width
        for k in range(3):
            pats_ref[k, base : base + LEFT, :] = none
            pats_ref[k, base + LEFT : base + LEFT + tile_y, :] = values[k][i * tile_y : (i + 1) * tile_y]
            pats_ref[k, base + LEFT + tile_y : base + width, :] = none


OFFSETS = [(dx, dy) for dx in range(-2, 3) for dy in range(-2, 3) if max(abs(dx), abs(dy)) == 2]


def local_kernel(
    tile_x, tile_y, live_ref, pats, near_ref, low_ref, lower_ref, field_ref, cells, shifted, tables, sums,
):
    lanes = lower_ref.shape[2]
    width = tile_y + 2 * LEFT
    none = jnp.zeros((LEFT, lanes), F32)
    ends = jnp.zeros((tile_y, 6 * lanes), BF16)
    shifted[0:tile_y, :] = ends
    shifted[(tile_x + 1) * tile_y : (tile_x + 2) * tile_y, :] = ends
    shifted[tile_y : (tile_x + 1) * tile_y, 2 * lanes : 4 * lanes] = live_ref[...]
    for part in range(2):
        cols = slice(part * lanes, (part + 1) * lanes)
        for i in range(tile_x):
            base = i * width
            cells[part, base : base + LEFT, :] = none
            cells[part, base + LEFT : base + LEFT + tile_y, :] = live_ref[
                i * tile_y : (i + 1) * tile_y, cols
            ].astype(F32)
            cells[part, base + LEFT + tile_y : base + width, :] = none
            for shift in (-1, 1):
                place = (2 * (shift + 1) + part) * lanes
                shifted[(i + 1) * tile_y : (i + 2) * tile_y, place : place + lanes] = cells[
                    part, base + LEFT + shift : base + LEFT + shift + tile_y, :
                ].astype(BF16)
    for k in range(len(OFFSETS)):
        t_real, t_imag = low_ref[2 * k : 2 * k + 1, :], low_ref[2 * k + 1 : 2 * k + 2, :]
        for n, value in enumerate((t_imag - t_real, t_imag + t_real, t_real)):
            tables[3 * k + n] = jnp.broadcast_to(value, (8, lanes))

    passes = [
        [(dx, dy) for dx, dy in OFFSETS if dy == -2],
        [(dx, dy) for dx, dy in OFFSETS if dy == 2],
        [(dx, dy) for dx, dy in OFFSETS if abs(dy) < 2],
    ]
    blocks = tile_y // 8
    size = tile_x * tile_y // blocks

    def block(b, carry):
        total = None
        for shift in range(3):
            start = pl.multiple_of(b * size + shift * tile_y, tile_y)
            term = mm(shifted[pl.ds(start, size), :], near_ref[shift])
            total = term if total is None else total + term
        start = pl.multiple_of(b * size, size)
        field_ref[0, pl.ds(start, size), :] = total[:, :lanes]
        field_ref[1, pl.ds(start, size), :] = total[:, lanes:]
        shift_y = pl.multiple_of(b * 8, 8)
        for number, offsets in enumerate(passes):
            running = {}
            for row in range(tile_x):
                for dy in sorted({dy for _, dy in offsets}):
                    rows = pl.ds(shift_y + (row * width + LEFT + dy), 8)
                    source = [pats[k, rows, :] for k in range(3)]
                    for dx in range(-2, 3):
                        i = row - dx
                        if (dx, dy) not in offsets or not 0 <= i < tile_x:
                            continue
                        k = OFFSETS.index((dx, dy))
                        if i not in running:
                            running[i] = [None] * 3 if number == 0 else [sums[n, i] for n in range(3)]
                        running[i] = [
                            tables[3 * k + n] * source[n]
                            if running[i][n] is None
                            else running[i][n] + tables[3 * k + n] * source[n]
                            for n in range(3)
                        ]
                for i in sorted(running):
                    if i + 2 <= row or row == tile_x - 1:
                        value = running.pop(i)
                        if number < 2:
                            for n in range(3):
                                sums[n, i] = value[n]
                        else:
                            place = pl.ds(pl.multiple_of(shift_y + i * tile_y, 8), 8)
                            lower_ref[0, place, :] = value[2] - value[1]
                            lower_ref[1, place, :] = value[2] + value[0]
        return carry

    lax.fori_loop(0, blocks, block, 0)


def halos_kernel(
    tile_x, tile_y, inner_y, outer_y, inner_x, outer_x, agg_ref, near_ref, low_ref, lower_in, field_in, kept_in,
    lower_ref, field_ref, kept_ref, columns, rims, line_ref,
):
    lanes = lower_in.shape[2]
    width = tile_y + 2 * LEFT
    halo = halo_pair(inner_y, outer_y, "gy") + halo_pair(inner_x, outer_x, "gx")
    half_x, half_y = tile_x // 2, tile_y // 2
    for child in range(4):
        for p in range(half_x):
            rows = slice(p * half_y, (p + 1) * half_y)
            boxes = pl.ds((2 * p + child // 2) * tile_y + child % 2, half_y, stride=2)
            for part in range(2):
                lower_ref[part, child, rows, :] = lower_in[part, boxes, :]
                field_ref[part, child, rows, :] = field_in[part, boxes, :]
            kept_ref[child, rows, :] = kept_in[boxes, :]

    def add_column(ref, part, box, value):
        line_ref[...] = value
        for side_x in range(2):
            child, rows = 2 * side_x + box % 2, pl.ds(box // 2, half_x, stride=half_y)
            ref[part, child, rows, :] = ref[part, child, rows, :] + line_ref[pl.ds(side_x, half_x, stride=2), :]

    def add_row(ref, part, box, value):
        line_ref[...] = value
        for side_y in range(2):
            child, rows = 2 * (box % 2) + side_y, slice(box // 2 * half_y, (box // 2 + 1) * half_y)
            ref[part, child, rows, :] = ref[part, child, rows, :] + line_ref[pl.ds(side_y, half_y, stride=2), :]

    halo = jnp.concatenate(halo, axis=0)
    pattern = mm(halo.astype(BF16), agg_ref[...]).astype(BF16).astype(F32)
    values = [halo[:, :lanes], halo[:, lanes:], pattern[:, :lanes], pattern[:, lanes:]]
    two = jnp.zeros((8, lanes), F32)
    rim_size = inner_x.shape[0]
    for n, value in enumerate(values):
        for side in range(2):
            for c in range(2):
                at = (2 * side + c) * tile_x
                columns[n, 2 * side + c, 0:8, :] = two
                columns[n, 2 * side + c, 8 : 8 + tile_x, :] = value[at : at + tile_x]
                columns[n, 2 * side + c, 8 + tile_x : 16 + tile_x, :] = two
        for end in range(2):
            at = 4 * tile_x + end * rim_size
            corner = at + 2 * tile_y
            for row in range(2):
                base = (2 * end + row) * width + LEFT
                rims[n, base : base + tile_y, :] = value[at + row * tile_y : at + (row + 1) * tile_y]
                for side in range(2):
                    for c in range(2):
                        place = base + (tile_y + c if side else c - 2)
                        line = corner + 4 * side + 2 * c + row
                        rims[n, place : place + 1, :] = value[line : line + 1]

    def translate(terms):
        first = second = 0.0
        for dx, dy, real, imag in terms:
            k = OFFSETS.index((dx, dy))
            t_real, t_imag = low_ref[2 * k : 2 * k + 1, :], low_ref[2 * k + 1 : 2 * k + 2, :]
            first = first + (t_real * real - t_imag * imag)
            second = second + (t_real * imag + t_imag * real)
        return first, second

    def column(n, side, c, dx):
        return columns[n, 2 * side + c, 8 + dx : 8 + dx + tile_x, :]

    def rim(n, end, row, dy):
        base = (2 * end + row) * width + LEFT + dy
        return rims[n, base : base + tile_y, :]

    for side in range(2):
        for box in ((tile_y - 1, tile_y - 2) if side else (0, 1)):
            terms = []
            for c in range(2):
                dy = (tile_y + c if side else c - 2) - box
                for dx in range(-2, 3):
                    if (dx, dy) in OFFSETS:
                        terms.append((dx, dy, column(2, side, c, dx), column(3, side, c, dx)))
            for part, value in enumerate(translate(terms)):
                add_column(lower_ref, part, box, value)
        source = jnp.concatenate(
            [column(part, side, 1 - side, dx) for dx in range(-1, 2) for part in range(2)], axis=1
        ).astype(BF16)
        weights = [near_ref[dx, (4 * side) * lanes : (4 * side + 2) * lanes, :] for dx in range(3)]
        value = mm(source, jnp.concatenate(weights, axis=0))
        for part in range(2):
            add_column(field_ref, part, tile_y - 1 if side else 0, value[:, part * lanes : (part + 1) * lanes])
    for end in range(2):
        for box in ((tile_x - 1, tile_x - 2) if end else (0, 1)):
            terms = []
            for row in range(2):
                dx = (tile_x + row if end else row - 2) - box
                for dy in range(-2, 3):
                    if (dx, dy) in OFFSETS:
                        terms.append((dx, dy, rim(2, end, row, dy), rim(3, end, row, dy)))
            for part, value in enumerate(translate(terms)):
                add_row(lower_ref, part, box, value)
        source = jnp.concatenate(
            [rim(part, end, 1 - end, dy) for dy in range(-1, 2) for part in range(2)], axis=1
        ).astype(BF16)
        value = mm(source, near_ref[2 * end])
        for part in range(2):
            add_row(field_ref, part, tile_x - 1 if end else 0, value[:, part * lanes : (part + 1) * lanes])


ROW = 8
GROUP = 16


def order_kernel(
    chunks, kinds, parents_x, parents_y, list_ref, kind_ref, count_ref, table_ref, early_ref, late_ref, table8, words
):
    width = table_ref.shape[1]
    for place, row in enumerate((0, 2, 0, 2, 1, 3, 1, 3)):
        table8[pl.ds(place, kinds, stride=8), :] = table_ref[pl.ds(row, kinds, stride=4), :]
    table8[8 * kinds : 8 * kinds + 8, :] = jnp.zeros((8, width), F32)
    parents = parents_x * parents_y
    slots = list_ref.shape[1]
    groups = parents // ROW
    lanes = early_ref.shape[1]
    across = parents_y * chunks
    entry = list_ref[...]
    line, place = entry // across, entry % across
    chunk = (place // parents_y) ^ lax.axis_index("gy")
    is_late = (chunk > 0) & (chunk < chunks - 1)
    chunk = jnp.where(is_late, chunk - 1, jnp.where(chunk > 0, 1, 0))
    source = chunk * parents + line * parents_y + place % parents_y
    column = count_rows(count_ref, parents_x, parents_y, slots)
    used = lax.broadcasted_iota(jnp.int32, (parents, slots), 1).astype(F32) < column
    part = jnp.where(used, jnp.where(is_late, 2, 1), 0)
    words[:, 0:slots] = (source * 128 + kind_ref[...] + part * (1 << 20)).astype(F32)
    turned = words[...].T[0:slots].astype(jnp.int32)
    word, turned_part = turned & ((1 << 20) - 1), turned >> 20

    down = lax.broadcasted_iota(jnp.int32, (parents, parents), 0)
    along = lax.broadcasted_iota(jnp.int32, (parents, parents), 1)
    wanted = (ROW * (down % groups) + down // groups).astype(F32)
    earlier = lax.broadcasted_iota(jnp.int32, (slots, slots), 1) < lax.broadcasted_iota(jnp.int32, (slots, slots), 0)
    earlier = jnp.where(earlier, 1.0, 0.0).astype(BF16)
    slot = lax.broadcasted_iota(jnp.int32, (slots, parents), 0)
    from_lane = lax.broadcasted_iota(jnp.int32, (ROW * lanes, lanes), 0)
    to_lane = lax.broadcasted_iota(jnp.int32, (ROW * lanes, lanes), 1)
    spreads = [
        jnp.where(from_lane == (to_lane // slots) * lanes + n * slots + to_lane % slots, 1.0, 0.0).astype(BF16)
        for n in range(4)
    ]
    least = (slots - 1 - 2 * lax.broadcasted_iota(jnp.int32, (parents, lanes), 1)).astype(F32)
    for number, at_ref in ((1, early_ref), (2, late_ref)):
        hit = jnp.where(turned_part == number, 1.0, 0.0)
        mine = jnp.where(part == number, 1.0, 0.0).astype(BF16)
        column = mm(mine, jnp.ones((slots, parents), BF16))
        row = jnp.sum(hit, axis=0, keepdims=True)
        before = (column > row) | ((column == row) & (down < along))
        rank = jnp.sum(jnp.where(before, 1.0, 0.0), axis=0, keepdims=True)
        place = mm(earlier, hit.astype(BF16)).astype(jnp.int32)
        place = jnp.where(turned_part == number, place, -1)
        dense = jnp.zeros((slots, parents), jnp.int32)
        for n in range(slots):
            dense = dense + jnp.where(place[n : n + 1] == slot, word[n : n + 1], 0)
        kind = jnp.where(slot.astype(F32) < row, dense & 127, kinds)
        source = dense >> 7
        rest = jnp.zeros((lanes - 4 * slots, parents), F32)
        values = [source >> 8, source & 255, kind, along[0:slots]]
        values = jnp.concatenate([value.astype(F32) for value in values] + [rest], axis=0).astype(BF16)
        move = jnp.where(wanted == rank, 1.0, 0.0).astype(BF16)
        moved = lax.dot_general(move, values, (((1,), (1,)), ((), ())), preferred_element_type=F32).astype(BF16)
        moved = jnp.concatenate([moved[k * groups : (k + 1) * groups] for k in range(ROW)], axis=1)
        high, low, kind, parent = [mm(moved, spread).astype(jnp.int32) for spread in spreads]
        at_ref[0:groups, :] = (high * 256 + low) * 8
        at_ref[groups : 2 * groups, :] = kind * 8
        at_ref[2 * groups : 3 * groups, :] = parent * 8
        reach = jnp.sum(jnp.where(column[:, :lanes] >= least, 1.0, 0.0), axis=0, keepdims=True).astype(jnp.int32)
        at_ref[3 * groups :, :] = jnp.broadcast_to((reach + (GROUP - 1)) // GROUP, (8, lanes))


def expand(sources, cells):
    lanes = cells.shape[1]
    count = sources[0].shape[0] // 8
    pairs = cells.reshape(len(sources) * count, 2, 8, lanes)
    upper = lax.broadcasted_iota(jnp.int32, (count, 8, lanes), 1) < 4
    for c, source in enumerate(sources):
        rows = source[...].astype(F32).reshape(count, 8, lanes)
        turned = pltpu.roll(rows, 4, axis=1)
        pairs[c * count : (c + 1) * count, 0] = jnp.where(upper, rows, turned)
        pairs[c * count : (c + 1) * count, 1] = jnp.where(upper, turned, rows)


def add_lists(parents, slots, at, cells, table8, sums):
    lanes = cells.shape[1]
    groups = parents // GROUP

    def step(length, n, carry):
        first = n * (GROUP * slots)
        second, third = first + parents * slots, first + 2 * parents * slots
        for k in range(GROUP):
            total = [None, None]
            for s in range(length):
                source = pl.multiple_of(at[first + (k * slots + s)], 8)
                kind = pl.multiple_of(at[second + (k * slots + s)], 8)
                term = cells[pl.ds(source, 8), :] * table8[pl.ds(kind, 8), :]
                total[s % 2] = term if total[s % 2] is None else total[s % 2] + term
            total = total[0] + total[1] if length else jnp.zeros((8, lanes), F32)
            sums[pl.ds(pl.multiple_of(at[third + k * slots], 8), 8), :] = total
        return carry

    start = 0
    for j, length in enumerate(range(slots, 0, -2)):
        end = at[3 * parents * slots + j]
        lax.fori_loop(start, end, functools.partial(step, length), 0)
        start = end
    lax.fori_loop(start, groups, functools.partial(step, 0), 0)


def early_kernel(count, parents, slots, *refs):
    sources = refs[:count]
    at_any, table8, sums, cells, at, sem = refs[count:]
    load = pltpu.make_async_copy(at_any, at, sem)
    load.start()
    expand(sources, cells)
    load.wait()
    add_lists(parents, slots, at, cells, table8, sums)


def late_kernel(count, tile_x, tile_y, slots, *refs):
    sources = refs[:count]
    (at_any, table8, early_ref, kept_ref, lower_ref, near_ref, recv_ref, down_hbm, out_hbm,
     cells, sums, lines, at, down_ref, total_ref, out_ref, sems) = refs[count:]
    parents_x, parents_y = tile_x // 2, tile_y // 2
    parents = parents_x * parents_y
    lanes = table8.shape[1]
    loads = [
        pltpu.make_async_copy(at_any, at, sems.at[0]),
        pltpu.make_async_copy(down_hbm, down_ref, sems.at[1]),
    ]
    for load in loads:
        load.start()
    expand(sources, cells)
    loads[0].wait()
    add_lists(parents, slots, at, cells, table8, sums)
    raw = (sums[...] + early_ref[...]).reshape(parents // 2, 2, 8, lanes)
    one, other = raw[:, 0], raw[:, 1]
    line = lax.broadcasted_iota(jnp.int32, one.shape, 1)
    with_real = jnp.where(line < 4, one, pltpu.roll(other, 4, axis=1))
    with_imag = jnp.where(line < 4, pltpu.roll(one, 4, axis=1), other)
    turned = jnp.where(line % 4 < 2, -pltpu.roll(with_imag, 6, axis=1), pltpu.roll(with_imag, 2, axis=1))
    lines[...] = (with_real + turned).reshape(4 * parents, lanes)
    ordered = [lines[pl.ds(place, parents, stride=4), :].astype(BF16) for place in range(4)]
    incoming = jnp.concatenate(ordered, axis=1)
    loads[1].wait()
    for child in range(4):
        down = mm(incoming, down_ref[child])
        for part in range(2):
            value = down[:, part * lanes : (part + 1) * lanes] + lower_ref[part, child]
            total_ref[child, :, part * lanes : (part + 1) * lanes] = value.astype(BF16)
    stores = []
    for half in range(2):
        first, size = half * parents // 2, parents // 2
        rows = slice(first, first + size)
        for child in range(4):
            field = mm(total_ref[child, rows, :], recv_ref[...])
            mask = kept_ref[child, rows, :]
            for part in range(2):
                value = (field[:, part * lanes : (part + 1) * lanes] + near_ref[part, child, rows, :]) * mask
                for p in range(parents_x // 2):
                    line = (2 * (half * parents_x // 2 + p) + child // 2) * tile_y + child % 2
                    out_ref[pl.ds(2 * line + part, parents_y, stride=4), :] = value[
                        p * parents_y : (p + 1) * parents_y
                    ]
        size = out_ref.shape[0] // 2
        rows = pl.ds(half * size, size)
        stores.append(pltpu.make_async_copy(out_ref.at[rows], out_hbm.at[rows], sems.at[2 + half]))
        stores[-1].start()
    for store in stores:
        store.wait()


def swap(low, high, axis):
    count = lax.axis_size(axis)
    lows = [(i, i ^ 1) for i in range(count)]
    highs = [(i, (((i + 1) % count ^ 1) - 1) % count) for i in range(count)]
    return lax.ppermute(low, axis, lows), lax.ppermute(high, axis, highs)


def body(
    currents, box_count, aggregate, near_blocks, low_translator, child_to_parent, coarse_list,
    coarse_kind, coarse_count, up_translator, parent_to_child, receive_map,
):
    tile_x, tile_y = box_count.shape
    boxes = tile_x * tile_y
    lanes = currents.shape[-1]
    parents_x, parents_y, slots = coarse_list.shape
    parents = parents_x * parents_y
    kinds, _, half = up_translator.shape
    wide = 2 * half
    chunks = lax.axis_size("gy")
    in_hbm = pl.BlockSpec(memory_space=pltpu.HBM)

    edge = jax.ShapeDtypeStruct((2 * tile_x, 2 * lanes), BF16)
    edge = jax.ShapeDtypeStruct((2 * tile_x, 2 * lanes), BF16)
    width = tile_y + 2 * LEFT
    live, kept, low, high, agg_near, up_near = pl.pallas_call(
        functools.partial(live_kernel, tile_x, tile_y),
        name="live",
        out_shape=[
            jax.ShapeDtypeStruct((boxes, 2 * lanes), BF16),
            jax.ShapeDtypeStruct((boxes, lanes), F32),
            edge,
            edge,
            jax.ShapeDtypeStruct((2 * lanes, 2 * lanes), BF16),
            jax.ShapeDtypeStruct((8 * lanes, wide), BF16),
        ],
        in_specs=[in_hbm] * 4,
        out_specs=vmem(6),
        scratch_shapes=[
            pltpu.VMEM((2 * boxes, lanes), BF16),
            pltpu.VMEM((tile_x, tile_y), jnp.int32),
            pltpu.VMEM((2 * boxes, lanes), F32),
            pltpu.SemaphoreType.DMA((4,)),
        ],
        compiler_params=params(10),
        cost_estimate=cost(100 * MIB, 3 * MIB),
    )(
        hbm(currents.reshape(2 * boxes, lanes)), hbm(box_count), hbm(aggregate),
        hbm(child_to_parent.reshape(8 * lanes, wide)),
    )
    coarse, pats = pl.pallas_call(
        functools.partial(parents_kernel, tile_x, tile_y),
        name="parents",
        out_shape=[
            jax.ShapeDtypeStruct((4 * parents, wide // 4), BF16),
            jax.ShapeDtypeStruct((3, tile_x * width, lanes), F32),
        ],
        in_specs=vmem(3),
        out_specs=vmem(2),
        scratch_shapes=[
            pltpu.VMEM((2, boxes, lanes), F32),
            pltpu.VMEM((4 * parents, wide // 4), F32),
        ],
        compiler_params=params(10),
        cost_estimate=cost(200 * MIB, 3 * MIB),
    )(live, agg_near, up_near)
    inner_y, outer_y = swap(low, high, "gy")
    sources = [coarse] + [
        lax.ppermute(coarse, "gy", [(i, i ^ d) for i in range(chunks)])
        for d in [chunks - 1] + list(range(1, chunks - 1))
    ]

    rim = 2 * tile_y + 8
    rim += -rim % 16
    low, high = pl.pallas_call(
        functools.partial(rims_kernel, tile_x, tile_y),
        name="rims",
        out_shape=[jax.ShapeDtypeStruct((rim, 2 * lanes), BF16)] * 2,
        in_specs=vmem(3),
        out_specs=vmem(2),
        scratch_shapes=[pltpu.VMEM((rim, 2 * lanes), F32)] * 2,
        compiler_params=params(10),
        cost_estimate=cost(1 * MIB, MIB),
    )(live, inner_y, outer_y)
    inner_x, outer_x = swap(low, high, "gx")
    live, coarse_count, _ = lax.optimization_barrier((live, coarse_count, low))

    near_rows = near_blocks.reshape(3, 6 * lanes, 2 * lanes)
    low_rows = low_translator.reshape(-1, lanes)
    pair = [jax.ShapeDtypeStruct((2, boxes, lanes), F32)] * 2
    lower, near = pl.pallas_call(
        functools.partial(local_kernel, tile_x, tile_y),
        name="local",
        out_shape=pair,
        in_specs=vmem(4),
        out_specs=vmem(2),
        scratch_shapes=[
            pltpu.VMEM((2, tile_x * width, lanes), F32),
            pltpu.VMEM(((tile_x + 2) * tile_y, 6 * lanes), BF16),
            pltpu.VMEM((3 * len(OFFSETS), 8, lanes), F32),
            pltpu.VMEM((3, tile_x, 8, lanes), F32),
        ],
        compiler_params=params(10),
        cost_estimate=cost(2000 * MIB, 5 * MIB),
    )(live, pats, near_rows, low_rows)

    pair = [jax.ShapeDtypeStruct((2, 4, parents, lanes), F32)] * 2
    lower, near, kept = pl.pallas_call(
        functools.partial(halos_kernel, tile_x, tile_y),
        name="halos",
        out_shape=pair + [jax.ShapeDtypeStruct((4, parents, lanes), F32)],
        in_specs=vmem(10),
        out_specs=vmem(3),
        scratch_shapes=[
            pltpu.VMEM((4, 4, tile_x + 16, lanes), F32),
            pltpu.VMEM((4, 4 * width, lanes), F32),
            pltpu.VMEM((tile_x, lanes), F32),
        ],
        compiler_params=params(10),
        cost_estimate=cost(100 * MIB, 5 * MIB),
    )(inner_y, outer_y, inner_x, outer_x, agg_near, near_rows, low_rows, lower, near, kept)

    table = up_translator.reshape(kinds, 2, 2, half // 2).transpose(0, 2, 1, 3).reshape(4 * kinds, half // 2)
    places = jax.ShapeDtypeStruct((3 * parents // ROW + 8, ROW * slots), jnp.int32)
    early_at, late_at, table8 = pl.pallas_call(
        functools.partial(order_kernel, chunks, kinds, parents_x, parents_y),
        name="order",
        out_shape=[places, places, jax.ShapeDtypeStruct((8 * kinds + 8, half // 2), F32)],
        in_specs=vmem(4),
        out_specs=vmem(3),
        scratch_shapes=[pltpu.VMEM((parents, 128), F32)],
        compiler_params=params(10),
        cost_estimate=cost(300 * MIB, MIB),
    )(coarse_list.reshape(parents, slots), coarse_kind.reshape(parents, slots), coarse_count, table)
    early_at, late_at = early_at.reshape(-1), late_at.reshape(-1)
    anywhere = pl.BlockSpec(memory_space=pl.ANY)
    early, late = sources[:2], sources[2:]
    early_sums = pl.pallas_call(
        functools.partial(early_kernel, len(early), parents, slots),
        name="early",
        out_shape=jax.ShapeDtypeStruct((8 * parents, wide // 4), F32),
        in_specs=vmem(len(early)) + [anywhere] + vmem(1),
        out_specs=pl.BlockSpec(memory_space=pltpu.VMEM),
        scratch_shapes=[
            pltpu.VMEM((len(early) * parents * 8, wide // 4), F32),
            pltpu.SMEM(early_at.shape, jnp.int32),
            pltpu.SemaphoreType.DMA,
        ],
        compiler_params=params(10),
        cost_estimate=cost(1000 * MIB, 4 * MIB),
    )(*early, early_at, table8)
    out = pl.pallas_call(
        functools.partial(late_kernel, len(late), tile_x, tile_y, slots),
        name="late",
        out_shape=jax.ShapeDtypeStruct((2 * boxes, lanes), F32),
        in_specs=vmem(len(late)) + [anywhere] + vmem(6) + [in_hbm],
        out_specs=in_hbm,
        scratch_shapes=[
            pltpu.VMEM((len(late) * parents * 8, wide // 4), F32),
            pltpu.VMEM((8 * parents, wide // 4), F32),
            pltpu.VMEM((4 * parents, wide // 4), F32),
            pltpu.SMEM(late_at.shape, jnp.int32),
            pltpu.VMEM((4, wide, 2 * lanes), BF16),
            pltpu.VMEM((4, parents, 2 * lanes), BF16),
            pltpu.VMEM((2 * boxes, lanes), F32),
            pltpu.SemaphoreType.DMA((4,)),
        ],
        compiler_params=params(16 if chunks <= 4 else 40),
        cost_estimate=cost(2000 * MIB, 8 * MIB),
    )(*late, late_at, table8, early_sums, kept, lower, near, receive_map, hbm(parent_to_child))
    return out.reshape(tile_x, tile_y, 2, lanes)


def solution(mesh):
    tiles = P("gx", "gy")
    in_specs = (tiles, tiles, P(), P(), P(), P(), tiles, tiles, tiles, P(), P(), P())
    return jax.shard_map(body, mesh=mesh, in_specs=in_specs, out_specs=tiles, check_vma=False)
```

```python
import functools

import jax
import jax.numpy as jnp
from jax import lax
from jax.experimental import pallas as pl
from jax.experimental.pallas import tpu as pltpu
from jax.sharding import PartitionSpec as P

F32 = jnp.float32
BF16 = jnp.bfloat16
MIB = 1 << 20


def vmem(count):
    return [pl.BlockSpec(memory_space=pltpu.VMEM)] * count


def hbm(array):
    return pltpu.with_memory_space_constraint(array, pltpu.HBM)


def params(mib):
    return pltpu.CompilerParams(vmem_limit_bytes=mib * MIB)


def cost(macs, moved):
    return pl.CostEstimate(flops=2 * macs, bytes_accessed=moved, transcendentals=0)


def mm(left, right):
    return jnp.dot(left, right, preferred_element_type=F32)


def count_rows(counts_ref, tile_x, tile_y, lanes):
    eye = lax.broadcasted_iota(jnp.int32, (tile_y, tile_y), 0) == lax.broadcasted_iota(
        jnp.int32, (tile_y, tile_y), 1
    )
    counts = counts_ref[...].astype(F32)
    diag = [
        jnp.where(eye, jnp.broadcast_to(counts[i : i + 1], (tile_y, tile_y)), 0.0) for i in range(tile_x)
    ]
    return mm(jnp.concatenate(diag, axis=0).astype(BF16), jnp.ones((tile_y, lanes), BF16))


def halo_pair(inner_ref, outer_ref, axis):
    at = lax.axis_index(axis)
    odd = at % 2 == 1
    inner, outer = inner_ref[...].astype(F32), outer_ref[...].astype(F32)
    before, after = jnp.where(odd, inner, outer), jnp.where(odd, outer, inner)
    return jnp.where(at > 0, before, 0.0), jnp.where(at < lax.axis_size(axis) - 1, after, 0.0)


LEFT = 8


def live_kernel(tile_x, tile_y, cur_hbm, counts_hbm, agg_hbm, up_hbm,
                live_ref, kept_ref, low_ref, high_ref, agg_ref, up_ref, cur_ref, counts_ref, wide, sems):
    pairs = [(counts_hbm, counts_ref), (cur_hbm, cur_ref), (agg_hbm, agg_ref), (up_hbm, up_ref)]
    loads = [
        pltpu.make_async_copy(source, target, sems.at[k]) for k, (source, target) in enumerate(pairs)
    ]
    for load in loads:
        load.start()
    lanes = cur_ref.shape[1]
    boxes = tile_x * tile_y
    loads[0].wait()
    limits = count_rows(counts_ref, tile_x, tile_y, lanes)
    keep = lax.broadcasted_iota(jnp.int32, (boxes, lanes), 1).astype(F32) < limits
    kept_ref[...] = jnp.where(keep, 1.0, 0.0)
    odd = lax.axis_index("gy") % 2 == 1
    loads[1].wait()
    wide[...] = cur_ref[...].astype(F32)
    for part in range(2):
        cols = slice(part * lanes, (part + 1) * lanes)
        live_ref[:, cols] = jnp.where(keep, wide[pl.ds(part, boxes, stride=2), :], 0.0).astype(BF16)

        def edge(column):
            rows = wide[pl.ds(2 * column + part, tile_x, stride=2 * tile_y), :]
            return rows * kept_ref[pl.ds(column, tile_x, stride=tile_y), :]

        first = jnp.concatenate([edge(0), edge(1)], axis=0).astype(BF16)
        last = jnp.concatenate([edge(tile_y - 2), edge(tile_y - 1)], axis=0).astype(BF16)
        low_ref[:, cols] = jnp.where(odd, first, last)
        high_ref[:, cols] = jnp.where(odd, last, first)
    for load in loads[2:]:
        load.wait()


def rims_kernel(tile_x, tile_y, live_ref, inner_ref, outer_ref, low_ref, high_ref, first, last):
    odd = lax.axis_index("gx") % 2 == 1
    sides = halo_pair(inner_ref, outer_ref, "gy")
    for rim, start in ((first, 0), (last, tile_x - 2)):
        rim[0 : 2 * tile_y, :] = live_ref[start * tile_y : (start + 2) * tile_y, :].astype(F32)
        place = 2 * tile_y
        for side in sides:
            for column in range(2):
                at = column * tile_x + start
                rim[place : place + 2, :] = side[at : at + 2]
                place += 2
        rim[place:, :] = jnp.zeros((rim.shape[0] - place, rim.shape[1]), F32)
    low_ref[...] = jnp.where(odd, first[...], last[...]).astype(BF16)
    high_ref[...] = jnp.where(odd, last[...], first[...]).astype(BF16)


def parents_kernel(tile_x, tile_y, live_ref, agg_ref, up_ref, coarse_ref, pats_ref, pats, rows4):
    lanes = pats.shape[2]
    width = tile_y + 2 * LEFT
    pattern = mm(live_ref[...], agg_ref[...])
    pats[0] = pattern[:, :lanes]
    pats[1] = pattern[:, lanes:]
    children = []
    for side_x in range(2):
        for side_y in range(2):
            for part in range(2):
                rows = [
                    pats[part, pl.ds((2 * p + side_x) * tile_y + side_y, tile_y // 2, stride=2), :]
                    for p in range(tile_x // 2)
                ]
                children.append(jnp.concatenate(rows, axis=0).astype(BF16))
    coarse = mm(jnp.concatenate(children, axis=1), up_ref[...])
    for place in range(4):
        rows4[pl.ds(place, coarse.shape[0], stride=4), :] = coarse[:, place * 128 : (place + 1) * 128]
    coarse_ref[...] = rows4[...].astype(BF16)
    pattern = pattern.astype(BF16).astype(F32)
    values = [pattern[:, :lanes], pattern[:, lanes:], pattern[:, :lanes] + pattern[:, lanes:]]
    none = jnp.zeros((LEFT, lanes), F32)
    for i in range(tile_x):
        base = i * width
        for k in range(3):
            pats_ref[k, base : base + LEFT, :] = none
            pats_ref[k, base + LEFT : base + LEFT + tile_y, :] = values[k][i * tile_y : (i + 1) * tile_y]
            pats_ref[k, base + LEFT + tile_y : base + width, :] = none


OFFSETS = [(dx, dy) for dx in range(-2, 3) for dy in range(-2, 3) if max(abs(dx), abs(dy)) == 2]


def local_kernel(
    tile_x, tile_y, live_ref, pats, near_ref, low_ref, lower_ref, field_ref, cells, shifted, tables, sums,
):
    lanes = lower_ref.shape[2]
    width = tile_y + 2 * LEFT
    none = jnp.zeros((LEFT, lanes), F32)
    ends = jnp.zeros((tile_y, 6 * lanes), BF16)
    shifted[0:tile_y, :] = ends
    shifted[(tile_x + 1) * tile_y : (tile_x + 2) * tile_y, :] = ends
    shifted[tile_y : (tile_x + 1) * tile_y, 2 * lanes : 4 * lanes] = live_ref[...]
    for part in range(2):
        cols = slice(part * lanes, (part + 1) * lanes)
        for i in range(tile_x):
            base = i * width
            cells[part, base : base + LEFT, :] = none
            cells[part, base + LEFT : base + LEFT + tile_y, :] = live_ref[
                i * tile_y : (i + 1) * tile_y, cols
            ].astype(F32)
            cells[part, base + LEFT + tile_y : base + width, :] = none
            for shift in (-1, 1):
                place = (2 * (shift + 1) + part) * lanes
                shifted[(i + 1) * tile_y : (i + 2) * tile_y, place : place + lanes] = cells[
                    part, base + LEFT + shift : base + LEFT + shift + tile_y, :
                ].astype(BF16)
    for k in range(len(OFFSETS)):
        t_real, t_imag = low_ref[2 * k : 2 * k + 1, :], low_ref[2 * k + 1 : 2 * k + 2, :]
        for n, value in enumerate((t_imag - t_real, t_imag + t_real, t_real)):
            tables[3 * k + n] = jnp.broadcast_to(value, (8, lanes))

    passes = [
        [(dx, dy) for dx, dy in OFFSETS if dy == -2],
        [(dx, dy) for dx, dy in OFFSETS if dy == 2],
        [(dx, dy) for dx, dy in OFFSETS if abs(dy) < 2],
    ]
    blocks = tile_y // 8
    size = tile_x * tile_y // blocks

    def block(b, carry):
        total = None
        for shift in range(3):
            start = pl.multiple_of(b * size + shift * tile_y, tile_y)
            term = mm(shifted[pl.ds(start, size), :], near_ref[shift])
            total = term if total is None else total + term
        start = pl.multiple_of(b * size, size)
        field_ref[0, pl.ds(start, size), :] = total[:, :lanes]
        field_ref[1, pl.ds(start, size), :] = total[:, lanes:]
        shift_y = pl.multiple_of(b * 8, 8)
        for number, offsets in enumerate(passes):
            running = {}
            for row in range(tile_x):
                for dy in sorted({dy for _, dy in offsets}):
                    rows = pl.ds(shift_y + (row * width + LEFT + dy), 8)
                    source = [pats[k, rows, :] for k in range(3)]
                    for dx in range(-2, 3):
                        i = row - dx
                        if (dx, dy) not in offsets or not 0 <= i < tile_x:
                            continue
                        k = OFFSETS.index((dx, dy))
                        if i not in running:
                            running[i] = [None] * 3 if number == 0 else [sums[n, i] for n in range(3)]
                        running[i] = [
                            tables[3 * k + n] * source[n]
                            if running[i][n] is None
                            else running[i][n] + tables[3 * k + n] * source[n]
                            for n in range(3)
                        ]
                for i in sorted(running):
                    if i + 2 <= row or row == tile_x - 1:
                        value = running.pop(i)
                        if number < 2:
                            for n in range(3):
                                sums[n, i] = value[n]
                        else:
                            place = pl.ds(pl.multiple_of(shift_y + i * tile_y, 8), 8)
                            lower_ref[0, place, :] = value[2] - value[1]
                            lower_ref[1, place, :] = value[2] + value[0]
        return carry

    lax.fori_loop(0, blocks, block, 0)


def halos_kernel(
    tile_x, tile_y, inner_y, outer_y, inner_x, outer_x, agg_ref, near_ref, low_ref, lower_in, field_in, kept_in,
    lower_ref, field_ref, kept_ref, columns, rims, line_ref,
):
    lanes = lower_in.shape[2]
    width = tile_y + 2 * LEFT
    halo = halo_pair(inner_y, outer_y, "gy") + halo_pair(inner_x, outer_x, "gx")
    half_x, half_y = tile_x // 2, tile_y // 2
    for child in range(4):
        for p in range(half_x):
            rows = slice(p * half_y, (p + 1) * half_y)
            boxes = pl.ds((2 * p + child // 2) * tile_y + child % 2, half_y, stride=2)
            for part in range(2):
                lower_ref[part, child, rows, :] = lower_in[part, boxes, :]
                field_ref[part, child, rows, :] = field_in[part, boxes, :]
            kept_ref[child, rows, :] = kept_in[boxes, :]

    def add_column(ref, part, box, value):
        line_ref[...] = value
        for side_x in range(2):
            child, rows = 2 * side_x + box % 2, pl.ds(box // 2, half_x, stride=half_y)
            ref[part, child, rows, :] = ref[part, child, rows, :] + line_ref[pl.ds(side_x, half_x, stride=2), :]

    def add_row(ref, part, box, value):
        line_ref[...] = value
        for side_y in range(2):
            child, rows = 2 * (box % 2) + side_y, slice(box // 2 * half_y, (box // 2 + 1) * half_y)
            ref[part, child, rows, :] = ref[part, child, rows, :] + line_ref[pl.ds(side_y, half_y, stride=2), :]

    halo = jnp.concatenate(halo, axis=0)
    pattern = mm(halo.astype(BF16), agg_ref[...]).astype(BF16).astype(F32)
    values = [halo[:, :lanes], halo[:, lanes:], pattern[:, :lanes], pattern[:, lanes:]]
    two = jnp.zeros((8, lanes), F32)
    rim_size = inner_x.shape[0]
    for n, value in enumerate(values):
        for side in range(2):
            for c in range(2):
                at = (2 * side + c) * tile_x
                columns[n, 2 * side + c, 0:8, :] = two
                columns[n, 2 * side + c, 8 : 8 + tile_x, :] = value[at : at + tile_x]
                columns[n, 2 * side + c, 8 + tile_x : 16 + tile_x, :] = two
        for end in range(2):
            at = 4 * tile_x + end * rim_size
            corner = at + 2 * tile_y
            for row in range(2):
                base = (2 * end + row) * width + LEFT
                rims[n, base : base + tile_y, :] = value[at + row * tile_y : at + (row + 1) * tile_y]
                for side in range(2):
                    for c in range(2):
                        place = base + (tile_y + c if side else c - 2)
                        line = corner + 4 * side + 2 * c + row
                        rims[n, place : place + 1, :] = value[line : line + 1]

    def translate(terms):
        first = second = 0.0
        for dx, dy, real, imag in terms:
            k = OFFSETS.index((dx, dy))
            t_real, t_imag = low_ref[2 * k : 2 * k + 1, :], low_ref[2 * k + 1 : 2 * k + 2, :]
            first = first + (t_real * real - t_imag * imag)
            second = second + (t_real * imag + t_imag * real)
        return first, second

    def column(n, side, c, dx):
        return columns[n, 2 * side + c, 8 + dx : 8 + dx + tile_x, :]

    def rim(n, end, row, dy):
        base = (2 * end + row) * width + LEFT + dy
        return rims[n, base : base + tile_y, :]

    for side in range(2):
        for box in ((tile_y - 1, tile_y - 2) if side else (0, 1)):
            terms = []
            for c in range(2):
                dy = (tile_y + c if side else c - 2) - box
                for dx in range(-2, 3):
                    if (dx, dy) in OFFSETS:
                        terms.append((dx, dy, column(2, side, c, dx), column(3, side, c, dx)))
            for part, value in enumerate(translate(terms)):
                add_column(lower_ref, part, box, value)
        source = jnp.concatenate(
            [column(part, side, 1 - side, dx) for dx in range(-1, 2) for part in range(2)], axis=1
        ).astype(BF16)
        weights = [near_ref[dx, (4 * side) * lanes : (4 * side + 2) * lanes, :] for dx in range(3)]
        value = mm(source, jnp.concatenate(weights, axis=0))
        for part in range(2):
            add_column(field_ref, part, tile_y - 1 if side else 0, value[:, part * lanes : (part + 1) * lanes])
    for end in range(2):
        for box in ((tile_x - 1, tile_x - 2) if end else (0, 1)):
            terms = []
            for row in range(2):
                dx = (tile_x + row if end else row - 2) - box
                for dy in range(-2, 3):
                    if (dx, dy) in OFFSETS:
                        terms.append((dx, dy, rim(2, end, row, dy), rim(3, end, row, dy)))
            for part, value in enumerate(translate(terms)):
                add_row(lower_ref, part, box, value)
        source = jnp.concatenate(
            [rim(part, end, 1 - end, dy) for dy in range(-1, 2) for part in range(2)], axis=1
        ).astype(BF16)
        value = mm(source, near_ref[2 * end])
        for part in range(2):
            add_row(field_ref, part, tile_x - 1 if end else 0, value[:, part * lanes : (part + 1) * lanes])


ROW = 8
GROUP = 16
QUARTERS = 4


def order_kernel(
    chunks, kinds, parents_x, parents_y, list_ref, kind_ref, count_ref, table_ref, early_ref, late_ref, table8, words
):
    width = table_ref.shape[1]
    for place, row in enumerate((0, 2, 0, 2, 1, 3, 1, 3)):
        table8[pl.ds(place, kinds, stride=8), :] = table_ref[pl.ds(row, kinds, stride=4), :]
    table8[8 * kinds : 8 * kinds + 8, :] = jnp.zeros((8, width), F32)
    parents = parents_x * parents_y
    slots = list_ref.shape[1]
    groups = parents // ROW
    lanes = early_ref.shape[1]
    across = parents_y * chunks
    entry = list_ref[...]
    line, place = entry // across, entry % across
    chunk = (place // parents_y) ^ lax.axis_index("gy")
    is_late = (chunk > 0) & (chunk < chunks - 1)
    chunk = jnp.where(is_late, chunk - 1, jnp.where(chunk > 0, 1, 0))
    source = chunk * parents + line * parents_y + place % parents_y
    column = count_rows(count_ref, parents_x, parents_y, slots)
    used = lax.broadcasted_iota(jnp.int32, (parents, slots), 1).astype(F32) < column
    part = jnp.where(used, jnp.where(is_late, 2, 1), 0)
    words[:, 0:slots] = (source * 128 + kind_ref[...] + part * (1 << 20)).astype(F32)
    turned = words[...].T[0:slots].astype(jnp.int32)
    word, turned_part = turned & ((1 << 20) - 1), turned >> 20

    down = lax.broadcasted_iota(jnp.int32, (parents, parents), 0)
    along = lax.broadcasted_iota(jnp.int32, (parents, parents), 1)
    wanted = (ROW * (down % groups) + down // groups).astype(F32)
    earlier = lax.broadcasted_iota(jnp.int32, (slots, slots), 1) < lax.broadcasted_iota(jnp.int32, (slots, slots), 0)
    earlier = jnp.where(earlier, 1.0, 0.0).astype(BF16)
    slot = lax.broadcasted_iota(jnp.int32, (slots, parents), 0)
    from_lane = lax.broadcasted_iota(jnp.int32, (ROW * lanes, lanes), 0)
    to_lane = lax.broadcasted_iota(jnp.int32, (ROW * lanes, lanes), 1)
    spreads = [
        jnp.where(from_lane == (to_lane // slots) * lanes + n * slots + to_lane % slots, 1.0, 0.0).astype(BF16)
        for n in range(3)
    ]
    least = (slots - 1 - 2 * lax.broadcasted_iota(jnp.int32, (parents, lanes), 1)).astype(F32)
    for number, at_ref in ((1, early_ref), (2, late_ref)):
        hit = jnp.where(turned_part == number, 1.0, 0.0)
        mine = jnp.where(part == number, 1.0, 0.0).astype(BF16)
        column = mm(mine, jnp.ones((slots, parents), BF16))
        row = jnp.sum(hit, axis=0, keepdims=True)
        before = (column > row) | ((column == row) & (down < along))
        rank = jnp.sum(jnp.where(before, 1.0, 0.0), axis=0, keepdims=True)
        place = mm(earlier, hit.astype(BF16)).astype(jnp.int32)
        place = jnp.where(turned_part == number, place, -1)
        dense = jnp.zeros((slots, parents), jnp.int32)
        for n in range(slots):
            dense = dense + jnp.where(place[n : n + 1] == slot, word[n : n + 1], 0)
        kind = jnp.where(slot.astype(F32) < row, dense & 127, kinds)
        source = dense >> 7
        rest = jnp.zeros((lanes - 3 * slots, parents), F32)
        values = [source >> 8, source & 255, kind]
        values = jnp.concatenate([value.astype(F32) for value in values] + [rest], axis=0).astype(BF16)
        move = jnp.where(wanted == rank, 1.0, 0.0).astype(BF16)
        moved = lax.dot_general(move, values, (((1,), (1,)), ((), ())), preferred_element_type=F32).astype(BF16)
        moved = jnp.concatenate([moved[k * groups : (k + 1) * groups] for k in range(ROW)], axis=1)
        high, low, kind = [mm(moved, spread).astype(jnp.int32) for spread in spreads]
        source, kind = (high * 256 + low) * 8, kind * 8
        rows = groups // QUARTERS
        for q in range(QUARTERS):
            at_ref[2 * q * rows : (2 * q + 1) * rows, :] = source[q * rows : (q + 1) * rows]
            at_ref[(2 * q + 1) * rows : (2 * q + 2) * rows, :] = kind[q * rows : (q + 1) * rows]
        ranked = jnp.where(down.astype(F32) == rank, 1.0, 0.0).astype(BF16)
        parent = lax.dot_general(
            along[0:8].astype(F32).astype(BF16), ranked, (((1,), (1,)), ((), ())), preferred_element_type=F32
        ).astype(jnp.int32) * 8
        reach = jnp.sum(jnp.where(column[:, :lanes] >= least, 1.0, 0.0), axis=0, keepdims=True).astype(jnp.int32)
        last = jnp.broadcast_to((reach + (GROUP - 1)) // GROUP, (8, lanes))
        line = lax.broadcasted_iota(jnp.int32, (8, lanes), 0)
        for n in range(parents // lanes):
            last = jnp.where(line == n, parent[:, n * lanes : (n + 1) * lanes], last)
        at_ref[2 * groups :, :] = last


def expand(sources, cells):
    lanes = cells.shape[1]
    count = sources[0].shape[0] // 8
    pairs = cells.reshape(len(sources) * count, 2, 8, lanes)
    upper = lax.broadcasted_iota(jnp.int32, (count, 8, lanes), 1) < 4
    for c, source in enumerate(sources):
        rows = source[...].astype(F32).reshape(count, 8, lanes)
        turned = pltpu.roll(rows, 4, axis=1)
        pairs[c * count : (c + 1) * count, 0] = jnp.where(upper, rows, turned)
        pairs[c * count : (c + 1) * count, 1] = jnp.where(upper, turned, rows)


def load_lists(at_any, at, sems):
    words = (at.shape[0] - 1024) // QUARTERS
    loads = []
    for n, (start, size) in enumerate([(QUARTERS * words, 1024)] + [(q * words, words) for q in range(QUARTERS)]):
        rows = pl.ds(start, size)
        loads.append(pltpu.make_async_copy(at_any.at[rows], at.at[rows], sems.at[n]))
        loads[-1].start()
    return loads


def add_lists(parents, slots, at_any, at, sems, cells, table8, sums):
    lanes = cells.shape[1]
    steps = parents // GROUP // QUARTERS
    words = (at.shape[0] - 1024) // QUARTERS
    tail = QUARTERS * words

    def step(length, q, n, carry):
        first = n * (GROUP * slots) + q * (words // 2)
        second = first + words // 2
        for k in range(GROUP):
            total = [None, None]
            for s in range(length):
                source = pl.multiple_of(at[first + (k * slots + s)], 8)
                kind = pl.multiple_of(at[second + (k * slots + s)], 8)
                term = cells[pl.ds(source, 8), :] * table8[pl.ds(kind, 8), :]
                total[s % 2] = term if total[s % 2] is None else total[s % 2] + term
            total = total[0] + total[1] if length else jnp.zeros((8, lanes), F32)
            place = pl.multiple_of(at[tail + n * GROUP + k], 8)
            sums[pl.ds(place, 8), :] = total
        return carry

    def quarter(q, carry):
        rows = pl.ds(pl.multiple_of(q * words, words), words)
        pltpu.make_async_copy(at_any.at[rows], at.at[rows], sems.at[1 + q]).wait()
        low, high = q * steps, (q + 1) * steps
        start = low
        for j, length in enumerate(range(slots, 0, -2)):
            end = jnp.clip(at[tail + parents + j], low, high)
            lax.fori_loop(start, end, functools.partial(step, length, q), 0)
            start = end
        lax.fori_loop(start, high, functools.partial(step, 0, q), 0)
        return carry

    lax.fori_loop(0, QUARTERS, quarter, 0)


def early_kernel(count, parents, slots, *refs):
    sources = refs[:count]
    at_any, table8, sums, cells, at, sems = refs[count:]
    loads = load_lists(at_any, at, sems)
    expand(sources, cells)
    loads[0].wait()
    add_lists(parents, slots, at_any, at, sems, cells, table8, sums)


def late_kernel(count, tile_x, tile_y, slots, *refs):
    sources = refs[:count]
    (at_any, table8, early_ref, kept_ref, lower_ref, near_ref, recv_ref, down_hbm, out_hbm,
     cells, sums, lines, at, down_ref, total_ref, out_ref, list_sems, sems) = refs[count:]
    parents_x, parents_y = tile_x // 2, tile_y // 2
    parents = parents_x * parents_y
    lanes = table8.shape[1]
    loads = load_lists(at_any, at, list_sems)
    weights = pltpu.make_async_copy(down_hbm, down_ref, sems.at[0])
    weights.start()
    expand(sources, cells)
    loads[0].wait()
    add_lists(parents, slots, at_any, at, list_sems, cells, table8, sums)
    raw = (sums[...] + early_ref[...]).reshape(parents // 2, 2, 8, lanes)
    one, other = raw[:, 0], raw[:, 1]
    line = lax.broadcasted_iota(jnp.int32, one.shape, 1)
    with_real = jnp.where(line < 4, one, pltpu.roll(other, 4, axis=1))
    with_imag = jnp.where(line < 4, pltpu.roll(one, 4, axis=1), other)
    turned = jnp.where(line % 4 < 2, -pltpu.roll(with_imag, 6, axis=1), pltpu.roll(with_imag, 2, axis=1))
    lines[...] = (with_real + turned).reshape(4 * parents, lanes)
    ordered = [lines[pl.ds(place, parents, stride=4), :].astype(BF16) for place in range(4)]
    incoming = jnp.concatenate(ordered, axis=1)
    weights.wait()
    for child in range(4):
        down = mm(incoming, down_ref[child])
        for part in range(2):
            value = down[:, part * lanes : (part + 1) * lanes] + lower_ref[part, child]
            total_ref[child, :, part * lanes : (part + 1) * lanes] = value.astype(BF16)
    stores = []
    for half in range(2):
        first, size = half * parents // 2, parents // 2
        rows = slice(first, first + size)
        for child in range(4):
            field = mm(total_ref[child, rows, :], recv_ref[...])
            mask = kept_ref[child, rows, :]
            for part in range(2):
                value = (field[:, part * lanes : (part + 1) * lanes] + near_ref[part, child, rows, :]) * mask
                for p in range(parents_x // 2):
                    line = (2 * (half * parents_x // 2 + p) + child // 2) * tile_y + child % 2
                    out_ref[pl.ds(2 * line + part, parents_y, stride=4), :] = value[
                        p * parents_y : (p + 1) * parents_y
                    ]
        size = out_ref.shape[0] // 2
        rows = pl.ds(half * size, size)
        stores.append(pltpu.make_async_copy(out_ref.at[rows], out_hbm.at[rows], sems.at[1 + half]))
        stores[-1].start()
    for store in stores:
        store.wait()


def swap(low, high, axis, ends):
    count = lax.axis_size(axis)
    lows = [(i, i ^ 1) for i in range(count)]
    highs = [(i, (((i + 1) % count ^ 1) - 1) % count) for i in range(0 if ends else 1, count if ends else count - 1)]
    return lax.ppermute(low, axis, lows), lax.ppermute(high, axis, highs)


def body(
    currents, box_count, aggregate, near_blocks, low_translator, child_to_parent, coarse_list,
    coarse_kind, coarse_count, up_translator, parent_to_child, receive_map,
):
    tile_x, tile_y = box_count.shape
    boxes = tile_x * tile_y
    lanes = currents.shape[-1]
    parents_x, parents_y, slots = coarse_list.shape
    parents = parents_x * parents_y
    kinds, _, half = up_translator.shape
    wide = 2 * half
    chunks = lax.axis_size("gy")
    in_hbm = pl.BlockSpec(memory_space=pltpu.HBM)

    edge = jax.ShapeDtypeStruct((2 * tile_x, 2 * lanes), BF16)
    edge = jax.ShapeDtypeStruct((2 * tile_x, 2 * lanes), BF16)
    width = tile_y + 2 * LEFT
    live, kept, low, high, agg_near, up_near = pl.pallas_call(
        functools.partial(live_kernel, tile_x, tile_y),
        name="live",
        out_shape=[
            jax.ShapeDtypeStruct((boxes, 2 * lanes), BF16),
            jax.ShapeDtypeStruct((boxes, lanes), F32),
            edge,
            edge,
            jax.ShapeDtypeStruct((2 * lanes, 2 * lanes), BF16),
            jax.ShapeDtypeStruct((8 * lanes, wide), BF16),
        ],
        in_specs=[in_hbm] * 4,
        out_specs=vmem(6),
        scratch_shapes=[
            pltpu.VMEM((2 * boxes, lanes), BF16),
            pltpu.VMEM((tile_x, tile_y), jnp.int32),
            pltpu.VMEM((2 * boxes, lanes), F32),
            pltpu.SemaphoreType.DMA((4,)),
        ],
        compiler_params=params(10),
        cost_estimate=cost(100 * MIB, 3 * MIB),
    )(
        hbm(currents.reshape(2 * boxes, lanes)), hbm(box_count), hbm(aggregate),
        hbm(child_to_parent.reshape(8 * lanes, wide)),
    )
    coarse, pats = pl.pallas_call(
        functools.partial(parents_kernel, tile_x, tile_y),
        name="parents",
        out_shape=[
            jax.ShapeDtypeStruct((4 * parents, wide // 4), BF16),
            jax.ShapeDtypeStruct((3, tile_x * width, lanes), F32),
        ],
        in_specs=vmem(3),
        out_specs=vmem(2),
        scratch_shapes=[
            pltpu.VMEM((2, boxes, lanes), F32),
            pltpu.VMEM((4 * parents, wide // 4), F32),
        ],
        compiler_params=params(10),
        cost_estimate=cost(200 * MIB, 3 * MIB),
    )(live, agg_near, up_near)
    inner_y, outer_y = swap(low, high, "gy", True)
    sources = [coarse] + [
        lax.ppermute(coarse, "gy", [(i, i ^ d) for i in range(chunks)])
        for d in [chunks - 1] + list(range(1, chunks - 1))
    ]

    rim = 2 * tile_y + 8
    rim += -rim % 16
    low, high = pl.pallas_call(
        functools.partial(rims_kernel, tile_x, tile_y),
        name="rims",
        out_shape=[jax.ShapeDtypeStruct((rim, 2 * lanes), BF16)] * 2,
        in_specs=vmem(3),
        out_specs=vmem(2),
        scratch_shapes=[pltpu.VMEM((rim, 2 * lanes), F32)] * 2,
        compiler_params=params(10),
        cost_estimate=cost(1 * MIB, MIB),
    )(live, inner_y, outer_y)
    inner_x, outer_x = swap(low, high, "gx", False)
    live, coarse_count, _ = lax.optimization_barrier((live, coarse_count, low))

    near_rows = near_blocks.reshape(3, 6 * lanes, 2 * lanes)
    low_rows = low_translator.reshape(-1, lanes)
    pair = [jax.ShapeDtypeStruct((2, boxes, lanes), F32)] * 2
    lower, near = pl.pallas_call(
        functools.partial(local_kernel, tile_x, tile_y),
        name="local",
        out_shape=pair,
        in_specs=vmem(4),
        out_specs=vmem(2),
        scratch_shapes=[
            pltpu.VMEM((2, tile_x * width, lanes), F32),
            pltpu.VMEM(((tile_x + 2) * tile_y, 6 * lanes), BF16),
            pltpu.VMEM((3 * len(OFFSETS), 8, lanes), F32),
            pltpu.VMEM((3, tile_x, 8, lanes), F32),
        ],
        compiler_params=params(10),
        cost_estimate=cost(2000 * MIB, 5 * MIB),
    )(live, pats, near_rows, low_rows)

    pair = [jax.ShapeDtypeStruct((2, 4, parents, lanes), F32)] * 2
    lower, near, kept = pl.pallas_call(
        functools.partial(halos_kernel, tile_x, tile_y),
        name="halos",
        out_shape=pair + [jax.ShapeDtypeStruct((4, parents, lanes), F32)],
        in_specs=vmem(10),
        out_specs=vmem(3),
        scratch_shapes=[
            pltpu.VMEM((4, 4, tile_x + 16, lanes), F32),
            pltpu.VMEM((4, 4 * width, lanes), F32),
            pltpu.VMEM((tile_x, lanes), F32),
        ],
        compiler_params=params(10),
        cost_estimate=cost(100 * MIB, 5 * MIB),
    )(inner_y, outer_y, inner_x, outer_x, agg_near, near_rows, low_rows, lower, near, kept)

    table = up_translator.reshape(kinds, 2, 2, half // 2).transpose(0, 2, 1, 3).reshape(4 * kinds, half // 2)
    places = jax.ShapeDtypeStruct((2 * parents // ROW + 8, ROW * slots), jnp.int32)
    early_at, late_at, table8 = pl.pallas_call(
        functools.partial(order_kernel, chunks, kinds, parents_x, parents_y),
        name="order",
        out_shape=[places, places, jax.ShapeDtypeStruct((8 * kinds + 8, half // 2), F32)],
        in_specs=vmem(4),
        out_specs=vmem(3),
        scratch_shapes=[pltpu.VMEM((parents, 128), F32)],
        compiler_params=params(10),
        cost_estimate=cost(300 * MIB, MIB),
    )(coarse_list.reshape(parents, slots), coarse_kind.reshape(parents, slots), coarse_count, table)
    early_at, late_at = early_at.reshape(-1), late_at.reshape(-1)
    anywhere = pl.BlockSpec(memory_space=pl.ANY)
    early, late = sources[:2], sources[2:]
    early_sums = pl.pallas_call(
        functools.partial(early_kernel, len(early), parents, slots),
        name="early",
        out_shape=jax.ShapeDtypeStruct((8 * parents, wide // 4), F32),
        in_specs=vmem(len(early)) + [anywhere] + vmem(1),
        out_specs=pl.BlockSpec(memory_space=pltpu.VMEM),
        scratch_shapes=[
            pltpu.VMEM((len(early) * parents * 8, wide // 4), F32),
            pltpu.SMEM(early_at.shape, jnp.int32),
            pltpu.SemaphoreType.DMA((1 + QUARTERS,)),
        ],
        compiler_params=params(10),
        cost_estimate=cost(1000 * MIB, 4 * MIB),
    )(*early, early_at, table8)
    out = pl.pallas_call(
        functools.partial(late_kernel, len(late), tile_x, tile_y, slots),
        name="late",
        out_shape=jax.ShapeDtypeStruct((2 * boxes, lanes), F32),
        in_specs=vmem(len(late)) + [anywhere] + vmem(6) + [in_hbm],
        out_specs=in_hbm,
        scratch_shapes=[
            pltpu.VMEM((len(late) * parents * 8, wide // 4), F32),
            pltpu.VMEM((8 * parents, wide // 4), F32),
            pltpu.VMEM((4 * parents, wide // 4), F32),
            pltpu.SMEM(late_at.shape, jnp.int32),
            pltpu.VMEM((4, wide, 2 * lanes), BF16),
            pltpu.VMEM((4, parents, 2 * lanes), BF16),
            pltpu.VMEM((2 * boxes, lanes), F32),
            pltpu.SemaphoreType.DMA((1 + QUARTERS,)),
            pltpu.SemaphoreType.DMA((3,)),
        ],
        compiler_params=params(16 if chunks <= 4 else 40),
        cost_estimate=cost(2000 * MIB, 8 * MIB),
    )(*late, late_at, table8, early_sums, kept, lower, near, receive_map, hbm(parent_to_child))
    return out.reshape(tile_x, tile_y, 2, lanes)


def solution(mesh):
    tiles = P("gx", "gy")
    in_specs = (tiles, tiles, P(), P(), P(), P(), tiles, tiles, tiles, P(), P(), P())
    return jax.shard_map(body, mesh=mesh, in_specs=in_specs, out_specs=tiles, check_vma=False)
```

```python
import functools

import jax
import jax.numpy as jnp
from jax import lax
from jax.experimental import pallas as pl
from jax.experimental.pallas import tpu as pltpu
from jax.sharding import PartitionSpec as P

F32 = jnp.float32
BF16 = jnp.bfloat16
MIB = 1 << 20


def vmem(count):
    return [pl.BlockSpec(memory_space=pltpu.VMEM)] * count


def hbm(array):
    return pltpu.with_memory_space_constraint(array, pltpu.HBM)


def params(mib):
    return pltpu.CompilerParams(vmem_limit_bytes=mib * MIB)


def cost(macs, moved):
    return pl.CostEstimate(flops=2 * macs, bytes_accessed=moved, transcendentals=0)


def mm(left, right):
    return jnp.dot(left, right, preferred_element_type=F32)


def count_rows(counts_ref, tile_x, tile_y, lanes):
    eye = lax.broadcasted_iota(jnp.int32, (tile_y, tile_y), 0) == lax.broadcasted_iota(
        jnp.int32, (tile_y, tile_y), 1
    )
    counts = counts_ref[...].astype(F32)
    diag = [
        jnp.where(eye, jnp.broadcast_to(counts[i : i + 1], (tile_y, tile_y)), 0.0) for i in range(tile_x)
    ]
    return mm(jnp.concatenate(diag, axis=0).astype(BF16), jnp.ones((tile_y, lanes), BF16))


def halo_pair(inner_ref, outer_ref, axis):
    at = lax.axis_index(axis)
    odd = at % 2 == 1
    inner, outer = inner_ref[...].astype(F32), outer_ref[...].astype(F32)
    before, after = jnp.where(odd, inner, outer), jnp.where(odd, outer, inner)
    return jnp.where(at > 0, before, 0.0), jnp.where(at < lax.axis_size(axis) - 1, after, 0.0)


LEFT = 8


def live_kernel(tile_x, tile_y, cur_hbm, counts_hbm, agg_hbm, up_hbm,
                live_ref, kept_ref, low_ref, high_ref, agg_ref, up_ref, cur_ref, counts_ref, wide, sems):
    pairs = [(counts_hbm, counts_ref), (cur_hbm, cur_ref), (agg_hbm, agg_ref), (up_hbm, up_ref)]
    loads = [
        pltpu.make_async_copy(source, target, sems.at[k]) for k, (source, target) in enumerate(pairs)
    ]
    for load in loads:
        load.start()
    lanes = cur_ref.shape[1]
    boxes = tile_x * tile_y
    loads[0].wait()
    limits = count_rows(counts_ref, tile_x, tile_y, lanes)
    keep = lax.broadcasted_iota(jnp.int32, (boxes, lanes), 1).astype(F32) < limits
    kept_ref[...] = jnp.where(keep, 1.0, 0.0)
    odd = lax.axis_index("gy") % 2 == 1
    loads[1].wait()
    wide[...] = cur_ref[...].astype(F32)
    for part in range(2):
        cols = slice(part * lanes, (part + 1) * lanes)
        live_ref[:, cols] = jnp.where(keep, wide[pl.ds(part, boxes, stride=2), :], 0.0).astype(BF16)

        def edge(column):
            rows = wide[pl.ds(2 * column + part, tile_x, stride=2 * tile_y), :]
            return rows * kept_ref[pl.ds(column, tile_x, stride=tile_y), :]

        first = jnp.concatenate([edge(0), edge(1)], axis=0).astype(BF16)
        last = jnp.concatenate([edge(tile_y - 2), edge(tile_y - 1)], axis=0).astype(BF16)
        low_ref[:, cols] = jnp.where(odd, first, last)
        high_ref[:, cols] = jnp.where(odd, last, first)
    for load in loads[2:]:
        load.wait()


def rims_kernel(tile_x, tile_y, live_ref, inner_ref, outer_ref, low_ref, high_ref, first, last):
    odd = lax.axis_index("gx") % 2 == 1
    sides = halo_pair(inner_ref, outer_ref, "gy")
    for rim, start in ((first, 0), (last, tile_x - 2)):
        rim[0 : 2 * tile_y, :] = live_ref[start * tile_y : (start + 2) * tile_y, :].astype(F32)
        place = 2 * tile_y
        for side in sides:
            for column in range(2):
                at = column * tile_x + start
                rim[place : place + 2, :] = side[at : at + 2]
                place += 2
        rim[place:, :] = jnp.zeros((rim.shape[0] - place, rim.shape[1]), F32)
    low_ref[...] = jnp.where(odd, first[...], last[...]).astype(BF16)
    high_ref[...] = jnp.where(odd, last[...], first[...]).astype(BF16)


def parents_kernel(tile_x, tile_y, live_ref, agg_ref, up_ref, coarse_ref, pats_ref, pats, rows4):
    lanes = pats.shape[2]
    width = tile_y + 2 * LEFT
    pattern = mm(live_ref[...], agg_ref[...])
    pats[0] = pattern[:, :lanes]
    pats[1] = pattern[:, lanes:]
    children = []
    for side_x in range(2):
        for side_y in range(2):
            for part in range(2):
                rows = [
                    pats[part, pl.ds((2 * p + side_x) * tile_y + side_y, tile_y // 2, stride=2), :]
                    for p in range(tile_x // 2)
                ]
                children.append(jnp.concatenate(rows, axis=0).astype(BF16))
    coarse = mm(jnp.concatenate(children, axis=1), up_ref[...])
    for place in range(4):
        rows4[pl.ds(place, coarse.shape[0], stride=4), :] = coarse[:, place * 128 : (place + 1) * 128]
    coarse_ref[...] = rows4[...].astype(BF16)
    pattern = pattern.astype(BF16).astype(F32)
    values = [pattern[:, :lanes], pattern[:, lanes:], pattern[:, :lanes] + pattern[:, lanes:]]
    none = jnp.zeros((LEFT, lanes), F32)
    for i in range(tile_x):
        base = i * width
        for k in range(3):
            pats_ref[k, base : base + LEFT, :] = none
            pats_ref[k, base + LEFT : base + LEFT + tile_y, :] = values[k][i * tile_y : (i + 1) * tile_y]
            pats_ref[k, base + LEFT + tile_y : base + width, :] = none


OFFSETS = [(dx, dy) for dx in range(-2, 3) for dy in range(-2, 3) if max(abs(dx), abs(dy)) == 2]


def local_kernel(
    tile_x, tile_y, live_ref, pats, near_ref, low_ref, lower_ref, field_ref, cells, shifted, tables, sums,
):
    lanes = lower_ref.shape[2]
    width = tile_y + 2 * LEFT
    none = jnp.zeros((LEFT, lanes), F32)
    ends = jnp.zeros((tile_y, 6 * lanes), BF16)
    shifted[0:tile_y, :] = ends
    shifted[(tile_x + 1) * tile_y : (tile_x + 2) * tile_y, :] = ends
    shifted[tile_y : (tile_x + 1) * tile_y, 2 * lanes : 4 * lanes] = live_ref[...]
    for part in range(2):
        cols = slice(part * lanes, (part + 1) * lanes)
        for i in range(tile_x):
            base = i * width
            cells[part, base : base + LEFT, :] = none
            cells[part, base + LEFT : base + LEFT + tile_y, :] = live_ref[
                i * tile_y : (i + 1) * tile_y, cols
            ].astype(F32)
            cells[part, base + LEFT + tile_y : base + width, :] = none
            for shift in (-1, 1):
                place = (2 * (shift + 1) + part) * lanes
                shifted[(i + 1) * tile_y : (i + 2) * tile_y, place : place + lanes] = cells[
                    part, base + LEFT + shift : base + LEFT + shift + tile_y, :
                ].astype(BF16)
    for k in range(len(OFFSETS)):
        t_real, t_imag = low_ref[2 * k : 2 * k + 1, :], low_ref[2 * k + 1 : 2 * k + 2, :]
        for n, value in enumerate((t_imag - t_real, t_imag + t_real, t_real)):
            tables[3 * k + n] = jnp.broadcast_to(value, (8, lanes))

    passes = [
        [(dx, dy) for dx, dy in OFFSETS if dy == -2],
        [(dx, dy) for dx, dy in OFFSETS if dy == 2],
        [(dx, dy) for dx, dy in OFFSETS if abs(dy) < 2],
    ]
    blocks = tile_y // 8
    size = tile_x * tile_y // blocks

    def block(b, carry):
        total = None
        for shift in range(3):
            start = pl.multiple_of(b * size + shift * tile_y, tile_y)
            term = mm(shifted[pl.ds(start, size), :], near_ref[shift])
            total = term if total is None else total + term
        start = pl.multiple_of(b * size, size)
        field_ref[0, pl.ds(start, size), :] = total[:, :lanes]
        field_ref[1, pl.ds(start, size), :] = total[:, lanes:]
        shift_y = pl.multiple_of(b * 8, 8)
        for number, offsets in enumerate(passes):
            running = {}
            for row in range(tile_x):
                for dy in sorted({dy for _, dy in offsets}):
                    rows = pl.ds(shift_y + (row * width + LEFT + dy), 8)
                    source = [pats[k, rows, :] for k in range(3)]
                    for dx in range(-2, 3):
                        i = row - dx
                        if (dx, dy) not in offsets or not 0 <= i < tile_x:
                            continue
                        k = OFFSETS.index((dx, dy))
                        if i not in running:
                            running[i] = [None] * 3 if number == 0 else [sums[n, i] for n in range(3)]
                        running[i] = [
                            tables[3 * k + n] * source[n]
                            if running[i][n] is None
                            else running[i][n] + tables[3 * k + n] * source[n]
                            for n in range(3)
                        ]
                for i in sorted(running):
                    if i + 2 <= row or row == tile_x - 1:
                        value = running.pop(i)
                        if number < 2:
                            for n in range(3):
                                sums[n, i] = value[n]
                        else:
                            place = pl.ds(pl.multiple_of(shift_y + i * tile_y, 8), 8)
                            lower_ref[0, place, :] = value[2] - value[1]
                            lower_ref[1, place, :] = value[2] + value[0]
        return carry

    lax.fori_loop(0, blocks, block, 0)


def halos_kernel(
    tile_x, tile_y, inner_y, outer_y, inner_x, outer_x, agg_ref, near_ref, low_ref, lower_in, field_in, kept_in,
    lower_ref, field_ref, kept_ref, columns, rims, line_ref,
):
    lanes = lower_in.shape[2]
    width = tile_y + 2 * LEFT
    halo = halo_pair(inner_y, outer_y, "gy") + halo_pair(inner_x, outer_x, "gx")
    half_x, half_y = tile_x // 2, tile_y // 2
    for child in range(4):
        for p in range(half_x):
            rows = slice(p * half_y, (p + 1) * half_y)
            boxes = pl.ds((2 * p + child // 2) * tile_y + child % 2, half_y, stride=2)
            for part in range(2):
                lower_ref[part, child, rows, :] = lower_in[part, boxes, :]
                field_ref[part, child, rows, :] = field_in[part, boxes, :]
            kept_ref[child, rows, :] = kept_in[boxes, :]

    def add_column(ref, part, box, value):
        line_ref[...] = value
        for side_x in range(2):
            child, rows = 2 * side_x + box % 2, pl.ds(box // 2, half_x, stride=half_y)
            ref[part, child, rows, :] = ref[part, child, rows, :] + line_ref[pl.ds(side_x, half_x, stride=2), :]

    def add_row(ref, part, box, value):
        line_ref[...] = value
        for side_y in range(2):
            child, rows = 2 * (box % 2) + side_y, slice(box // 2 * half_y, (box // 2 + 1) * half_y)
            ref[part, child, rows, :] = ref[part, child, rows, :] + line_ref[pl.ds(side_y, half_y, stride=2), :]

    halo = jnp.concatenate(halo, axis=0)
    pattern = mm(halo.astype(BF16), agg_ref[...]).astype(BF16).astype(F32)
    values = [halo[:, :lanes], halo[:, lanes:], pattern[:, :lanes], pattern[:, lanes:]]
    two = jnp.zeros((8, lanes), F32)
    rim_size = inner_x.shape[0]
    for n, value in enumerate(values):
        for side in range(2):
            for c in range(2):
                at = (2 * side + c) * tile_x
                columns[n, 2 * side + c, 0:8, :] = two
                columns[n, 2 * side + c, 8 : 8 + tile_x, :] = value[at : at + tile_x]
                columns[n, 2 * side + c, 8 + tile_x : 16 + tile_x, :] = two
        for end in range(2):
            at = 4 * tile_x + end * rim_size
            corner = at + 2 * tile_y
            for row in range(2):
                base = (2 * end + row) * width + LEFT
                rims[n, base : base + tile_y, :] = value[at + row * tile_y : at + (row + 1) * tile_y]
                for side in range(2):
                    for c in range(2):
                        place = base + (tile_y + c if side else c - 2)
                        line = corner + 4 * side + 2 * c + row
                        rims[n, place : place + 1, :] = value[line : line + 1]

    def translate(terms):
        first = second = 0.0
        for dx, dy, real, imag in terms:
            k = OFFSETS.index((dx, dy))
            t_real, t_imag = low_ref[2 * k : 2 * k + 1, :], low_ref[2 * k + 1 : 2 * k + 2, :]
            first = first + (t_real * real - t_imag * imag)
            second = second + (t_real * imag + t_imag * real)
        return first, second

    def column(n, side, c, dx):
        return columns[n, 2 * side + c, 8 + dx : 8 + dx + tile_x, :]

    def rim(n, end, row, dy):
        base = (2 * end + row) * width + LEFT + dy
        return rims[n, base : base + tile_y, :]

    for side in range(2):
        for box in ((tile_y - 1, tile_y - 2) if side else (0, 1)):
            terms = []
            for c in range(2):
                dy = (tile_y + c if side else c - 2) - box
                for dx in range(-2, 3):
                    if (dx, dy) in OFFSETS:
                        terms.append((dx, dy, column(2, side, c, dx), column(3, side, c, dx)))
            for part, value in enumerate(translate(terms)):
                add_column(lower_ref, part, box, value)
        source = jnp.concatenate(
            [column(part, side, 1 - side, dx) for dx in range(-1, 2) for part in range(2)], axis=1
        ).astype(BF16)
        weights = [near_ref[dx, (4 * side) * lanes : (4 * side + 2) * lanes, :] for dx in range(3)]
        value = mm(source, jnp.concatenate(weights, axis=0))
        for part in range(2):
            add_column(field_ref, part, tile_y - 1 if side else 0, value[:, part * lanes : (part + 1) * lanes])
    for end in range(2):
        for box in ((tile_x - 1, tile_x - 2) if end else (0, 1)):
            terms = []
            for row in range(2):
                dx = (tile_x + row if end else row - 2) - box
                for dy in range(-2, 3):
                    if (dx, dy) in OFFSETS:
                        terms.append((dx, dy, rim(2, end, row, dy), rim(3, end, row, dy)))
            for part, value in enumerate(translate(terms)):
                add_row(lower_ref, part, box, value)
        source = jnp.concatenate(
            [rim(part, end, 1 - end, dy) for dy in range(-1, 2) for part in range(2)], axis=1
        ).astype(BF16)
        value = mm(source, near_ref[2 * end])
        for part in range(2):
            add_row(field_ref, part, tile_x - 1 if end else 0, value[:, part * lanes : (part + 1) * lanes])


GROUP = 16
SEGMENT = 8


def order_kernel(
    chunks, kinds, parents_x, parents_y, list_ref, kind_ref, count_ref, table_ref, early_ref, late_ref, table8, words
):
    width = table_ref.shape[1]
    for place, row in enumerate((0, 2, 0, 2, 1, 3, 1, 3)):
        table8[pl.ds(place, kinds, stride=8), :] = table_ref[pl.ds(row, kinds, stride=4), :]
    table8[8 * kinds : 8 * kinds + 8, :] = jnp.zeros((8, width), F32)
    parents = parents_x * parents_y
    slots = list_ref.shape[1]
    lanes = early_ref.shape[1]
    across = parents_y * chunks
    entry = list_ref[...]
    line, place = entry // across, entry % across
    chunk = (place // parents_y) ^ lax.axis_index("gy")
    is_late = (chunk > 0) & (chunk < chunks - 1)
    chunk = jnp.where(is_late, chunk - 1, jnp.where(chunk > 0, 1, 0))
    source = chunk * parents + line * parents_y + place % parents_y
    column = count_rows(count_ref, parents_x, parents_y, slots)
    used = lax.broadcasted_iota(jnp.int32, (parents, slots), 1).astype(F32) < column
    part = jnp.where(used, jnp.where(is_late, 2, 1), 0)
    words[:, 0:slots] = (source * 128 + kind_ref[...] + part * (1 << 20)).astype(F32)
    turned = words[...].T[0:slots].astype(jnp.int32)
    word, turned_part = turned & ((1 << 20) - 1), turned >> 20

    down = lax.broadcasted_iota(jnp.int32, (parents, parents), 0)
    along = lax.broadcasted_iota(jnp.int32, (parents, parents), 1)
    earlier = lax.broadcasted_iota(jnp.int32, (slots, slots), 1) < lax.broadcasted_iota(jnp.int32, (slots, slots), 0)
    earlier = jnp.where(earlier, 1.0, 0.0).astype(BF16)
    slot = lax.broadcasted_iota(jnp.int32, (slots, parents), 0)
    most = (2 * lax.broadcasted_iota(jnp.int32, (parents, lanes), 1)).astype(F32)
    for number, at_ref in ((1, early_ref), (2, late_ref)):
        hit = jnp.where(turned_part == number, 1.0, 0.0)
        mine = jnp.where(part == number, 1.0, 0.0).astype(BF16)
        column = mm(mine, jnp.ones((slots, parents), BF16))
        row = jnp.sum(hit, axis=0, keepdims=True)
        before = (column < row) | ((column == row) & (down < along))
        rank = jnp.sum(jnp.where(before, 1.0, 0.0), axis=0, keepdims=True)
        place = mm(earlier, hit.astype(BF16)).astype(jnp.int32)
        place = jnp.where(turned_part == number, place, -1)
        dense = jnp.zeros((slots, parents), jnp.int32)
        for n in range(slots):
            dense = dense + jnp.where(place[n : n + 1] == slot, word[n : n + 1], 0)
        kind = jnp.where(slot.astype(F32) < row, dense & 127, kinds)
        source = dense >> 7
        values = [source >> 8, source & 255, kind, along[0:slots]]
        values = jnp.concatenate([value.astype(F32) for value in values], axis=0).astype(BF16)
        ranked = jnp.where(down.astype(F32) == rank, 1.0, 0.0).astype(BF16)
        moved = lax.dot_general(values, ranked, (((1,), (1,)), ((), ())), preferred_element_type=F32)
        high, low, kind, parent = [
            moved[n * slots : (n + 1) * slots].astype(jnp.int32) * 8 for n in range(4)
        ]
        reach = jnp.sum(jnp.where(column[:, :lanes] <= most, 1.0, 0.0), axis=0, keepdims=True).astype(jnp.int32)
        head = jnp.broadcast_to(reach // GROUP, (8, lanes))
        line = lax.broadcasted_iota(jnp.int32, (8, lanes), 0)
        for n in range(parents // lanes):
            head = jnp.where(line == n, parent[0:8, n * lanes : (n + 1) * lanes], head)
        at_ref[0:8, :] = head
        at = 8
        for segment in range(0, slots, SEGMENT):
            for value in (high * 256 + low, kind):
                for n in range(parents // lanes):
                    at_ref[at : at + SEGMENT, :] = value[segment : segment + SEGMENT, n * lanes : (n + 1) * lanes]
                    at += SEGMENT


def expand(sources, cells):
    lanes = cells.shape[1]
    count = sources[0].shape[0] // 8
    pairs = cells.reshape(len(sources) * count, 2, 8, lanes)
    upper = lax.broadcasted_iota(jnp.int32, (count, 8, lanes), 1) < 4
    for c, source in enumerate(sources):
        rows = source[...].astype(F32).reshape(count, 8, lanes)
        turned = pltpu.roll(rows, 4, axis=1)
        pairs[c * count : (c + 1) * count, 0] = jnp.where(upper, rows, turned)
        pairs[c * count : (c + 1) * count, 1] = jnp.where(upper, turned, rows)


def load_lists(at_any, at, sems):
    first = 1024 + (at.shape[0] - 1024) // 2
    loads = []
    for n, (start, size) in enumerate([(0, first), (first, at.shape[0] - first)]):
        rows = pl.ds(start, size)
        loads.append(pltpu.make_async_copy(at_any.at[rows], at.at[rows], sems.at[n]))
        loads[-1].start()
    return loads


def add_lists(parents, slots, loads, at, cells, table8, sums):
    lanes = cells.shape[1]
    words = parents * SEGMENT
    per_half = 128 // GROUP

    def step(length, n, carry):
        first = 1024 + (n // per_half) * (128 * SEGMENT) + (n % per_half) * GROUP
        for k in range(GROUP):
            total = [None, None]
            for s in range(length):
                place = first + ((s // SEGMENT) * 2 * words + (s % SEGMENT) * 128 + k)
                source = pl.multiple_of(at[place], 8)
                kind = pl.multiple_of(at[place + words], 8)
                term = cells[pl.ds(source, 8), :] * table8[pl.ds(kind, 8), :]
                total[s % 2] = term if total[s % 2] is None else total[s % 2] + term
            total = total[0] + total[1] if length else jnp.zeros((8, lanes), F32)
            sums[pl.ds(pl.multiple_of(at[n * GROUP + k], 8), 8), :] = total
        return carry

    loads[0].wait()
    start = 0
    for j, length in enumerate(range(0, slots + 1, 2)):
        if length == SEGMENT + 2:
            loads[1].wait()
        end = at[parents + j]
        lax.fori_loop(start, end, functools.partial(step, length), 0)
        start = end


def early_kernel(count, parents, slots, *refs):
    sources = refs[:count]
    at_any, table8, sums, cells, at, sems = refs[count:]
    loads = load_lists(at_any, at, sems)
    expand(sources, cells)
    add_lists(parents, slots, loads, at, cells, table8, sums)


def late_kernel(count, tile_x, tile_y, slots, *refs):
    sources = refs[:count]
    (at_any, table8, early_ref, kept_ref, lower_ref, near_ref, recv_ref, down_hbm, out_hbm,
     cells, sums, lines, at, down_ref, total_ref, out_ref, list_sems, sems) = refs[count:]
    parents_x, parents_y = tile_x // 2, tile_y // 2
    parents = parents_x * parents_y
    lanes = table8.shape[1]
    loads = load_lists(at_any, at, list_sems)
    weights = pltpu.make_async_copy(down_hbm, down_ref, sems.at[0])
    weights.start()
    expand(sources, cells)
    add_lists(parents, slots, loads, at, cells, table8, sums)
    raw = (sums[...] + early_ref[...]).reshape(parents // 2, 2, 8, lanes)
    one, other = raw[:, 0], raw[:, 1]
    line = lax.broadcasted_iota(jnp.int32, one.shape, 1)
    with_real = jnp.where(line < 4, one, pltpu.roll(other, 4, axis=1))
    with_imag = jnp.where(line < 4, pltpu.roll(one, 4, axis=1), other)
    turned = jnp.where(line % 4 < 2, -pltpu.roll(with_imag, 6, axis=1), pltpu.roll(with_imag, 2, axis=1))
    lines[...] = (with_real + turned).reshape(4 * parents, lanes)
    ordered = [lines[pl.ds(place, parents, stride=4), :].astype(BF16) for place in range(4)]
    incoming = jnp.concatenate(ordered, axis=1)
    weights.wait()
    for child in range(4):
        down = mm(incoming, down_ref[child])
        for part in range(2):
            value = down[:, part * lanes : (part + 1) * lanes] + lower_ref[part, child]
            total_ref[child, :, part * lanes : (part + 1) * lanes] = value.astype(BF16)
    stores = []
    for half in range(2):
        first, size = half * parents // 2, parents // 2
        rows = slice(first, first + size)
        for child in range(4):
            field = mm(total_ref[child, rows, :], recv_ref[...])
            mask = kept_ref[child, rows, :]
            for part in range(2):
                value = (field[:, part * lanes : (part + 1) * lanes] + near_ref[part, child, rows, :]) * mask
                for p in range(parents_x // 2):
                    line = (2 * (half * parents_x // 2 + p) + child // 2) * tile_y + child % 2
                    out_ref[pl.ds(2 * line + part, parents_y, stride=4), :] = value[
                        p * parents_y : (p + 1) * parents_y
                    ]
        size = out_ref.shape[0] // 2
        rows = pl.ds(half * size, size)
        stores.append(pltpu.make_async_copy(out_ref.at[rows], out_hbm.at[rows], sems.at[1 + half]))
        stores[-1].start()
    for store in stores:
        store.wait()


def swap(low, high, axis, other=None):
    count = lax.axis_size(axis)
    lows = [(i, i ^ 1) for i in range(count)]
    highs = [(i, (((i + 1) % count ^ 1) - 1) % count) for i in range(count)]
    if other is not None:
        breadth = lax.axis_size(other)
        highs = [
            (i * breadth + j, i * breadth + (j ^ 1) if i in (0, count - 1) else target * breadth + j)
            for i, target in highs
            for j in range(breadth)
        ]
    return lax.ppermute(low, axis, lows), lax.ppermute(high, axis if other is None else (axis, other), highs)


def body(
    currents, box_count, aggregate, near_blocks, low_translator, child_to_parent, coarse_list,
    coarse_kind, coarse_count, up_translator, parent_to_child, receive_map,
):
    tile_x, tile_y = box_count.shape
    boxes = tile_x * tile_y
    lanes = currents.shape[-1]
    parents_x, parents_y, slots = coarse_list.shape
    parents = parents_x * parents_y
    kinds, _, half = up_translator.shape
    wide = 2 * half
    chunks = lax.axis_size("gy")
    in_hbm = pl.BlockSpec(memory_space=pltpu.HBM)

    edge = jax.ShapeDtypeStruct((2 * tile_x, 2 * lanes), BF16)
    edge = jax.ShapeDtypeStruct((2 * tile_x, 2 * lanes), BF16)
    width = tile_y + 2 * LEFT
    live, kept, low, high, agg_near, up_near = pl.pallas_call(
        functools.partial(live_kernel, tile_x, tile_y),
        name="live",
        out_shape=[
            jax.ShapeDtypeStruct((boxes, 2 * lanes), BF16),
            jax.ShapeDtypeStruct((boxes, lanes), F32),
            edge,
            edge,
            jax.ShapeDtypeStruct((2 * lanes, 2 * lanes), BF16),
            jax.ShapeDtypeStruct((8 * lanes, wide), BF16),
        ],
        in_specs=[in_hbm] * 4,
        out_specs=vmem(6),
        scratch_shapes=[
            pltpu.VMEM((2 * boxes, lanes), BF16),
            pltpu.VMEM((tile_x, tile_y), jnp.int32),
            pltpu.VMEM((2 * boxes, lanes), F32),
            pltpu.SemaphoreType.DMA((4,)),
        ],
        compiler_params=params(10),
        cost_estimate=cost(100 * MIB, 3 * MIB),
    )(
        hbm(currents.reshape(2 * boxes, lanes)), hbm(box_count), hbm(aggregate),
        hbm(child_to_parent.reshape(8 * lanes, wide)),
    )
    coarse, pats = pl.pallas_call(
        functools.partial(parents_kernel, tile_x, tile_y),
        name="parents",
        out_shape=[
            jax.ShapeDtypeStruct((4 * parents, wide // 4), BF16),
            jax.ShapeDtypeStruct((3, tile_x * width, lanes), F32),
        ],
        in_specs=vmem(3),
        out_specs=vmem(2),
        scratch_shapes=[
            pltpu.VMEM((2, boxes, lanes), F32),
            pltpu.VMEM((4 * parents, wide // 4), F32),
        ],
        compiler_params=params(10),
        cost_estimate=cost(200 * MIB, 3 * MIB),
    )(live, agg_near, up_near)
    inner_y, outer_y = swap(low, high, "gy")
    sources = [coarse] + [
        lax.ppermute(coarse, "gy", [(i, i ^ d) for i in range(chunks)])
        for d in [chunks - 1] + list(range(1, chunks - 1))
    ]

    rim = 2 * tile_y + 8
    rim += -rim % 16
    low, high = pl.pallas_call(
        functools.partial(rims_kernel, tile_x, tile_y),
        name="rims",
        out_shape=[jax.ShapeDtypeStruct((rim, 2 * lanes), BF16)] * 2,
        in_specs=vmem(3),
        out_specs=vmem(2),
        scratch_shapes=[pltpu.VMEM((rim, 2 * lanes), F32)] * 2,
        compiler_params=params(10),
        cost_estimate=cost(1 * MIB, MIB),
    )(live, inner_y, outer_y)
    inner_x, outer_x = swap(low, high, "gx", "gy")
    live, coarse_count, _ = lax.optimization_barrier((live, coarse_count, low))

    near_rows = near_blocks.reshape(3, 6 * lanes, 2 * lanes)
    low_rows = low_translator.reshape(-1, lanes)
    pair = [jax.ShapeDtypeStruct((2, boxes, lanes), F32)] * 2
    lower, near = pl.pallas_call(
        functools.partial(local_kernel, tile_x, tile_y),
        name="local",
        out_shape=pair,
        in_specs=vmem(4),
        out_specs=vmem(2),
        scratch_shapes=[
            pltpu.VMEM((2, tile_x * width, lanes), F32),
            pltpu.VMEM(((tile_x + 2) * tile_y, 6 * lanes), BF16),
            pltpu.VMEM((3 * len(OFFSETS), 8, lanes), F32),
            pltpu.VMEM((3, tile_x, 8, lanes), F32),
        ],
        compiler_params=params(10),
        cost_estimate=cost(2000 * MIB, 5 * MIB),
    )(live, pats, near_rows, low_rows)

    table = up_translator.reshape(kinds, 2, 2, half // 2).transpose(0, 2, 1, 3).reshape(4 * kinds, half // 2)
    places = jax.ShapeDtypeStruct((8 + 2 * slots * parents // 128, 128), jnp.int32)
    early_at, late_at, table8 = pl.pallas_call(
        functools.partial(order_kernel, chunks, kinds, parents_x, parents_y),
        name="order",
        out_shape=[places, places, jax.ShapeDtypeStruct((8 * kinds + 8, half // 2), F32)],
        in_specs=vmem(4),
        out_specs=vmem(3),
        scratch_shapes=[pltpu.VMEM((parents, 128), F32)],
        compiler_params=params(10),
        cost_estimate=cost(300 * MIB, MIB),
    )(coarse_list.reshape(parents, slots), coarse_kind.reshape(parents, slots), coarse_count, table)
    early_at, late_at = early_at.reshape(-1), late_at.reshape(-1)
    anywhere = pl.BlockSpec(memory_space=pl.ANY)
    early, late = sources[:2], sources[2:]
    early_sums = pl.pallas_call(
        functools.partial(early_kernel, len(early), parents, slots),
        name="early",
        out_shape=jax.ShapeDtypeStruct((8 * parents, wide // 4), F32),
        in_specs=vmem(len(early)) + [anywhere] + vmem(1),
        out_specs=pl.BlockSpec(memory_space=pltpu.VMEM),
        scratch_shapes=[
            pltpu.VMEM((len(early) * parents * 8, wide // 4), F32),
            pltpu.SMEM(early_at.shape, jnp.int32),
            pltpu.SemaphoreType.DMA((2,)),
        ],
        compiler_params=params(10),
        cost_estimate=cost(1000 * MIB, 4 * MIB),
    )(*early, early_at, table8)
    lower, near, _ = lax.optimization_barrier((lower, near, early_sums))
    pair = [jax.ShapeDtypeStruct((2, 4, parents, lanes), F32)] * 2
    lower, near, kept = pl.pallas_call(
        functools.partial(halos_kernel, tile_x, tile_y),
        name="halos",
        out_shape=pair + [jax.ShapeDtypeStruct((4, parents, lanes), F32)],
        in_specs=vmem(10),
        out_specs=vmem(3),
        scratch_shapes=[
            pltpu.VMEM((4, 4, tile_x + 16, lanes), F32),
            pltpu.VMEM((4, 4 * width, lanes), F32),
            pltpu.VMEM((tile_x, lanes), F32),
        ],
        compiler_params=params(10),
        cost_estimate=cost(100 * MIB, 5 * MIB),
    )(inner_y, outer_y, inner_x, outer_x, agg_near, near_rows, low_rows, lower, near, kept)

    out = pl.pallas_call(
        functools.partial(late_kernel, len(late), tile_x, tile_y, slots),
        name="late",
        out_shape=jax.ShapeDtypeStruct((2 * boxes, lanes), F32),
        in_specs=vmem(len(late)) + [anywhere] + vmem(6) + [in_hbm],
        out_specs=in_hbm,
        scratch_shapes=[
            pltpu.VMEM((len(late) * parents * 8, wide // 4), F32),
            pltpu.VMEM((8 * parents, wide // 4), F32),
            pltpu.VMEM((4 * parents, wide // 4), F32),
            pltpu.SMEM(late_at.shape, jnp.int32),
            pltpu.VMEM((4, wide, 2 * lanes), BF16),
            pltpu.VMEM((4, parents, 2 * lanes), BF16),
            pltpu.VMEM((2 * boxes, lanes), F32),
            pltpu.SemaphoreType.DMA((2,)),
            pltpu.SemaphoreType.DMA((3,)),
        ],
        compiler_params=params(16 if chunks <= 4 else 40),
        cost_estimate=cost(2000 * MIB, 8 * MIB),
    )(*late, late_at, table8, early_sums, kept, lower, near, receive_map, hbm(parent_to_child))
    return out.reshape(tile_x, tile_y, 2, lanes)


def solution(mesh):
    tiles = P("gx", "gy")
    in_specs = (tiles, tiles, P(), P(), P(), P(), tiles, tiles, tiles, P(), P(), P())
    return jax.shard_map(body, mesh=mesh, in_specs=in_specs, out_specs=tiles, check_vma=False)
```

```python
import functools

import jax
import jax.numpy as jnp
from jax import lax
from jax.experimental import pallas as pl
from jax.experimental.pallas import tpu as pltpu
from jax.sharding import PartitionSpec as P

F32 = jnp.float32
BF16 = jnp.bfloat16
MIB = 1 << 20


def vmem(count):
    return [pl.BlockSpec(memory_space=pltpu.VMEM)] * count


def hbm(array):
    return pltpu.with_memory_space_constraint(array, pltpu.HBM)


def params(mib):
    return pltpu.CompilerParams(vmem_limit_bytes=mib * MIB)


def cost(macs, moved):
    return pl.CostEstimate(flops=2 * macs, bytes_accessed=moved, transcendentals=0)


def mm(left, right):
    return jnp.dot(left, right, preferred_element_type=F32)


def count_rows(counts_ref, tile_x, tile_y, lanes):
    eye = lax.broadcasted_iota(jnp.int32, (tile_y, tile_y), 0) == lax.broadcasted_iota(
        jnp.int32, (tile_y, tile_y), 1
    )
    counts = counts_ref[...].astype(F32)
    diag = [
        jnp.where(eye, jnp.broadcast_to(counts[i : i + 1], (tile_y, tile_y)), 0.0) for i in range(tile_x)
    ]
    return mm(jnp.concatenate(diag, axis=0).astype(BF16), jnp.ones((tile_y, lanes), BF16))


def halo_pair(inner_ref, outer_ref, axis):
    at = lax.axis_index(axis)
    odd = at % 2 == 1
    inner, outer = inner_ref[...].astype(F32), outer_ref[...].astype(F32)
    before, after = jnp.where(odd, inner, outer), jnp.where(odd, outer, inner)
    return jnp.where(at > 0, before, 0.0), jnp.where(at < lax.axis_size(axis) - 1, after, 0.0)


LEFT = 8


def live_kernel(tile_x, tile_y, cur_hbm, counts_hbm, agg_hbm, up_hbm,
                live_ref, kept_ref, low_ref, high_ref, agg_ref, up_ref, cur_ref, counts_ref, wide, sems):
    pairs = [(counts_hbm, counts_ref), (cur_hbm, cur_ref), (agg_hbm, agg_ref), (up_hbm, up_ref)]
    loads = [
        pltpu.make_async_copy(source, target, sems.at[k]) for k, (source, target) in enumerate(pairs)
    ]
    for load in loads:
        load.start()
    lanes = cur_ref.shape[1]
    boxes = tile_x * tile_y
    loads[0].wait()
    limits = count_rows(counts_ref, tile_x, tile_y, lanes)
    keep = lax.broadcasted_iota(jnp.int32, (boxes, lanes), 1).astype(F32) < limits
    kept_ref[...] = jnp.where(keep, 1.0, 0.0)
    odd = lax.axis_index("gy") % 2 == 1
    loads[1].wait()
    wide[...] = cur_ref[...].astype(F32)
    for part in range(2):
        cols = slice(part * lanes, (part + 1) * lanes)
        live_ref[:, cols] = jnp.where(keep, wide[pl.ds(part, boxes, stride=2), :], 0.0).astype(BF16)

        def edge(column):
            rows = wide[pl.ds(2 * column + part, tile_x, stride=2 * tile_y), :]
            return rows * kept_ref[pl.ds(column, tile_x, stride=tile_y), :]

        first = jnp.concatenate([edge(0), edge(1)], axis=0).astype(BF16)
        last = jnp.concatenate([edge(tile_y - 2), edge(tile_y - 1)], axis=0).astype(BF16)
        low_ref[:, cols] = jnp.where(odd, first, last)
        high_ref[:, cols] = jnp.where(odd, last, first)
    for load in loads[2:]:
        load.wait()


def rims_kernel(tile_x, tile_y, live_ref, inner_ref, outer_ref, low_ref, high_ref, first, last):
    odd = lax.axis_index("gx") % 2 == 1
    sides = halo_pair(inner_ref, outer_ref, "gy")
    for rim, start in ((first, 0), (last, tile_x - 2)):
        rim[0 : 2 * tile_y, :] = live_ref[start * tile_y : (start + 2) * tile_y, :].astype(F32)
        place = 2 * tile_y
        for side in sides:
            for column in range(2):
                at = column * tile_x + start
                rim[place : place + 2, :] = side[at : at + 2]
                place += 2
        rim[place:, :] = jnp.zeros((rim.shape[0] - place, rim.shape[1]), F32)
    low_ref[...] = jnp.where(odd, first[...], last[...]).astype(BF16)
    high_ref[...] = jnp.where(odd, last[...], first[...]).astype(BF16)


def parents_kernel(tile_x, tile_y, live_ref, agg_ref, up_ref, coarse_ref, pats_ref, pats, rows4):
    lanes = pats.shape[2]
    width = tile_y + 2 * LEFT
    pattern = mm(live_ref[...], agg_ref[...])
    pats[0] = pattern[:, :lanes]
    pats[1] = pattern[:, lanes:]
    children = []
    for side_x in range(2):
        for side_y in range(2):
            for part in range(2):
                rows = [
                    pats[part, pl.ds((2 * p + side_x) * tile_y + side_y, tile_y // 2, stride=2), :]
                    for p in range(tile_x // 2)
                ]
                children.append(jnp.concatenate(rows, axis=0).astype(BF16))
    coarse = mm(jnp.concatenate(children, axis=1), up_ref[...])
    for place in range(4):
        rows4[pl.ds(place, coarse.shape[0], stride=4), :] = coarse[:, place * 128 : (place + 1) * 128]
    coarse_ref[...] = rows4[...].astype(BF16)
    pattern = pattern.astype(BF16).astype(F32)
    values = [pattern[:, :lanes], pattern[:, lanes:], pattern[:, :lanes] + pattern[:, lanes:]]
    none = jnp.zeros((LEFT, lanes), F32)
    for i in range(tile_x):
        base = i * width
        for k in range(3):
            pats_ref[k, base : base + LEFT, :] = none
            pats_ref[k, base + LEFT : base + LEFT + tile_y, :] = values[k][i * tile_y : (i + 1) * tile_y]
            pats_ref[k, base + LEFT + tile_y : base + width, :] = none


OFFSETS = [(dx, dy) for dx in range(-2, 3) for dy in range(-2, 3) if max(abs(dx), abs(dy)) == 2]


def local_kernel(
    tile_x, tile_y, live_ref, pats, near_ref, low_ref, lower_ref, field_ref, cells, shifted, tables, sums,
):
    lanes = lower_ref.shape[2]
    width = tile_y + 2 * LEFT
    none = jnp.zeros((LEFT, lanes), F32)
    ends = jnp.zeros((tile_y, 6 * lanes), BF16)
    shifted[0:tile_y, :] = ends
    shifted[(tile_x + 1) * tile_y : (tile_x + 2) * tile_y, :] = ends
    shifted[tile_y : (tile_x + 1) * tile_y, 2 * lanes : 4 * lanes] = live_ref[...]
    for part in range(2):
        cols = slice(part * lanes, (part + 1) * lanes)
        for i in range(tile_x):
            base = i * width
            cells[part, base : base + LEFT, :] = none
            cells[part, base + LEFT : base + LEFT + tile_y, :] = live_ref[
                i * tile_y : (i + 1) * tile_y, cols
            ].astype(F32)
            cells[part, base + LEFT + tile_y : base + width, :] = none
            for shift in (-1, 1):
                place = (2 * (shift + 1) + part) * lanes
                shifted[(i + 1) * tile_y : (i + 2) * tile_y, place : place + lanes] = cells[
                    part, base + LEFT + shift : base + LEFT + shift + tile_y, :
                ].astype(BF16)
    for k in range(len(OFFSETS)):
        t_real, t_imag = low_ref[2 * k : 2 * k + 1, :], low_ref[2 * k + 1 : 2 * k + 2, :]
        for n, value in enumerate((t_imag - t_real, t_imag + t_real, t_real)):
            tables[3 * k + n] = jnp.broadcast_to(value, (8, lanes))

    passes = [
        [(dx, dy) for dx, dy in OFFSETS if dy == -2],
        [(dx, dy) for dx, dy in OFFSETS if dy == 2],
        [(dx, dy) for dx, dy in OFFSETS if abs(dy) < 2],
    ]
    blocks = tile_y // 8
    size = tile_x * tile_y // blocks

    def block(b, carry):
        total = None
        for shift in range(3):
            start = pl.multiple_of(b * size + shift * tile_y, tile_y)
            term = mm(shifted[pl.ds(start, size), :], near_ref[shift])
            total = term if total is None else total + term
        start = pl.multiple_of(b * size, size)
        field_ref[0, pl.ds(start, size), :] = total[:, :lanes]
        field_ref[1, pl.ds(start, size), :] = total[:, lanes:]
        shift_y = pl.multiple_of(b * 8, 8)
        for number, offsets in enumerate(passes):
            running = {}
            for row in range(tile_x):
                for dy in sorted({dy for _, dy in offsets}):
                    rows = pl.ds(shift_y + (row * width + LEFT + dy), 8)
                    source = [pats[k, rows, :] for k in range(3)]
                    for dx in range(-2, 3):
                        i = row - dx
                        if (dx, dy) not in offsets or not 0 <= i < tile_x:
                            continue
                        k = OFFSETS.index((dx, dy))
                        if i not in running:
                            running[i] = [None] * 3 if number == 0 else [sums[n, i] for n in range(3)]
                        running[i] = [
                            tables[3 * k + n] * source[n]
                            if running[i][n] is None
                            else running[i][n] + tables[3 * k + n] * source[n]
                            for n in range(3)
                        ]
                for i in sorted(running):
                    if i + 2 <= row or row == tile_x - 1:
                        value = running.pop(i)
                        if number < 2:
                            for n in range(3):
                                sums[n, i] = value[n]
                        else:
                            place = pl.ds(pl.multiple_of(shift_y + i * tile_y, 8), 8)
                            lower_ref[0, place, :] = value[2] - value[1]
                            lower_ref[1, place, :] = value[2] + value[0]
        return carry

    lax.fori_loop(0, blocks, block, 0)


def halos_kernel(
    tile_x, tile_y, inner_y, outer_y, inner_x, outer_x, agg_ref, near_ref, low_ref, recv_ref,
    lower_in, field_in, kept_in, field_ref, kept_ref, columns, rims, line_ref, lower_ref,
):
    lanes = lower_in.shape[2]
    width = tile_y + 2 * LEFT
    halo = halo_pair(inner_y, outer_y, "gy") + halo_pair(inner_x, outer_x, "gx")
    half_x, half_y = tile_x // 2, tile_y // 2
    for child in range(4):
        for p in range(half_x):
            rows = slice(p * half_y, (p + 1) * half_y)
            boxes = pl.ds((2 * p + child // 2) * tile_y + child % 2, half_y, stride=2)
            for part in range(2):
                lower_ref[part, child, rows, :] = lower_in[part, boxes, :]
                field_ref[part, child, rows, :] = field_in[part, boxes, :]
            kept_ref[child, rows, :] = kept_in[boxes, :]

    def add_column(ref, part, box, value):
        line_ref[...] = value
        for side_x in range(2):
            child, rows = 2 * side_x + box % 2, pl.ds(box // 2, half_x, stride=half_y)
            ref[part, child, rows, :] = ref[part, child, rows, :] + line_ref[pl.ds(side_x, half_x, stride=2), :]

    def add_row(ref, part, box, value):
        line_ref[...] = value
        for side_y in range(2):
            child, rows = 2 * (box % 2) + side_y, slice(box // 2 * half_y, (box // 2 + 1) * half_y)
            ref[part, child, rows, :] = ref[part, child, rows, :] + line_ref[pl.ds(side_y, half_y, stride=2), :]

    halo = jnp.concatenate(halo, axis=0)
    pattern = mm(halo.astype(BF16), agg_ref[...]).astype(BF16).astype(F32)
    values = [halo[:, :lanes], halo[:, lanes:], pattern[:, :lanes], pattern[:, lanes:]]
    two = jnp.zeros((8, lanes), F32)
    rim_size = inner_x.shape[0]
    for n, value in enumerate(values):
        for side in range(2):
            for c in range(2):
                at = (2 * side + c) * tile_x
                columns[n, 2 * side + c, 0:8, :] = two
                columns[n, 2 * side + c, 8 : 8 + tile_x, :] = value[at : at + tile_x]
                columns[n, 2 * side + c, 8 + tile_x : 16 + tile_x, :] = two
        for end in range(2):
            at = 4 * tile_x + end * rim_size
            corner = at + 2 * tile_y
            for row in range(2):
                base = (2 * end + row) * width + LEFT
                rims[n, base : base + tile_y, :] = value[at + row * tile_y : at + (row + 1) * tile_y]
                for side in range(2):
                    for c in range(2):
                        place = base + (tile_y + c if side else c - 2)
                        line = corner + 4 * side + 2 * c + row
                        rims[n, place : place + 1, :] = value[line : line + 1]

    def translate(terms):
        first = second = 0.0
        for dx, dy, real, imag in terms:
            k = OFFSETS.index((dx, dy))
            t_real, t_imag = low_ref[2 * k : 2 * k + 1, :], low_ref[2 * k + 1 : 2 * k + 2, :]
            first = first + (t_real * real - t_imag * imag)
            second = second + (t_real * imag + t_imag * real)
        return first, second

    def column(n, side, c, dx):
        return columns[n, 2 * side + c, 8 + dx : 8 + dx + tile_x, :]

    def rim(n, end, row, dy):
        base = (2 * end + row) * width + LEFT + dy
        return rims[n, base : base + tile_y, :]

    for side in range(2):
        for box in ((tile_y - 1, tile_y - 2) if side else (0, 1)):
            terms = []
            for c in range(2):
                dy = (tile_y + c if side else c - 2) - box
                for dx in range(-2, 3):
                    if (dx, dy) in OFFSETS:
                        terms.append((dx, dy, column(2, side, c, dx), column(3, side, c, dx)))
            for part, value in enumerate(translate(terms)):
                add_column(lower_ref, part, box, value)
        source = jnp.concatenate(
            [column(part, side, 1 - side, dx) for dx in range(-1, 2) for part in range(2)], axis=1
        ).astype(BF16)
        weights = [near_ref[dx, (4 * side) * lanes : (4 * side + 2) * lanes, :] for dx in range(3)]
        value = mm(source, jnp.concatenate(weights, axis=0))
        for part in range(2):
            add_column(field_ref, part, tile_y - 1 if side else 0, value[:, part * lanes : (part + 1) * lanes])
    for end in range(2):
        for box in ((tile_x - 1, tile_x - 2) if end else (0, 1)):
            terms = []
            for row in range(2):
                dx = (tile_x + row if end else row - 2) - box
                for dy in range(-2, 3):
                    if (dx, dy) in OFFSETS:
                        terms.append((dx, dy, rim(2, end, row, dy), rim(3, end, row, dy)))
            for part, value in enumerate(translate(terms)):
                add_row(lower_ref, part, box, value)
        source = jnp.concatenate(
            [rim(part, end, 1 - end, dy) for dy in range(-1, 2) for part in range(2)], axis=1
        ).astype(BF16)
        value = mm(source, near_ref[2 * end])
        for part in range(2):
            add_row(field_ref, part, tile_x - 1 if end else 0, value[:, part * lanes : (part + 1) * lanes])
    for child in range(4):
        total = jnp.concatenate([lower_ref[part, child] for part in range(2)], axis=1).astype(BF16)
        value = mm(total, recv_ref[...])
        for part in range(2):
            field_ref[part, child] = field_ref[part, child] + value[:, part * lanes : (part + 1) * lanes]


GROUP = 16
SEGMENT = 8


def order_kernel(
    chunks, kinds, parents_x, parents_y, list_ref, kind_ref, count_ref, table_ref, down_ref, recv_ref,
    early_ref, late_ref, table8, fold_ref, words
):
    for child in range(4):
        fold_ref[child] = mm(down_ref[child], recv_ref[...]).astype(BF16)
    width = table_ref.shape[1]
    for place, row in enumerate((0, 2, 0, 2, 1, 3, 1, 3)):
        table8[pl.ds(place, kinds, stride=8), :] = table_ref[pl.ds(row, kinds, stride=4), :]
    table8[8 * kinds : 8 * kinds + 8, :] = jnp.zeros((8, width), F32)
    parents = parents_x * parents_y
    slots = list_ref.shape[1]
    lanes = early_ref.shape[1]
    across = parents_y * chunks
    entry = list_ref[...]
    line, place = entry // across, entry % across
    chunk = (place // parents_y) ^ lax.axis_index("gy")
    is_late = (chunk > 0) & (chunk < chunks - 1)
    chunk = jnp.where(is_late, chunk - 1, jnp.where(chunk > 0, 1, 0))
    source = chunk * parents + line * parents_y + place % parents_y
    column = count_rows(count_ref, parents_x, parents_y, slots)
    used = lax.broadcasted_iota(jnp.int32, (parents, slots), 1).astype(F32) < column
    part = jnp.where(used, jnp.where(is_late, 2, 1), 0)
    words[:, 0:slots] = (source * 128 + kind_ref[...] + part * (1 << 20)).astype(F32)
    turned = words[...].T[0:slots].astype(jnp.int32)
    word, turned_part = turned & ((1 << 20) - 1), turned >> 20

    down = lax.broadcasted_iota(jnp.int32, (parents, parents), 0)
    along = lax.broadcasted_iota(jnp.int32, (parents, parents), 1)
    earlier = lax.broadcasted_iota(jnp.int32, (slots, slots), 1) < lax.broadcasted_iota(jnp.int32, (slots, slots), 0)
    earlier = jnp.where(earlier, 1.0, 0.0).astype(BF16)
    slot = lax.broadcasted_iota(jnp.int32, (slots, parents), 0)
    most = (2 * lax.broadcasted_iota(jnp.int32, (parents, lanes), 1)).astype(F32)
    for number, at_ref in ((1, early_ref), (2, late_ref)):
        hit = jnp.where(turned_part == number, 1.0, 0.0)
        mine = jnp.where(part == number, 1.0, 0.0).astype(BF16)
        column = mm(mine, jnp.ones((slots, parents), BF16))
        row = jnp.sum(hit, axis=0, keepdims=True)
        before = (column < row) | ((column == row) & (down < along))
        rank = jnp.sum(jnp.where(before, 1.0, 0.0), axis=0, keepdims=True)
        place = mm(earlier, hit.astype(BF16)).astype(jnp.int32)
        place = jnp.where(turned_part == number, place, -1)
        dense = jnp.zeros((slots, parents), jnp.int32)
        for n in range(slots):
            dense = dense + jnp.where(place[n : n + 1] == slot, word[n : n + 1], 0)
        kind = jnp.where(slot.astype(F32) < row, dense & 127, kinds)
        source = dense >> 7
        values = [source >> 8, source & 255, kind, along[0:slots]]
        values = jnp.concatenate([value.astype(F32) for value in values], axis=0).astype(BF16)
        ranked = jnp.where(down.astype(F32) == rank, 1.0, 0.0).astype(BF16)
        moved = lax.dot_general(values, ranked, (((1,), (1,)), ((), ())), preferred_element_type=F32)
        high, low, kind, parent = [
            moved[n * slots : (n + 1) * slots].astype(jnp.int32) * 8 for n in range(4)
        ]
        reach = jnp.sum(jnp.where(column[:, :lanes] <= most, 1.0, 0.0), axis=0, keepdims=True).astype(jnp.int32)
        head = jnp.broadcast_to(reach // GROUP, (8, lanes))
        line = lax.broadcasted_iota(jnp.int32, (8, lanes), 0)
        for n in range(parents // lanes):
            head = jnp.where(line == n, parent[0:8, n * lanes : (n + 1) * lanes], head)
        at_ref[0:8, :] = head
        at = 8
        for segment in range(0, slots, SEGMENT):
            for n in range(parents // lanes):
                for value in (high * 256 + low, kind):
                    at_ref[at : at + SEGMENT, :] = value[segment : segment + SEGMENT, n * lanes : (n + 1) * lanes]
                    at += SEGMENT


def expand(sources, cells):
    lanes = cells.shape[1]
    count = sources[0].shape[0] // 8
    pairs = cells.reshape(len(sources) * count, 2, 8, lanes)
    upper = lax.broadcasted_iota(jnp.int32, (count, 8, lanes), 1) < 4
    for c, source in enumerate(sources):
        rows = source[...].astype(F32).reshape(count, 8, lanes)
        turned = pltpu.roll(rows, 4, axis=1)
        pairs[c * count : (c + 1) * count, 0] = jnp.where(upper, rows, turned)
        pairs[c * count : (c + 1) * count, 1] = jnp.where(upper, turned, rows)


def load_lists(at_any, at, sems):
    block = 2 * 128 * SEGMENT
    half = 1024 + (at.shape[0] - 1024) // 2
    loads = []
    for n, (start, end) in enumerate([(0, 1024 + block), (1024 + block, half), (half, at.shape[0])]):
        rows = pl.ds(start, end - start)
        loads.append(pltpu.make_async_copy(at_any.at[rows], at.at[rows], sems.at[n]))
        loads[-1].start()
    return loads


def add_lists(parents, slots, loads, at, cells, table8, sums):
    lanes = cells.shape[1]
    words = 128 * SEGMENT
    per_block = 128 // GROUP

    def step(length, n, carry):
        @pl.when(n == per_block)
        def _():
            loads[1].wait()

        first = 1024 + (n // per_block) * (2 * words) + (n % per_block) * GROUP
        for k in range(GROUP):
            total = [None, None]
            for s in range(length):
                place = first + ((s // SEGMENT) * 2 * parents * SEGMENT + (s % SEGMENT) * 128 + k)
                source = pl.multiple_of(at[place], 8)
                kind = pl.multiple_of(at[place + words], 8)
                term = cells[pl.ds(source, 8), :] * table8[pl.ds(kind, 8), :]
                total[s % 2] = term if total[s % 2] is None else total[s % 2] + term
            total = total[0] + total[1] if length else jnp.zeros((8, lanes), F32)
            sums[pl.ds(pl.multiple_of(at[n * GROUP + k], 8), 8), :] = total
        return carry

    loads[0].wait()
    start = 0
    for j, length in enumerate(range(0, slots + 1, 2)):
        if length == SEGMENT + 2:
            loads[2].wait()
        end = at[parents + j]
        lax.fori_loop(start, end, functools.partial(step, length), 0)
        start = end


def early_kernel(count, parents, slots, *refs):
    sources = refs[:count]
    at_any, table8, sums, cells, at, sems = refs[count:]
    loads = load_lists(at_any, at, sems)
    expand(sources, cells)
    add_lists(parents, slots, loads, at, cells, table8, sums)


def late_kernel(count, tile_x, tile_y, slots, *refs):
    sources = refs[:count]
    (at_any, table8, early_ref, kept_ref, field_ref, fold_ref, out_hbm,
     cells, sums, lines, at, out_ref, list_sems, sems) = refs[count:]
    parents_x, parents_y = tile_x // 2, tile_y // 2
    parents = parents_x * parents_y
    lanes = table8.shape[1]
    loads = load_lists(at_any, at, list_sems)
    expand(sources, cells)
    add_lists(parents, slots, loads, at, cells, table8, sums)
    raw = (sums[...] + early_ref[...]).reshape(parents // 2, 2, 8, lanes)
    one, other = raw[:, 0], raw[:, 1]
    line = lax.broadcasted_iota(jnp.int32, one.shape, 1)
    with_real = jnp.where(line < 4, one, pltpu.roll(other, 4, axis=1))
    with_imag = jnp.where(line < 4, pltpu.roll(one, 4, axis=1), other)
    turned = jnp.where(line % 4 < 2, -pltpu.roll(with_imag, 6, axis=1), pltpu.roll(with_imag, 2, axis=1))
    lines[...] = (with_real + turned).reshape(4 * parents, lanes)
    ordered = [lines[pl.ds(place, parents, stride=4), :].astype(BF16) for place in range(4)]
    incoming = jnp.concatenate(ordered, axis=1)
    fields = [mm(incoming, fold_ref[child]) for child in range(4)]
    stores = []
    for half in range(2):
        first, size = half * parents // 2, parents // 2
        rows = slice(first, first + size)
        for child in range(4):
            mask = kept_ref[child, rows, :]
            for part in range(2):
                value = fields[child][rows, part * lanes : (part + 1) * lanes]
                value = (value + field_ref[part, child, rows, :]) * mask
                for p in range(parents_x // 2):
                    line = (2 * (half * parents_x // 2 + p) + child // 2) * tile_y + child % 2
                    out_ref[pl.ds(2 * line + part, parents_y, stride=4), :] = value[
                        p * parents_y : (p + 1) * parents_y
                    ]
        size = out_ref.shape[0] // 2
        rows = pl.ds(half * size, size)
        stores.append(pltpu.make_async_copy(out_ref.at[rows], out_hbm.at[rows], sems.at[half]))
        stores[-1].start()
    for store in stores:
        store.wait()


def swap(low, high, axis, other=None):
    count = lax.axis_size(axis)
    lows = [(i, i ^ 1) for i in range(count)]
    highs = [(i, (((i + 1) % count ^ 1) - 1) % count) for i in range(count)]
    if other is not None:
        breadth = lax.axis_size(other)
        highs = [
            (i * breadth + j, i * breadth + (j ^ 1) if i in (0, count - 1) else target * breadth + j)
            for i, target in highs
            for j in range(breadth)
        ]
    return lax.ppermute(low, axis, lows), lax.ppermute(high, axis if other is None else (axis, other), highs)


def body(
    currents, box_count, aggregate, near_blocks, low_translator, child_to_parent, coarse_list,
    coarse_kind, coarse_count, up_translator, parent_to_child, receive_map,
):
    tile_x, tile_y = box_count.shape
    boxes = tile_x * tile_y
    lanes = currents.shape[-1]
    parents_x, parents_y, slots = coarse_list.shape
    parents = parents_x * parents_y
    kinds, _, half = up_translator.shape
    wide = 2 * half
    chunks = lax.axis_size("gy")
    in_hbm = pl.BlockSpec(memory_space=pltpu.HBM)

    edge = jax.ShapeDtypeStruct((2 * tile_x, 2 * lanes), BF16)
    edge = jax.ShapeDtypeStruct((2 * tile_x, 2 * lanes), BF16)
    width = tile_y + 2 * LEFT
    live, kept, low, high, agg_near, up_near = pl.pallas_call(
        functools.partial(live_kernel, tile_x, tile_y),
        name="live",
        out_shape=[
            jax.ShapeDtypeStruct((boxes, 2 * lanes), BF16),
            jax.ShapeDtypeStruct((boxes, lanes), F32),
            edge,
            edge,
            jax.ShapeDtypeStruct((2 * lanes, 2 * lanes), BF16),
            jax.ShapeDtypeStruct((8 * lanes, wide), BF16),
        ],
        in_specs=[in_hbm] * 4,
        out_specs=vmem(6),
        scratch_shapes=[
            pltpu.VMEM((2 * boxes, lanes), BF16),
            pltpu.VMEM((tile_x, tile_y), jnp.int32),
            pltpu.VMEM((2 * boxes, lanes), F32),
            pltpu.SemaphoreType.DMA((4,)),
        ],
        compiler_params=params(10),
        cost_estimate=cost(100 * MIB, 3 * MIB),
    )(
        hbm(currents.reshape(2 * boxes, lanes)), hbm(box_count), hbm(aggregate),
        hbm(child_to_parent.reshape(8 * lanes, wide)),
    )
    coarse, pats = pl.pallas_call(
        functools.partial(parents_kernel, tile_x, tile_y),
        name="parents",
        out_shape=[
            jax.ShapeDtypeStruct((4 * parents, wide // 4), BF16),
            jax.ShapeDtypeStruct((3, tile_x * width, lanes), F32),
        ],
        in_specs=vmem(3),
        out_specs=vmem(2),
        scratch_shapes=[
            pltpu.VMEM((2, boxes, lanes), F32),
            pltpu.VMEM((4 * parents, wide // 4), F32),
        ],
        compiler_params=params(10),
        cost_estimate=cost(200 * MIB, 3 * MIB),
    )(live, agg_near, up_near)
    inner_y, outer_y = swap(low, high, "gy")
    sources = [coarse] + [
        lax.ppermute(coarse, "gy", [(i, i ^ d) for i in range(chunks)])
        for d in [chunks - 1] + list(range(1, chunks - 1))
    ]

    rim = 2 * tile_y + 8
    rim += -rim % 16
    low, high = pl.pallas_call(
        functools.partial(rims_kernel, tile_x, tile_y),
        name="rims",
        out_shape=[jax.ShapeDtypeStruct((rim, 2 * lanes), BF16)] * 2,
        in_specs=vmem(3),
        out_specs=vmem(2),
        scratch_shapes=[pltpu.VMEM((rim, 2 * lanes), F32)] * 2,
        compiler_params=params(10),
        cost_estimate=cost(1 * MIB, MIB),
    )(live, inner_y, outer_y)
    inner_x, outer_x = swap(low, high, "gx", "gy")
    live, coarse_count, _ = lax.optimization_barrier((live, coarse_count, low))

    near_rows = near_blocks.reshape(3, 6 * lanes, 2 * lanes)
    low_rows = low_translator.reshape(-1, lanes)
    pair = [jax.ShapeDtypeStruct((2, boxes, lanes), F32)] * 2
    lower, near = pl.pallas_call(
        functools.partial(local_kernel, tile_x, tile_y),
        name="local",
        out_shape=pair,
        in_specs=vmem(4),
        out_specs=vmem(2),
        scratch_shapes=[
            pltpu.VMEM((2, tile_x * width, lanes), F32),
            pltpu.VMEM(((tile_x + 2) * tile_y, 6 * lanes), BF16),
            pltpu.VMEM((3 * len(OFFSETS), 8, lanes), F32),
            pltpu.VMEM((3, tile_x, 8, lanes), F32),
        ],
        compiler_params=params(10),
        cost_estimate=cost(2000 * MIB, 5 * MIB),
    )(live, pats, near_rows, low_rows)

    table = up_translator.reshape(kinds, 2, 2, half // 2).transpose(0, 2, 1, 3).reshape(4 * kinds, half // 2)
    places = jax.ShapeDtypeStruct((8 + 2 * slots * parents // 128, 128), jnp.int32)
    early_at, late_at, table8, fold = pl.pallas_call(
        functools.partial(order_kernel, chunks, kinds, parents_x, parents_y),
        name="order",
        out_shape=[
            places,
            places,
            jax.ShapeDtypeStruct((8 * kinds + 8, half // 2), F32),
            jax.ShapeDtypeStruct((4, wide, 2 * lanes), BF16),
        ],
        in_specs=vmem(6),
        out_specs=vmem(4),
        scratch_shapes=[pltpu.VMEM((parents, 128), F32)],
        compiler_params=params(10),
        cost_estimate=cost(300 * MIB, MIB),
    )(
        coarse_list.reshape(parents, slots), coarse_kind.reshape(parents, slots), coarse_count, table,
        parent_to_child, receive_map,
    )
    early_at, late_at = early_at.reshape(-1), late_at.reshape(-1)
    anywhere = pl.BlockSpec(memory_space=pl.ANY)
    early, late = sources[:2], sources[2:]
    early_sums = pl.pallas_call(
        functools.partial(early_kernel, len(early), parents, slots),
        name="early",
        out_shape=jax.ShapeDtypeStruct((8 * parents, wide // 4), F32),
        in_specs=vmem(len(early)) + [anywhere] + vmem(1),
        out_specs=pl.BlockSpec(memory_space=pltpu.VMEM),
        scratch_shapes=[
            pltpu.VMEM((len(early) * parents * 8, wide // 4), F32),
            pltpu.SMEM(early_at.shape, jnp.int32),
            pltpu.SemaphoreType.DMA((3,)),
        ],
        compiler_params=params(10),
        cost_estimate=cost(1000 * MIB, 4 * MIB),
    )(*early, early_at, table8)
    lower, near, _ = lax.optimization_barrier((lower, near, early_sums))
    field, kept = pl.pallas_call(
        functools.partial(halos_kernel, tile_x, tile_y),
        name="halos",
        out_shape=[
            jax.ShapeDtypeStruct((2, 4, parents, lanes), F32),
            jax.ShapeDtypeStruct((4, parents, lanes), F32),
        ],
        in_specs=vmem(11),
        out_specs=vmem(2),
        scratch_shapes=[
            pltpu.VMEM((4, 4, tile_x + 16, lanes), F32),
            pltpu.VMEM((4, 4 * width, lanes), F32),
            pltpu.VMEM((tile_x, lanes), F32),
            pltpu.VMEM((2, 4, parents, lanes), F32),
        ],
        compiler_params=params(10),
        cost_estimate=cost(100 * MIB, 5 * MIB),
    )(inner_y, outer_y, inner_x, outer_x, agg_near, near_rows, low_rows, receive_map, lower, near, kept)

    out = pl.pallas_call(
        functools.partial(late_kernel, len(late), tile_x, tile_y, slots),
        name="late",
        out_shape=jax.ShapeDtypeStruct((2 * boxes, lanes), F32),
        in_specs=vmem(len(late)) + [anywhere] + vmem(5),
        out_specs=in_hbm,
        scratch_shapes=[
            pltpu.VMEM((len(late) * parents * 8, wide // 4), F32),
            pltpu.VMEM((8 * parents, wide // 4), F32),
            pltpu.VMEM((4 * parents, wide // 4), F32),
            pltpu.SMEM(late_at.shape, jnp.int32),
            pltpu.VMEM((2 * boxes, lanes), F32),
            pltpu.SemaphoreType.DMA((3,)),
            pltpu.SemaphoreType.DMA((2,)),
        ],
        compiler_params=params(16 if chunks <= 4 else 40),
        cost_estimate=cost(2000 * MIB, 8 * MIB),
    )(*late, late_at, table8, early_sums, kept, field, fold)
    return out.reshape(tile_x, tile_y, 2, lanes)


def solution(mesh):
    tiles = P("gx", "gy")
    in_specs = (tiles, tiles, P(), P(), P(), P(), tiles, tiles, tiles, P(), P(), P())
    return jax.shard_map(body, mesh=mesh, in_specs=in_specs, out_specs=tiles, check_vma=False)
```

```python
import functools

import jax
import jax.numpy as jnp
from jax import lax
from jax.experimental import pallas as pl
from jax.experimental.pallas import tpu as pltpu
from jax.sharding import PartitionSpec as P

F32 = jnp.float32
BF16 = jnp.bfloat16
MIB = 1 << 20


def vmem(count):
    return [pl.BlockSpec(memory_space=pltpu.VMEM)] * count


def hbm(array):
    return pltpu.with_memory_space_constraint(array, pltpu.HBM)


def params(mib):
    return pltpu.CompilerParams(vmem_limit_bytes=mib * MIB)


def cost(macs, moved):
    return pl.CostEstimate(flops=2 * macs, bytes_accessed=moved, transcendentals=0)


def mm(left, right):
    return jnp.dot(left, right, preferred_element_type=F32)


def count_rows(counts_ref, tile_x, tile_y, lanes):
    eye = lax.broadcasted_iota(jnp.int32, (tile_y, tile_y), 0) == lax.broadcasted_iota(
        jnp.int32, (tile_y, tile_y), 1
    )
    counts = counts_ref[...].astype(F32)
    diag = [
        jnp.where(eye, jnp.broadcast_to(counts[i : i + 1], (tile_y, tile_y)), 0.0) for i in range(tile_x)
    ]
    return mm(jnp.concatenate(diag, axis=0).astype(BF16), jnp.ones((tile_y, lanes), BF16))


def halo_pair(inner_ref, outer_ref, axis):
    at = lax.axis_index(axis)
    odd = at % 2 == 1
    inner, outer = inner_ref[...].astype(F32), outer_ref[...].astype(F32)
    before, after = jnp.where(odd, inner, outer), jnp.where(odd, outer, inner)
    return jnp.where(at > 0, before, 0.0), jnp.where(at < lax.axis_size(axis) - 1, after, 0.0)


LEFT = 8


def live_kernel(tile_x, tile_y, cur_hbm, counts_hbm, agg_hbm, up_hbm,
                live_ref, kept_ref, low_ref, high_ref, agg_ref, up_ref, cur_ref, counts_ref, wide, sems):
    pairs = [(counts_hbm, counts_ref), (cur_hbm, cur_ref), (agg_hbm, agg_ref), (up_hbm, up_ref)]
    loads = [
        pltpu.make_async_copy(source, target, sems.at[k]) for k, (source, target) in enumerate(pairs)
    ]
    for load in loads:
        load.start()
    lanes = cur_ref.shape[1]
    boxes = tile_x * tile_y
    loads[0].wait()
    limits = count_rows(counts_ref, tile_x, tile_y, lanes)
    keep = lax.broadcasted_iota(jnp.int32, (boxes, lanes), 1).astype(F32) < limits
    kept_ref[...] = jnp.where(keep, 1.0, 0.0)
    odd = lax.axis_index("gy") % 2 == 1
    loads[1].wait()
    wide[...] = cur_ref[...].astype(F32)
    for part in range(2):
        cols = slice(part * lanes, (part + 1) * lanes)
        live_ref[:, cols] = jnp.where(keep, wide[pl.ds(part, boxes, stride=2), :], 0.0).astype(BF16)

        def edge(column):
            rows = wide[pl.ds(2 * column + part, tile_x, stride=2 * tile_y), :]
            return rows * kept_ref[pl.ds(column, tile_x, stride=tile_y), :]

        first = jnp.concatenate([edge(0), edge(1)], axis=0).astype(BF16)
        last = jnp.concatenate([edge(tile_y - 2), edge(tile_y - 1)], axis=0).astype(BF16)
        low_ref[:, cols] = jnp.where(odd, first, last)
        high_ref[:, cols] = jnp.where(odd, last, first)
    for load in loads[2:]:
        load.wait()


def rims_kernel(tile_x, tile_y, live_ref, inner_ref, outer_ref, low_ref, high_ref, first, last):
    odd = lax.axis_index("gx") % 2 == 1
    sides = halo_pair(inner_ref, outer_ref, "gy")
    for rim, start in ((first, 0), (last, tile_x - 2)):
        rim[0 : 2 * tile_y, :] = live_ref[start * tile_y : (start + 2) * tile_y, :].astype(F32)
        place = 2 * tile_y
        for side in sides:
            for column in range(2):
                at = column * tile_x + start
                rim[place : place + 2, :] = side[at : at + 2]
                place += 2
        rim[place:, :] = jnp.zeros((rim.shape[0] - place, rim.shape[1]), F32)
    low_ref[...] = jnp.where(odd, first[...], last[...]).astype(BF16)
    high_ref[...] = jnp.where(odd, last[...], first[...]).astype(BF16)


def parents_kernel(tile_x, tile_y, live_ref, agg_ref, up_ref, coarse_ref, pats_ref, pats, rows4):
    lanes = pats.shape[2]
    width = tile_y + 2 * LEFT
    pattern = mm(live_ref[...], agg_ref[...])
    pats[0] = pattern[:, :lanes]
    pats[1] = pattern[:, lanes:]
    children = []
    for side_x in range(2):
        for side_y in range(2):
            for part in range(2):
                rows = [
                    pats[part, pl.ds((2 * p + side_x) * tile_y + side_y, tile_y // 2, stride=2), :]
                    for p in range(tile_x // 2)
                ]
                children.append(jnp.concatenate(rows, axis=0).astype(BF16))
    coarse = mm(jnp.concatenate(children, axis=1), up_ref[...])
    for place in range(4):
        rows4[pl.ds(place, coarse.shape[0], stride=4), :] = coarse[:, place * 128 : (place + 1) * 128]
    coarse_ref[...] = rows4[...].astype(BF16)
    pattern = pattern.astype(BF16).astype(F32)
    values = [pattern[:, :lanes], pattern[:, lanes:], pattern[:, :lanes] + pattern[:, lanes:]]
    none = jnp.zeros((LEFT, lanes), F32)
    for i in range(tile_x):
        base = i * width
        for k in range(3):
            pats_ref[k, base : base + LEFT, :] = none
            pats_ref[k, base + LEFT : base + LEFT + tile_y, :] = values[k][i * tile_y : (i + 1) * tile_y]
            pats_ref[k, base + LEFT + tile_y : base + width, :] = none


OFFSETS = [(dx, dy) for dx in range(-2, 3) for dy in range(-2, 3) if max(abs(dx), abs(dy)) == 2]


def local_kernel(
    tile_x, tile_y, live_ref, pats, near_ref, low_ref, lower_ref, field_ref, cells, shifted, tables, sums,
):
    lanes = lower_ref.shape[2]
    width = tile_y + 2 * LEFT
    none = jnp.zeros((LEFT, lanes), F32)
    ends = jnp.zeros((tile_y, 6 * lanes), BF16)
    shifted[0:tile_y, :] = ends
    shifted[(tile_x + 1) * tile_y : (tile_x + 2) * tile_y, :] = ends
    shifted[tile_y : (tile_x + 1) * tile_y, 2 * lanes : 4 * lanes] = live_ref[...]
    for part in range(2):
        cols = slice(part * lanes, (part + 1) * lanes)
        for i in range(tile_x):
            base = i * width
            cells[part, base : base + LEFT, :] = none
            cells[part, base + LEFT : base + LEFT + tile_y, :] = live_ref[
                i * tile_y : (i + 1) * tile_y, cols
            ].astype(F32)
            cells[part, base + LEFT + tile_y : base + width, :] = none
            for shift in (-1, 1):
                place = (2 * (shift + 1) + part) * lanes
                shifted[(i + 1) * tile_y : (i + 2) * tile_y, place : place + lanes] = cells[
                    part, base + LEFT + shift : base + LEFT + shift + tile_y, :
                ].astype(BF16)
    for k in range(len(OFFSETS)):
        t_real, t_imag = low_ref[2 * k : 2 * k + 1, :], low_ref[2 * k + 1 : 2 * k + 2, :]
        for n, value in enumerate((t_imag - t_real, t_imag + t_real, t_real)):
            tables[3 * k + n] = jnp.broadcast_to(value, (8, lanes))

    passes = [
        [(dx, dy) for dx, dy in OFFSETS if dy == -2],
        [(dx, dy) for dx, dy in OFFSETS if dy == 2],
        [(dx, dy) for dx, dy in OFFSETS if abs(dy) < 2],
    ]
    blocks = tile_y // 8
    size = tile_x * tile_y // blocks

    def block(b, carry):
        total = None
        for shift in range(3):
            start = pl.multiple_of(b * size + shift * tile_y, tile_y)
            term = mm(shifted[pl.ds(start, size), :], near_ref[shift])
            total = term if total is None else total + term
        start = pl.multiple_of(b * size, size)
        field_ref[0, pl.ds(start, size), :] = total[:, :lanes]
        field_ref[1, pl.ds(start, size), :] = total[:, lanes:]
        shift_y = pl.multiple_of(b * 8, 8)
        for number, offsets in enumerate(passes):
            running = {}
            for row in range(tile_x):
                for dy in sorted({dy for _, dy in offsets}):
                    rows = pl.ds(shift_y + (row * width + LEFT + dy), 8)
                    source = [pats[k, rows, :] for k in range(3)]
                    for dx in range(-2, 3):
                        i = row - dx
                        if (dx, dy) not in offsets or not 0 <= i < tile_x:
                            continue
                        k = OFFSETS.index((dx, dy))
                        if i not in running:
                            running[i] = [None] * 3 if number == 0 else [sums[n, i] for n in range(3)]
                        running[i] = [
                            tables[3 * k + n] * source[n]
                            if running[i][n] is None
                            else running[i][n] + tables[3 * k + n] * source[n]
                            for n in range(3)
                        ]
                for i in sorted(running):
                    if i + 2 <= row or row == tile_x - 1:
                        value = running.pop(i)
                        if number < 2:
                            for n in range(3):
                                sums[n, i] = value[n]
                        else:
                            place = pl.ds(pl.multiple_of(shift_y + i * tile_y, 8), 8)
                            lower_ref[0, place, :] = value[2] - value[1]
                            lower_ref[1, place, :] = value[2] + value[0]
        return carry

    lax.fori_loop(0, blocks, block, 0)


def halos_kernel(
    tile_x, tile_y, inner_y, outer_y, inner_x, outer_x, agg_ref, near_ref, low_ref, recv_ref,
    lower_in, field_in, kept_in, field_ref, kept_ref, columns, rims, line_ref, lower_ref,
):
    lanes = lower_in.shape[2]
    width = tile_y + 2 * LEFT
    halo = halo_pair(inner_y, outer_y, "gy") + halo_pair(inner_x, outer_x, "gx")
    half_x, half_y = tile_x // 2, tile_y // 2
    for child in range(4):
        for p in range(half_x):
            rows = slice(p * half_y, (p + 1) * half_y)
            boxes = pl.ds((2 * p + child // 2) * tile_y + child % 2, half_y, stride=2)
            for part in range(2):
                lower_ref[part, child, rows, :] = lower_in[part, boxes, :]
                field_ref[part, child, rows, :] = field_in[part, boxes, :]
            kept_ref[child, rows, :] = kept_in[boxes, :]

    def add_column(ref, part, box, value):
        line_ref[...] = value
        for side_x in range(2):
            child, rows = 2 * side_x + box % 2, pl.ds(box // 2, half_x, stride=half_y)
            ref[part, child, rows, :] = ref[part, child, rows, :] + line_ref[pl.ds(side_x, half_x, stride=2), :]

    def add_row(ref, part, box, value):
        line_ref[...] = value
        for side_y in range(2):
            child, rows = 2 * (box % 2) + side_y, slice(box // 2 * half_y, (box // 2 + 1) * half_y)
            ref[part, child, rows, :] = ref[part, child, rows, :] + line_ref[pl.ds(side_y, half_y, stride=2), :]

    halo = jnp.concatenate(halo, axis=0)
    pattern = mm(halo.astype(BF16), agg_ref[...]).astype(BF16).astype(F32)
    values = [halo[:, :lanes], halo[:, lanes:], pattern[:, :lanes], pattern[:, lanes:]]
    two = jnp.zeros((8, lanes), F32)
    rim_size = inner_x.shape[0]
    for n, value in enumerate(values):
        for side in range(2):
            for c in range(2):
                at = (2 * side + c) * tile_x
                columns[n, 2 * side + c, 0:8, :] = two
                columns[n, 2 * side + c, 8 : 8 + tile_x, :] = value[at : at + tile_x]
                columns[n, 2 * side + c, 8 + tile_x : 16 + tile_x, :] = two
        for end in range(2):
            at = 4 * tile_x + end * rim_size
            corner = at + 2 * tile_y
            for row in range(2):
                base = (2 * end + row) * width + LEFT
                rims[n, base : base + tile_y, :] = value[at + row * tile_y : at + (row + 1) * tile_y]
                for side in range(2):
                    for c in range(2):
                        place = base + (tile_y + c if side else c - 2)
                        line = corner + 4 * side + 2 * c + row
                        rims[n, place : place + 1, :] = value[line : line + 1]

    def translate(terms):
        first = second = 0.0
        for dx, dy, real, imag in terms:
            k = OFFSETS.index((dx, dy))
            t_real, t_imag = low_ref[2 * k : 2 * k + 1, :], low_ref[2 * k + 1 : 2 * k + 2, :]
            first = first + (t_real * real - t_imag * imag)
            second = second + (t_real * imag + t_imag * real)
        return first, second

    def column(n, side, c, dx):
        return columns[n, 2 * side + c, 8 + dx : 8 + dx + tile_x, :]

    def rim(n, end, row, dy):
        base = (2 * end + row) * width + LEFT + dy
        return rims[n, base : base + tile_y, :]

    for side in range(2):
        for box in ((tile_y - 1, tile_y - 2) if side else (0, 1)):
            terms = []
            for c in range(2):
                dy = (tile_y + c if side else c - 2) - box
                for dx in range(-2, 3):
                    if (dx, dy) in OFFSETS:
                        terms.append((dx, dy, column(2, side, c, dx), column(3, side, c, dx)))
            for part, value in enumerate(translate(terms)):
                add_column(lower_ref, part, box, value)
        source = jnp.concatenate(
            [column(part, side, 1 - side, dx) for dx in range(-1, 2) for part in range(2)], axis=1
        ).astype(BF16)
        weights = [near_ref[dx, (4 * side) * lanes : (4 * side + 2) * lanes, :] for dx in range(3)]
        value = mm(source, jnp.concatenate(weights, axis=0))
        for part in range(2):
            add_column(field_ref, part, tile_y - 1 if side else 0, value[:, part * lanes : (part + 1) * lanes])
    for end in range(2):
        for box in ((tile_x - 1, tile_x - 2) if end else (0, 1)):
            terms = []
            for row in range(2):
                dx = (tile_x + row if end else row - 2) - box
                for dy in range(-2, 3):
                    if (dx, dy) in OFFSETS:
                        terms.append((dx, dy, rim(2, end, row, dy), rim(3, end, row, dy)))
            for part, value in enumerate(translate(terms)):
                add_row(lower_ref, part, box, value)
        source = jnp.concatenate(
            [rim(part, end, 1 - end, dy) for dy in range(-1, 2) for part in range(2)], axis=1
        ).astype(BF16)
        value = mm(source, near_ref[2 * end])
        for part in range(2):
            add_row(field_ref, part, tile_x - 1 if end else 0, value[:, part * lanes : (part + 1) * lanes])
    for child in range(4):
        total = jnp.concatenate([lower_ref[part, child] for part in range(2)], axis=1).astype(BF16)
        value = mm(total, recv_ref[...])
        for part in range(2):
            field_ref[part, child] = field_ref[part, child] + value[:, part * lanes : (part + 1) * lanes]


GROUP = 16
SEGMENT = 8


def order_kernel(
    chunks, kinds, parents_x, parents_y, list_ref, kind_ref, count_ref, table_ref, down_ref, recv_ref,
    early_ref, late_ref, table8, fold_ref, words
):
    for child in range(4):
        fold_ref[child] = mm(down_ref[child], recv_ref[...]).astype(BF16)
    width = table_ref.shape[1]
    for place, row in enumerate((0, 2, 0, 2, 1, 3, 1, 3)):
        table8[pl.ds(place, kinds, stride=8), :] = table_ref[pl.ds(row, kinds, stride=4), :]
    table8[8 * kinds : 8 * kinds + 8, :] = jnp.zeros((8, width), F32)
    parents = parents_x * parents_y
    slots = list_ref.shape[1]
    lanes = early_ref.shape[1]
    across = parents_y * chunks
    entry = list_ref[...]
    line, place = entry // across, entry % across
    chunk = (place // parents_y) ^ lax.axis_index("gy")
    is_late = (chunk > 0) & (chunk < chunks - 1)
    chunk = jnp.where(is_late, chunk - 1, jnp.where(chunk > 0, 1, 0))
    source = chunk * parents + line * parents_y + place % parents_y
    column = count_rows(count_ref, parents_x, parents_y, slots)
    used = lax.broadcasted_iota(jnp.int32, (parents, slots), 1).astype(F32) < column
    part = jnp.where(used, jnp.where(is_late, 2, 1), 0)
    words[:, 0:slots] = (source * 128 + kind_ref[...] + part * (1 << 20)).astype(F32)
    turned = words[...].T[0:slots].astype(jnp.int32)
    word, turned_part = turned & ((1 << 20) - 1), turned >> 20

    down = lax.broadcasted_iota(jnp.int32, (parents, parents), 0)
    along = lax.broadcasted_iota(jnp.int32, (parents, parents), 1)
    earlier = lax.broadcasted_iota(jnp.int32, (slots, slots), 1) < lax.broadcasted_iota(jnp.int32, (slots, slots), 0)
    earlier = jnp.where(earlier, 1.0, 0.0).astype(BF16)
    slot = lax.broadcasted_iota(jnp.int32, (slots, parents), 0)
    most = (2 * lax.broadcasted_iota(jnp.int32, (parents, lanes), 1)).astype(F32)
    for number, at_ref in ((1, early_ref), (2, late_ref)):
        hit = jnp.where(turned_part == number, 1.0, 0.0)
        mine = jnp.where(part == number, 1.0, 0.0).astype(BF16)
        column = mm(mine, jnp.ones((slots, parents), BF16))
        row = jnp.sum(hit, axis=0, keepdims=True)
        before = (column < row) | ((column == row) & (down < along))
        rank = jnp.sum(jnp.where(before, 1.0, 0.0), axis=0, keepdims=True)
        place = mm(earlier, hit.astype(BF16)).astype(jnp.int32)
        place = jnp.where(turned_part == number, place, -1)
        dense = jnp.zeros((slots, parents), jnp.int32)
        for n in range(slots):
            dense = dense + jnp.where(place[n : n + 1] == slot, word[n : n + 1], 0)
        kind = jnp.where(slot.astype(F32) < row, dense & 127, kinds)
        source = dense >> 7
        values = [source >> 8, source & 255, kind, along[0:slots]]
        values = jnp.concatenate([value.astype(F32) for value in values], axis=0).astype(BF16)
        ranked = jnp.where(down.astype(F32) == rank, 1.0, 0.0).astype(BF16)
        moved = lax.dot_general(values, ranked, (((1,), (1,)), ((), ())), preferred_element_type=F32)
        high, low, kind, parent = [
            moved[n * slots : (n + 1) * slots].astype(jnp.int32) for n in range(4)
        ]
        reach = jnp.sum(jnp.where(column[:, :lanes] <= most, 1.0, 0.0), axis=0, keepdims=True).astype(jnp.int32)
        head = jnp.broadcast_to(reach // GROUP, (8, lanes))
        line = lax.broadcasted_iota(jnp.int32, (8, lanes), 0)
        for n in range(parents // lanes):
            head = jnp.where(line == n, parent[0:8, n * lanes : (n + 1) * lanes], head)
        at_ref[0:8, :] = head
        at = 8
        for segment in range(0, slots, SEGMENT):
            for n in range(parents // lanes):
                for value in (high * 256 + low, kind):
                    at_ref[at : at + SEGMENT, :] = value[segment : segment + SEGMENT, n * lanes : (n + 1) * lanes]
                    at += SEGMENT


def expand(sources, cells):
    lanes = cells.shape[1]
    count = sources[0].shape[0] // 8
    pairs = cells.reshape(len(sources) * count, 2, 8, lanes)
    upper = lax.broadcasted_iota(jnp.int32, (count, 8, lanes), 1) < 4
    for c, source in enumerate(sources):
        rows = source[...].astype(F32).reshape(count, 8, lanes)
        turned = pltpu.roll(rows, 4, axis=1)
        pairs[c * count : (c + 1) * count, 0] = jnp.where(upper, rows, turned)
        pairs[c * count : (c + 1) * count, 1] = jnp.where(upper, turned, rows)


def load_lists(at_any, at, sems):
    block = 2 * 128 * SEGMENT
    half = 1024 + (at.shape[0] - 1024) // 2
    loads = []
    for n, (start, end) in enumerate([(0, 1024 + block), (1024 + block, half), (half, at.shape[0])]):
        rows = pl.ds(start, end - start)
        loads.append(pltpu.make_async_copy(at_any.at[rows], at.at[rows], sems.at[n]))
        loads[-1].start()
    return loads


def add_lists(parents, slots, loads, at, cells, table8, sums):
    lanes = cells.shape[1]
    tiles, kind_tiles, sum_tiles = [ref.reshape(ref.shape[0] // 8, 8, lanes) for ref in (cells, table8, sums)]
    words = 128 * SEGMENT
    per_block = 128 // GROUP

    def step(length, n, carry):
        @pl.when(n == per_block)
        def _():
            loads[1].wait()

        first = 1024 + (n // per_block) * (2 * words) + (n % per_block) * GROUP
        for k in range(GROUP):
            total = [None, None]
            for s in range(length):
                place = first + ((s // SEGMENT) * 2 * parents * SEGMENT + (s % SEGMENT) * 128 + k)
                term = tiles[at[place]] * kind_tiles[at[place + words]]
                total[s % 2] = term if total[s % 2] is None else total[s % 2] + term
            total = total[0] + total[1] if length else jnp.zeros((8, lanes), F32)
            sum_tiles[at[n * GROUP + k]] = total
        return carry

    loads[0].wait()
    start = 0
    for j, length in enumerate(range(0, slots + 1, 2)):
        if length == SEGMENT + 2:
            loads[2].wait()
        end = at[parents + j]
        lax.fori_loop(start, end, functools.partial(step, length), 0)
        start = end


def early_kernel(count, parents, slots, *refs):
    sources = refs[:count]
    at_any, table8, sums, cells, at, sems = refs[count:]
    loads = load_lists(at_any, at, sems)
    expand(sources, cells)
    add_lists(parents, slots, loads, at, cells, table8, sums)


def late_kernel(count, tile_x, tile_y, slots, *refs):
    sources = refs[:count]
    (at_any, table8, early_ref, kept_ref, field_ref, fold_ref, out_hbm,
     cells, sums, lines, at, out_ref, list_sems, sems) = refs[count:]
    parents_x, parents_y = tile_x // 2, tile_y // 2
    parents = parents_x * parents_y
    lanes = table8.shape[1]
    loads = load_lists(at_any, at, list_sems)
    expand(sources, cells)
    add_lists(parents, slots, loads, at, cells, table8, sums)
    raw = (sums[...] + early_ref[...]).reshape(parents // 2, 2, 8, lanes)
    one, other = raw[:, 0], raw[:, 1]
    line = lax.broadcasted_iota(jnp.int32, one.shape, 1)
    with_real = jnp.where(line < 4, one, pltpu.roll(other, 4, axis=1))
    with_imag = jnp.where(line < 4, pltpu.roll(one, 4, axis=1), other)
    turned = jnp.where(line % 4 < 2, -pltpu.roll(with_imag, 6, axis=1), pltpu.roll(with_imag, 2, axis=1))
    lines[...] = (with_real + turned).reshape(4 * parents, lanes)
    ordered = [lines[pl.ds(place, parents, stride=4), :].astype(BF16) for place in range(4)]
    incoming = jnp.concatenate(ordered, axis=1)
    fields = [mm(incoming, fold_ref[child]) for child in range(4)]
    stores = []
    for half in range(2):
        first, size = half * parents // 2, parents // 2
        rows = slice(first, first + size)
        for child in range(4):
            mask = kept_ref[child, rows, :]
            for part in range(2):
                value = fields[child][rows, part * lanes : (part + 1) * lanes]
                value = (value + field_ref[part, child, rows, :]) * mask
                for p in range(parents_x // 2):
                    line = (2 * (half * parents_x // 2 + p) + child // 2) * tile_y + child % 2
                    out_ref[pl.ds(2 * line + part, parents_y, stride=4), :] = value[
                        p * parents_y : (p + 1) * parents_y
                    ]
        size = out_ref.shape[0] // 2
        rows = pl.ds(half * size, size)
        stores.append(pltpu.make_async_copy(out_ref.at[rows], out_hbm.at[rows], sems.at[half]))
        stores[-1].start()
    for store in stores:
        store.wait()


def swap(low, high, axis, other=None):
    count = lax.axis_size(axis)
    lows = [(i, i ^ 1) for i in range(count)]
    highs = [(i, (((i + 1) % count ^ 1) - 1) % count) for i in range(count)]
    if other is not None:
        breadth = lax.axis_size(other)
        highs = [
            (i * breadth + j, i * breadth + (j ^ 1) if i in (0, count - 1) else target * breadth + j)
            for i, target in highs
            for j in range(breadth)
        ]
    return lax.ppermute(low, axis, lows), lax.ppermute(high, axis if other is None else (axis, other), highs)


def body(
    currents, box_count, aggregate, near_blocks, low_translator, child_to_parent, coarse_list,
    coarse_kind, coarse_count, up_translator, parent_to_child, receive_map,
):
    tile_x, tile_y = box_count.shape
    boxes = tile_x * tile_y
    lanes = currents.shape[-1]
    parents_x, parents_y, slots = coarse_list.shape
    parents = parents_x * parents_y
    kinds, _, half = up_translator.shape
    wide = 2 * half
    chunks = lax.axis_size("gy")
    in_hbm = pl.BlockSpec(memory_space=pltpu.HBM)

    edge = jax.ShapeDtypeStruct((2 * tile_x, 2 * lanes), BF16)
    edge = jax.ShapeDtypeStruct((2 * tile_x, 2 * lanes), BF16)
    width = tile_y + 2 * LEFT
    live, kept, low, high, agg_near, up_near = pl.pallas_call(
        functools.partial(live_kernel, tile_x, tile_y),
        name="live",
        out_shape=[
            jax.ShapeDtypeStruct((boxes, 2 * lanes), BF16),
            jax.ShapeDtypeStruct((boxes, lanes), F32),
            edge,
            edge,
            jax.ShapeDtypeStruct((2 * lanes, 2 * lanes), BF16),
            jax.ShapeDtypeStruct((8 * lanes, wide), BF16),
        ],
        in_specs=[in_hbm] * 4,
        out_specs=vmem(6),
        scratch_shapes=[
            pltpu.VMEM((2 * boxes, lanes), BF16),
            pltpu.VMEM((tile_x, tile_y), jnp.int32),
            pltpu.VMEM((2 * boxes, lanes), F32),
            pltpu.SemaphoreType.DMA((4,)),
        ],
        compiler_params=params(10),
        cost_estimate=cost(100 * MIB, 3 * MIB),
    )(
        hbm(currents.reshape(2 * boxes, lanes)), hbm(box_count), hbm(aggregate),
        hbm(child_to_parent.reshape(8 * lanes, wide)),
    )
    coarse, pats = pl.pallas_call(
        functools.partial(parents_kernel, tile_x, tile_y),
        name="parents",
        out_shape=[
            jax.ShapeDtypeStruct((4 * parents, wide // 4), BF16),
            jax.ShapeDtypeStruct((3, tile_x * width, lanes), F32),
        ],
        in_specs=vmem(3),
        out_specs=vmem(2),
        scratch_shapes=[
            pltpu.VMEM((2, boxes, lanes), F32),
            pltpu.VMEM((4 * parents, wide // 4), F32),
        ],
        compiler_params=params(10),
        cost_estimate=cost(200 * MIB, 3 * MIB),
    )(live, agg_near, up_near)
    inner_y, outer_y = swap(low, high, "gy")
    sources = [coarse] + [
        lax.ppermute(coarse, "gy", [(i, i ^ d) for i in range(chunks)])
        for d in [chunks - 1] + list(range(1, chunks - 1))
    ]

    rim = 2 * tile_y + 8
    rim += -rim % 16
    low, high = pl.pallas_call(
        functools.partial(rims_kernel, tile_x, tile_y),
        name="rims",
        out_shape=[jax.ShapeDtypeStruct((rim, 2 * lanes), BF16)] * 2,
        in_specs=vmem(3),
        out_specs=vmem(2),
        scratch_shapes=[pltpu.VMEM((rim, 2 * lanes), F32)] * 2,
        compiler_params=params(10),
        cost_estimate=cost(1 * MIB, MIB),
    )(live, inner_y, outer_y)
    inner_x, outer_x = swap(low, high, "gx", "gy")
    live, coarse_count, _ = lax.optimization_barrier((live, coarse_count, low))

    near_rows = near_blocks.reshape(3, 6 * lanes, 2 * lanes)
    low_rows = low_translator.reshape(-1, lanes)
    pair = [jax.ShapeDtypeStruct((2, boxes, lanes), F32)] * 2
    lower, near = pl.pallas_call(
        functools.partial(local_kernel, tile_x, tile_y),
        name="local",
        out_shape=pair,
        in_specs=vmem(4),
        out_specs=vmem(2),
        scratch_shapes=[
            pltpu.VMEM((2, tile_x * width, lanes), F32),
            pltpu.VMEM(((tile_x + 2) * tile_y, 6 * lanes), BF16),
            pltpu.VMEM((3 * len(OFFSETS), 8, lanes), F32),
            pltpu.VMEM((3, tile_x, 8, lanes), F32),
        ],
        compiler_params=params(10),
        cost_estimate=cost(2000 * MIB, 5 * MIB),
    )(live, pats, near_rows, low_rows)

    table = up_translator.reshape(kinds, 2, 2, half // 2).transpose(0, 2, 1, 3).reshape(4 * kinds, half // 2)
    places = jax.ShapeDtypeStruct((8 + 2 * slots * parents // 128, 128), jnp.int32)
    early_at, late_at, table8, fold = pl.pallas_call(
        functools.partial(order_kernel, chunks, kinds, parents_x, parents_y),
        name="order",
        out_shape=[
            places,
            places,
            jax.ShapeDtypeStruct((8 * kinds + 8, half // 2), F32),
            jax.ShapeDtypeStruct((4, wide, 2 * lanes), BF16),
        ],
        in_specs=vmem(6),
        out_specs=vmem(4),
        scratch_shapes=[pltpu.VMEM((parents, 128), F32)],
        compiler_params=params(10),
        cost_estimate=cost(300 * MIB, MIB),
    )(
        coarse_list.reshape(parents, slots), coarse_kind.reshape(parents, slots), coarse_count, table,
        parent_to_child, receive_map,
    )
    early_at, late_at = early_at.reshape(-1), late_at.reshape(-1)
    anywhere = pl.BlockSpec(memory_space=pl.ANY)
    early, late = sources[:2], sources[2:]
    early_sums = pl.pallas_call(
        functools.partial(early_kernel, len(early), parents, slots),
        name="early",
        out_shape=jax.ShapeDtypeStruct((8 * parents, wide // 4), F32),
        in_specs=vmem(len(early)) + [anywhere] + vmem(1),
        out_specs=pl.BlockSpec(memory_space=pltpu.VMEM),
        scratch_shapes=[
            pltpu.VMEM((len(early) * parents * 8, wide // 4), F32),
            pltpu.SMEM(early_at.shape, jnp.int32),
            pltpu.SemaphoreType.DMA((3,)),
        ],
        compiler_params=params(10),
        cost_estimate=cost(1000 * MIB, 4 * MIB),
    )(*early, early_at, table8)
    lower, near, _ = lax.optimization_barrier((lower, near, early_sums))
    field, kept = pl.pallas_call(
        functools.partial(halos_kernel, tile_x, tile_y),
        name="halos",
        out_shape=[
            jax.ShapeDtypeStruct((2, 4, parents, lanes), F32),
            jax.ShapeDtypeStruct((4, parents, lanes), F32),
        ],
        in_specs=vmem(11),
        out_specs=vmem(2),
        scratch_shapes=[
            pltpu.VMEM((4, 4, tile_x + 16, lanes), F32),
            pltpu.VMEM((4, 4 * width, lanes), F32),
            pltpu.VMEM((tile_x, lanes), F32),
            pltpu.VMEM((2, 4, parents, lanes), F32),
        ],
        compiler_params=params(10),
        cost_estimate=cost(100 * MIB, 5 * MIB),
    )(inner_y, outer_y, inner_x, outer_x, agg_near, near_rows, low_rows, receive_map, lower, near, kept)

    out = pl.pallas_call(
        functools.partial(late_kernel, len(late), tile_x, tile_y, slots),
        name="late",
        out_shape=jax.ShapeDtypeStruct((2 * boxes, lanes), F32),
        in_specs=vmem(len(late)) + [anywhere] + vmem(5),
        out_specs=in_hbm,
        scratch_shapes=[
            pltpu.VMEM((len(late) * parents * 8, wide // 4), F32),
            pltpu.VMEM((8 * parents, wide // 4), F32),
            pltpu.VMEM((4 * parents, wide // 4), F32),
            pltpu.SMEM(late_at.shape, jnp.int32),
            pltpu.VMEM((2 * boxes, lanes), F32),
            pltpu.SemaphoreType.DMA((3,)),
            pltpu.SemaphoreType.DMA((2,)),
        ],
        compiler_params=params(16 if chunks <= 4 else 40),
        cost_estimate=cost(2000 * MIB, 8 * MIB),
    )(*late, late_at, table8, early_sums, kept, field, fold)
    return out.reshape(tile_x, tile_y, 2, lanes)


def solution(mesh):
    tiles = P("gx", "gy")
    in_specs = (tiles, tiles, P(), P(), P(), P(), tiles, tiles, tiles, P(), P(), P())
    return jax.shard_map(body, mesh=mesh, in_specs=in_specs, out_specs=tiles, check_vma=False)
```

```python
import functools

import jax
import jax.numpy as jnp
from jax import lax
from jax.experimental import pallas as pl
from jax.experimental.pallas import tpu as pltpu
from jax.sharding import PartitionSpec as P

F32 = jnp.float32
BF16 = jnp.bfloat16
MIB = 1 << 20


def vmem(count):
    return [pl.BlockSpec(memory_space=pltpu.VMEM)] * count


def hbm(array):
    return pltpu.with_memory_space_constraint(array, pltpu.HBM)


def params(mib):
    return pltpu.CompilerParams(vmem_limit_bytes=mib * MIB)


def cost(macs, moved):
    return pl.CostEstimate(flops=2 * macs, bytes_accessed=moved, transcendentals=0)


def mm(left, right):
    return jnp.dot(left, right, preferred_element_type=F32)


def count_rows(counts_ref, tile_x, tile_y, lanes):
    eye = lax.broadcasted_iota(jnp.int32, (tile_y, tile_y), 0) == lax.broadcasted_iota(
        jnp.int32, (tile_y, tile_y), 1
    )
    counts = counts_ref[...].astype(F32)
    diag = [
        jnp.where(eye, jnp.broadcast_to(counts[i : i + 1], (tile_y, tile_y)), 0.0) for i in range(tile_x)
    ]
    return mm(jnp.concatenate(diag, axis=0).astype(BF16), jnp.ones((tile_y, lanes), BF16))


def halo_pair(inner_ref, outer_ref, axis):
    at = lax.axis_index(axis)
    odd = at % 2 == 1
    inner, outer = inner_ref[...].astype(F32), outer_ref[...].astype(F32)
    before, after = jnp.where(odd, inner, outer), jnp.where(odd, outer, inner)
    return jnp.where(at > 0, before, 0.0), jnp.where(at < lax.axis_size(axis) - 1, after, 0.0)


LEFT = 8


def live_kernel(tile_x, tile_y, cur_hbm, counts_hbm, agg_hbm, up_hbm,
                live_ref, kept_ref, low_ref, high_ref, agg_ref, up_ref, cur_ref, counts_ref, wide, sems):
    pairs = [(counts_hbm, counts_ref), (cur_hbm, cur_ref), (agg_hbm, agg_ref), (up_hbm, up_ref)]
    loads = [
        pltpu.make_async_copy(source, target, sems.at[k]) for k, (source, target) in enumerate(pairs)
    ]
    for load in loads:
        load.start()
    lanes = cur_ref.shape[1]
    boxes = tile_x * tile_y
    loads[0].wait()
    limits = count_rows(counts_ref, tile_x, tile_y, lanes)
    keep = lax.broadcasted_iota(jnp.int32, (boxes, lanes), 1).astype(F32) < limits
    kept_ref[...] = jnp.where(keep, 1.0, 0.0)
    odd = lax.axis_index("gy") % 2 == 1
    loads[1].wait()
    wide[...] = cur_ref[...].astype(F32)
    for part in range(2):
        cols = slice(part * lanes, (part + 1) * lanes)
        live_ref[:, cols] = jnp.where(keep, wide[pl.ds(part, boxes, stride=2), :], 0.0).astype(BF16)

        def edge(column):
            rows = wide[pl.ds(2 * column + part, tile_x, stride=2 * tile_y), :]
            return rows * kept_ref[pl.ds(column, tile_x, stride=tile_y), :]

        first = jnp.concatenate([edge(0), edge(1)], axis=0).astype(BF16)
        last = jnp.concatenate([edge(tile_y - 2), edge(tile_y - 1)], axis=0).astype(BF16)
        low_ref[:, cols] = jnp.where(odd, first, last)
        high_ref[:, cols] = jnp.where(odd, last, first)
    for load in loads[2:]:
        load.wait()


def rims_kernel(tile_x, tile_y, live_ref, inner_ref, outer_ref, low_ref, high_ref, first, last):
    odd = lax.axis_index("gx") % 2 == 1
    sides = halo_pair(inner_ref, outer_ref, "gy")
    for rim, start in ((first, 0), (last, tile_x - 2)):
        rim[0 : 2 * tile_y, :] = live_ref[start * tile_y : (start + 2) * tile_y, :].astype(F32)
        place = 2 * tile_y
        for side in sides:
            for column in range(2):
                at = column * tile_x + start
                rim[place : place + 2, :] = side[at : at + 2]
                place += 2
        rim[place:, :] = jnp.zeros((rim.shape[0] - place, rim.shape[1]), F32)
    low_ref[...] = jnp.where(odd, first[...], last[...]).astype(BF16)
    high_ref[...] = jnp.where(odd, last[...], first[...]).astype(BF16)


def parents_kernel(tile_x, tile_y, live_ref, agg_ref, up_ref, coarse_ref, pats_ref, pats, rows4):
    lanes = pats.shape[2]
    width = tile_y + 2 * LEFT
    pattern = mm(live_ref[...], agg_ref[...])
    pats[0] = pattern[:, :lanes]
    pats[1] = pattern[:, lanes:]
    children = []
    for side_x in range(2):
        for side_y in range(2):
            for part in range(2):
                rows = [
                    pats[part, pl.ds((2 * p + side_x) * tile_y + side_y, tile_y // 2, stride=2), :]
                    for p in range(tile_x // 2)
                ]
                children.append(jnp.concatenate(rows, axis=0).astype(BF16))
    coarse = mm(jnp.concatenate(children, axis=1), up_ref[...])
    for place in range(4):
        rows4[pl.ds(place, coarse.shape[0], stride=4), :] = coarse[:, place * 128 : (place + 1) * 128]
    coarse_ref[...] = rows4[...].astype(BF16)
    pattern = pattern.astype(BF16).astype(F32)
    values = [pattern[:, :lanes], pattern[:, lanes:], pattern[:, :lanes] + pattern[:, lanes:]]
    none = jnp.zeros((LEFT, lanes), F32)
    for i in range(tile_x):
        base = i * width
        for k in range(3):
            pats_ref[k, base : base + LEFT, :] = none
            pats_ref[k, base + LEFT : base + LEFT + tile_y, :] = values[k][i * tile_y : (i + 1) * tile_y]
            pats_ref[k, base + LEFT + tile_y : base + width, :] = none


OFFSETS = [(dx, dy) for dx in range(-2, 3) for dy in range(-2, 3) if max(abs(dx), abs(dy)) == 2]


def local_kernel(
    tile_x, tile_y, live_ref, pats, near_ref, low_ref, lower_ref, field_ref, cells, shifted, tables, sums,
):
    lanes = lower_ref.shape[2]
    width = tile_y + 2 * LEFT
    none = jnp.zeros((LEFT, lanes), F32)
    ends = jnp.zeros((tile_y, 6 * lanes), BF16)
    shifted[0:tile_y, :] = ends
    shifted[(tile_x + 1) * tile_y : (tile_x + 2) * tile_y, :] = ends
    shifted[tile_y : (tile_x + 1) * tile_y, 2 * lanes : 4 * lanes] = live_ref[...]
    for part in range(2):
        cols = slice(part * lanes, (part + 1) * lanes)
        for i in range(tile_x):
            base = i * width
            cells[part, base : base + LEFT, :] = none
            cells[part, base + LEFT : base + LEFT + tile_y, :] = live_ref[
                i * tile_y : (i + 1) * tile_y, cols
            ].astype(F32)
            cells[part, base + LEFT + tile_y : base + width, :] = none
            for shift in (-1, 1):
                place = (2 * (shift + 1) + part) * lanes
                shifted[(i + 1) * tile_y : (i + 2) * tile_y, place : place + lanes] = cells[
                    part, base + LEFT + shift : base + LEFT + shift + tile_y, :
                ].astype(BF16)
    for k in range(len(OFFSETS)):
        t_real, t_imag = low_ref[2 * k : 2 * k + 1, :], low_ref[2 * k + 1 : 2 * k + 2, :]
        for n, value in enumerate((t_imag - t_real, t_imag + t_real, t_real)):
            tables[3 * k + n] = jnp.broadcast_to(value, (8, lanes))

    passes = [
        [(dx, dy) for dx, dy in OFFSETS if dy == -2],
        [(dx, dy) for dx, dy in OFFSETS if dy == 2],
        [(dx, dy) for dx, dy in OFFSETS if abs(dy) < 2],
    ]
    blocks = tile_y // 8
    size = tile_x * tile_y // blocks

    def block(b, carry):
        total = None
        for shift in range(3):
            start = pl.multiple_of(b * size + shift * tile_y, tile_y)
            term = mm(shifted[pl.ds(start, size), :], near_ref[shift])
            total = term if total is None else total + term
        start = pl.multiple_of(b * size, size)
        field_ref[0, pl.ds(start, size), :] = total[:, :lanes]
        field_ref[1, pl.ds(start, size), :] = total[:, lanes:]
        shift_y = pl.multiple_of(b * 8, 8)
        for number, offsets in enumerate(passes):
            running = {}
            for row in range(tile_x):
                for dy in sorted({dy for _, dy in offsets}):
                    rows = pl.ds(shift_y + (row * width + LEFT + dy), 8)
                    source = [pats[k, rows, :] for k in range(3)]
                    for dx in range(-2, 3):
                        i = row - dx
                        if (dx, dy) not in offsets or not 0 <= i < tile_x:
                            continue
                        k = OFFSETS.index((dx, dy))
                        if i not in running:
                            running[i] = [None] * 3 if number == 0 else [sums[n, i] for n in range(3)]
                        running[i] = [
                            tables[3 * k + n] * source[n]
                            if running[i][n] is None
                            else running[i][n] + tables[3 * k + n] * source[n]
                            for n in range(3)
                        ]
                for i in sorted(running):
                    if i + 2 <= row or row == tile_x - 1:
                        value = running.pop(i)
                        if number < 2:
                            for n in range(3):
                                sums[n, i] = value[n]
                        else:
                            place = pl.ds(pl.multiple_of(shift_y + i * tile_y, 8), 8)
                            lower_ref[0, place, :] = value[2] - value[1]
                            lower_ref[1, place, :] = value[2] + value[0]
        return carry

    lax.fori_loop(0, blocks, block, 0)


def halos_kernel(
    tile_x, tile_y, inner_y, outer_y, inner_x, outer_x, agg_ref, near_ref, low_ref, recv_ref,
    lower_in, field_in, kept_in, field_ref, kept_ref, columns, rims, line_ref, lower_ref,
):
    lanes = lower_in.shape[2]
    width = tile_y + 2 * LEFT
    halo = halo_pair(inner_y, outer_y, "gy") + halo_pair(inner_x, outer_x, "gx")
    half_x, half_y = tile_x // 2, tile_y // 2
    for child in range(4):
        for p in range(half_x):
            rows = slice(p * half_y, (p + 1) * half_y)
            boxes = pl.ds((2 * p + child // 2) * tile_y + child % 2, half_y, stride=2)
            for part in range(2):
                lower_ref[part, child, rows, :] = lower_in[part, boxes, :]
                field_ref[part, child, rows, :] = field_in[part, boxes, :]
            kept_ref[child, rows, :] = kept_in[boxes, :]

    def add_column(ref, part, box, value):
        line_ref[...] = value
        for side_x in range(2):
            child, rows = 2 * side_x + box % 2, pl.ds(box // 2, half_x, stride=half_y)
            ref[part, child, rows, :] = ref[part, child, rows, :] + line_ref[pl.ds(side_x, half_x, stride=2), :]

    def add_row(ref, part, box, value):
        line_ref[...] = value
        for side_y in range(2):
            child, rows = 2 * (box % 2) + side_y, slice(box // 2 * half_y, (box // 2 + 1) * half_y)
            ref[part, child, rows, :] = ref[part, child, rows, :] + line_ref[pl.ds(side_y, half_y, stride=2), :]

    halo = jnp.concatenate(halo, axis=0)
    pattern = mm(halo.astype(BF16), agg_ref[...]).astype(BF16).astype(F32)
    values = [halo[:, :lanes], halo[:, lanes:], pattern[:, :lanes], pattern[:, lanes:]]
    two = jnp.zeros((8, lanes), F32)
    rim_size = inner_x.shape[0]
    for n, value in enumerate(values):
        for side in range(2):
            for c in range(2):
                at = (2 * side + c) * tile_x
                columns[n, 2 * side + c, 0:8, :] = two
                columns[n, 2 * side + c, 8 : 8 + tile_x, :] = value[at : at + tile_x]
                columns[n, 2 * side + c, 8 + tile_x : 16 + tile_x, :] = two
        for end in range(2):
            at = 4 * tile_x + end * rim_size
            corner = at + 2 * tile_y
            for row in range(2):
                base = (2 * end + row) * width + LEFT
                rims[n, base : base + tile_y, :] = value[at + row * tile_y : at + (row + 1) * tile_y]
                for side in range(2):
                    for c in range(2):
                        place = base + (tile_y + c if side else c - 2)
                        line = corner + 4 * side + 2 * c + row
                        rims[n, place : place + 1, :] = value[line : line + 1]

    def translate(terms):
        first = second = 0.0
        for dx, dy, real, imag in terms:
            k = OFFSETS.index((dx, dy))
            t_real, t_imag = low_ref[2 * k : 2 * k + 1, :], low_ref[2 * k + 1 : 2 * k + 2, :]
            first = first + (t_real * real - t_imag * imag)
            second = second + (t_real * imag + t_imag * real)
        return first, second

    def column(n, side, c, dx):
        return columns[n, 2 * side + c, 8 + dx : 8 + dx + tile_x, :]

    def rim(n, end, row, dy):
        base = (2 * end + row) * width + LEFT + dy
        return rims[n, base : base + tile_y, :]

    for side in range(2):
        for box in ((tile_y - 1, tile_y - 2) if side else (0, 1)):
            terms = []
            for c in range(2):
                dy = (tile_y + c if side else c - 2) - box
                for dx in range(-2, 3):
                    if (dx, dy) in OFFSETS:
                        terms.append((dx, dy, column(2, side, c, dx), column(3, side, c, dx)))
            for part, value in enumerate(translate(terms)):
                add_column(lower_ref, part, box, value)
        source = jnp.concatenate(
            [column(part, side, 1 - side, dx) for dx in range(-1, 2) for part in range(2)], axis=1
        ).astype(BF16)
        weights = [near_ref[dx, (4 * side) * lanes : (4 * side + 2) * lanes, :] for dx in range(3)]
        value = mm(source, jnp.concatenate(weights, axis=0))
        for part in range(2):
            add_column(field_ref, part, tile_y - 1 if side else 0, value[:, part * lanes : (part + 1) * lanes])
    for end in range(2):
        for box in ((tile_x - 1, tile_x - 2) if end else (0, 1)):
            terms = []
            for row in range(2):
                dx = (tile_x + row if end else row - 2) - box
                for dy in range(-2, 3):
                    if (dx, dy) in OFFSETS:
                        terms.append((dx, dy, rim(2, end, row, dy), rim(3, end, row, dy)))
            for part, value in enumerate(translate(terms)):
                add_row(lower_ref, part, box, value)
        source = jnp.concatenate(
            [rim(part, end, 1 - end, dy) for dy in range(-1, 2) for part in range(2)], axis=1
        ).astype(BF16)
        value = mm(source, near_ref[2 * end])
        for part in range(2):
            add_row(field_ref, part, tile_x - 1 if end else 0, value[:, part * lanes : (part + 1) * lanes])
    for child in range(4):
        total = jnp.concatenate([lower_ref[part, child] for part in range(2)], axis=1).astype(BF16)
        value = mm(total, recv_ref[...])
        for part in range(2):
            field_ref[part, child] = field_ref[part, child] + value[:, part * lanes : (part + 1) * lanes]


GROUP = 16
SEGMENT = 8


def order_kernel(
    chunks, kinds, parents_x, parents_y, list_ref, kind_ref, count_ref, table_ref, down_ref, recv_ref,
    early_ref, late_ref, table8, fold_ref, words
):
    for child in range(4):
        fold_ref[child] = mm(down_ref[child], recv_ref[...]).astype(BF16)
    width = table_ref.shape[1]
    for place, row in enumerate((0, 2, 0, 2, 1, 3, 1, 3)):
        table8[pl.ds(place, kinds, stride=8), :] = table_ref[pl.ds(row, kinds, stride=4), :]
    table8[8 * kinds : 8 * kinds + 8, :] = jnp.zeros((8, width), F32)
    parents = parents_x * parents_y
    slots = list_ref.shape[1]
    lanes = early_ref.shape[1]
    across = parents_y * chunks
    entry = list_ref[...]
    line, place = entry // across, entry % across
    chunk = (place // parents_y) ^ lax.axis_index("gy")
    is_late = (chunk > 0) & (chunk < chunks - 1)
    chunk = jnp.where(is_late, chunk - 1, jnp.where(chunk > 0, 1, 0))
    source = chunk * parents + line * parents_y + place % parents_y
    column = count_rows(count_ref, parents_x, parents_y, slots)
    used = lax.broadcasted_iota(jnp.int32, (parents, slots), 1).astype(F32) < column
    part = jnp.where(used, jnp.where(is_late, 2, 1), 0)
    words[:, 0:slots] = (source * 128 + kind_ref[...] + part * (1 << 20)).astype(F32)
    turned = words[...].T[0:slots].astype(jnp.int32)
    word, turned_part = turned & ((1 << 20) - 1), turned >> 20

    down = lax.broadcasted_iota(jnp.int32, (parents, parents), 0)
    along = lax.broadcasted_iota(jnp.int32, (parents, parents), 1)
    earlier = lax.broadcasted_iota(jnp.int32, (slots, slots), 1) < lax.broadcasted_iota(jnp.int32, (slots, slots), 0)
    earlier = jnp.where(earlier, 1.0, 0.0).astype(BF16)
    slot = lax.broadcasted_iota(jnp.int32, (slots, parents), 0)
    most = (2 * lax.broadcasted_iota(jnp.int32, (parents, lanes), 1)).astype(F32)
    for number, at_ref in ((1, early_ref), (2, late_ref)):
        hit = jnp.where(turned_part == number, 1.0, 0.0)
        mine = jnp.where(part == number, 1.0, 0.0).astype(BF16)
        column = mm(mine, jnp.ones((slots, parents), BF16))
        row = jnp.sum(hit, axis=0, keepdims=True)
        before = (column < row) | ((column == row) & (down < along))
        rank = jnp.sum(jnp.where(before, 1.0, 0.0), axis=0, keepdims=True)
        place = mm(earlier, hit.astype(BF16)).astype(jnp.int32)
        place = jnp.where(turned_part == number, place, -1)
        dense = jnp.zeros((slots, parents), jnp.int32)
        for n in range(slots):
            dense = dense + jnp.where(place[n : n + 1] == slot, word[n : n + 1], 0)
        kind = jnp.where(slot.astype(F32) < row, dense & 127, kinds)
        source = dense >> 7
        values = [source >> 8, source & 255, kind, along[0:slots]]
        values = jnp.concatenate([value.astype(F32) for value in values], axis=0).astype(BF16)
        ranked = jnp.where(down.astype(F32) == rank, 1.0, 0.0).astype(BF16)
        moved = lax.dot_general(values, ranked, (((1,), (1,)), ((), ())), preferred_element_type=F32)
        high, low, kind, parent = [
            moved[n * slots : (n + 1) * slots].astype(jnp.int32) * 8 for n in range(4)
        ]
        reach = jnp.sum(jnp.where(column[:, :lanes] <= most, 1.0, 0.0), axis=0, keepdims=True).astype(jnp.int32)
        head = jnp.broadcast_to(reach // GROUP, (8, lanes))
        line = lax.broadcasted_iota(jnp.int32, (8, lanes), 0)
        for n in range(parents // lanes):
            head = jnp.where(line == n, parent[0:8, n * lanes : (n + 1) * lanes], head)
        at_ref[0:8, :] = head
        at = 8
        for segment in range(0, slots, SEGMENT):
            for n in range(parents // lanes):
                for value in (high * 256 + low, kind):
                    at_ref[at : at + SEGMENT, :] = value[segment : segment + SEGMENT, n * lanes : (n + 1) * lanes]
                    at += SEGMENT


def expand(sources, cells):
    lanes = cells.shape[1]
    count = sources[0].shape[0] // 8
    pairs = cells.reshape(len(sources) * count, 2, 8, lanes)
    upper = lax.broadcasted_iota(jnp.int32, (count, 8, lanes), 1) < 4
    for c, source in enumerate(sources):
        rows = source[...].astype(F32).reshape(count, 8, lanes)
        turned = pltpu.roll(rows, 4, axis=1)
        pairs[c * count : (c + 1) * count, 0] = jnp.where(upper, rows, turned)
        pairs[c * count : (c + 1) * count, 1] = jnp.where(upper, turned, rows)


def load_lists(at_any, at, sems):
    block = 2 * 128 * SEGMENT
    half = 1024 + (at.shape[0] - 1024) // 2
    loads = []
    for n, (start, end) in enumerate([(0, 1024 + block), (1024 + block, half), (half, at.shape[0])]):
        rows = pl.ds(start, end - start)
        loads.append(pltpu.make_async_copy(at_any.at[rows], at.at[rows], sems.at[n]))
        loads[-1].start()
    return loads


def add_lists(parents, slots, loads, at, cells, table8, sums):
    lanes = cells.shape[1]
    words = 128 * SEGMENT
    per_block = 128 // GROUP

    def step(length, n, carry):
        @pl.when(n == per_block)
        def _():
            loads[1].wait()

        first = 1024 + (n // per_block) * (2 * words) + (n % per_block) * GROUP
        totals = []
        for k in range(GROUP):
            total = [None, None]
            for s in range(length):
                place = first + ((s // SEGMENT) * 2 * parents * SEGMENT + (s % SEGMENT) * 128 + k)
                source = pl.multiple_of(at[place], 8)
                kind = pl.multiple_of(at[place + words], 8)
                term = cells[pl.ds(source, 8), :] * table8[pl.ds(kind, 8), :]
                total[s % 2] = term if total[s % 2] is None else total[s % 2] + term
            totals.append(total[0] + total[1] if length else jnp.zeros((8, lanes), F32))
        for k in range(GROUP):
            sums[pl.ds(pl.multiple_of(at[n * GROUP + k], 8), 8), :] = totals[k]
        return carry

    loads[0].wait()
    start = 0
    for j, length in enumerate(range(0, slots + 1, 2)):
        if length == SEGMENT + 2:
            loads[2].wait()
        end = at[parents + j]
        lax.fori_loop(start, end, functools.partial(step, length), 0)
        start = end


def early_kernel(count, parents, slots, *refs):
    sources = refs[:count]
    at_any, table8, sums, cells, at, sems = refs[count:]
    loads = load_lists(at_any, at, sems)
    expand(sources, cells)
    add_lists(parents, slots, loads, at, cells, table8, sums)


def late_kernel(count, tile_x, tile_y, slots, *refs):
    sources = refs[:count]
    (at_any, table8, early_ref, kept_ref, field_ref, fold_ref, out_hbm,
     cells, sums, lines, at, out_ref, list_sems, sems) = refs[count:]
    parents_x, parents_y = tile_x // 2, tile_y // 2
    parents = parents_x * parents_y
    lanes = table8.shape[1]
    loads = load_lists(at_any, at, list_sems)
    expand(sources, cells)
    add_lists(parents, slots, loads, at, cells, table8, sums)
    raw = (sums[...] + early_ref[...]).reshape(parents // 2, 2, 8, lanes)
    one, other = raw[:, 0], raw[:, 1]
    line = lax.broadcasted_iota(jnp.int32, one.shape, 1)
    with_real = jnp.where(line < 4, one, pltpu.roll(other, 4, axis=1))
    with_imag = jnp.where(line < 4, pltpu.roll(one, 4, axis=1), other)
    turned = jnp.where(line % 4 < 2, -pltpu.roll(with_imag, 6, axis=1), pltpu.roll(with_imag, 2, axis=1))
    lines[...] = (with_real + turned).reshape(4 * parents, lanes)
    ordered = [lines[pl.ds(place, parents, stride=4), :].astype(BF16) for place in range(4)]
    incoming = jnp.concatenate(ordered, axis=1)
    fields = [mm(incoming, fold_ref[child]) for child in range(4)]
    stores = []
    for half in range(2):
        first, size = half * parents // 2, parents // 2
        rows = slice(first, first + size)
        for child in range(4):
            mask = kept_ref[child, rows, :]
            for part in range(2):
                value = fields[child][rows, part * lanes : (part + 1) * lanes]
                value = (value + field_ref[part, child, rows, :]) * mask
                for p in range(parents_x // 2):
                    line = (2 * (half * parents_x // 2 + p) + child // 2) * tile_y + child % 2
                    out_ref[pl.ds(2 * line + part, parents_y, stride=4), :] = value[
                        p * parents_y : (p + 1) * parents_y
                    ]
        size = out_ref.shape[0] // 2
        rows = pl.ds(half * size, size)
        stores.append(pltpu.make_async_copy(out_ref.at[rows], out_hbm.at[rows], sems.at[half]))
        stores[-1].start()
    for store in stores:
        store.wait()


def swap(low, high, axis, other=None):
    count = lax.axis_size(axis)
    lows = [(i, i ^ 1) for i in range(count)]
    highs = [(i, (((i + 1) % count ^ 1) - 1) % count) for i in range(count)]
    if other is not None:
        breadth = lax.axis_size(other)
        highs = [
            (i * breadth + j, i * breadth + (j ^ 1) if i in (0, count - 1) else target * breadth + j)
            for i, target in highs
            for j in range(breadth)
        ]
    return lax.ppermute(low, axis, lows), lax.ppermute(high, axis if other is None else (axis, other), highs)


def body(
    currents, box_count, aggregate, near_blocks, low_translator, child_to_parent, coarse_list,
    coarse_kind, coarse_count, up_translator, parent_to_child, receive_map,
):
    tile_x, tile_y = box_count.shape
    boxes = tile_x * tile_y
    lanes = currents.shape[-1]
    parents_x, parents_y, slots = coarse_list.shape
    parents = parents_x * parents_y
    kinds, _, half = up_translator.shape
    wide = 2 * half
    chunks = lax.axis_size("gy")
    in_hbm = pl.BlockSpec(memory_space=pltpu.HBM)

    edge = jax.ShapeDtypeStruct((2 * tile_x, 2 * lanes), BF16)
    edge = jax.ShapeDtypeStruct((2 * tile_x, 2 * lanes), BF16)
    width = tile_y + 2 * LEFT
    live, kept, low, high, agg_near, up_near = pl.pallas_call(
        functools.partial(live_kernel, tile_x, tile_y),
        name="live",
        out_shape=[
            jax.ShapeDtypeStruct((boxes, 2 * lanes), BF16),
            jax.ShapeDtypeStruct((boxes, lanes), F32),
            edge,
            edge,
            jax.ShapeDtypeStruct((2 * lanes, 2 * lanes), BF16),
            jax.ShapeDtypeStruct((8 * lanes, wide), BF16),
        ],
        in_specs=[in_hbm] * 4,
        out_specs=vmem(6),
        scratch_shapes=[
            pltpu.VMEM((2 * boxes, lanes), BF16),
            pltpu.VMEM((tile_x, tile_y), jnp.int32),
            pltpu.VMEM((2 * boxes, lanes), F32),
            pltpu.SemaphoreType.DMA((4,)),
        ],
        compiler_params=params(10),
        cost_estimate=cost(100 * MIB, 3 * MIB),
    )(
        hbm(currents.reshape(2 * boxes, lanes)), hbm(box_count), hbm(aggregate),
        hbm(child_to_parent.reshape(8 * lanes, wide)),
    )
    coarse, pats = pl.pallas_call(
        functools.partial(parents_kernel, tile_x, tile_y),
        name="parents",
        out_shape=[
            jax.ShapeDtypeStruct((4 * parents, wide // 4), BF16),
            jax.ShapeDtypeStruct((3, tile_x * width, lanes), F32),
        ],
        in_specs=vmem(3),
        out_specs=vmem(2),
        scratch_shapes=[
            pltpu.VMEM((2, boxes, lanes), F32),
            pltpu.VMEM((4 * parents, wide // 4), F32),
        ],
        compiler_params=params(10),
        cost_estimate=cost(200 * MIB, 3 * MIB),
    )(live, agg_near, up_near)
    inner_y, outer_y = swap(low, high, "gy")
    sources = [coarse] + [
        lax.ppermute(coarse, "gy", [(i, i ^ d) for i in range(chunks)])
        for d in [chunks - 1] + list(range(1, chunks - 1))
    ]

    rim = 2 * tile_y + 8
    rim += -rim % 16
    low, high = pl.pallas_call(
        functools.partial(rims_kernel, tile_x, tile_y),
        name="rims",
        out_shape=[jax.ShapeDtypeStruct((rim, 2 * lanes), BF16)] * 2,
        in_specs=vmem(3),
        out_specs=vmem(2),
        scratch_shapes=[pltpu.VMEM((rim, 2 * lanes), F32)] * 2,
        compiler_params=params(10),
        cost_estimate=cost(1 * MIB, MIB),
    )(live, inner_y, outer_y)
    inner_x, outer_x = swap(low, high, "gx", "gy")
    live, coarse_count, _ = lax.optimization_barrier((live, coarse_count, low))

    near_rows = near_blocks.reshape(3, 6 * lanes, 2 * lanes)
    low_rows = low_translator.reshape(-1, lanes)
    pair = [jax.ShapeDtypeStruct((2, boxes, lanes), F32)] * 2
    lower, near = pl.pallas_call(
        functools.partial(local_kernel, tile_x, tile_y),
        name="local",
        out_shape=pair,
        in_specs=vmem(4),
        out_specs=vmem(2),
        scratch_shapes=[
            pltpu.VMEM((2, tile_x * width, lanes), F32),
            pltpu.VMEM(((tile_x + 2) * tile_y, 6 * lanes), BF16),
            pltpu.VMEM((3 * len(OFFSETS), 8, lanes), F32),
            pltpu.VMEM((3, tile_x, 8, lanes), F32),
        ],
        compiler_params=params(10),
        cost_estimate=cost(2000 * MIB, 5 * MIB),
    )(live, pats, near_rows, low_rows)

    table = up_translator.reshape(kinds, 2, 2, half // 2).transpose(0, 2, 1, 3).reshape(4 * kinds, half // 2)
    places = jax.ShapeDtypeStruct((8 + 2 * slots * parents // 128, 128), jnp.int32)
    early_at, late_at, table8, fold = pl.pallas_call(
        functools.partial(order_kernel, chunks, kinds, parents_x, parents_y),
        name="order",
        out_shape=[
            places,
            places,
            jax.ShapeDtypeStruct((8 * kinds + 8, half // 2), F32),
            jax.ShapeDtypeStruct((4, wide, 2 * lanes), BF16),
        ],
        in_specs=vmem(6),
        out_specs=vmem(4),
        scratch_shapes=[pltpu.VMEM((parents, 128), F32)],
        compiler_params=params(10),
        cost_estimate=cost(300 * MIB, MIB),
    )(
        coarse_list.reshape(parents, slots), coarse_kind.reshape(parents, slots), coarse_count, table,
        parent_to_child, receive_map,
    )
    early_at, late_at = early_at.reshape(-1), late_at.reshape(-1)
    anywhere = pl.BlockSpec(memory_space=pl.ANY)
    early, late = sources[:2], sources[2:]
    early_sums = pl.pallas_call(
        functools.partial(early_kernel, len(early), parents, slots),
        name="early",
        out_shape=jax.ShapeDtypeStruct((8 * parents, wide // 4), F32),
        in_specs=vmem(len(early)) + [anywhere] + vmem(1),
        out_specs=pl.BlockSpec(memory_space=pltpu.VMEM),
        scratch_shapes=[
            pltpu.VMEM((len(early) * parents * 8, wide // 4), F32),
            pltpu.SMEM(early_at.shape, jnp.int32),
            pltpu.SemaphoreType.DMA((3,)),
        ],
        compiler_params=params(10),
        cost_estimate=cost(1000 * MIB, 4 * MIB),
    )(*early, early_at, table8)
    lower, near, _ = lax.optimization_barrier((lower, near, early_sums))
    field, kept = pl.pallas_call(
        functools.partial(halos_kernel, tile_x, tile_y),
        name="halos",
        out_shape=[
            jax.ShapeDtypeStruct((2, 4, parents, lanes), F32),
            jax.ShapeDtypeStruct((4, parents, lanes), F32),
        ],
        in_specs=vmem(11),
        out_specs=vmem(2),
        scratch_shapes=[
            pltpu.VMEM((4, 4, tile_x + 16, lanes), F32),
            pltpu.VMEM((4, 4 * width, lanes), F32),
            pltpu.VMEM((tile_x, lanes), F32),
            pltpu.VMEM((2, 4, parents, lanes), F32),
        ],
        compiler_params=params(10),
        cost_estimate=cost(100 * MIB, 5 * MIB),
    )(inner_y, outer_y, inner_x, outer_x, agg_near, near_rows, low_rows, receive_map, lower, near, kept)

    out = pl.pallas_call(
        functools.partial(late_kernel, len(late), tile_x, tile_y, slots),
        name="late",
        out_shape=jax.ShapeDtypeStruct((2 * boxes, lanes), F32),
        in_specs=vmem(len(late)) + [anywhere] + vmem(5),
        out_specs=in_hbm,
        scratch_shapes=[
            pltpu.VMEM((len(late) * parents * 8, wide // 4), F32),
            pltpu.VMEM((8 * parents, wide // 4), F32),
            pltpu.VMEM((4 * parents, wide // 4), F32),
            pltpu.SMEM(late_at.shape, jnp.int32),
            pltpu.VMEM((2 * boxes, lanes), F32),
            pltpu.SemaphoreType.DMA((3,)),
            pltpu.SemaphoreType.DMA((2,)),
        ],
        compiler_params=params(16 if chunks <= 4 else 40),
        cost_estimate=cost(2000 * MIB, 8 * MIB),
    )(*late, late_at, table8, early_sums, kept, field, fold)
    return out.reshape(tile_x, tile_y, 2, lanes)


def solution(mesh):
    tiles = P("gx", "gy")
    in_specs = (tiles, tiles, P(), P(), P(), P(), tiles, tiles, tiles, P(), P(), P())
    return jax.shard_map(body, mesh=mesh, in_specs=in_specs, out_specs=tiles, check_vma=False)
```

```python
import functools

import jax
import jax.numpy as jnp
from jax import lax
from jax.experimental import pallas as pl
from jax.experimental.pallas import tpu as pltpu
from jax.sharding import PartitionSpec as P

F32 = jnp.float32
BF16 = jnp.bfloat16
MIB = 1 << 20


def vmem(count):
    return [pl.BlockSpec(memory_space=pltpu.VMEM)] * count


def hbm(array):
    return pltpu.with_memory_space_constraint(array, pltpu.HBM)


def params(mib):
    return pltpu.CompilerParams(vmem_limit_bytes=mib * MIB)


def cost(macs, moved):
    return pl.CostEstimate(flops=2 * macs, bytes_accessed=moved, transcendentals=0)


def mm(left, right):
    return jnp.dot(left, right, preferred_element_type=F32)


def count_rows(counts_ref, tile_x, tile_y, lanes):
    eye = lax.broadcasted_iota(jnp.int32, (tile_y, tile_y), 0) == lax.broadcasted_iota(
        jnp.int32, (tile_y, tile_y), 1
    )
    counts = counts_ref[...].astype(F32)
    diag = [
        jnp.where(eye, jnp.broadcast_to(counts[i : i + 1], (tile_y, tile_y)), 0.0) for i in range(tile_x)
    ]
    return mm(jnp.concatenate(diag, axis=0).astype(BF16), jnp.ones((tile_y, lanes), BF16))


def halo_pair(inner_ref, outer_ref, axis):
    at = lax.axis_index(axis)
    odd = at % 2 == 1
    inner, outer = inner_ref[...].astype(F32), outer_ref[...].astype(F32)
    before, after = jnp.where(odd, inner, outer), jnp.where(odd, outer, inner)
    return jnp.where(at > 0, before, 0.0), jnp.where(at < lax.axis_size(axis) - 1, after, 0.0)


LEFT = 8


def live_kernel(tile_x, tile_y, cur_hbm, counts_hbm, agg_hbm, up_hbm,
                live_ref, kept_ref, low_ref, high_ref, agg_ref, up_ref, cur_ref, counts_ref, wide, sems):
    pairs = [(counts_hbm, counts_ref), (cur_hbm, cur_ref), (agg_hbm, agg_ref), (up_hbm, up_ref)]
    loads = [
        pltpu.make_async_copy(source, target, sems.at[k]) for k, (source, target) in enumerate(pairs)
    ]
    for load in loads:
        load.start()
    lanes = cur_ref.shape[1]
    boxes = tile_x * tile_y
    loads[0].wait()
    limits = count_rows(counts_ref, tile_x, tile_y, lanes)
    keep = lax.broadcasted_iota(jnp.int32, (boxes, lanes), 1).astype(F32) < limits
    kept_ref[...] = jnp.where(keep, 1.0, 0.0)
    odd = lax.axis_index("gy") % 2 == 1
    loads[1].wait()
    wide[...] = cur_ref[...].astype(F32)
    for part in range(2):
        cols = slice(part * lanes, (part + 1) * lanes)
        live_ref[:, cols] = jnp.where(keep, wide[pl.ds(part, boxes, stride=2), :], 0.0).astype(BF16)

        def edge(column):
            rows = wide[pl.ds(2 * column + part, tile_x, stride=2 * tile_y), :]
            return rows * kept_ref[pl.ds(column, tile_x, stride=tile_y), :]

        first = jnp.concatenate([edge(0), edge(1)], axis=0).astype(BF16)
        last = jnp.concatenate([edge(tile_y - 2), edge(tile_y - 1)], axis=0).astype(BF16)
        low_ref[:, cols] = jnp.where(odd, first, last)
        high_ref[:, cols] = jnp.where(odd, last, first)
    for load in loads[2:]:
        load.wait()


def rims_kernel(tile_x, tile_y, live_ref, inner_ref, outer_ref, low_ref, high_ref, first, last):
    odd = lax.axis_index("gx") % 2 == 1
    sides = halo_pair(inner_ref, outer_ref, "gy")
    for rim, start in ((first, 0), (last, tile_x - 2)):
        rim[0 : 2 * tile_y, :] = live_ref[start * tile_y : (start + 2) * tile_y, :].astype(F32)
        place = 2 * tile_y
        for side in sides:
            for column in range(2):
                at = column * tile_x + start
                rim[place : place + 2, :] = side[at : at + 2]
                place += 2
        rim[place:, :] = jnp.zeros((rim.shape[0] - place, rim.shape[1]), F32)
    low_ref[...] = jnp.where(odd, first[...], last[...]).astype(BF16)
    high_ref[...] = jnp.where(odd, last[...], first[...]).astype(BF16)


def parents_kernel(tile_x, tile_y, live_ref, agg_ref, up_ref, coarse_ref, pats_ref, pats, rows4):
    lanes = pats.shape[2]
    width = tile_y + 2 * LEFT
    pattern = mm(live_ref[...], agg_ref[...])
    pats[0] = pattern[:, :lanes]
    pats[1] = pattern[:, lanes:]
    children = []
    for side_x in range(2):
        for side_y in range(2):
            for part in range(2):
                rows = [
                    pats[part, pl.ds((2 * p + side_x) * tile_y + side_y, tile_y // 2, stride=2), :]
                    for p in range(tile_x // 2)
                ]
                children.append(jnp.concatenate(rows, axis=0).astype(BF16))
    coarse = mm(jnp.concatenate(children, axis=1), up_ref[...])
    for place in range(4):
        rows4[pl.ds(place, coarse.shape[0], stride=4), :] = coarse[:, place * 128 : (place + 1) * 128]
    coarse_ref[...] = rows4[...].astype(BF16)
    pattern = pattern.astype(BF16).astype(F32)
    values = [pattern[:, :lanes], pattern[:, lanes:], pattern[:, :lanes] + pattern[:, lanes:]]
    none = jnp.zeros((LEFT, lanes), F32)
    for i in range(tile_x):
        base = i * width
        for k in range(3):
            pats_ref[k, base : base + LEFT, :] = none
            pats_ref[k, base + LEFT : base + LEFT + tile_y, :] = values[k][i * tile_y : (i + 1) * tile_y]
            pats_ref[k, base + LEFT + tile_y : base + width, :] = none


OFFSETS = [(dx, dy) for dx in range(-2, 3) for dy in range(-2, 3) if max(abs(dx), abs(dy)) == 2]


def local_kernel(
    tile_x, tile_y, live_ref, pats, near_ref, low_ref, lower_ref, field_ref, cells, shifted, tables, sums,
):
    lanes = lower_ref.shape[2]
    width = tile_y + 2 * LEFT
    none = jnp.zeros((LEFT, lanes), F32)
    ends = jnp.zeros((tile_y, 6 * lanes), BF16)
    shifted[0:tile_y, :] = ends
    shifted[(tile_x + 1) * tile_y : (tile_x + 2) * tile_y, :] = ends
    shifted[tile_y : (tile_x + 1) * tile_y, 2 * lanes : 4 * lanes] = live_ref[...]
    for part in range(2):
        cols = slice(part * lanes, (part + 1) * lanes)
        for i in range(tile_x):
            base = i * width
            cells[part, base : base + LEFT, :] = none
            cells[part, base + LEFT : base + LEFT + tile_y, :] = live_ref[
                i * tile_y : (i + 1) * tile_y, cols
            ].astype(F32)
            cells[part, base + LEFT + tile_y : base + width, :] = none
            for shift in (-1, 1):
                place = (2 * (shift + 1) + part) * lanes
                shifted[(i + 1) * tile_y : (i + 2) * tile_y, place : place + lanes] = cells[
                    part, base + LEFT + shift : base + LEFT + shift + tile_y, :
                ].astype(BF16)
    for k in range(len(OFFSETS)):
        t_real, t_imag = low_ref[2 * k : 2 * k + 1, :], low_ref[2 * k + 1 : 2 * k + 2, :]
        for n, value in enumerate((t_imag - t_real, t_imag + t_real, t_real)):
            tables[3 * k + n] = jnp.broadcast_to(value, (8, lanes))

    passes = [
        [(dx, dy) for dx, dy in OFFSETS if dy == -2],
        [(dx, dy) for dx, dy in OFFSETS if dy == 2],
        [(dx, dy) for dx, dy in OFFSETS if abs(dy) < 2],
    ]
    blocks = tile_y // 8
    size = tile_x * tile_y // blocks

    def block(b, carry):
        total = None
        for shift in range(3):
            start = pl.multiple_of(b * size + shift * tile_y, tile_y)
            term = mm(shifted[pl.ds(start, size), :], near_ref[shift])
            total = term if total is None else total + term
        start = pl.multiple_of(b * size, size)
        field_ref[0, pl.ds(start, size), :] = total[:, :lanes]
        field_ref[1, pl.ds(start, size), :] = total[:, lanes:]
        shift_y = pl.multiple_of(b * 8, 8)
        for number, offsets in enumerate(passes):
            running = {}
            for row in range(tile_x):
                for dy in sorted({dy for _, dy in offsets}):
                    rows = pl.ds(shift_y + (row * width + LEFT + dy), 8)
                    source = [pats[k, rows, :] for k in range(3)]
                    for dx in range(-2, 3):
                        i = row - dx
                        if (dx, dy) not in offsets or not 0 <= i < tile_x:
                            continue
                        k = OFFSETS.index((dx, dy))
                        if i not in running:
                            running[i] = [None] * 3 if number == 0 else [sums[n, i] for n in range(3)]
                        running[i] = [
                            tables[3 * k + n] * source[n]
                            if running[i][n] is None
                            else running[i][n] + tables[3 * k + n] * source[n]
                            for n in range(3)
                        ]
                for i in sorted(running):
                    if i + 2 <= row or row == tile_x - 1:
                        value = running.pop(i)
                        if number < 2:
                            for n in range(3):
                                sums[n, i] = value[n]
                        else:
                            place = pl.ds(pl.multiple_of(shift_y + i * tile_y, 8), 8)
                            lower_ref[0, place, :] = value[2] - value[1]
                            lower_ref[1, place, :] = value[2] + value[0]
        return carry

    lax.fori_loop(0, blocks, block, 0)


def halos_kernel(
    tile_x, tile_y, inner_y, outer_y, inner_x, outer_x, agg_ref, near_ref, low_ref, recv_ref,
    lower_in, field_in, kept_in, field_ref, kept_ref, columns, rims, line_ref, lower_ref,
):
    lanes = lower_in.shape[2]
    width = tile_y + 2 * LEFT
    halo = halo_pair(inner_y, outer_y, "gy") + halo_pair(inner_x, outer_x, "gx")
    half_x, half_y = tile_x // 2, tile_y // 2
    for child in range(4):
        for p in range(half_x):
            rows = slice(p * half_y, (p + 1) * half_y)
            boxes = pl.ds((2 * p + child // 2) * tile_y + child % 2, half_y, stride=2)
            for part in range(2):
                lower_ref[part, child, rows, :] = lower_in[part, boxes, :]
                field_ref[part, child, rows, :] = field_in[part, boxes, :]
            kept_ref[child, rows, :] = kept_in[boxes, :]

    def add_column(ref, part, box, value):
        line_ref[...] = value
        for side_x in range(2):
            child, rows = 2 * side_x + box % 2, pl.ds(box // 2, half_x, stride=half_y)
            ref[part, child, rows, :] = ref[part, child, rows, :] + line_ref[pl.ds(side_x, half_x, stride=2), :]

    def add_row(ref, part, box, value):
        line_ref[...] = value
        for side_y in range(2):
            child, rows = 2 * (box % 2) + side_y, slice(box // 2 * half_y, (box // 2 + 1) * half_y)
            ref[part, child, rows, :] = ref[part, child, rows, :] + line_ref[pl.ds(side_y, half_y, stride=2), :]

    halo = jnp.concatenate(halo, axis=0)
    pattern = mm(halo.astype(BF16), agg_ref[...]).astype(BF16).astype(F32)
    values = [halo[:, :lanes], halo[:, lanes:], pattern[:, :lanes], pattern[:, lanes:]]
    two = jnp.zeros((8, lanes), F32)
    rim_size = inner_x.shape[0]
    for n, value in enumerate(values):
        for side in range(2):
            for c in range(2):
                at = (2 * side + c) * tile_x
                columns[n, 2 * side + c, 0:8, :] = two
                columns[n, 2 * side + c, 8 : 8 + tile_x, :] = value[at : at + tile_x]
                columns[n, 2 * side + c, 8 + tile_x : 16 + tile_x, :] = two
        for end in range(2):
            at = 4 * tile_x + end * rim_size
            corner = at + 2 * tile_y
            for row in range(2):
                base = (2 * end + row) * width + LEFT
                rims[n, base : base + tile_y, :] = value[at + row * tile_y : at + (row + 1) * tile_y]
                for side in range(2):
                    for c in range(2):
                        place = base + (tile_y + c if side else c - 2)
                        line = corner + 4 * side + 2 * c + row
                        rims[n, place : place + 1, :] = value[line : line + 1]

    def translate(terms):
        first = second = 0.0
        for dx, dy, real, imag in terms:
            k = OFFSETS.index((dx, dy))
            t_real, t_imag = low_ref[2 * k : 2 * k + 1, :], low_ref[2 * k + 1 : 2 * k + 2, :]
            first = first + (t_real * real - t_imag * imag)
            second = second + (t_real * imag + t_imag * real)
        return first, second

    def column(n, side, c, dx):
        return columns[n, 2 * side + c, 8 + dx : 8 + dx + tile_x, :]

    def rim(n, end, row, dy):
        base = (2 * end + row) * width + LEFT + dy
        return rims[n, base : base + tile_y, :]

    for side in range(2):
        for box in ((tile_y - 1, tile_y - 2) if side else (0, 1)):
            terms = []
            for c in range(2):
                dy = (tile_y + c if side else c - 2) - box
                for dx in range(-2, 3):
                    if (dx, dy) in OFFSETS:
                        terms.append((dx, dy, column(2, side, c, dx), column(3, side, c, dx)))
            for part, value in enumerate(translate(terms)):
                add_column(lower_ref, part, box, value)
        source = jnp.concatenate(
            [column(part, side, 1 - side, dx) for dx in range(-1, 2) for part in range(2)], axis=1
        ).astype(BF16)
        weights = [near_ref[dx, (4 * side) * lanes : (4 * side + 2) * lanes, :] for dx in range(3)]
        value = mm(source, jnp.concatenate(weights, axis=0))
        for part in range(2):
            add_column(field_ref, part, tile_y - 1 if side else 0, value[:, part * lanes : (part + 1) * lanes])
    for end in range(2):
        for box in ((tile_x - 1, tile_x - 2) if end else (0, 1)):
            terms = []
            for row in range(2):
                dx = (tile_x + row if end else row - 2) - box
                for dy in range(-2, 3):
                    if (dx, dy) in OFFSETS:
                        terms.append((dx, dy, rim(2, end, row, dy), rim(3, end, row, dy)))
            for part, value in enumerate(translate(terms)):
                add_row(lower_ref, part, box, value)
        source = jnp.concatenate(
            [rim(part, end, 1 - end, dy) for dy in range(-1, 2) for part in range(2)], axis=1
        ).astype(BF16)
        value = mm(source, near_ref[2 * end])
        for part in range(2):
            add_row(field_ref, part, tile_x - 1 if end else 0, value[:, part * lanes : (part + 1) * lanes])
    for child in range(4):
        total = jnp.concatenate([lower_ref[part, child] for part in range(2)], axis=1).astype(BF16)
        value = mm(total, recv_ref[...])
        for part in range(2):
            field_ref[part, child] = field_ref[part, child] + value[:, part * lanes : (part + 1) * lanes]


GROUP = 8
SEGMENT = 8


def order_kernel(
    chunks, kinds, parents_x, parents_y, list_ref, kind_ref, count_ref, table_ref, down_ref, recv_ref,
    early_ref, late_ref, table8, fold_ref, words
):
    for child in range(4):
        fold_ref[child] = mm(down_ref[child], recv_ref[...]).astype(BF16)
    width = table_ref.shape[1]
    for place, row in enumerate((0, 2, 0, 2, 1, 3, 1, 3)):
        table8[pl.ds(place, kinds, stride=8), :] = table_ref[pl.ds(row, kinds, stride=4), :]
    table8[8 * kinds : 8 * kinds + 8, :] = jnp.zeros((8, width), F32)
    parents = parents_x * parents_y
    slots = list_ref.shape[1]
    lanes = early_ref.shape[1]
    across = parents_y * chunks
    entry = list_ref[...]
    line, place = entry // across, entry % across
    chunk = (place // parents_y) ^ lax.axis_index("gy")
    is_late = (chunk > 0) & (chunk < chunks - 1)
    chunk = jnp.where(is_late, chunk - 1, jnp.where(chunk > 0, 1, 0))
    source = chunk * parents + line * parents_y + place % parents_y
    column = count_rows(count_ref, parents_x, parents_y, slots)
    used = lax.broadcasted_iota(jnp.int32, (parents, slots), 1).astype(F32) < column
    part = jnp.where(used, jnp.where(is_late, 2, 1), 0)
    words[:, 0:slots] = (source * 128 + kind_ref[...] + part * (1 << 20)).astype(F32)
    turned = words[...].T[0:slots].astype(jnp.int32)
    word, turned_part = turned & ((1 << 20) - 1), turned >> 20

    down = lax.broadcasted_iota(jnp.int32, (parents, parents), 0)
    along = lax.broadcasted_iota(jnp.int32, (parents, parents), 1)
    earlier = lax.broadcasted_iota(jnp.int32, (slots, slots), 1) < lax.broadcasted_iota(jnp.int32, (slots, slots), 0)
    earlier = jnp.where(earlier, 1.0, 0.0).astype(BF16)
    slot = lax.broadcasted_iota(jnp.int32, (slots, parents), 0)
    most = (2 * lax.broadcasted_iota(jnp.int32, (parents, lanes), 1)).astype(F32)
    for number, at_ref in ((1, early_ref), (2, late_ref)):
        hit = jnp.where(turned_part == number, 1.0, 0.0)
        mine = jnp.where(part == number, 1.0, 0.0).astype(BF16)
        column = mm(mine, jnp.ones((slots, parents), BF16))
        row = jnp.sum(hit, axis=0, keepdims=True)
        before = (column < row) | ((column == row) & (down < along))
        rank = jnp.sum(jnp.where(before, 1.0, 0.0), axis=0, keepdims=True)
        place = mm(earlier, hit.astype(BF16)).astype(jnp.int32)
        place = jnp.where(turned_part == number, place, -1)
        dense = jnp.zeros((slots, parents), jnp.int32)
        for n in range(slots):
            dense = dense + jnp.where(place[n : n + 1] == slot, word[n : n + 1], 0)
        kind = jnp.where(slot.astype(F32) < row, dense & 127, kinds)
        source = dense >> 7
        values = [source >> 8, source & 255, kind, along[0:slots]]
        values = jnp.concatenate([value.astype(F32) for value in values], axis=0).astype(BF16)
        ranked = jnp.where(down.astype(F32) == rank, 1.0, 0.0).astype(BF16)
        moved = lax.dot_general(values, ranked, (((1,), (1,)), ((), ())), preferred_element_type=F32)
        high, low, kind, parent = [
            moved[n * slots : (n + 1) * slots].astype(jnp.int32) * 8 for n in range(4)
        ]
        reach = jnp.sum(jnp.where(column[:, :lanes] <= most, 1.0, 0.0), axis=0, keepdims=True).astype(jnp.int32)
        head = jnp.broadcast_to(reach // GROUP, (8, lanes))
        line = lax.broadcasted_iota(jnp.int32, (8, lanes), 0)
        for n in range(parents // lanes):
            head = jnp.where(line == n, parent[0:8, n * lanes : (n + 1) * lanes], head)
        at_ref[0:8, :] = head
        at = 8
        for segment in range(0, slots, SEGMENT):
            for n in range(parents // lanes):
                for value in (high * 256 + low, kind):
                    at_ref[at : at + SEGMENT, :] = value[segment : segment + SEGMENT, n * lanes : (n + 1) * lanes]
                    at += SEGMENT


def expand(sources, cells):
    lanes = cells.shape[1]
    count = sources[0].shape[0] // 8
    pairs = cells.reshape(len(sources) * count, 2, 8, lanes)
    upper = lax.broadcasted_iota(jnp.int32, (count, 8, lanes), 1) < 4
    for c, source in enumerate(sources):
        rows = source[...].astype(F32).reshape(count, 8, lanes)
        turned = pltpu.roll(rows, 4, axis=1)
        pairs[c * count : (c + 1) * count, 0] = jnp.where(upper, rows, turned)
        pairs[c * count : (c + 1) * count, 1] = jnp.where(upper, turned, rows)


def load_lists(at_any, at, sems):
    block = 2 * 128 * SEGMENT
    half = 1024 + (at.shape[0] - 1024) // 2
    loads = []
    for n, (start, end) in enumerate([(0, 1024 + block), (1024 + block, half), (half, at.shape[0])]):
        rows = pl.ds(start, end - start)
        loads.append(pltpu.make_async_copy(at_any.at[rows], at.at[rows], sems.at[n]))
        loads[-1].start()
    return loads


def add_lists(parents, slots, loads, at, cells, table8, sums):
    lanes = cells.shape[1]
    words = 128 * SEGMENT
    per_block = 128 // GROUP

    def step(length, n, carry):
        @pl.when(n == per_block)
        def _():
            loads[1].wait()

        first = 1024 + (n // per_block) * (2 * words) + (n % per_block) * GROUP
        totals = []
        for k in range(GROUP):
            total = [None, None]
            for s in range(length):
                place = first + ((s // SEGMENT) * 2 * parents * SEGMENT + (s % SEGMENT) * 128 + k)
                source = pl.multiple_of(at[place], 8)
                kind = pl.multiple_of(at[place + words], 8)
                term = cells[pl.ds(source, 8), :] * table8[pl.ds(kind, 8), :]
                total[s % 2] = term if total[s % 2] is None else total[s % 2] + term
            totals.append(total[0] + total[1] if length else jnp.zeros((8, lanes), F32))
        for k in range(GROUP):
            sums[pl.ds(pl.multiple_of(at[n * GROUP + k], 8), 8), :] = totals[k]
        return carry

    loads[0].wait()
    start = 0
    for j, length in enumerate(range(0, slots + 1, 2)):
        if length == SEGMENT + 2:
            loads[2].wait()
        end = at[parents + j]
        lax.fori_loop(start, end, functools.partial(step, length), 0)
        start = end


def early_kernel(count, parents, slots, *refs):
    sources = refs[:count]
    at_any, table8, sums, cells, at, sems = refs[count:]
    loads = load_lists(at_any, at, sems)
    expand(sources, cells)
    add_lists(parents, slots, loads, at, cells, table8, sums)


def late_kernel(count, tile_x, tile_y, slots, *refs):
    sources = refs[:count]
    (at_any, table8, early_ref, kept_ref, field_ref, fold_ref, out_hbm,
     cells, sums, lines, at, out_ref, list_sems, sems) = refs[count:]
    parents_x, parents_y = tile_x // 2, tile_y // 2
    parents = parents_x * parents_y
    lanes = table8.shape[1]
    loads = load_lists(at_any, at, list_sems)
    expand(sources, cells)
    add_lists(parents, slots, loads, at, cells, table8, sums)
    raw = (sums[...] + early_ref[...]).reshape(parents // 2, 2, 8, lanes)
    one, other = raw[:, 0], raw[:, 1]
    line = lax.broadcasted_iota(jnp.int32, one.shape, 1)
    with_real = jnp.where(line < 4, one, pltpu.roll(other, 4, axis=1))
    with_imag = jnp.where(line < 4, pltpu.roll(one, 4, axis=1), other)
    turned = jnp.where(line % 4 < 2, -pltpu.roll(with_imag, 6, axis=1), pltpu.roll(with_imag, 2, axis=1))
    lines[...] = (with_real + turned).reshape(4 * parents, lanes)
    ordered = [lines[pl.ds(place, parents, stride=4), :].astype(BF16) for place in range(4)]
    incoming = jnp.concatenate(ordered, axis=1)
    fields = [mm(incoming, fold_ref[child]) for child in range(4)]
    stores = []
    for half in range(2):
        first, size = half * parents // 2, parents // 2
        rows = slice(first, first + size)
        for child in range(4):
            mask = kept_ref[child, rows, :]
            for part in range(2):
                value = fields[child][rows, part * lanes : (part + 1) * lanes]
                value = (value + field_ref[part, child, rows, :]) * mask
                for p in range(parents_x // 2):
                    line = (2 * (half * parents_x // 2 + p) + child // 2) * tile_y + child % 2
                    out_ref[pl.ds(2 * line + part, parents_y, stride=4), :] = value[
                        p * parents_y : (p + 1) * parents_y
                    ]
        size = out_ref.shape[0] // 2
        rows = pl.ds(half * size, size)
        stores.append(pltpu.make_async_copy(out_ref.at[rows], out_hbm.at[rows], sems.at[half]))
        stores[-1].start()
    for store in stores:
        store.wait()


def swap(low, high, axis, other=None):
    count = lax.axis_size(axis)
    lows = [(i, i ^ 1) for i in range(count)]
    highs = [(i, (((i + 1) % count ^ 1) - 1) % count) for i in range(count)]
    if other is not None:
        breadth = lax.axis_size(other)
        highs = [
            (i * breadth + j, i * breadth + (j ^ 1) if i in (0, count - 1) else target * breadth + j)
            for i, target in highs
            for j in range(breadth)
        ]
    return lax.ppermute(low, axis, lows), lax.ppermute(high, axis if other is None else (axis, other), highs)


def body(
    currents, box_count, aggregate, near_blocks, low_translator, child_to_parent, coarse_list,
    coarse_kind, coarse_count, up_translator, parent_to_child, receive_map,
):
    tile_x, tile_y = box_count.shape
    boxes = tile_x * tile_y
    lanes = currents.shape[-1]
    parents_x, parents_y, slots = coarse_list.shape
    parents = parents_x * parents_y
    kinds, _, half = up_translator.shape
    wide = 2 * half
    chunks = lax.axis_size("gy")
    in_hbm = pl.BlockSpec(memory_space=pltpu.HBM)

    edge = jax.ShapeDtypeStruct((2 * tile_x, 2 * lanes), BF16)
    edge = jax.ShapeDtypeStruct((2 * tile_x, 2 * lanes), BF16)
    width = tile_y + 2 * LEFT
    live, kept, low, high, agg_near, up_near = pl.pallas_call(
        functools.partial(live_kernel, tile_x, tile_y),
        name="live",
        out_shape=[
            jax.ShapeDtypeStruct((boxes, 2 * lanes), BF16),
            jax.ShapeDtypeStruct((boxes, lanes), F32),
            edge,
            edge,
            jax.ShapeDtypeStruct((2 * lanes, 2 * lanes), BF16),
            jax.ShapeDtypeStruct((8 * lanes, wide), BF16),
        ],
        in_specs=[in_hbm] * 4,
        out_specs=vmem(6),
        scratch_shapes=[
            pltpu.VMEM((2 * boxes, lanes), BF16),
            pltpu.VMEM((tile_x, tile_y), jnp.int32),
            pltpu.VMEM((2 * boxes, lanes), F32),
            pltpu.SemaphoreType.DMA((4,)),
        ],
        compiler_params=params(10),
        cost_estimate=cost(100 * MIB, 3 * MIB),
    )(
        hbm(currents.reshape(2 * boxes, lanes)), hbm(box_count), hbm(aggregate),
        hbm(child_to_parent.reshape(8 * lanes, wide)),
    )
    coarse, pats = pl.pallas_call(
        functools.partial(parents_kernel, tile_x, tile_y),
        name="parents",
        out_shape=[
            jax.ShapeDtypeStruct((4 * parents, wide // 4), BF16),
            jax.ShapeDtypeStruct((3, tile_x * width, lanes), F32),
        ],
        in_specs=vmem(3),
        out_specs=vmem(2),
        scratch_shapes=[
            pltpu.VMEM((2, boxes, lanes), F32),
            pltpu.VMEM((4 * parents, wide // 4), F32),
        ],
        compiler_params=params(10),
        cost_estimate=cost(200 * MIB, 3 * MIB),
    )(live, agg_near, up_near)
    inner_y, outer_y = swap(low, high, "gy")
    sources = [coarse] + [
        lax.ppermute(coarse, "gy", [(i, i ^ d) for i in range(chunks)])
        for d in [chunks - 1] + list(range(1, chunks - 1))
    ]

    rim = 2 * tile_y + 8
    rim += -rim % 16
    low, high = pl.pallas_call(
        functools.partial(rims_kernel, tile_x, tile_y),
        name="rims",
        out_shape=[jax.ShapeDtypeStruct((rim, 2 * lanes), BF16)] * 2,
        in_specs=vmem(3),
        out_specs=vmem(2),
        scratch_shapes=[pltpu.VMEM((rim, 2 * lanes), F32)] * 2,
        compiler_params=params(10),
        cost_estimate=cost(1 * MIB, MIB),
    )(live, inner_y, outer_y)
    inner_x, outer_x = swap(low, high, "gx", "gy")
    live, coarse_count, _ = lax.optimization_barrier((live, coarse_count, low))

    near_rows = near_blocks.reshape(3, 6 * lanes, 2 * lanes)
    low_rows = low_translator.reshape(-1, lanes)
    pair = [jax.ShapeDtypeStruct((2, boxes, lanes), F32)] * 2
    lower, near = pl.pallas_call(
        functools.partial(local_kernel, tile_x, tile_y),
        name="local",
        out_shape=pair,
        in_specs=vmem(4),
        out_specs=vmem(2),
        scratch_shapes=[
            pltpu.VMEM((2, tile_x * width, lanes), F32),
            pltpu.VMEM(((tile_x + 2) * tile_y, 6 * lanes), BF16),
            pltpu.VMEM((3 * len(OFFSETS), 8, lanes), F32),
            pltpu.VMEM((3, tile_x, 8, lanes), F32),
        ],
        compiler_params=params(10),
        cost_estimate=cost(2000 * MIB, 5 * MIB),
    )(live, pats, near_rows, low_rows)

    table = up_translator.reshape(kinds, 2, 2, half // 2).transpose(0, 2, 1, 3).reshape(4 * kinds, half // 2)
    places = jax.ShapeDtypeStruct((8 + 2 * slots * parents // 128, 128), jnp.int32)
    early_at, late_at, table8, fold = pl.pallas_call(
        functools.partial(order_kernel, chunks, kinds, parents_x, parents_y),
        name="order",
        out_shape=[
            places,
            places,
            jax.ShapeDtypeStruct((8 * kinds + 8, half // 2), F32),
            jax.ShapeDtypeStruct((4, wide, 2 * lanes), BF16),
        ],
        in_specs=vmem(6),
        out_specs=vmem(4),
        scratch_shapes=[pltpu.VMEM((parents, 128), F32)],
        compiler_params=params(10),
        cost_estimate=cost(300 * MIB, MIB),
    )(
        coarse_list.reshape(parents, slots), coarse_kind.reshape(parents, slots), coarse_count, table,
        parent_to_child, receive_map,
    )
    early_at, late_at = early_at.reshape(-1), late_at.reshape(-1)
    anywhere = pl.BlockSpec(memory_space=pl.ANY)
    early, late = sources[:2], sources[2:]
    early_sums = pl.pallas_call(
        functools.partial(early_kernel, len(early), parents, slots),
        name="early",
        out_shape=jax.ShapeDtypeStruct((8 * parents, wide // 4), F32),
        in_specs=vmem(len(early)) + [anywhere] + vmem(1),
        out_specs=pl.BlockSpec(memory_space=pltpu.VMEM),
        scratch_shapes=[
            pltpu.VMEM((len(early) * parents * 8, wide // 4), F32),
            pltpu.SMEM(early_at.shape, jnp.int32),
            pltpu.SemaphoreType.DMA((3,)),
        ],
        compiler_params=params(10),
        cost_estimate=cost(1000 * MIB, 4 * MIB),
    )(*early, early_at, table8)
    lower, near, _ = lax.optimization_barrier((lower, near, early_sums))
    field, kept = pl.pallas_call(
        functools.partial(halos_kernel, tile_x, tile_y),
        name="halos",
        out_shape=[
            jax.ShapeDtypeStruct((2, 4, parents, lanes), F32),
            jax.ShapeDtypeStruct((4, parents, lanes), F32),
        ],
        in_specs=vmem(11),
        out_specs=vmem(2),
        scratch_shapes=[
            pltpu.VMEM((4, 4, tile_x + 16, lanes), F32),
            pltpu.VMEM((4, 4 * width, lanes), F32),
            pltpu.VMEM((tile_x, lanes), F32),
            pltpu.VMEM((2, 4, parents, lanes), F32),
        ],
        compiler_params=params(10),
        cost_estimate=cost(100 * MIB, 5 * MIB),
    )(inner_y, outer_y, inner_x, outer_x, agg_near, near_rows, low_rows, receive_map, lower, near, kept)

    out = pl.pallas_call(
        functools.partial(late_kernel, len(late), tile_x, tile_y, slots),
        name="late",
        out_shape=jax.ShapeDtypeStruct((2 * boxes, lanes), F32),
        in_specs=vmem(len(late)) + [anywhere] + vmem(5),
        out_specs=in_hbm,
        scratch_shapes=[
            pltpu.VMEM((len(late) * parents * 8, wide // 4), F32),
            pltpu.VMEM((8 * parents, wide // 4), F32),
            pltpu.VMEM((4 * parents, wide // 4), F32),
            pltpu.SMEM(late_at.shape, jnp.int32),
            pltpu.VMEM((2 * boxes, lanes), F32),
            pltpu.SemaphoreType.DMA((3,)),
            pltpu.SemaphoreType.DMA((2,)),
        ],
        compiler_params=params(16 if chunks <= 4 else 40),
        cost_estimate=cost(2000 * MIB, 8 * MIB),
    )(*late, late_at, table8, early_sums, kept, field, fold)
    return out.reshape(tile_x, tile_y, 2, lanes)


def solution(mesh):
    tiles = P("gx", "gy")
    in_specs = (tiles, tiles, P(), P(), P(), P(), tiles, tiles, tiles, P(), P(), P())
    return jax.shard_map(body, mesh=mesh, in_specs=in_specs, out_specs=tiles, check_vma=False)
```

```python
import functools

import jax
import jax.numpy as jnp
from jax import lax
from jax.experimental import pallas as pl
from jax.experimental.pallas import tpu as pltpu
from jax.sharding import PartitionSpec as P

F32 = jnp.float32
BF16 = jnp.bfloat16
MIB = 1 << 20


def vmem(count):
    return [pl.BlockSpec(memory_space=pltpu.VMEM)] * count


def hbm(array):
    return pltpu.with_memory_space_constraint(array, pltpu.HBM)


def params(mib):
    return pltpu.CompilerParams(vmem_limit_bytes=mib * MIB)


def cost(macs, moved):
    return pl.CostEstimate(flops=2 * macs, bytes_accessed=moved, transcendentals=0)


def mm(left, right):
    return jnp.dot(left, right, preferred_element_type=F32)


def count_rows(counts_ref, tile_x, tile_y, lanes):
    eye = lax.broadcasted_iota(jnp.int32, (tile_y, tile_y), 0) == lax.broadcasted_iota(
        jnp.int32, (tile_y, tile_y), 1
    )
    counts = counts_ref[...].astype(F32)
    diag = [
        jnp.where(eye, jnp.broadcast_to(counts[i : i + 1], (tile_y, tile_y)), 0.0) for i in range(tile_x)
    ]
    return mm(jnp.concatenate(diag, axis=0).astype(BF16), jnp.ones((tile_y, lanes), BF16))


def halo_pair(inner_ref, outer_ref, axis):
    at = lax.axis_index(axis)
    odd = at % 2 == 1
    inner, outer = inner_ref[...].astype(F32), outer_ref[...].astype(F32)
    before, after = jnp.where(odd, inner, outer), jnp.where(odd, outer, inner)
    return jnp.where(at > 0, before, 0.0), jnp.where(at < lax.axis_size(axis) - 1, after, 0.0)


LEFT = 8


def live_kernel(tile_x, tile_y, cur_hbm, counts_hbm, agg_hbm, up_hbm,
                live_ref, kept_ref, low_ref, high_ref, agg_ref, up_ref, cur_ref, counts_ref, wide, sems):
    pairs = [(counts_hbm, counts_ref), (cur_hbm, cur_ref), (agg_hbm, agg_ref), (up_hbm, up_ref)]
    loads = [
        pltpu.make_async_copy(source, target, sems.at[k]) for k, (source, target) in enumerate(pairs)
    ]
    for load in loads:
        load.start()
    lanes = cur_ref.shape[1]
    boxes = tile_x * tile_y
    loads[0].wait()
    limits = count_rows(counts_ref, tile_x, tile_y, lanes)
    keep = lax.broadcasted_iota(jnp.int32, (boxes, lanes), 1).astype(F32) < limits
    kept_ref[...] = jnp.where(keep, 1.0, 0.0)
    odd = lax.axis_index("gy") % 2 == 1
    loads[1].wait()
    wide[...] = cur_ref[...].astype(F32)
    for part in range(2):
        cols = slice(part * lanes, (part + 1) * lanes)
        live_ref[:, cols] = jnp.where(keep, wide[pl.ds(part, boxes, stride=2), :], 0.0).astype(BF16)

        def edge(column):
            rows = wide[pl.ds(2 * column + part, tile_x, stride=2 * tile_y), :]
            return rows * kept_ref[pl.ds(column, tile_x, stride=tile_y), :]

        first = jnp.concatenate([edge(0), edge(1)], axis=0).astype(BF16)
        last = jnp.concatenate([edge(tile_y - 2), edge(tile_y - 1)], axis=0).astype(BF16)
        low_ref[:, cols] = jnp.where(odd, first, last)
        high_ref[:, cols] = jnp.where(odd, last, first)
    for load in loads[2:]:
        load.wait()


def rims_kernel(tile_x, tile_y, live_ref, inner_ref, outer_ref, low_ref, high_ref, first, last):
    odd = lax.axis_index("gx") % 2 == 1
    sides = halo_pair(inner_ref, outer_ref, "gy")
    for rim, start in ((first, 0), (last, tile_x - 2)):
        rim[0 : 2 * tile_y, :] = live_ref[start * tile_y : (start + 2) * tile_y, :].astype(F32)
        place = 2 * tile_y
        for side in sides:
            for column in range(2):
                at = column * tile_x + start
                rim[place : place + 2, :] = side[at : at + 2]
                place += 2
        rim[place:, :] = jnp.zeros((rim.shape[0] - place, rim.shape[1]), F32)
    low_ref[...] = jnp.where(odd, first[...], last[...]).astype(BF16)
    high_ref[...] = jnp.where(odd, last[...], first[...]).astype(BF16)


def parents_kernel(tile_x, tile_y, live_ref, agg_ref, up_ref, coarse_ref, pats_ref, pats, rows4):
    lanes = pats.shape[2]
    width = tile_y + 2 * LEFT
    pattern = mm(live_ref[...], agg_ref[...])
    pats[0] = pattern[:, :lanes]
    pats[1] = pattern[:, lanes:]
    children = []
    for side_x in range(2):
        for side_y in range(2):
            for part in range(2):
                rows = [
                    pats[part, pl.ds((2 * p + side_x) * tile_y + side_y, tile_y // 2, stride=2), :]
                    for p in range(tile_x // 2)
                ]
                children.append(jnp.concatenate(rows, axis=0).astype(BF16))
    coarse = mm(jnp.concatenate(children, axis=1), up_ref[...])
    for place in range(4):
        rows4[pl.ds(place, coarse.shape[0], stride=4), :] = coarse[:, place * 128 : (place + 1) * 128]
    coarse_ref[...] = rows4[...].astype(BF16)
    pattern = pattern.astype(BF16).astype(F32)
    values = [pattern[:, :lanes], pattern[:, lanes:], pattern[:, :lanes] + pattern[:, lanes:]]
    none = jnp.zeros((LEFT, lanes), F32)
    for i in range(tile_x):
        base = i * width
        for k in range(3):
            pats_ref[k, base : base + LEFT, :] = none
            pats_ref[k, base + LEFT : base + LEFT + tile_y, :] = values[k][i * tile_y : (i + 1) * tile_y]
            pats_ref[k, base + LEFT + tile_y : base + width, :] = none


OFFSETS = [(dx, dy) for dx in range(-2, 3) for dy in range(-2, 3) if max(abs(dx), abs(dy)) == 2]


def local_kernel(
    tile_x, tile_y, live_ref, pats, near_ref, low_ref, lower_ref, field_ref, cells, shifted, tables, sums,
):
    lanes = lower_ref.shape[2]
    width = tile_y + 2 * LEFT
    none = jnp.zeros((LEFT, lanes), F32)
    ends = jnp.zeros((tile_y, 6 * lanes), BF16)
    shifted[0:tile_y, :] = ends
    shifted[(tile_x + 1) * tile_y : (tile_x + 2) * tile_y, :] = ends
    shifted[tile_y : (tile_x + 1) * tile_y, 2 * lanes : 4 * lanes] = live_ref[...]
    for part in range(2):
        cols = slice(part * lanes, (part + 1) * lanes)
        for i in range(tile_x):
            base = i * width
            cells[part, base : base + LEFT, :] = none
            cells[part, base + LEFT : base + LEFT + tile_y, :] = live_ref[
                i * tile_y : (i + 1) * tile_y, cols
            ].astype(F32)
            cells[part, base + LEFT + tile_y : base + width, :] = none
            for shift in (-1, 1):
                place = (2 * (shift + 1) + part) * lanes
                shifted[(i + 1) * tile_y : (i + 2) * tile_y, place : place + lanes] = cells[
                    part, base + LEFT + shift : base + LEFT + shift + tile_y, :
                ].astype(BF16)
    for k in range(len(OFFSETS)):
        t_real, t_imag = low_ref[2 * k : 2 * k + 1, :], low_ref[2 * k + 1 : 2 * k + 2, :]
        for n, value in enumerate((t_imag - t_real, t_imag + t_real, t_real)):
            tables[3 * k + n] = jnp.broadcast_to(value, (8, lanes))

    passes = [
        [(dx, dy) for dx, dy in OFFSETS if dy == -2],
        [(dx, dy) for dx, dy in OFFSETS if dy == 2],
        [(dx, dy) for dx, dy in OFFSETS if abs(dy) < 2],
    ]
    blocks = tile_y // 8
    size = tile_x * tile_y // blocks

    def block(b, carry):
        total = None
        for shift in range(3):
            start = pl.multiple_of(b * size + shift * tile_y, tile_y)
            term = mm(shifted[pl.ds(start, size), :], near_ref[shift])
            total = term if total is None else total + term
        start = pl.multiple_of(b * size, size)
        field_ref[0, pl.ds(start, size), :] = total[:, :lanes]
        field_ref[1, pl.ds(start, size), :] = total[:, lanes:]
        shift_y = pl.multiple_of(b * 8, 8)
        for number, offsets in enumerate(passes):
            running = {}
            for row in range(tile_x):
                for dy in sorted({dy for _, dy in offsets}):
                    rows = pl.ds(shift_y + (row * width + LEFT + dy), 8)
                    source = [pats[k, rows, :] for k in range(3)]
                    for dx in range(-2, 3):
                        i = row - dx
                        if (dx, dy) not in offsets or not 0 <= i < tile_x:
                            continue
                        k = OFFSETS.index((dx, dy))
                        if i not in running:
                            running[i] = [None] * 3 if number == 0 else [sums[n, i] for n in range(3)]
                        running[i] = [
                            tables[3 * k + n] * source[n]
                            if running[i][n] is None
                            else running[i][n] + tables[3 * k + n] * source[n]
                            for n in range(3)
                        ]
                for i in sorted(running):
                    if i + 2 <= row or row == tile_x - 1:
                        value = running.pop(i)
                        if number < 2:
                            for n in range(3):
                                sums[n, i] = value[n]
                        else:
                            place = pl.ds(pl.multiple_of(shift_y + i * tile_y, 8), 8)
                            lower_ref[0, place, :] = value[2] - value[1]
                            lower_ref[1, place, :] = value[2] + value[0]
        return carry

    lax.fori_loop(0, blocks, block, 0)


def halos_kernel(
    tile_x, tile_y, inner_y, outer_y, inner_x, outer_x, agg_ref, near_ref, low_ref, recv_ref,
    lower_in, field_in, kept_in, field_ref, kept_ref, columns, rims, line_ref, lower_ref,
):
    lanes = lower_in.shape[2]
    width = tile_y + 2 * LEFT
    halo = halo_pair(inner_y, outer_y, "gy") + halo_pair(inner_x, outer_x, "gx")
    half_x, half_y = tile_x // 2, tile_y // 2
    for child in range(4):
        for p in range(half_x):
            rows = slice(p * half_y, (p + 1) * half_y)
            boxes = pl.ds((2 * p + child // 2) * tile_y + child % 2, half_y, stride=2)
            for part in range(2):
                lower_ref[part, child, rows, :] = lower_in[part, boxes, :]
                field_ref[part, child, rows, :] = field_in[part, boxes, :]
            kept_ref[child, rows, :] = kept_in[boxes, :]

    def add_column(ref, part, box, value):
        line_ref[...] = value
        for side_x in range(2):
            child, rows = 2 * side_x + box % 2, pl.ds(box // 2, half_x, stride=half_y)
            ref[part, child, rows, :] = ref[part, child, rows, :] + line_ref[pl.ds(side_x, half_x, stride=2), :]

    def add_row(ref, part, box, value):
        line_ref[...] = value
        for side_y in range(2):
            child, rows = 2 * (box % 2) + side_y, slice(box // 2 * half_y, (box // 2 + 1) * half_y)
            ref[part, child, rows, :] = ref[part, child, rows, :] + line_ref[pl.ds(side_y, half_y, stride=2), :]

    halo = jnp.concatenate(halo, axis=0)
    pattern = mm(halo.astype(BF16), agg_ref[...]).astype(BF16).astype(F32)
    values = [halo[:, :lanes], halo[:, lanes:], pattern[:, :lanes], pattern[:, lanes:]]
    two = jnp.zeros((8, lanes), F32)
    rim_size = inner_x.shape[0]
    for n, value in enumerate(values):
        for side in range(2):
            for c in range(2):
                at = (2 * side + c) * tile_x
                columns[n, 2 * side + c, 0:8, :] = two
                columns[n, 2 * side + c, 8 : 8 + tile_x, :] = value[at : at + tile_x]
                columns[n, 2 * side + c, 8 + tile_x : 16 + tile_x, :] = two
        for end in range(2):
            at = 4 * tile_x + end * rim_size
            corner = at + 2 * tile_y
            for row in range(2):
                base = (2 * end + row) * width + LEFT
                rims[n, base : base + tile_y, :] = value[at + row * tile_y : at + (row + 1) * tile_y]
                for side in range(2):
                    for c in range(2):
                        place = base + (tile_y + c if side else c - 2)
                        line = corner + 4 * side + 2 * c + row
                        rims[n, place : place + 1, :] = value[line : line + 1]

    def translate(terms):
        first = second = 0.0
        for dx, dy, real, imag in terms:
            k = OFFSETS.index((dx, dy))
            t_real, t_imag = low_ref[2 * k : 2 * k + 1, :], low_ref[2 * k + 1 : 2 * k + 2, :]
            first = first + (t_real * real - t_imag * imag)
            second = second + (t_real * imag + t_imag * real)
        return first, second

    def column(n, side, c, dx):
        return columns[n, 2 * side + c, 8 + dx : 8 + dx + tile_x, :]

    def rim(n, end, row, dy):
        base = (2 * end + row) * width + LEFT + dy
        return rims[n, base : base + tile_y, :]

    for side in range(2):
        for box in ((tile_y - 1, tile_y - 2) if side else (0, 1)):
            terms = []
            for c in range(2):
                dy = (tile_y + c if side else c - 2) - box
                for dx in range(-2, 3):
                    if (dx, dy) in OFFSETS:
                        terms.append((dx, dy, column(2, side, c, dx), column(3, side, c, dx)))
            for part, value in enumerate(translate(terms)):
                add_column(lower_ref, part, box, value)
        source = jnp.concatenate(
            [column(part, side, 1 - side, dx) for dx in range(-1, 2) for part in range(2)], axis=1
        ).astype(BF16)
        weights = [near_ref[dx, (4 * side) * lanes : (4 * side + 2) * lanes, :] for dx in range(3)]
        value = mm(source, jnp.concatenate(weights, axis=0))
        for part in range(2):
            add_column(field_ref, part, tile_y - 1 if side else 0, value[:, part * lanes : (part + 1) * lanes])
    for end in range(2):
        for box in ((tile_x - 1, tile_x - 2) if end else (0, 1)):
            terms = []
            for row in range(2):
                dx = (tile_x + row if end else row - 2) - box
                for dy in range(-2, 3):
                    if (dx, dy) in OFFSETS:
                        terms.append((dx, dy, rim(2, end, row, dy), rim(3, end, row, dy)))
            for part, value in enumerate(translate(terms)):
                add_row(lower_ref, part, box, value)
        source = jnp.concatenate(
            [rim(part, end, 1 - end, dy) for dy in range(-1, 2) for part in range(2)], axis=1
        ).astype(BF16)
        value = mm(source, near_ref[2 * end])
        for part in range(2):
            add_row(field_ref, part, tile_x - 1 if end else 0, value[:, part * lanes : (part + 1) * lanes])
    for child in range(4):
        total = jnp.concatenate([lower_ref[part, child] for part in range(2)], axis=1).astype(BF16)
        value = mm(total, recv_ref[...])
        for part in range(2):
            field_ref[part, child] = field_ref[part, child] + value[:, part * lanes : (part + 1) * lanes]


GROUP = 32
SEGMENT = 8


def order_kernel(
    chunks, kinds, parents_x, parents_y, list_ref, kind_ref, count_ref, table_ref, down_ref, recv_ref,
    early_ref, late_ref, table8, fold_ref, words
):
    for child in range(4):
        fold_ref[child] = mm(down_ref[child], recv_ref[...]).astype(BF16)
    width = table_ref.shape[1]
    for place, row in enumerate((0, 2, 0, 2, 1, 3, 1, 3)):
        table8[pl.ds(place, kinds, stride=8), :] = table_ref[pl.ds(row, kinds, stride=4), :]
    table8[8 * kinds : 8 * kinds + 8, :] = jnp.zeros((8, width), F32)
    parents = parents_x * parents_y
    slots = list_ref.shape[1]
    lanes = early_ref.shape[1]
    across = parents_y * chunks
    entry = list_ref[...]
    line, place = entry // across, entry % across
    chunk = (place // parents_y) ^ lax.axis_index("gy")
    is_late = (chunk > 0) & (chunk < chunks - 1)
    chunk = jnp.where(is_late, chunk - 1, jnp.where(chunk > 0, 1, 0))
    source = chunk * parents + line * parents_y + place % parents_y
    column = count_rows(count_ref, parents_x, parents_y, slots)
    used = lax.broadcasted_iota(jnp.int32, (parents, slots), 1).astype(F32) < column
    part = jnp.where(used, jnp.where(is_late, 2, 1), 0)
    words[:, 0:slots] = (source * 128 + kind_ref[...] + part * (1 << 20)).astype(F32)
    turned = words[...].T[0:slots].astype(jnp.int32)
    word, turned_part = turned & ((1 << 20) - 1), turned >> 20

    down = lax.broadcasted_iota(jnp.int32, (parents, parents), 0)
    along = lax.broadcasted_iota(jnp.int32, (parents, parents), 1)
    earlier = lax.broadcasted_iota(jnp.int32, (slots, slots), 1) < lax.broadcasted_iota(jnp.int32, (slots, slots), 0)
    earlier = jnp.where(earlier, 1.0, 0.0).astype(BF16)
    slot = lax.broadcasted_iota(jnp.int32, (slots, parents), 0)
    most = (2 * lax.broadcasted_iota(jnp.int32, (parents, lanes), 1)).astype(F32)
    for number, at_ref in ((1, early_ref), (2, late_ref)):
        hit = jnp.where(turned_part == number, 1.0, 0.0)
        mine = jnp.where(part == number, 1.0, 0.0).astype(BF16)
        column = mm(mine, jnp.ones((slots, parents), BF16))
        row = jnp.sum(hit, axis=0, keepdims=True)
        before = (column < row) | ((column == row) & (down < along))
        rank = jnp.sum(jnp.where(before, 1.0, 0.0), axis=0, keepdims=True)
        place = mm(earlier, hit.astype(BF16)).astype(jnp.int32)
        place = jnp.where(turned_part == number, place, -1)
        dense = jnp.zeros((slots, parents), jnp.int32)
        for n in range(slots):
            dense = dense + jnp.where(place[n : n + 1] == slot, word[n : n + 1], 0)
        kind = jnp.where(slot.astype(F32) < row, dense & 127, kinds)
        source = dense >> 7
        values = [source >> 8, source & 255, kind, along[0:slots]]
        values = jnp.concatenate([value.astype(F32) for value in values], axis=0).astype(BF16)
        ranked = jnp.where(down.astype(F32) == rank, 1.0, 0.0).astype(BF16)
        moved = lax.dot_general(values, ranked, (((1,), (1,)), ((), ())), preferred_element_type=F32)
        high, low, kind, parent = [
            moved[n * slots : (n + 1) * slots].astype(jnp.int32) * 8 for n in range(4)
        ]
        reach = jnp.sum(jnp.where(column[:, :lanes] <= most, 1.0, 0.0), axis=0, keepdims=True).astype(jnp.int32)
        head = jnp.broadcast_to(reach // GROUP, (8, lanes))
        line = lax.broadcasted_iota(jnp.int32, (8, lanes), 0)
        for n in range(parents // lanes):
            head = jnp.where(line == n, parent[0:8, n * lanes : (n + 1) * lanes], head)
        at_ref[0:8, :] = head
        at = 8
        for segment in range(0, slots, SEGMENT):
            for n in range(parents // lanes):
                for value in (high * 256 + low, kind):
                    at_ref[at : at + SEGMENT, :] = value[segment : segment + SEGMENT, n * lanes : (n + 1) * lanes]
                    at += SEGMENT


def expand(sources, cells):
    lanes = cells.shape[1]
    count = sources[0].shape[0] // 8
    pairs = cells.reshape(len(sources) * count, 2, 8, lanes)
    upper = lax.broadcasted_iota(jnp.int32, (count, 8, lanes), 1) < 4
    for c, source in enumerate(sources):
        rows = source[...].astype(F32).reshape(count, 8, lanes)
        turned = pltpu.roll(rows, 4, axis=1)
        pairs[c * count : (c + 1) * count, 0] = jnp.where(upper, rows, turned)
        pairs[c * count : (c + 1) * count, 1] = jnp.where(upper, turned, rows)


def load_lists(at_any, at, sems):
    block = 2 * 128 * SEGMENT
    half = 1024 + (at.shape[0] - 1024) // 2
    loads = []
    for n, (start, end) in enumerate([(0, 1024 + block), (1024 + block, half), (half, at.shape[0])]):
        rows = pl.ds(start, end - start)
        loads.append(pltpu.make_async_copy(at_any.at[rows], at.at[rows], sems.at[n]))
        loads[-1].start()
    return loads


def add_lists(parents, slots, loads, at, cells, table8, sums):
    lanes = cells.shape[1]
    words = 128 * SEGMENT
    per_block = 128 // GROUP

    def step(length, n, carry):
        @pl.when(n == per_block)
        def _():
            loads[1].wait()

        first = 1024 + (n // per_block) * (2 * words) + (n % per_block) * GROUP
        totals = []
        for k in range(GROUP):
            total = [None, None]
            for s in range(length):
                place = first + ((s // SEGMENT) * 2 * parents * SEGMENT + (s % SEGMENT) * 128 + k)
                source = pl.multiple_of(at[place], 8)
                kind = pl.multiple_of(at[place + words], 8)
                term = cells[pl.ds(source, 8), :] * table8[pl.ds(kind, 8), :]
                total[s % 2] = term if total[s % 2] is None else total[s % 2] + term
            totals.append(total[0] + total[1] if length else jnp.zeros((8, lanes), F32))
        for k in range(GROUP):
            sums[pl.ds(pl.multiple_of(at[n * GROUP + k], 8), 8), :] = totals[k]
        return carry

    loads[0].wait()
    start = 0
    for j, length in enumerate(range(0, slots + 1, 2)):
        if length == SEGMENT + 2:
            loads[2].wait()
        end = at[parents + j]
        lax.fori_loop(start, end, functools.partial(step, length), 0)
        start = end


def early_kernel(count, parents, slots, *refs):
    sources = refs[:count]
    at_any, table8, sums, cells, at, sems = refs[count:]
    loads = load_lists(at_any, at, sems)
    expand(sources, cells)
    add_lists(parents, slots, loads, at, cells, table8, sums)


def late_kernel(count, tile_x, tile_y, slots, *refs):
    sources = refs[:count]
    (at_any, table8, early_ref, kept_ref, field_ref, fold_ref, out_hbm,
     cells, sums, lines, at, out_ref, list_sems, sems) = refs[count:]
    parents_x, parents_y = tile_x // 2, tile_y // 2
    parents = parents_x * parents_y
    lanes = table8.shape[1]
    loads = load_lists(at_any, at, list_sems)
    expand(sources, cells)
    add_lists(parents, slots, loads, at, cells, table8, sums)
    raw = (sums[...] + early_ref[...]).reshape(parents // 2, 2, 8, lanes)
    one, other = raw[:, 0], raw[:, 1]
    line = lax.broadcasted_iota(jnp.int32, one.shape, 1)
    with_real = jnp.where(line < 4, one, pltpu.roll(other, 4, axis=1))
    with_imag = jnp.where(line < 4, pltpu.roll(one, 4, axis=1), other)
    turned = jnp.where(line % 4 < 2, -pltpu.roll(with_imag, 6, axis=1), pltpu.roll(with_imag, 2, axis=1))
    lines[...] = (with_real + turned).reshape(4 * parents, lanes)
    ordered = [lines[pl.ds(place, parents, stride=4), :].astype(BF16) for place in range(4)]
    incoming = jnp.concatenate(ordered, axis=1)
    fields = [mm(incoming, fold_ref[child]) for child in range(4)]
    stores = []
    for half in range(2):
        first, size = half * parents // 2, parents // 2
        rows = slice(first, first + size)
        for child in range(4):
            mask = kept_ref[child, rows, :]
            for part in range(2):
                value = fields[child][rows, part * lanes : (part + 1) * lanes]
                value = (value + field_ref[part, child, rows, :]) * mask
                for p in range(parents_x // 2):
                    line = (2 * (half * parents_x // 2 + p) + child // 2) * tile_y + child % 2
                    out_ref[pl.ds(2 * line + part, parents_y, stride=4), :] = value[
                        p * parents_y : (p + 1) * parents_y
                    ]
        size = out_ref.shape[0] // 2
        rows = pl.ds(half * size, size)
        stores.append(pltpu.make_async_copy(out_ref.at[rows], out_hbm.at[rows], sems.at[half]))
        stores[-1].start()
    for store in stores:
        store.wait()


def swap(low, high, axis, other=None):
    count = lax.axis_size(axis)
    lows = [(i, i ^ 1) for i in range(count)]
    highs = [(i, (((i + 1) % count ^ 1) - 1) % count) for i in range(count)]
    if other is not None:
        breadth = lax.axis_size(other)
        highs = [
            (i * breadth + j, i * breadth + (j ^ 1) if i in (0, count - 1) else target * breadth + j)
            for i, target in highs
            for j in range(breadth)
        ]
    return lax.ppermute(low, axis, lows), lax.ppermute(high, axis if other is None else (axis, other), highs)


def body(
    currents, box_count, aggregate, near_blocks, low_translator, child_to_parent, coarse_list,
    coarse_kind, coarse_count, up_translator, parent_to_child, receive_map,
):
    tile_x, tile_y = box_count.shape
    boxes = tile_x * tile_y
    lanes = currents.shape[-1]
    parents_x, parents_y, slots = coarse_list.shape
    parents = parents_x * parents_y
    kinds, _, half = up_translator.shape
    wide = 2 * half
    chunks = lax.axis_size("gy")
    in_hbm = pl.BlockSpec(memory_space=pltpu.HBM)

    edge = jax.ShapeDtypeStruct((2 * tile_x, 2 * lanes), BF16)
    edge = jax.ShapeDtypeStruct((2 * tile_x, 2 * lanes), BF16)
    width = tile_y + 2 * LEFT
    live, kept, low, high, agg_near, up_near = pl.pallas_call(
        functools.partial(live_kernel, tile_x, tile_y),
        name="live",
        out_shape=[
            jax.ShapeDtypeStruct((boxes, 2 * lanes), BF16),
            jax.ShapeDtypeStruct((boxes, lanes), F32),
            edge,
            edge,
            jax.ShapeDtypeStruct((2 * lanes, 2 * lanes), BF16),
            jax.ShapeDtypeStruct((8 * lanes, wide), BF16),
        ],
        in_specs=[in_hbm] * 4,
        out_specs=vmem(6),
        scratch_shapes=[
            pltpu.VMEM((2 * boxes, lanes), BF16),
            pltpu.VMEM((tile_x, tile_y), jnp.int32),
            pltpu.VMEM((2 * boxes, lanes), F32),
            pltpu.SemaphoreType.DMA((4,)),
        ],
        compiler_params=params(10),
        cost_estimate=cost(100 * MIB, 3 * MIB),
    )(
        hbm(currents.reshape(2 * boxes, lanes)), hbm(box_count), hbm(aggregate),
        hbm(child_to_parent.reshape(8 * lanes, wide)),
    )
    coarse, pats = pl.pallas_call(
        functools.partial(parents_kernel, tile_x, tile_y),
        name="parents",
        out_shape=[
            jax.ShapeDtypeStruct((4 * parents, wide // 4), BF16),
            jax.ShapeDtypeStruct((3, tile_x * width, lanes), F32),
        ],
        in_specs=vmem(3),
        out_specs=vmem(2),
        scratch_shapes=[
            pltpu.VMEM((2, boxes, lanes), F32),
            pltpu.VMEM((4 * parents, wide // 4), F32),
        ],
        compiler_params=params(10),
        cost_estimate=cost(200 * MIB, 3 * MIB),
    )(live, agg_near, up_near)
    inner_y, outer_y = swap(low, high, "gy")
    sources = [coarse] + [
        lax.ppermute(coarse, "gy", [(i, i ^ d) for i in range(chunks)])
        for d in [chunks - 1] + list(range(1, chunks - 1))
    ]

    rim = 2 * tile_y + 8
    rim += -rim % 16
    low, high = pl.pallas_call(
        functools.partial(rims_kernel, tile_x, tile_y),
        name="rims",
        out_shape=[jax.ShapeDtypeStruct((rim, 2 * lanes), BF16)] * 2,
        in_specs=vmem(3),
        out_specs=vmem(2),
        scratch_shapes=[pltpu.VMEM((rim, 2 * lanes), F32)] * 2,
        compiler_params=params(10),
        cost_estimate=cost(1 * MIB, MIB),
    )(live, inner_y, outer_y)
    inner_x, outer_x = swap(low, high, "gx", "gy")
    live, coarse_count, _ = lax.optimization_barrier((live, coarse_count, low))

    near_rows = near_blocks.reshape(3, 6 * lanes, 2 * lanes)
    low_rows = low_translator.reshape(-1, lanes)
    pair = [jax.ShapeDtypeStruct((2, boxes, lanes), F32)] * 2
    lower, near = pl.pallas_call(
        functools.partial(local_kernel, tile_x, tile_y),
        name="local",
        out_shape=pair,
        in_specs=vmem(4),
        out_specs=vmem(2),
        scratch_shapes=[
            pltpu.VMEM((2, tile_x * width, lanes), F32),
            pltpu.VMEM(((tile_x + 2) * tile_y, 6 * lanes), BF16),
            pltpu.VMEM((3 * len(OFFSETS), 8, lanes), F32),
            pltpu.VMEM((3, tile_x, 8, lanes), F32),
        ],
        compiler_params=params(10),
        cost_estimate=cost(2000 * MIB, 5 * MIB),
    )(live, pats, near_rows, low_rows)

    table = up_translator.reshape(kinds, 2, 2, half // 2).transpose(0, 2, 1, 3).reshape(4 * kinds, half // 2)
    places = jax.ShapeDtypeStruct((8 + 2 * slots * parents // 128, 128), jnp.int32)
    early_at, late_at, table8, fold = pl.pallas_call(
        functools.partial(order_kernel, chunks, kinds, parents_x, parents_y),
        name="order",
        out_shape=[
            places,
            places,
            jax.ShapeDtypeStruct((8 * kinds + 8, half // 2), F32),
            jax.ShapeDtypeStruct((4, wide, 2 * lanes), BF16),
        ],
        in_specs=vmem(6),
        out_specs=vmem(4),
        scratch_shapes=[pltpu.VMEM((parents, 128), F32)],
        compiler_params=params(10),
        cost_estimate=cost(300 * MIB, MIB),
    )(
        coarse_list.reshape(parents, slots), coarse_kind.reshape(parents, slots), coarse_count, table,
        parent_to_child, receive_map,
    )
    early_at, late_at = early_at.reshape(-1), late_at.reshape(-1)
    anywhere = pl.BlockSpec(memory_space=pl.ANY)
    early, late = sources[:2], sources[2:]
    early_sums = pl.pallas_call(
        functools.partial(early_kernel, len(early), parents, slots),
        name="early",
        out_shape=jax.ShapeDtypeStruct((8 * parents, wide // 4), F32),
        in_specs=vmem(len(early)) + [anywhere] + vmem(1),
        out_specs=pl.BlockSpec(memory_space=pltpu.VMEM),
        scratch_shapes=[
            pltpu.VMEM((len(early) * parents * 8, wide // 4), F32),
            pltpu.SMEM(early_at.shape, jnp.int32),
            pltpu.SemaphoreType.DMA((3,)),
        ],
        compiler_params=params(10),
        cost_estimate=cost(1000 * MIB, 4 * MIB),
    )(*early, early_at, table8)
    lower, near, _ = lax.optimization_barrier((lower, near, early_sums))
    field, kept = pl.pallas_call(
        functools.partial(halos_kernel, tile_x, tile_y),
        name="halos",
        out_shape=[
            jax.ShapeDtypeStruct((2, 4, parents, lanes), F32),
            jax.ShapeDtypeStruct((4, parents, lanes), F32),
        ],
        in_specs=vmem(11),
        out_specs=vmem(2),
        scratch_shapes=[
            pltpu.VMEM((4, 4, tile_x + 16, lanes), F32),
            pltpu.VMEM((4, 4 * width, lanes), F32),
            pltpu.VMEM((tile_x, lanes), F32),
            pltpu.VMEM((2, 4, parents, lanes), F32),
        ],
        compiler_params=params(10),
        cost_estimate=cost(100 * MIB, 5 * MIB),
    )(inner_y, outer_y, inner_x, outer_x, agg_near, near_rows, low_rows, receive_map, lower, near, kept)

    out = pl.pallas_call(
        functools.partial(late_kernel, len(late), tile_x, tile_y, slots),
        name="late",
        out_shape=jax.ShapeDtypeStruct((2 * boxes, lanes), F32),
        in_specs=vmem(len(late)) + [anywhere] + vmem(5),
        out_specs=in_hbm,
        scratch_shapes=[
            pltpu.VMEM((len(late) * parents * 8, wide // 4), F32),
            pltpu.VMEM((8 * parents, wide // 4), F32),
            pltpu.VMEM((4 * parents, wide // 4), F32),
            pltpu.SMEM(late_at.shape, jnp.int32),
            pltpu.VMEM((2 * boxes, lanes), F32),
            pltpu.SemaphoreType.DMA((3,)),
            pltpu.SemaphoreType.DMA((2,)),
        ],
        compiler_params=params(16 if chunks <= 4 else 40),
        cost_estimate=cost(2000 * MIB, 8 * MIB),
    )(*late, late_at, table8, early_sums, kept, field, fold)
    return out.reshape(tile_x, tile_y, 2, lanes)


def solution(mesh):
    tiles = P("gx", "gy")
    in_specs = (tiles, tiles, P(), P(), P(), P(), tiles, tiles, tiles, P(), P(), P())
    return jax.shard_map(body, mesh=mesh, in_specs=in_specs, out_specs=tiles, check_vma=False)
```
